32 devices in a mesh: cfg: 2 (over x), space: 8 (over z, y), diag: 2 (over core).
Axes of the slice: x: 2, y: 2, z: 4, core: 2. Of those that a mesh axis runs over, the one named last changes fastest.
Arguments:
- eigvecs: bfloat16 [8, 2, 3, 128, 16, 256], P('cfg', None, None, None, ('space', 'diag')), parts along dimension 0, may hold values from -6 to 6
- gauge_links: float32 [8, 3, 2, 3, 3, 16, 256], P('cfg', None, None, None, None, ('space', 'diag')), parts along dimension 0, may hold values from -6 to 6
- momenta: int32 [4, 3], replicated, may hold values from -2 to 2
- spin_mix: float32 [16, 4, 4], replicated, may hold values from -4 to 4
- perambulators: bfloat16 [64, 4, 2, 128, 512], P(('cfg', 'space', 'diag')), parts along dimension 0, may hold values from -0.375 to 0.375
- contraction_list: int32 [32, 3], P(('space', 'diag')), may hold values from 0 to 63, as said below
Outputs:
- diagrams: bfloat16 [64, 4, 2, 128, 512], P(('cfg', 'space', 'diag')), parts along dimension 0
The draws below stay inside these ranges and needn't reach their ends.
There are 2 independent parts, one for each index of `cfg`. The reference program is written for one: setup_inputs(seed, part) draws one part's arguments, and reference() takes and returns one part's arrays. A program takes and returns all parts, laid end to end along the dimension named above; an argument that names none is the same for every part. Nothing has to cross between parts.
Inputs may be any that keep to these rules, and one draw needn't show every extreme that they name: `contraction_list`: row j is one diagram. Column 0 is an elemental item below 64, column 1 a spin structure below 16, column 2 a perambulator q with q // 2 == j // 2; each aligned group of 2 rows names each of its 2 perambulators exactly once.
All inputs are finite; a program needn't handle non-finite values.
Results may differ from the reference program's by a relative error of at most 0.0064.
Values may be sent and summed in bfloat16 or wider, within the bound.
No kernel may reach another device: no remote copies, remote signals or barrier semaphores. Data moves between devices by JAX's collectives and lax.ppermute only.
A program may use at most 128 MiB of HBM per device.

```python
import math
import jax
import jax.numpy as jnp
from jax import lax

TW = 4
NEV = 128
NCOL = 3
NSPIN = 4
NMOM = 4
NDISP = 4
NGAMMA = 16
LX = 16
LY = 16
DIAG_DEV = 2
PERAM_DEV = 2
NZ = 16
NITEM = 64
NDIAG = 32
NPERAM = 32


def draw_contraction_list(key, part):
    key_elem = jax.random.fold_in(key, 11)
    key_spin = jax.random.fold_in(key, 12)
    key_slot = jax.random.fold_in(key, 13)
    owners = NDIAG // DIAG_DEV
    element = jax.random.randint(key_elem, (NDIAG,), 0, NITEM)
    element = element.at[0].set(NITEM - 1)
    structure = jax.random.randint(key_spin, (NDIAG,), 0, NGAMMA)
    pattern = jnp.arange(DIAG_DEV) % PERAM_DEV
    slots = jax.vmap(lambda sub_key: jax.random.permutation(sub_key, pattern))(jax.random.split(key_slot, owners))
    peram_index = (jnp.arange(owners)[:, None] * PERAM_DEV + slots).reshape(NDIAG)
    return jnp.stack([element, structure, peram_index], 1).astype(jnp.int32)


def plant(entries, own_key, smallest, largest):
    spot = [jax.random.randint(jax.random.fold_in(own_key, axis), (), 0, length) for axis, length in enumerate(entries.shape)]
    main_axis = entries.shape.index(max(entries.shape))
    beside = spot[:main_axis] + [(spot[main_axis] + 1) % entries.shape[main_axis]] + spot[main_axis + 1:]
    return entries.at[tuple(spot)].set(smallest).at[tuple(beside)].set(largest)


def shard_levels(rng, shape, cuts, least, top_value):
    loudness, own = 1.0, jax.random.fold_in(rng, 6)
    for dim, shards_of in cuts:
        steps = jnp.exp(jax.random.uniform(jax.random.fold_in(own, dim), (shards_of,), jnp.float32, least / len(cuts), top_value / len(cuts)))
        loudness = loudness * jnp.repeat(steps, shape[dim] // shards_of).reshape([-1 if axis == dim else 1 for axis in range(len(shape))])
    return loudness


def normal_values(own_key, dims, spread, most, cuts=(), dtype=jnp.bfloat16):
    drawn = jax.random.normal(own_key, dims, jnp.float32) * spread
    if len(cuts) > 0:
        drawn = shard_levels(own_key, dims, cuts, -0.22, 0.18) * drawn
    return jnp.clip(drawn, min=-most, max=most).astype(dtype)


def setup_inputs(seed: int = 0, part: int = 0) -> dict:
    arg_keys = jax.random.split(jax.random.key(seed), 7)
    part_keys = jax.random.split(jax.random.fold_in(arg_keys[6], part), 7)
    return {
        "eigvecs": normal_values(part_keys[0], (TW, 2, NCOL, NEV, NZ, LX * LY), 1.0, 6.0, ((4, 16),)),
        "gauge_links": normal_values(part_keys[1], (TW, 3, 2, NCOL, NCOL, NZ, LX * LY), 0.6, 6.0, ((5, 16),), jnp.float32),
        "momenta": plant(jax.random.randint(arg_keys[2], (NMOM, 3), -2, 3), jax.random.fold_in(arg_keys[2], 1), -2, 2).astype(jnp.int32),
        "spin_mix": normal_values(arg_keys[3], (NGAMMA, NSPIN, NSPIN), 0.5, 4.0, (), jnp.float32),
        "perambulators": normal_values(part_keys[4], (NPERAM, NSPIN, 2, NEV, NSPIN * NEV), (2 * NEV) ** -0.5, 0.375, ((0, 16),)),
        "contraction_list": draw_contraction_list(jax.random.fold_in(arg_keys[6], 71), part),
    }


highest = lax.Precision.HIGHEST

def widen(value):
    return lax.optimization_barrier(value).astype(jnp.float32)

def color_apply(matrix, vector):
    real_rows = []
    imag_rows = []
    for row in range(3):
        real_part = jnp.zeros(vector.shape[2:], jnp.float32)
        imag_part = jnp.zeros(vector.shape[2:], jnp.float32)
        for column in range(3):
            mreal = matrix[0, row, column][None]
            mimag = matrix[1, row, column][None]
            real_part = real_part + mreal * vector[0, column] - mimag * vector[1, column]
            imag_part = imag_part + mreal * vector[1, column] + mimag * vector[0, column]
        real_rows.append(real_part)
        imag_rows.append(imag_part)
    return jnp.stack([jnp.stack(real_rows), jnp.stack(imag_rows)])

def color_adjoint(matrix, vector):
    real_rows = []
    imag_rows = []
    for row in range(3):
        real_part = jnp.zeros(vector.shape[2:], jnp.float32)
        imag_part = jnp.zeros(vector.shape[2:], jnp.float32)
        for column in range(3):
            mreal = matrix[0, column, row][None]
            mimag = matrix[1, column, row][None]
            real_part = real_part + mreal * vector[0, column] + mimag * vector[1, column]
            imag_part = imag_part + mreal * vector[1, column] - mimag * vector[0, column]
        real_rows.append(real_part)
        imag_rows.append(imag_part)
    return jnp.stack([jnp.stack(real_rows), jnp.stack(imag_rows)])

def neighbour(field, direction, offset, width):
    xcoord = jnp.arange(field.shape[-1]) % width
    if direction == 0:
        if offset == 1:
            return jnp.where(xcoord == width - 1, jnp.roll(field, width - 1, -1), jnp.roll(field, -1, -1))
        return jnp.where(xcoord == 0, jnp.roll(field, 1 - width, -1), jnp.roll(field, 1, -1))
    if direction == 1:
        return jnp.roll(field, -offset * width, -1)
    return jnp.roll(field, -offset, -2)

def phase_table(momenta, zcoord, plane, total_z):
    flat = jnp.arange(plane)
    xcoord = (flat % LX).astype(jnp.float32)
    ycoord = (flat // LX).astype(jnp.float32)
    moment = momenta.astype(jnp.float32)
    zvalue = zcoord.astype(jnp.float32)
    angle = 2.0 * math.pi * (moment[:, 0, None, None] * xcoord[None, None, :] / LX + moment[:, 1, None, None] * ycoord[None, None, :] / LY + moment[:, 2, None, None] * zvalue[None, :, None] / total_z)
    return (jnp.cos(angle), jnp.sin(angle))

def phase_apply(cosine, sine, vector):
    cos_part = cosine[:, None, None]
    sin_part = sine[:, None, None]
    real_part = cos_part * vector[0] - sin_part * vector[1]
    imag_part = sin_part * vector[0] + cos_part * vector[1]
    return jnp.stack([real_part, imag_part], 1).astype(jnp.bfloat16)

def reference(eigvecs, gauge_links, momenta, spin_mix, perambulators, contraction_list):
    total_z = eigvecs.shape[4]
    plane = eigvecs.shape[5]
    scale = 1.0 / math.sqrt(3 * plane * total_z)
    cosine, sine = phase_table(momenta, jnp.arange(total_z), plane, total_z)
    item_list = []
    for slice_index in range(TW):
        vector = eigvecs[slice_index].astype(jnp.float32)
        links_now = gauge_links[slice_index]
        shifted_list = [eigvecs[slice_index]]
        for direction in range(3):
            adjoint = color_adjoint(links_now[direction], vector).astype(jnp.bfloat16)
            forward = color_apply(links_now[direction], neighbour(vector, direction, 1, LX))
            backward = neighbour(widen(adjoint), direction, -1, LX)
            shifted_list.append((0.5 * (forward - backward)).astype(jnp.bfloat16))
        phased = widen(phase_apply(cosine, sine, vector))
        per_disp = []
        for shifted in shifted_list:
            wide = widen(shifted)
            rhs = jnp.stack([wide, jnp.stack([wide[1], -wide[0]])])
            per_disp.append(jnp.einsum('mpckzs,opclzs->mokl', phased, rhs, precision=highest))
        grams = jnp.stack(per_disp, 1)
        item_list.append(grams.reshape(NMOM * NDISP, 2, NEV, NEV))
    elementals = (jnp.concatenate(item_list) * scale).astype(jnp.bfloat16)

    def diagram(entry):
        chosen = elementals[entry[0]].astype(jnp.float32)
        upper_rows = jnp.concatenate([chosen[0], -chosen[1]], 1)
        lower_rows = jnp.concatenate([chosen[1], chosen[0]], 1)
        square = jnp.concatenate([upper_rows, lower_rows], 0)
        tau = perambulators[entry[2]].astype(jnp.float32).reshape(NSPIN, 2 * NEV, NSPIN * NEV)
        blocks = jnp.einsum('ab,sbc->sac', square, tau, precision=highest)
        weights = spin_mix[entry[1]].astype(jnp.float32)
        mixed = weights[:, 0, None, None] * blocks[0][None]
        for spin in range(1, NSPIN):
            mixed = mixed + weights[:, spin, None, None] * blocks[spin][None]
        return mixed.astype(jnp.bfloat16).reshape(NSPIN, 2, NEV, NSPIN * NEV)
    return lax.map(diagram, contraction_list)
```

```python
import functools
import math

import jax
import jax.numpy as jnp
from jax import lax
from jax.experimental import pallas as pl
from jax.experimental.pallas import tpu as pltpu
from jax.sharding import PartitionSpec as P

NCOL = 3
NMOM = 4
NDISP = 4
LX = 16
LY = 16
LANES = 128
ROWS = 16
SITES = ("space", "diag")
VMEM_LIMIT = 40 * 1024 * 1024


def shifted(value, axis, by):
    size = lax.axis_size(axis)
    return lax.ppermute(value, axis, [(i, (i + by) % size) for i in range(size)])


def adjoint_into(links, vector, store):
    nvec, width = vector.shape
    for lane in range(0, width, LANES):
        lanes = pl.ds(lane, LANES)
        matrix = [
            [[links(part, row, col, lanes) for col in range(NCOL)] for row in range(NCOL)]
            for part in range(2)
        ]

        def step(index, carry):
            rows = pl.ds(pl.multiple_of(index * ROWS, ROWS), ROWS)
            real = [vector.load(0, col, rows, lanes) for col in range(NCOL)]
            imag = [vector.load(1, col, rows, lanes) for col in range(NCOL)]
            for row in range(NCOL):
                real_part = imag_part = None
                for col in range(NCOL):
                    mreal = matrix[0][col][row]
                    mimag = matrix[1][col][row]
                    one = mreal * real[col] + mimag * imag[col]
                    two = mreal * imag[col] - mimag * real[col]
                    real_part = one if real_part is None else real_part + one
                    imag_part = two if imag_part is None else imag_part + two
                store(0, row, rows, lanes, real_part)
                store(1, row, rows, lanes, imag_part)
            return carry

        lax.fori_loop(0, nvec // ROWS, step, 0)


class Vectors:
    def __init__(self, ref):
        self.ref = ref
        self.shape = ref.shape[3:]

    def load(self, part, color, rows, lanes):
        return self.ref[0, part, color, rows, lanes].astype(jnp.float32)


def links_loader(ref, direction):
    return lambda part, row, col, lanes: ref[0, direction, part, row, col, :, lanes]


def adjoint_kernel(vector_ref, link_ref, out_ref):
    def store(part, row, rows, lanes, value):
        out_ref[0, part, row, rows, lanes] = value

    adjoint_into(links_loader(link_ref, 0), Vectors(vector_ref), store)


def adjoint_products(vectors, links, direction):
    slices, _, _, nvec, width = vectors.shape
    return pl.pallas_call(
        adjoint_kernel,
        grid=(slices,),
        in_specs=[
            pl.BlockSpec((1, 2, NCOL, nvec, width), lambda t: (t, 0, 0, 0, 0)),
            pl.BlockSpec((1, 1, 2, NCOL, NCOL, 1, width), lambda t: (t, direction, 0, 0, 0, 0, 0)),
        ],
        out_specs=pl.BlockSpec((1, 2, NCOL, nvec, width), lambda t: (t, 0, 0, 0, 0)),
        out_shape=jax.ShapeDtypeStruct(vectors.shape, jnp.float32),
        compiler_params=pltpu.CompilerParams(vmem_limit_bytes=VMEM_LIMIT),
        cost_estimate=pl.CostEstimate(
            flops=72 * slices * nvec * width, bytes_accessed=6 * vectors.size, transcendentals=0
        ),
        name="adjoint_products",
    )(vectors, links)


def bond_gram(item, phase_ref, coef_ref, lhs_ref, own, ahead):
    moment = (item // NDISP) % NMOM
    disp = item % NDISP
    cosine = phase_ref[moment, 0]
    sine = phase_ref[moment, 1]
    nvec = lhs_ref.shape[1] // 4
    total = None
    for color in range(NCOL):
        for part in range(2):
            value = own(part, color)
            lhs_ref[color, pl.ds(part * nvec, nvec), :] = (cosine * value).astype(jnp.bfloat16)
            lhs_ref[color, pl.ds((2 + part) * nvec, nvec), :] = (sine * value).astype(jnp.bfloat16)
        rhs = jnp.concatenate([ahead(0, color), ahead(1, color)], 0)
        term = lax.dot_general(
            lhs_ref[color], rhs, (((1,), (1,)), ((), ())), preferred_element_type=jnp.float32
        )
        total = term if total is None else total + term
    block = [[total[i * nvec : (i + 1) * nvec, j * nvec : (j + 1) * nvec] for j in range(2)] for i in range(4)]
    cos_real = block[0][0] + block[1][1]
    cos_imag = block[0][1] - block[1][0]
    sin_real = block[2][0] + block[3][1]
    sin_imag = block[2][1] - block[3][0]
    place = (moment * NDISP + disp) * 3
    direct = coef_ref[place]
    turn_cos = coef_ref[place + 1]
    turn_sin = coef_ref[place + 2]
    back_real = cos_real - sin_imag
    back_imag = cos_imag + sin_real
    real = direct * (cos_real + sin_imag) - (turn_cos * back_real - turn_sin * back_imag).T
    imag = direct * (cos_imag - sin_real) + (turn_cos * back_imag + turn_sin * back_real).T
    return real, imag


def plane_kernel(count, items_ref, coef_ref, vector_ref, link_ref, phase_ref, out_ref, own_ref, ahead_ref, lhs_ref, perm_ref):
    now = pl.program_id(0)
    nvec, width = vector_ref.shape[3:]

    @pl.when(now == 0)
    def _():
        source = lax.broadcasted_iota(jnp.int32, (width, width), 0)
        site = lax.broadcasted_iota(jnp.int32, (width, width), 1)
        xcoord = site % LX
        ycoord = (site // LX) % LY
        along_x = site - xcoord + (xcoord + 1) % LX
        along_y = site - ycoord * LX + (ycoord + 1) % LY * LX
        perm_ref[0] = (source == along_x).astype(jnp.float32).astype(jnp.bfloat16)
        perm_ref[1] = (source == along_y).astype(jnp.float32).astype(jnp.bfloat16)

    ahead_ref[0] = vector_ref[0]
    own_ref[0] = vector_ref[0].astype(jnp.float32)
    for direction in range(2):

        def store(part, row, rows, lanes, value):
            own_ref[direction + 1, part, row, rows, lanes] = value

        adjoint_into(links_loader(link_ref, direction), Vectors(vector_ref), store)
        for part in range(2):
            for color in range(NCOL):
                moved = jnp.dot(
                    vector_ref[0, part, color], perm_ref[direction], preferred_element_type=jnp.float32
                )
                ahead_ref[direction + 1, part, color] = moved.astype(jnp.bfloat16)

    @pl.loop(0, count)
    def _(row):
        item = items_ref[row]
        disp = item % NDISP

        @pl.when((item // (NMOM * NDISP) == now) & (disp != NDISP - 1))
        def _():
            real, imag = bond_gram(
                item,
                phase_ref,
                coef_ref,
                lhs_ref,
                lambda part, color: own_ref[disp, part, color],
                lambda part, color: ahead_ref[disp, part, color],
            )
            out_ref[row, 0] = real.astype(out_ref.dtype)
            out_ref[row, 1] = imag.astype(out_ref.dtype)


def plane_items(items, coef, vectors, links, phase):
    slices, _, _, nvec, width = vectors.shape
    count = items.shape[0]
    return pl.pallas_call(
        functools.partial(plane_kernel, count),
        grid_spec=pltpu.PrefetchScalarGridSpec(
            num_scalar_prefetch=2,
            grid=(slices,),
            in_specs=[
                pl.BlockSpec((1, 2, NCOL, nvec, width), lambda t, *_: (t, 0, 0, 0, 0)),
                pl.BlockSpec((1, 2, 2, NCOL, NCOL, 1, width), lambda t, *_: (t, 0, 0, 0, 0, 0, 0)),
                pl.BlockSpec((NMOM, 2, 1, width), lambda t, *_: (0, 0, 0, 0)),
            ],
            out_specs=pl.BlockSpec((count, 2, nvec, nvec), lambda t, *_: (0, 0, 0, 0)),
            scratch_shapes=[
                pltpu.VMEM((3, 2, NCOL, nvec, width), jnp.float32),
                pltpu.VMEM((3, 2, NCOL, nvec, width), jnp.bfloat16),
                pltpu.VMEM((NCOL, 4 * nvec, width), jnp.bfloat16),
                pltpu.VMEM((2, width, width), jnp.bfloat16),
            ],
        ),
        out_shape=jax.ShapeDtypeStruct((count, 2, nvec, nvec), jnp.bfloat16),
        compiler_params=pltpu.CompilerParams(vmem_limit_bytes=VMEM_LIMIT),
        cost_estimate=pl.CostEstimate(
            flops=count * 16 * nvec * nvec * NCOL * width,
            bytes_accessed=2 * vectors.size + 4 * links.size,
            transcendentals=0,
        ),
        name="plane_items",
    )(items, coef, vectors, links, phase)


def layer_kernel(count, items_ref, coef_ref, own_ref, ahead_ref, phase_ref, partial_ref, out_ref, result_ref, lhs_ref, sems):
    now = pl.program_id(0)

    def mine(row, slice_index):
        item = items_ref[row]
        return (item // (NMOM * NDISP) == slice_index) & (item % NDISP == NDISP - 1)

    @pl.loop(0, count)
    def _(row):
        @pl.when(mine(row, now))
        def _():
            real, imag = bond_gram(
                items_ref[row],
                phase_ref,
                coef_ref,
                lhs_ref,
                lambda part, color: own_ref[0, part, color],
                lambda part, color: ahead_ref[0, part, color],
            )
            result_ref[row, 0] = real.astype(result_ref.dtype)
            result_ref[row, 1] = imag.astype(result_ref.dtype)
            pltpu.make_async_copy(result_ref.at[row], out_ref.at[row], sems.at[row]).start()

    @pl.when(now == pl.num_programs(0) - 1)
    def _():
        @pl.loop(0, count)
        def _(row):
            @pl.when(items_ref[row] % NDISP == NDISP - 1)
            def _():
                pltpu.make_async_copy(result_ref.at[row], out_ref.at[row], sems.at[row]).wait()


def layer_items(items, coef, own, ahead, phase, partial):
    slices, _, _, nvec, width = own.shape
    count = items.shape[0]
    return pl.pallas_call(
        functools.partial(layer_kernel, count),
        grid_spec=pltpu.PrefetchScalarGridSpec(
            num_scalar_prefetch=2,
            grid=(slices,),
            in_specs=[
                pl.BlockSpec((1, 2, NCOL, nvec, width), lambda t, *_: (t, 0, 0, 0, 0)),
                pl.BlockSpec((1, 2, NCOL, nvec, width), lambda t, *_: (t, 0, 0, 0, 0)),
                pl.BlockSpec((NMOM, 2, 1, width), lambda t, *_: (0, 0, 0, 0)),
                pl.BlockSpec(memory_space=pl.ANY),
            ],
            out_specs=pl.BlockSpec(memory_space=pl.ANY),
            scratch_shapes=[
                pltpu.VMEM((count, 2, nvec, nvec), partial.dtype),
                pltpu.VMEM((NCOL, 4 * nvec, width), jnp.bfloat16),
                pltpu.SemaphoreType.DMA((count,)),
            ],
        ),
        out_shape=jax.ShapeDtypeStruct(partial.shape, partial.dtype),
        input_output_aliases={5: 0},
        compiler_params=pltpu.CompilerParams(vmem_limit_bytes=VMEM_LIMIT),
        cost_estimate=pl.CostEstimate(
            flops=count * 4 * nvec * nvec * NCOL * width, bytes_accessed=6 * own.size, transcendentals=0
        ),
        name="layer_items",
    )(items, coef, own, ahead, phase, partial)


def mix_kernel(slot_ref, structure_ref, weight_ref, tau_ref, out_ref):
    spins, _, nvec, width = tau_ref.shape[1:]
    base = structure_ref[pl.program_id(0)] * spins * spins
    weight = [[weight_ref[base + r * spins + s] for s in range(spins)] for r in range(spins)]

    @pl.loop(0, 2 * nvec // ROWS)
    def _(index):
        part = index // (nvec // ROWS)
        rows = pl.ds(pl.multiple_of(index % (nvec // ROWS) * ROWS, ROWS), ROWS)
        tau = [tau_ref[0, s, part, rows, :].astype(jnp.float32) for s in range(spins)]
        for r in range(spins):
            mixed = weight[r][0] * tau[0]
            for s in range(1, spins):
                mixed = mixed + weight[r][s] * tau[s]
            out_ref[0, r, part, rows, :] = mixed.astype(jnp.bfloat16)


def mixed_perambulators(slots, structures, weights, perambulators):
    block = (1,) + perambulators.shape[1:]
    count = slots.shape[0]
    return pl.pallas_call(
        mix_kernel,
        grid_spec=pltpu.PrefetchScalarGridSpec(
            num_scalar_prefetch=3,
            grid=(count,),
            in_specs=[pl.BlockSpec(block, lambda j, slot, *_: (slot[j], 0, 0, 0, 0))],
            out_specs=pl.BlockSpec(block, lambda j, *_: (j, 0, 0, 0, 0)),
        ),
        out_shape=jax.ShapeDtypeStruct((count,) + perambulators.shape[1:], jnp.bfloat16),
        compiler_params=pltpu.CompilerParams(vmem_limit_bytes=VMEM_LIMIT),
        cost_estimate=pl.CostEstimate(
            flops=8 * perambulators.size, bytes_accessed=4 * perambulators.size, transcendentals=0
        ),
        name="mixed_perambulators",
    )(slots, structures, weights, perambulators)


def diagram_kernel(chosen_ref, tau_ref, out_ref):
    spins, _, nvec, width = tau_ref.shape[1:]
    real = chosen_ref[0, 0].astype(jnp.float32)
    imag = chosen_ref[0, 1].astype(jnp.float32)
    square = jnp.concatenate(
        [jnp.concatenate([real, -imag], 1), jnp.concatenate([imag, real], 1)], 0
    ).astype(jnp.bfloat16)
    for r in range(spins):
        tau = tau_ref[0, r].reshape(2 * nvec, width)
        block = jnp.dot(square, tau, preferred_element_type=jnp.float32)
        out_ref[0, r] = block.astype(jnp.bfloat16).reshape(2, nvec, width)


def diagrams(chosen, tau):
    count, spins, _, nvec, width = tau.shape
    half = spins // 2
    block = (1, half, 2, nvec, width)
    return pl.pallas_call(
        diagram_kernel,
        grid=(count, spins // half),
        in_specs=[
            pl.BlockSpec((1, 2, nvec, nvec), lambda j, r: (j, 0, 0, 0)),
            pl.BlockSpec(block, lambda j, r: (j, r, 0, 0, 0)),
        ],
        out_specs=pl.BlockSpec(block, lambda j, r: (j, r, 0, 0, 0)),
        out_shape=jax.ShapeDtypeStruct(tau.shape, jnp.bfloat16),
        compiler_params=pltpu.CompilerParams(vmem_limit_bytes=VMEM_LIMIT),
        cost_estimate=pl.CostEstimate(
            flops=8 * nvec * nvec * width * spins * count, bytes_accessed=4 * tau.size, transcendentals=0
        ),
        name="diagrams",
    )(chosen, tau)


def phase_tables(momenta, zcoord, plane, total_z, scale):
    flat = jnp.arange(plane)
    xcoord = (flat % LX).astype(jnp.float32)
    ycoord = (flat // LX).astype(jnp.float32)
    moment = momenta.astype(jnp.float32)
    zvalue = zcoord.astype(jnp.float32)
    angle = (
        2.0
        * math.pi
        * (
            moment[:, 0, None, None] * xcoord[None, None, :] / LX
            + moment[:, 1, None, None] * ycoord[None, None, :] / LY
            + moment[:, 2, None, None] * zvalue[None, :, None] / total_z
        )
    ).reshape(moment.shape[0], 1, -1)
    table = jnp.stack([jnp.cos(angle), jnp.sin(angle)], 1)
    turn = 2.0 * math.pi * moment / jnp.array([LX, LY, total_z], jnp.float32)
    half = jnp.full_like(turn, 0.5 * scale)
    moved = jnp.stack([half, half * jnp.cos(turn), half * jnp.sin(turn)], 2)
    still = jnp.broadcast_to(jnp.array([scale, 0.0, 0.0], jnp.float32), (moment.shape[0], 1, 3))
    return table, jnp.concatenate([still, moved], 1).reshape(-1)


def body(eigvecs, gauge_links, momenta, spin_mix, perambulators, contraction_list):
    slices, _, _, nvec, depth, plane = eigvecs.shape
    devices = lax.axis_size(SITES)
    position = lax.axis_index(SITES)
    total_z = depth * devices
    width = depth * plane
    scale = 1.0 / math.sqrt(NCOL * plane * total_z)
    upper = shifted(eigvecs[:, :, :, :, :1, :], SITES, -1)
    items = lax.all_gather(contraction_list[:, 0], SITES, axis=0, tiled=True)
    zcoord = position * depth + jnp.arange(depth)
    phase, coef = phase_tables(momenta, zcoord, plane, total_z, scale)
    vectors = eigvecs.reshape(slices, 2, NCOL, nvec, width)
    links = gauge_links.reshape(slices, 3, 2, NCOL, NCOL, 1, width)
    own = adjoint_products(vectors, links, 2)
    partial = plane_items(items, coef, vectors, links, phase)
    ahead = jnp.concatenate([eigvecs[:, :, :, :, 1:, :], upper], 4).reshape(vectors.shape)
    partial = layer_items(items, coef, own, ahead, phase, partial)
    chosen = lax.psum_scatter(partial, SITES, scatter_dimension=0, tiled=True)
    slots = contraction_list[:, 2] - position * perambulators.shape[0]
    tau = mixed_perambulators(slots, contraction_list[:, 1], spin_mix.reshape(-1), perambulators)
    return diagrams(chosen, tau)


def solution(mesh):
    placed = (
        P("cfg", None, None, None, ("space", "diag"), None),
        P("cfg", None, None, None, None, ("space", "diag"), None),
        P(),
        P(),
        P(("cfg", "space", "diag"), None, None, None, None),
        P(("space", "diag"), None),
    )
    return jax.shard_map(
        body,
        mesh=mesh,
        in_specs=placed,
        out_specs=P(("cfg", "space", "diag"), None, None, None, None),
        check_vma=False,
    )
```

```python
import functools
import math

import jax
import jax.numpy as jnp
from jax import lax
from jax.experimental import pallas as pl
from jax.experimental.pallas import tpu as pltpu
from jax.sharding import PartitionSpec as P

NCOL = 3
NMOM = 4
NDISP = 4
LX = 16
LY = 16
LANES = 128
ROWS = 16
SITES = ("space", "diag")
VMEM_LIMIT = 32 * 1024 * 1024


def shifted(value, axis, by):
    size = lax.axis_size(axis)
    return lax.ppermute(value, axis, [(i, (i + by) % size) for i in range(size)])


def exchanged(value, bit):
    size = lax.axis_size(SITES)
    return lax.ppermute(value, SITES, [(i, i ^ (1 << bit)) for i in range(size)])


def color_product(matrix, real, imag, adjoint):
    rows = []
    for row in range(NCOL):
        real_part = imag_part = None
        for col in range(NCOL):
            if adjoint:
                mreal, mimag = matrix[0][col][row], matrix[1][col][row]
                one = mreal * real[col] + mimag * imag[col]
                two = mreal * imag[col] - mimag * real[col]
            else:
                mreal, mimag = matrix[0][row][col], matrix[1][row][col]
                one = mreal * real[col] - mimag * imag[col]
                two = mreal * imag[col] + mimag * real[col]
            real_part = one if real_part is None else real_part + one
            imag_part = two if imag_part is None else imag_part + two
        rows.append((real_part, imag_part))
    return rows


def color_loop(link_ref, direction, nvec, width, load, store, adjoint):
    for lane in range(0, width, LANES):
        lanes = pl.ds(lane, LANES)
        matrix = [
            [[link_ref[0, direction, part, row, col, :, lanes] for col in range(NCOL)] for row in range(NCOL)]
            for part in range(2)
        ]

        def step(index, carry):
            rows = pl.ds(pl.multiple_of(index * ROWS, ROWS), ROWS)
            real = [load(0, color, rows, lanes) for color in range(NCOL)]
            imag = [load(1, color, rows, lanes) for color in range(NCOL)]
            for color, (one, two) in enumerate(color_product(matrix, real, imag, adjoint)):
                store(0, color, rows, lanes, one)
                store(1, color, rows, lanes, two)
            return carry

        lax.fori_loop(0, nvec // ROWS, step, 0)


def fill_tables(position, total_z, plane, momenta_ref, phase_ref, turn_ref):
    width = phase_ref.shape[-1]
    flat = lax.broadcasted_iota(jnp.int32, (1, width), 1)
    xcoord = (flat % LX).astype(jnp.float32)
    ycoord = (flat % plane // LX).astype(jnp.float32)
    zcoord = (position * (width // plane) + flat // plane).astype(jnp.float32)
    for moment in range(NMOM):
        along_x = momenta_ref[moment, 0].astype(jnp.float32)
        along_y = momenta_ref[moment, 1].astype(jnp.float32)
        along_z = momenta_ref[moment, 2].astype(jnp.float32)
        angle = (
            2.0 * math.pi * (along_x * xcoord / LX + along_y * ycoord / LY + along_z * zcoord / total_z)
        )
        phase_ref[moment, 0] = jnp.cos(angle)
        phase_ref[moment, 1] = jnp.sin(angle)
        turn = jnp.full((1, turn_ref.shape[-1]), 2.0 * math.pi / total_z, jnp.float32) * along_z
        turn_ref[moment, 0] = jnp.cos(turn)
        turn_ref[moment, 1] = jnp.sin(turn)


def fill_moves(move_ref):
    width = move_ref.shape[-1]
    source = lax.broadcasted_iota(jnp.int32, (width, width), 0)
    site = lax.broadcasted_iota(jnp.int32, (width, width), 1)
    xcoord = site % LX
    ycoord = site // LX % LY
    for sign, by in enumerate((1, -1)):
        along_x = site - xcoord + (xcoord + LX + by) % LX
        along_y = site + ((ycoord + LY + by) % LY - ycoord) * LX
        move_ref[0, sign] = (source == along_x).astype(jnp.float32).astype(jnp.bfloat16)
        move_ref[1, sign] = (source == along_y).astype(jnp.float32).astype(jnp.bfloat16)


def plane_kernel(
    total_z, plane, scale,
    position_ref, momenta_ref, vector_ref, link_ref,
    item_ref, own_ref, phase_ref, turn_ref,
    ahead_ref, forward_ref, adjoint_ref, phased_ref, moved_ref, move_ref,
):
    nvec, width = vector_ref.shape[3:]

    @pl.when(pl.program_id(0) == 0)
    def _():
        fill_tables(position_ref[0], total_z, plane, momenta_ref, phase_ref, turn_ref)
        fill_moves(move_ref)

    def vector(part, color, rows, lanes):
        return vector_ref[0, part, color, rows, lanes].astype(jnp.float32)

    def own(part, color, rows, lanes, value):
        own_ref[0, part, color, rows, lanes] = value

    color_loop(link_ref, 2, nvec, width, vector, own, True)
    for color in range(NCOL):
        span = pl.ds(color * width, width)
        for part in range(2):
            moved_ref[0, pl.ds(part * nvec, nvec), span] = vector_ref[0, part, color]

        @pl.loop(0, nvec // ROWS)
        def _(index):
            rows = pl.ds(pl.multiple_of(index * ROWS, ROWS), ROWS)
            real = vector_ref[0, 0, color, rows, :].astype(jnp.float32)
            imag = vector_ref[0, 1, color, rows, :].astype(jnp.float32)
            for moment in range(NMOM):
                cosine = phase_ref[moment, 0]
                sine = phase_ref[moment, 1]
                first = pl.ds(pl.multiple_of(2 * moment * nvec + index * ROWS, ROWS), ROWS)
                second = pl.ds(pl.multiple_of((2 * moment + 1) * nvec + index * ROWS, ROWS), ROWS)
                phased_ref[first, span] = (cosine * real - sine * imag).astype(jnp.bfloat16)
                phased_ref[second, span] = (sine * real + cosine * imag).astype(jnp.bfloat16)

    for direction in range(2):
        for part in range(2):
            for color in range(NCOL):
                ahead_ref[part, color] = jnp.dot(
                    vector_ref[0, part, color], move_ref[direction, 0], preferred_element_type=jnp.float32
                )

        def ahead(part, color, rows, lanes):
            return ahead_ref[part, color, rows, lanes]

        def forward(part, color, rows, lanes, value):
            forward_ref[part, color, rows, lanes] = value

        def adjoint(part, color, rows, lanes, value):
            adjoint_ref[part, color, rows, lanes] = value.astype(jnp.bfloat16)

        color_loop(link_ref, direction, nvec, width, ahead, forward, False)
        color_loop(link_ref, direction, nvec, width, vector, adjoint, True)
        for part in range(2):
            for color in range(NCOL):
                behind = jnp.dot(
                    adjoint_ref[part, color], move_ref[direction, 1], preferred_element_type=jnp.float32
                )
                moved_ref[direction + 1, pl.ds(part * nvec, nvec), pl.ds(color * width, width)] = (
                    0.5 * (forward_ref[part, color] - behind)
                ).astype(jnp.bfloat16)

    for disp in range(NDISP - 1):
        gram = lax.dot_general(
            phased_ref[...], moved_ref[disp], (((1,), (1,)), ((), ())), preferred_element_type=jnp.float32
        )
        for moment in range(NMOM):
            start = 2 * moment * nvec
            upper = gram[start : start + nvec]
            lower = gram[start + nvec : start + 2 * nvec]
            item_ref[0, moment, disp, 0] = (scale * (upper[:, :nvec] + lower[:, nvec:])).astype(item_ref.dtype)
            item_ref[0, moment, disp, 1] = (scale * (upper[:, nvec:] - lower[:, :nvec])).astype(item_ref.dtype)


def plane_items(position, momenta, vectors, links, total_z, plane, scale):
    slices, _, _, nvec, width = vectors.shape
    color_block = (2, NCOL, nvec, width)
    return pl.pallas_call(
        functools.partial(plane_kernel, total_z, plane, scale),
        grid=(slices,),
        in_specs=[
            pl.BlockSpec(memory_space=pltpu.SMEM),
            pl.BlockSpec(memory_space=pltpu.SMEM),
            pl.BlockSpec((1,) + color_block, lambda t: (t, 0, 0, 0, 0)),
            pl.BlockSpec((1, 3, 2, NCOL, NCOL, 1, width), lambda t: (t, 0, 0, 0, 0, 0, 0)),
        ],
        out_specs=[
            pl.BlockSpec((1, NMOM, NDISP - 1, 2, nvec, nvec), lambda t: (t, 0, 0, 0, 0, 0)),
            pl.BlockSpec((1,) + color_block, lambda t: (t, 0, 0, 0, 0)),
            pl.BlockSpec((NMOM, 2, 1, width), lambda t: (0, 0, 0, 0)),
            pl.BlockSpec((NMOM, 2, 1, nvec), lambda t: (0, 0, 0, 0)),
        ],
        out_shape=[
            jax.ShapeDtypeStruct((slices, NMOM, NDISP - 1, 2, nvec, nvec), jnp.bfloat16),
            jax.ShapeDtypeStruct(vectors.shape, jnp.float32),
            jax.ShapeDtypeStruct((NMOM, 2, 1, width), jnp.float32),
            jax.ShapeDtypeStruct((NMOM, 2, 1, nvec), jnp.float32),
        ],
        scratch_shapes=[
            pltpu.VMEM(color_block, jnp.float32),
            pltpu.VMEM(color_block, jnp.float32),
            pltpu.VMEM(color_block, jnp.bfloat16),
            pltpu.VMEM((NMOM * 2 * nvec, NCOL * width), jnp.bfloat16),
            pltpu.VMEM((NDISP - 1, 2 * nvec, NCOL * width), jnp.bfloat16),
            pltpu.VMEM((2, 2, width, width), jnp.bfloat16),
        ],
        compiler_params=pltpu.CompilerParams(vmem_limit_bytes=VMEM_LIMIT),
        cost_estimate=pl.CostEstimate(
            flops=slices * 16 * NMOM * nvec * nvec * NCOL * width,
            bytes_accessed=6 * vectors.size + 4 * links.size,
            transcendentals=0,
        ),
        name="plane_items",
    )(position, momenta, vectors, links)


def layer_kernel(
    slot, slots, scale,
    position_ref, rows_ref, item_ref, own_ref, ahead_ref, phase_ref, turn_ref,
    keep_ref, send_ref, lhs_ref,
):
    nvec, width = own_ref.shape[3:]
    sites = keep_ref.shape[0]

    def one(target, place, item):
        slice_index = item // (NMOM * NDISP)
        moment = item // NDISP % NMOM
        disp = item % NDISP

        @pl.when(disp != NDISP - 1)
        def _():
            target[place] = item_ref[slice_index, moment, disp].astype(target.dtype)

        @pl.when(disp == NDISP - 1)
        def _():
            cosine = phase_ref[moment, 0]
            sine = phase_ref[moment, 1]
            for color in range(NCOL):
                span = pl.ds(color * width, width)
                for part in range(2):
                    value = own_ref[slice_index, part, color]
                    lhs_ref[pl.ds(part * nvec, nvec), span] = (cosine * value).astype(jnp.bfloat16)
                    lhs_ref[pl.ds((2 + part) * nvec, nvec), span] = (sine * value).astype(jnp.bfloat16)
            rhs = jnp.concatenate(
                [
                    jnp.concatenate([ahead_ref[slice_index, part, color] for color in range(NCOL)], 1)
                    for part in range(2)
                ],
                0,
            )
            gram = lax.dot_general(
                lhs_ref[...], rhs, (((1,), (1,)), ((), ())), preferred_element_type=jnp.float32
            )
            block = [
                [gram[i * nvec : (i + 1) * nvec, j * nvec : (j + 1) * nvec] for j in range(2)]
                for i in range(4)
            ]
            cos_real = block[0][0] + block[1][1]
            cos_imag = block[0][1] - block[1][0]
            sin_real = block[2][0] + block[3][1]
            sin_imag = block[2][1] - block[3][0]
            half = 0.5 * scale
            turn_cos = half * turn_ref[moment, 0]
            turn_sin = half * turn_ref[moment, 1]
            back_real = cos_real - sin_imag
            back_imag = cos_imag + sin_real
            real = half * (cos_real + sin_imag) - (turn_cos * back_real - turn_sin * back_imag).T
            imag = half * (cos_imag - sin_real) + (turn_cos * back_imag + turn_sin * back_real).T
            target[place, 0] = real.astype(target.dtype)
            target[place, 1] = imag.astype(target.dtype)

    @pl.loop(0, sites)
    def _(place):
        for core, target in enumerate((keep_ref, send_ref)):
            device = position_ref[0] ^ (2 * place + core)
            one(target, place, rows_ref[device, slot * slots])


def layer_items(slot, slots, position, rows, item, own, ahead, phase, turn, scale):
    slices, _, _, nvec, width = own.shape
    shape = jax.ShapeDtypeStruct((rows.shape[0] // 2, 2, nvec, nvec), jnp.bfloat16)
    whole = pl.BlockSpec(memory_space=pltpu.VMEM)
    scalar = pl.BlockSpec(memory_space=pltpu.SMEM)
    return pl.pallas_call(
        functools.partial(layer_kernel, slot, slots, scale),
        in_specs=[scalar, scalar, whole, whole, whole, whole, whole],
        out_specs=[whole, whole],
        out_shape=[shape, shape],
        scratch_shapes=[pltpu.VMEM((4 * nvec, NCOL * width), jnp.bfloat16)],
        compiler_params=pltpu.CompilerParams(vmem_limit_bytes=VMEM_LIMIT),
        cost_estimate=pl.CostEstimate(
            flops=rows.shape[0] * 4 * nvec * nvec * NCOL * width,
            bytes_accessed=2 * own.size,
            transcendentals=0,
        ),
        name="layer_items",
    )(position, rows, item, own, ahead, phase, turn)


def summed(keep, send, order):
    bits = len(order)
    tail = keep.shape[1:]
    keep = keep.reshape((2,) * bits + tail)
    arrived = exchanged(send, 0).reshape(keep.shape)
    left = list(range(bits, 0, -1))
    for bit in order:
        axis = left.index(bit)
        left.remove(bit)
        near = [lax.index_in_dim(value, 0, axis, keepdims=False) for value in (keep, arrived)]
        far = [lax.index_in_dim(value, 1, axis, keepdims=False) for value in (keep, arrived)]
        outgoing = (far[0].astype(jnp.float32) + far[1].astype(jnp.float32)).astype(jnp.bfloat16)
        arrived = exchanged(outgoing, bit)
        keep = near[0].astype(jnp.float32) + near[1].astype(jnp.float32)
    return keep, arrived


def mix_kernel(slot_ref, structure_ref, weight_ref, tau_ref, out_ref):
    spins, _, nvec, width = tau_ref.shape[1:]
    base = structure_ref[pl.program_id(0)] * spins * spins
    weight = [[weight_ref[base + r * spins + s] for s in range(spins)] for r in range(spins)]

    @pl.loop(0, 2 * nvec // ROWS)
    def _(index):
        part = index // (nvec // ROWS)
        rows = pl.ds(pl.multiple_of(index % (nvec // ROWS) * ROWS, ROWS), ROWS)
        tau = [tau_ref[0, s, part, rows, :].astype(jnp.float32) for s in range(spins)]
        for r in range(spins):
            mixed = weight[r][0] * tau[0]
            for s in range(1, spins):
                mixed = mixed + weight[r][s] * tau[s]
            out_ref[0, r, part, rows, :] = mixed.astype(jnp.bfloat16)


def mixed_perambulators(slots, structures, weights, perambulators):
    block = (1,) + perambulators.shape[1:]
    count = slots.shape[0]
    return pl.pallas_call(
        mix_kernel,
        grid_spec=pltpu.PrefetchScalarGridSpec(
            num_scalar_prefetch=3,
            grid=(count,),
            in_specs=[pl.BlockSpec(block, lambda j, slot, *_: (slot[j], 0, 0, 0, 0))],
            out_specs=pl.BlockSpec(block, lambda j, *_: (j, 0, 0, 0, 0)),
        ),
        out_shape=jax.ShapeDtypeStruct((count,) + perambulators.shape[1:], jnp.bfloat16),
        compiler_params=pltpu.CompilerParams(vmem_limit_bytes=VMEM_LIMIT),
        cost_estimate=pl.CostEstimate(
            flops=8 * perambulators.size, bytes_accessed=4 * perambulators.size, transcendentals=0
        ),
        name="mixed_perambulators",
    )(slots, structures, weights, perambulators)


def diagram_kernel(count, *refs):
    pairs, tau_ref, out_ref = refs[: 2 * count], refs[-2], refs[-1]
    spins, _, nvec, width = tau_ref.shape[1:]

    def one(keep_ref, arrived_ref):
        real, imag = (keep_ref[part] + arrived_ref[part].astype(jnp.float32) for part in range(2))
        square = jnp.concatenate(
            [jnp.concatenate([real, -imag], 1), jnp.concatenate([imag, real], 1)], 0
        ).astype(jnp.bfloat16)
        for r in range(spins):
            tau = tau_ref[0, r].reshape(2 * nvec, width)
            block = jnp.dot(square, tau, preferred_element_type=jnp.float32)
            out_ref[0, r] = block.astype(jnp.bfloat16).reshape(2, nvec, width)

    for index in range(count):

        @pl.when(pl.program_id(0) == index)
        def _():
            one(pairs[2 * index], pairs[2 * index + 1])


def diagrams(pairs, tau):
    count, spins, _, nvec, width = tau.shape
    half = spins // 2
    block = (1, half, 2, nvec, width)
    small = pl.BlockSpec((2, nvec, nvec), lambda j, r: (0, 0, 0))
    return pl.pallas_call(
        functools.partial(diagram_kernel, count),
        grid=(count, spins // half),
        in_specs=[small] * (2 * count) + [pl.BlockSpec(block, lambda j, r: (j, r, 0, 0, 0))],
        out_specs=pl.BlockSpec(block, lambda j, r: (j, r, 0, 0, 0)),
        out_shape=jax.ShapeDtypeStruct(tau.shape, jnp.bfloat16),
        compiler_params=pltpu.CompilerParams(vmem_limit_bytes=VMEM_LIMIT),
        cost_estimate=pl.CostEstimate(
            flops=8 * nvec * nvec * width * spins * count, bytes_accessed=4 * tau.size, transcendentals=0
        ),
        name="diagrams",
    )(*[value for pair in pairs for value in pair], tau)


def body(eigvecs, gauge_links, momenta, spin_mix, perambulators, contraction_list):
    slices, _, _, nvec, depth, plane = eigvecs.shape
    devices = lax.axis_size(SITES)
    position = lax.axis_index(SITES)
    bits = devices.bit_length() - 1
    count, columns = contraction_list.shape
    total_z = depth * devices
    width = depth * plane
    scale = 1.0 / math.sqrt(NCOL * plane * total_z)
    upper = shifted(eigvecs[:, :, :, :, :1, :], SITES, -1)
    padded = jnp.pad(contraction_list.reshape(1, -1), ((0, 0), (0, LANES - count * columns)))
    rows = lax.all_gather(padded, SITES, axis=0, tiled=True)
    place = position.reshape(1)
    vectors = eigvecs.reshape(slices, 2, NCOL, nvec, width)
    links = gauge_links.reshape(slices, 3, 2, NCOL, NCOL, 1, width)
    item, own, phase, turn = plane_items(place, momenta, vectors, links, total_z, plane, scale)
    ahead = jnp.concatenate([eigvecs[:, :, :, :, 1:, :], upper], 4).reshape(vectors.shape)
    pairs = []
    for slot in range(count):
        keep, send = layer_items(slot, columns, place, rows, item, own, ahead, phase, turn, scale)
        order = [1 + (slot + step) % (bits - 1) for step in range(bits - 1)]
        pairs.append(summed(keep, send, order))
    slots = contraction_list[:, 2] - position * perambulators.shape[0]
    tau = mixed_perambulators(slots, contraction_list[:, 1], spin_mix.reshape(-1), perambulators)
    return diagrams(pairs, tau)


def solution(mesh):
    placed = (
        P("cfg", None, None, None, ("space", "diag"), None),
        P("cfg", None, None, None, None, ("space", "diag"), None),
        P(),
        P(),
        P(("cfg", "space", "diag"), None, None, None, None),
        P(("space", "diag"), None),
    )
    return jax.shard_map(
        body,
        mesh=mesh,
        in_specs=placed,
        out_specs=P(("cfg", "space", "diag"), None, None, None, None),
        check_vma=False,
    )
```

```python
import functools
import math

import jax
import jax.numpy as jnp
from jax import lax
from jax.experimental import pallas as pl
from jax.experimental.pallas import tpu as pltpu
from jax.sharding import PartitionSpec as P

NCOL = 3
NMOM = 4
NDISP = 4
LX = 16
LY = 16
LANES = 128
ROWS = 16
SITES = ("space", "diag")
VMEM_LIMIT = 32 * 1024 * 1024


def shifted(value, axis, by):
    size = lax.axis_size(axis)
    return lax.ppermute(value, axis, [(i, (i + by) % size) for i in range(size)])


def exchanged(value, mask):
    size = lax.axis_size(SITES)
    return lax.ppermute(value, SITES, [(i, i ^ mask) for i in range(size)])


def gathered(rows, token):
    bits = lax.axis_size(SITES).bit_length() - 1
    parts = [rows[None]]
    for low in range(0, bits, 2):
        value = parts[0] if len(parts) == 1 else jnp.concatenate(parts)
        value, token = lax.optimization_barrier((value, token))
        parts = [value] + [exchanged(value, step << low) for step in range(1, 1 << min(2, bits - low))]
    return parts, token


def color_product(matrix, real, imag, adjoint):
    rows = []
    for row in range(NCOL):
        real_part = imag_part = None
        for col in range(NCOL):
            if adjoint:
                mreal, mimag = matrix[0][col][row], matrix[1][col][row]
                one = mreal * real[col] + mimag * imag[col]
                two = mreal * imag[col] - mimag * real[col]
            else:
                mreal, mimag = matrix[0][row][col], matrix[1][row][col]
                one = mreal * real[col] - mimag * imag[col]
                two = mreal * imag[col] + mimag * real[col]
            real_part = one if real_part is None else real_part + one
            imag_part = two if imag_part is None else imag_part + two
        rows.append((real_part, imag_part))
    return rows


def color_loop(link, nvec, width, load, store, adjoint):
    height = math.gcd(nvec, 2 * ROWS)
    for lane in range(0, width, LANES):
        lanes = pl.ds(lane, LANES)
        matrix = [
            [[link(part, row, col, lanes) for col in range(NCOL)] for row in range(NCOL)] for part in range(2)
        ]

        def step(index, carry):
            rows = pl.ds(pl.multiple_of(index * height, height), height)
            real = [load(0, color, rows, lanes) for color in range(NCOL)]
            imag = [load(1, color, rows, lanes) for color in range(NCOL)]
            for color, (one, two) in enumerate(color_product(matrix, real, imag, adjoint)):
                store(0, color, rows, lanes, one)
                store(1, color, rows, lanes, two)
            return carry

        lax.fori_loop(0, nvec // height, step, 0)


def fill_tables(position, total_z, plane, momenta_ref, phase_ref, turn_ref):
    width = phase_ref.shape[-1]
    flat = lax.broadcasted_iota(jnp.int32, (1, width), 1)
    xcoord = (flat % LX).astype(jnp.float32)
    ycoord = (flat % plane // LX).astype(jnp.float32)
    zcoord = (position * (width // plane) + flat // plane).astype(jnp.float32)
    for moment in range(NMOM):
        along_x = momenta_ref[moment, 0].astype(jnp.float32)
        along_y = momenta_ref[moment, 1].astype(jnp.float32)
        along_z = momenta_ref[moment, 2].astype(jnp.float32)
        angle = (
            2.0 * math.pi * (along_x * xcoord / LX + along_y * ycoord / LY + along_z * zcoord / total_z)
        )
        phase_ref[moment, 0] = jnp.cos(angle)
        phase_ref[moment, 1] = jnp.sin(angle)
        turn = jnp.full((1, turn_ref.shape[-1]), 2.0 * math.pi / total_z, jnp.float32) * along_z
        turn_ref[moment, 0] = jnp.cos(turn)
        turn_ref[moment, 1] = jnp.sin(turn)


def fill_moves(move_ref):
    width = move_ref.shape[-1]
    source = lax.broadcasted_iota(jnp.int32, (width, width), 0)
    site = lax.broadcasted_iota(jnp.int32, (width, width), 1)
    xcoord = site % LX
    ycoord = site // LX % LY
    for sign, by in enumerate((1, -1)):
        along_x = site - xcoord + (xcoord + LX + by) % LX
        along_y = site + ((ycoord + LY + by) % LY - ycoord) * LX
        move_ref[0, sign] = (source == along_x).astype(jnp.float32).astype(jnp.bfloat16)
        move_ref[1, sign] = (source == along_y).astype(jnp.float32).astype(jnp.bfloat16)


def adjoint_kernel(vector_ref, link_ref, out_ref):
    nvec, width = vector_ref.shape[3:]

    def link(part, row, col, lanes):
        return link_ref[0, 0, part, row, col, :, lanes]

    def vector(part, color, rows, lanes):
        return vector_ref[0, part, color, rows, lanes].astype(jnp.float32)

    def store(part, color, rows, lanes, value):
        out_ref[0, part, color, rows, lanes] = value

    color_loop(link, nvec, width, vector, store, True)


def adjoint_products(vectors, links, direction):
    slices, _, _, nvec, width = vectors.shape
    block = pl.BlockSpec((1, 2, NCOL, nvec, width), lambda t: (t, 0, 0, 0, 0))
    return pl.pallas_call(
        adjoint_kernel,
        grid=(slices,),
        in_specs=[
            block,
            pl.BlockSpec((1, 1, 2, NCOL, NCOL, 1, width), lambda t: (t, direction, 0, 0, 0, 0, 0)),
        ],
        out_specs=block,
        out_shape=jax.ShapeDtypeStruct(vectors.shape, jnp.float32),
        compiler_params=pltpu.CompilerParams(vmem_limit_bytes=VMEM_LIMIT),
        cost_estimate=pl.CostEstimate(
            flops=72 * slices * nvec * width, bytes_accessed=6 * vectors.size, transcendentals=0
        ),
        name="adjoint_products",
    )(vectors, links)


def plane_kernel(
    total_z, plane, scale,
    position_ref, momenta_in, vector_in, link_in,
    item_ref, phase_ref, turn_ref,
    momenta_ref, vector_ref, link_ref,
    ahead_ref, forward_ref, adjoint_ref, phased_ref, moved_ref, move_ref, momenta_sem, sems,
):
    now = pl.program_id(0)
    slices, _, _, nvec, width = vector_ref.shape

    def copies(index):
        return (
            pltpu.make_async_copy(vector_in.at[index], vector_ref.at[index], sems.at[0, index]),
            pltpu.make_async_copy(link_in.at[index], link_ref.at[index], sems.at[1, index]),
        )

    @pl.when(now == 0)
    def _():
        moments = pltpu.make_async_copy(momenta_in, momenta_ref, momenta_sem)
        moments.start()
        for index in range(slices):
            for copy in copies(index):
                copy.start()
        fill_moves(move_ref)
        moments.wait()
        fill_tables(position_ref[0], total_z, plane, momenta_ref, phase_ref, turn_ref)

    for copy in copies(now):
        copy.wait()

    def vector(part, color, rows, lanes):
        return vector_ref[now, part, color, rows, lanes].astype(jnp.float32)

    for color in range(NCOL):
        span = pl.ds(color * width, width)
        for part in range(2):
            moved_ref[0, pl.ds(part * nvec, nvec), span] = vector_ref[now, part, color]

        @pl.loop(0, nvec // ROWS)
        def _(index):
            rows = pl.ds(pl.multiple_of(index * ROWS, ROWS), ROWS)
            real = vector_ref[now, 0, color, rows, :].astype(jnp.float32)
            imag = vector_ref[now, 1, color, rows, :].astype(jnp.float32)
            for moment in range(NMOM):
                cosine = phase_ref[moment, 0]
                sine = phase_ref[moment, 1]
                first = pl.ds(pl.multiple_of(2 * moment * nvec + index * ROWS, ROWS), ROWS)
                second = pl.ds(pl.multiple_of((2 * moment + 1) * nvec + index * ROWS, ROWS), ROWS)
                phased_ref[first, span] = (cosine * real - sine * imag).astype(jnp.bfloat16)
                phased_ref[second, span] = (sine * real + cosine * imag).astype(jnp.bfloat16)

    for direction in range(2):
        for part in range(2):
            for color in range(NCOL):
                ahead_ref[part, color] = jnp.dot(
                    vector_ref[now, part, color], move_ref[direction, 0], preferred_element_type=jnp.float32
                )

        def link(part, row, col, lanes):
            return link_ref[now, direction, part, row, col, :, lanes]

        def ahead(part, color, rows, lanes):
            return ahead_ref[part, color, rows, lanes]

        def forward(part, color, rows, lanes, value):
            forward_ref[part, color, rows, lanes] = value

        def adjoint(part, color, rows, lanes, value):
            adjoint_ref[part, color, rows, lanes] = value.astype(jnp.bfloat16)

        color_loop(link, nvec, width, ahead, forward, False)
        color_loop(link, nvec, width, vector, adjoint, True)
        for part in range(2):
            for color in range(NCOL):
                behind = jnp.dot(
                    adjoint_ref[part, color], move_ref[direction, 1], preferred_element_type=jnp.float32
                )
                moved_ref[direction + 1, pl.ds(part * nvec, nvec), pl.ds(color * width, width)] = (
                    0.5 * (forward_ref[part, color] - behind)
                ).astype(jnp.bfloat16)

    for disp in range(NDISP - 1):
        gram = lax.dot_general(
            phased_ref[...], moved_ref[disp], (((1,), (1,)), ((), ())), preferred_element_type=jnp.float32
        )
        for moment in range(NMOM):
            start = 2 * moment * nvec
            upper = gram[start : start + nvec]
            lower = gram[start + nvec : start + 2 * nvec]
            item_ref[0, moment, disp, 0] = (scale * (upper[:, :nvec] + lower[:, nvec:])).astype(item_ref.dtype)
            item_ref[0, moment, disp, 1] = (scale * (upper[:, nvec:] - lower[:, :nvec])).astype(item_ref.dtype)


def plane_items(position, momenta, vectors, links, total_z, plane, scale):
    slices, _, _, nvec, width = vectors.shape
    color_block = (2, NCOL, nvec, width)
    return pl.pallas_call(
        functools.partial(plane_kernel, total_z, plane, scale),
        grid=(slices,),
        in_specs=[pl.BlockSpec(memory_space=pltpu.SMEM)] + [pl.BlockSpec(memory_space=pltpu.HBM)] * 3,
        out_specs=[
            pl.BlockSpec((1, NMOM, NDISP - 1, 2, nvec, nvec), lambda t: (t, 0, 0, 0, 0, 0)),
            pl.BlockSpec((NMOM, 2, 1, width), lambda t: (0, 0, 0, 0)),
            pl.BlockSpec((NMOM, 2, 1, nvec), lambda t: (0, 0, 0, 0)),
        ],
        out_shape=[
            jax.ShapeDtypeStruct((slices, NMOM, NDISP - 1, 2, nvec, nvec), jnp.bfloat16),
            jax.ShapeDtypeStruct((NMOM, 2, 1, width), jnp.float32),
            jax.ShapeDtypeStruct((NMOM, 2, 1, nvec), jnp.float32),
        ],
        scratch_shapes=[
            pltpu.SMEM(momenta.shape, jnp.int32),
            pltpu.VMEM(vectors.shape, jnp.bfloat16),
            pltpu.VMEM(links.shape, jnp.float32),
            pltpu.VMEM(color_block, jnp.float32),
            pltpu.VMEM(color_block, jnp.float32),
            pltpu.VMEM(color_block, jnp.bfloat16),
            pltpu.VMEM((NMOM * 2 * nvec, NCOL * width), jnp.bfloat16),
            pltpu.VMEM((NDISP - 1, 2 * nvec, NCOL * width), jnp.bfloat16),
            pltpu.VMEM((2, 2, width, width), jnp.bfloat16),
            pltpu.SemaphoreType.DMA,
            pltpu.SemaphoreType.DMA((2, slices)),
        ],
        compiler_params=pltpu.CompilerParams(vmem_limit_bytes=VMEM_LIMIT),
        cost_estimate=pl.CostEstimate(
            flops=slices * 16 * NMOM * nvec * nvec * NCOL * width,
            bytes_accessed=6 * vectors.size + 4 * links.size,
            transcendentals=0,
        ),
        name="plane_items",
    )(position, momenta, vectors, links)


def layer_kernel(slot, groups, scale, *refs):
    rows_refs = refs[:groups]
    item_ref, own_ref, ahead_ref, phase_ref, turn_ref, keep_ref, send_ref, lhs_ref, wanted_ref = refs[groups:]
    nvec, width = own_ref.shape[3:]
    sites = keep_ref.shape[0]
    for index, rows_ref in enumerate(rows_refs):
        for row in range(rows_ref.shape[0]):
            wanted_ref[index * rows_ref.shape[0] + row] = rows_ref[row, slot, 0]

    def one(target, place, item):
        slice_index = item // (NMOM * NDISP)
        moment = item // NDISP % NMOM
        disp = item % NDISP

        @pl.when(disp != NDISP - 1)
        def _():
            target[place] = item_ref[slice_index, moment, disp].astype(target.dtype)

        @pl.when(disp == NDISP - 1)
        def _():
            cosine = phase_ref[moment, 0]
            sine = phase_ref[moment, 1]
            for color in range(NCOL):
                span = pl.ds(color * width, width)
                for part in range(2):
                    value = own_ref[slice_index, part, color]
                    lhs_ref[pl.ds(part * nvec, nvec), span] = (cosine * value).astype(jnp.bfloat16)
                    lhs_ref[pl.ds((2 + part) * nvec, nvec), span] = (sine * value).astype(jnp.bfloat16)
            rhs = jnp.concatenate(
                [
                    jnp.concatenate([ahead_ref[slice_index, part, color] for color in range(NCOL)], 1)
                    for part in range(2)
                ],
                0,
            )
            gram = lax.dot_general(
                lhs_ref[...], rhs, (((1,), (1,)), ((), ())), preferred_element_type=jnp.float32
            )
            block = [
                [gram[i * nvec : (i + 1) * nvec, j * nvec : (j + 1) * nvec] for j in range(2)]
                for i in range(4)
            ]
            cos_real = block[0][0] + block[1][1]
            cos_imag = block[0][1] - block[1][0]
            sin_real = block[2][0] + block[3][1]
            sin_imag = block[2][1] - block[3][0]
            half = 0.5 * scale
            turn_cos = half * turn_ref[moment, 0]
            turn_sin = half * turn_ref[moment, 1]
            back_real = cos_real - sin_imag
            back_imag = cos_imag + sin_real
            real = half * (cos_real + sin_imag) - (turn_cos * back_real - turn_sin * back_imag).T
            imag = half * (cos_imag - sin_real) + (turn_cos * back_imag + turn_sin * back_real).T
            target[place, 0] = real.astype(target.dtype)
            target[place, 1] = imag.astype(target.dtype)

    @pl.loop(0, sites)
    def _(place):
        for core, target in enumerate((keep_ref, send_ref)):
            one(target, place, wanted_ref[2 * place + core])


def layer_items(slot, rows, item, own, ahead, phase, turn, scale):
    slices, _, _, nvec, width = own.shape
    devices = sum(part.shape[0] for part in rows)
    shape = jax.ShapeDtypeStruct((devices // 2, 2, nvec, nvec), jnp.bfloat16)
    whole = pl.BlockSpec(memory_space=pltpu.VMEM)
    scalar = pl.BlockSpec(memory_space=pltpu.SMEM)
    return pl.pallas_call(
        functools.partial(layer_kernel, slot, len(rows), scale),
        in_specs=[scalar] * len(rows) + [whole] * 5,
        out_specs=[whole, whole],
        out_shape=[shape, shape],
        scratch_shapes=[
            pltpu.VMEM((4 * nvec, NCOL * width), jnp.bfloat16),
            pltpu.SMEM((devices,), jnp.int32),
        ],
        compiler_params=pltpu.CompilerParams(vmem_limit_bytes=VMEM_LIMIT),
        cost_estimate=pl.CostEstimate(
            flops=devices * 4 * nvec * nvec * NCOL * width,
            bytes_accessed=2 * own.size,
            transcendentals=0,
        ),
        name="layer_items",
    )(*rows, item, own, ahead, phase, turn)


def rounded_sum(values):
    total = values[0].astype(jnp.float32)
    for value in values[1:]:
        total = total + value.astype(jnp.float32)
    return total.astype(jnp.bfloat16)


def halved(keep, send, order):
    entries = list(range(keep.shape[0]))
    terms = [(entries, keep), (entries, exchanged(send, 1))]
    for bit in order[:-2]:
        far = [r for r in entries if r >> (bit - 1) & 1]
        entries = [r for r in entries if r not in far]
        terms.append((entries, exchanged(rounded_sum([picked(term, far) for term in terms]), 1 << bit)))
    return terms


def picked(term, wanted):
    entries, value = term
    at = [entries.index(r) for r in wanted]
    run = 1
    while run < len(at) and at[run] == at[0] + run:
        run += 1
    step = at[run] - at[0] if run < len(at) else value.shape[0]
    tail = value.shape[1:]
    if len(at) == run:
        return lax.slice_in_dim(value, at[0], at[0] + run)
    blocks = value.reshape((value.shape[0] // step, step) + tail)
    return lax.slice_in_dim(blocks, at[0] % step, at[0] % step + run, axis=1).reshape((len(at),) + tail)


def outgoing(terms):
    return {r: rounded_sum([picked(term, [r]) for term in terms]) for r in terms[-1][0] if r}


def mix_kernel(slot_ref, structure_ref, weight_ref, tau_ref, out_ref):
    spins, _, nvec, width = tau_ref.shape[1:]
    base = structure_ref[pl.program_id(0)] * spins * spins
    weight = [[weight_ref[base + r * spins + s] for s in range(spins)] for r in range(spins)]

    @pl.loop(0, 2 * nvec // ROWS)
    def _(index):
        part = index // (nvec // ROWS)
        rows = pl.ds(pl.multiple_of(index % (nvec // ROWS) * ROWS, ROWS), ROWS)
        tau = [tau_ref[0, s, part, rows, :].astype(jnp.float32) for s in range(spins)]
        for r in range(spins):
            mixed = weight[r][0] * tau[0]
            for s in range(1, spins):
                mixed = mixed + weight[r][s] * tau[s]
            out_ref[0, r, part, rows, :] = mixed.astype(jnp.bfloat16)


def mixed_perambulators(slots, structures, weights, perambulators):
    block = (1,) + perambulators.shape[1:]
    count = slots.shape[0]
    return pl.pallas_call(
        mix_kernel,
        grid_spec=pltpu.PrefetchScalarGridSpec(
            num_scalar_prefetch=3,
            grid=(count,),
            in_specs=[pl.BlockSpec(block, lambda j, slot, *_: (slot[j], 0, 0, 0, 0))],
            out_specs=pl.BlockSpec(block, lambda j, *_: (j, 0, 0, 0, 0)),
        ),
        out_shape=jax.ShapeDtypeStruct((count,) + perambulators.shape[1:], jnp.bfloat16),
        compiler_params=pltpu.CompilerParams(vmem_limit_bytes=VMEM_LIMIT),
        cost_estimate=pl.CostEstimate(
            flops=8 * perambulators.size, bytes_accessed=4 * perambulators.size, transcendentals=0
        ),
        name="mixed_perambulators",
    )(slots, structures, weights, perambulators)


def diagram_kernel(count, *refs):
    terms = refs[: -4]
    tau_ref, out_ref, block_ref, sems = refs[-4:]
    spins, _, nvec, width = tau_ref.shape[1:]
    each = len(terms) // count

    def copy(index, r):
        return pltpu.make_async_copy(block_ref.at[index, r], out_ref.at[index, r], sems.at[index, r])

    for index in range(count):
        real, imag = (
            sum(ref[0, part].astype(jnp.float32) for ref in terms[index * each : (index + 1) * each])
            for part in range(2)
        )
        square = jnp.concatenate(
            [jnp.concatenate([real, -imag], 1), jnp.concatenate([imag, real], 1)], 0
        ).astype(jnp.bfloat16)
        for r in range(spins):
            tau = tau_ref[index, r].reshape(2 * nvec, width)
            block = jnp.dot(square, tau, preferred_element_type=jnp.float32)
            block_ref[index, r] = block.astype(jnp.bfloat16).reshape(2, nvec, width)
            copy(index, r).start()
    for index in range(count):
        for r in range(spins):
            copy(index, r).wait()


def diagrams(terms, tau):
    count, spins, _, nvec, width = tau.shape
    whole = pl.BlockSpec(memory_space=pltpu.VMEM)
    flat = [value for group in terms for value in group]
    return pl.pallas_call(
        functools.partial(diagram_kernel, count),
        in_specs=[whole] * (len(flat) + 1),
        out_specs=pl.BlockSpec(memory_space=pltpu.HBM),
        out_shape=jax.ShapeDtypeStruct(tau.shape, jnp.bfloat16),
        scratch_shapes=[
            pltpu.VMEM(tau.shape, jnp.bfloat16),
            pltpu.SemaphoreType.DMA((count, spins)),
        ],
        compiler_params=pltpu.CompilerParams(vmem_limit_bytes=VMEM_LIMIT),
        cost_estimate=pl.CostEstimate(
            flops=8 * nvec * nvec * width * spins * count, bytes_accessed=4 * tau.size, transcendentals=0
        ),
        name="diagrams",
    )(*flat, tau)


def body(eigvecs, gauge_links, momenta, spin_mix, perambulators, contraction_list):
    slices, _, _, nvec, depth, plane = eigvecs.shape
    devices = lax.axis_size(SITES)
    position = lax.axis_index(SITES)
    bits = devices.bit_length() - 1
    total_z = depth * devices
    width = depth * plane
    scale = 1.0 / math.sqrt(NCOL * plane * total_z)
    upper = shifted(eigvecs[:, :, :, :, :1, :], SITES, -1)
    place = position.reshape(1)
    vectors = eigvecs.reshape(slices, 2, NCOL, nvec, width)
    links = gauge_links.reshape(slices, 3, 2, NCOL, NCOL, 1, width)
    own = adjoint_products(vectors, links, 2)
    rows, place = gathered(contraction_list, place)
    item, phase, turn = plane_items(place, momenta, vectors, links, total_z, plane, scale)
    ahead = jnp.concatenate([eigvecs[:, :, :, :, 1:, :], upper], 4).reshape(vectors.shape)
    slots = contraction_list[:, 2] - position * perambulators.shape[0]
    tau = mixed_perambulators(slots, contraction_list[:, 1], spin_mix.reshape(-1), perambulators)
    terms = []
    for slot in range(contraction_list.shape[0]):
        keep, send = layer_items(slot, rows, item, own, ahead, phase, turn, scale)
        order = [1 + (slot + step) % (bits - 1) for step in range(bits - 1)]
        terms.append(halved(keep, send, order))
    parts = []
    for group in terms:
        leaving = outgoing(group)
        if group is terms[-1]:
            leaving, tau = lax.optimization_barrier((leaving, tau))
        parts.append([value for _, value in group] + [exchanged(value, 2 * r) for r, value in leaving.items()])
    return diagrams(parts, tau)


def solution(mesh):
    placed = (
        P("cfg", None, None, None, ("space", "diag"), None),
        P("cfg", None, None, None, None, ("space", "diag"), None),
        P(),
        P(),
        P(("cfg", "space", "diag"), None, None, None, None),
        P(("space", "diag"), None),
    )
    return jax.shard_map(
        body,
        mesh=mesh,
        in_specs=placed,
        out_specs=P(("cfg", "space", "diag"), None, None, None, None),
        check_vma=False,
    )
```

```python
import functools
import math

import jax
import jax.numpy as jnp
from jax import lax
from jax.experimental import pallas as pl
from jax.experimental.pallas import tpu as pltpu
from jax.sharding import PartitionSpec as P

NCOL = 3
NMOM = 4
NDISP = 4
LX = 16
LY = 16
LANES = 128
ROWS = 16
SITES = ("space", "diag")
VMEM_LIMIT = 32 * 1024 * 1024


def shifted(value, axis, by):
    size = lax.axis_size(axis)
    return lax.ppermute(value, axis, [(i, (i + by) % size) for i in range(size)])


def exchanged(value, mask):
    size = lax.axis_size(SITES)
    return lax.ppermute(value, SITES, [(i, i ^ mask) for i in range(size)])


def gathered(rows, token):
    bits = lax.axis_size(SITES).bit_length() - 1
    value = rows[None]
    for low in range(0, bits, 2):
        if low:
            value, token = lax.optimization_barrier((value, token)) if low == 2 else (value, token)
        steps = range(1, 1 << min(2, bits - low))
        value = jnp.concatenate([value] + [exchanged(value, step << low) for step in steps])
    return value, token


def color_product(matrix, real, imag, adjoint):
    rows = []
    for row in range(NCOL):
        real_part = imag_part = None
        for col in range(NCOL):
            if adjoint:
                mreal, mimag = matrix[0][col][row], matrix[1][col][row]
                one = mreal * real[col] + mimag * imag[col]
                two = mreal * imag[col] - mimag * real[col]
            else:
                mreal, mimag = matrix[0][row][col], matrix[1][row][col]
                one = mreal * real[col] - mimag * imag[col]
                two = mreal * imag[col] + mimag * real[col]
            real_part = one if real_part is None else real_part + one
            imag_part = two if imag_part is None else imag_part + two
        rows.append((real_part, imag_part))
    return rows


def color_loop(link, nvec, width, load, store, adjoint):
    height = math.gcd(nvec, 2 * ROWS)
    for lane in range(0, width, LANES):
        lanes = pl.ds(lane, LANES)
        matrix = [
            [[link(part, row, col, lanes) for col in range(NCOL)] for row in range(NCOL)] for part in range(2)
        ]
        for start in range(0, nvec, height):
            rows = pl.ds(start, height)
            real = [load(0, color, rows, lanes) for color in range(NCOL)]
            imag = [load(1, color, rows, lanes) for color in range(NCOL)]
            for color, (one, two) in enumerate(color_product(matrix, real, imag, adjoint)):
                store(0, color, rows, lanes, one)
                store(1, color, rows, lanes, two)


def fill_tables(position, total_z, plane, momenta_ref, phase_ref, turn_ref):
    width = phase_ref.shape[-1]
    flat = lax.broadcasted_iota(jnp.int32, (1, width), 1)
    xcoord = (flat % LX).astype(jnp.float32)
    ycoord = (flat % plane // LX).astype(jnp.float32)
    zcoord = (position * (width // plane) + flat // plane).astype(jnp.float32)
    for moment in range(NMOM):
        along_x = momenta_ref[moment, 0].astype(jnp.float32)
        along_y = momenta_ref[moment, 1].astype(jnp.float32)
        along_z = momenta_ref[moment, 2].astype(jnp.float32)
        angle = (
            2.0 * math.pi * (along_x * xcoord / LX + along_y * ycoord / LY + along_z * zcoord / total_z)
        )
        phase_ref[moment, 0] = jnp.cos(angle)
        phase_ref[moment, 1] = jnp.sin(angle)
        turn = jnp.full((1, turn_ref.shape[-1]), 2.0 * math.pi / total_z, jnp.float32) * along_z
        turn_ref[moment, 0] = jnp.cos(turn)
        turn_ref[moment, 1] = jnp.sin(turn)


def fill_moves(move_ref):
    width = move_ref.shape[-1]
    source = lax.broadcasted_iota(jnp.int32, (width, width), 0)
    site = lax.broadcasted_iota(jnp.int32, (width, width), 1)
    xcoord = site % LX
    ycoord = site // LX % LY
    for sign, by in enumerate((1, -1)):
        along_x = site - xcoord + (xcoord + LX + by) % LX
        along_y = site + ((ycoord + LY + by) % LY - ycoord) * LX
        move_ref[0, sign] = (source == along_x).astype(jnp.float32).astype(jnp.bfloat16)
        move_ref[1, sign] = (source == along_y).astype(jnp.float32).astype(jnp.bfloat16)


def plane_kernel(
    total_z, plane, scale,
    position_ref, momenta_in, vector_in, link_in,
    item_ref, own_ref, phase_ref, turn_ref,
    momenta_ref, vector_ref, link_ref,
    ahead_x_ref, ahead_y_ref, behind_x_ref, behind_y_ref, adjoint_x_ref, adjoint_y_ref,
    phased_ref, still_ref, moved_x_ref, moved_y_ref, move_ref, momenta_sem, sems,
):
    now = pl.program_id(0)
    slices, _, _, nvec, width = vector_ref.shape

    def copies(index):
        return (
            pltpu.make_async_copy(vector_in.at[index], vector_ref.at[index], sems.at[0, index]),
            pltpu.make_async_copy(link_in.at[index], link_ref.at[index], sems.at[1, index]),
        )

    @pl.when(now == 0)
    def _():
        moments = pltpu.make_async_copy(momenta_in, momenta_ref, momenta_sem)
        moments.start()
        for index in range(slices):
            for copy in copies(index):
                copy.start()
        fill_moves(move_ref)
        moments.wait()
        fill_tables(position_ref[0], total_z, plane, momenta_ref, phase_ref, turn_ref)

    for copy in copies(now):
        copy.wait()

    def linker(direction):
        return lambda part, row, col, lanes: link_ref[now, direction, part, row, col, :, lanes]

    def vector(part, color, rows, lanes):
        return vector_ref[now, part, color, rows, lanes].astype(jnp.float32)

    def gram(moved_ref, disp):
        product = lax.dot_general(
            phased_ref[...], moved_ref[...], (((1,), (1,)), ((), ())), preferred_element_type=jnp.float32
        )
        for moment in range(NMOM):
            start = 2 * moment * nvec
            upper = product[start : start + nvec]
            lower = product[start + nvec : start + 2 * nvec]
            item_ref[0, moment, disp, 0] = (scale * (upper[:, :nvec] + lower[:, nvec:])).astype(item_ref.dtype)
            item_ref[0, moment, disp, 1] = (scale * (upper[:, nvec:] - lower[:, :nvec])).astype(item_ref.dtype)

    flat = vector_ref[now].reshape(2 * NCOL * nvec, width)
    for direction, ahead_ref in enumerate((ahead_x_ref, ahead_y_ref)):
        ahead_ref[...] = jnp.dot(
            flat, move_ref[direction, 0], preferred_element_type=jnp.float32
        ).reshape(ahead_ref.shape)

    for color in range(NCOL):
        span = pl.ds(color * width, width)
        for part in range(2):
            still_ref[pl.ds(part * nvec, nvec), span] = vector_ref[now, part, color]
        for start in range(0, nvec, ROWS):
            real = vector_ref[now, 0, color, pl.ds(start, ROWS), :].astype(jnp.float32)
            imag = vector_ref[now, 1, color, pl.ds(start, ROWS), :].astype(jnp.float32)
            for moment in range(NMOM):
                cosine = phase_ref[moment, 0]
                sine = phase_ref[moment, 1]
                first = 2 * moment * nvec + start
                phased_ref[pl.ds(first, ROWS), span] = (cosine * real - sine * imag).astype(jnp.bfloat16)
                phased_ref[pl.ds(first + nvec, ROWS), span] = (sine * real + cosine * imag).astype(jnp.bfloat16)
    gram(still_ref, 0)

    for direction, (adjoint_ref, behind_ref) in enumerate(
        ((adjoint_x_ref, behind_x_ref), (adjoint_y_ref, behind_y_ref))
    ):

        def adjoint(part, color, rows, lanes, value):
            adjoint_ref[part, color, rows, lanes] = value.astype(jnp.bfloat16)

        color_loop(linker(direction), nvec, width, vector, adjoint, True)
        behind_ref[...] = jnp.dot(
            adjoint_ref[...].reshape(2 * NCOL * nvec, width),
            move_ref[direction, 1],
            preferred_element_type=jnp.float32,
        ).reshape(behind_ref.shape)

    for direction, (ahead_ref, behind_ref, moved_ref) in enumerate(
        ((ahead_x_ref, behind_x_ref, moved_x_ref), (ahead_y_ref, behind_y_ref, moved_y_ref))
    ):

        def ahead(part, color, rows, lanes):
            return ahead_ref[part, color, rows, lanes]

        def forward(part, color, rows, lanes, value):
            moved_ref[
                pl.ds(part * nvec + rows.start, rows.size), pl.ds(color * width + lanes.start, lanes.size)
            ] = (0.5 * (value - behind_ref[part, color, rows, lanes])).astype(jnp.bfloat16)

        color_loop(linker(direction), nvec, width, ahead, forward, False)
        gram(moved_ref, direction + 1)

    def own(part, color, rows, lanes, value):
        own_ref[0, part, color, rows, lanes] = value

    color_loop(linker(2), nvec, width, vector, own, True)


def plane_items(position, momenta, vectors, links, total_z, plane, scale):
    slices, _, _, nvec, width = vectors.shape
    color_block = (2, NCOL, nvec, width)
    return pl.pallas_call(
        functools.partial(plane_kernel, total_z, plane, scale),
        grid=(slices,),
        in_specs=[pl.BlockSpec(memory_space=pltpu.SMEM)] + [pl.BlockSpec(memory_space=pltpu.HBM)] * 3,
        out_specs=[
            pl.BlockSpec((1, NMOM, NDISP - 1, 2, nvec, nvec), lambda t: (t, 0, 0, 0, 0, 0)),
            pl.BlockSpec((1,) + color_block, lambda t: (t, 0, 0, 0, 0)),
            pl.BlockSpec((NMOM, 2, 1, width), lambda t: (0, 0, 0, 0)),
            pl.BlockSpec((NMOM, 2, 1, nvec), lambda t: (0, 0, 0, 0)),
        ],
        out_shape=[
            jax.ShapeDtypeStruct((slices, NMOM, NDISP - 1, 2, nvec, nvec), jnp.bfloat16),
            jax.ShapeDtypeStruct(vectors.shape, jnp.float32),
            jax.ShapeDtypeStruct((NMOM, 2, 1, width), jnp.float32),
            jax.ShapeDtypeStruct((NMOM, 2, 1, nvec), jnp.float32),
        ],
        scratch_shapes=[
            pltpu.SMEM(momenta.shape, jnp.int32),
            pltpu.VMEM(vectors.shape, jnp.bfloat16),
            pltpu.VMEM(links.shape, jnp.float32),
        ]
        + [pltpu.VMEM(color_block, jnp.float32)] * 4
        + [pltpu.VMEM(color_block, jnp.bfloat16)] * 2
        + [pltpu.VMEM((NMOM * 2 * nvec, NCOL * width), jnp.bfloat16)]
        + [pltpu.VMEM((2 * nvec, NCOL * width), jnp.bfloat16)] * 3
        + [
            pltpu.VMEM((2, 2, width, width), jnp.bfloat16),
            pltpu.SemaphoreType.DMA,
            pltpu.SemaphoreType.DMA((2, slices)),
        ],
        compiler_params=pltpu.CompilerParams(vmem_limit_bytes=VMEM_LIMIT),
        cost_estimate=pl.CostEstimate(
            flops=slices * 16 * NMOM * nvec * nvec * NCOL * width,
            bytes_accessed=6 * vectors.size + 4 * links.size,
            transcendentals=0,
        ),
        name="plane_items",
    )(position, momenta, vectors, links)


def layer_kernel(
    slot, scale, rows_ref, item_ref, own_ref, ahead_ref, phase_ref, turn_ref, keep_ref, send_ref, lhs_ref
):
    nvec, width = own_ref.shape[3:]
    sites = keep_ref.shape[0]

    def one(target, place, item):
        slice_index = item // (NMOM * NDISP)
        moment = item // NDISP % NMOM
        disp = item % NDISP

        @pl.when(disp != NDISP - 1)
        def _():
            target[place] = item_ref[slice_index, moment, disp].astype(target.dtype)

        @pl.when(disp == NDISP - 1)
        def _():
            cosine = phase_ref[moment, 0]
            sine = phase_ref[moment, 1]
            for color in range(NCOL):
                span = pl.ds(color * width, width)
                for part in range(2):
                    value = own_ref[slice_index, part, color]
                    lhs_ref[pl.ds(part * nvec, nvec), span] = (cosine * value).astype(jnp.bfloat16)
                    lhs_ref[pl.ds((2 + part) * nvec, nvec), span] = (sine * value).astype(jnp.bfloat16)
            rhs = jnp.concatenate(
                [
                    jnp.concatenate([ahead_ref[slice_index, part, color] for color in range(NCOL)], 1)
                    for part in range(2)
                ],
                0,
            )
            gram = lax.dot_general(
                lhs_ref[...], rhs, (((1,), (1,)), ((), ())), preferred_element_type=jnp.float32
            )
            block = [
                [gram[i * nvec : (i + 1) * nvec, j * nvec : (j + 1) * nvec] for j in range(2)]
                for i in range(4)
            ]
            cos_real = block[0][0] + block[1][1]
            cos_imag = block[0][1] - block[1][0]
            sin_real = block[2][0] + block[3][1]
            sin_imag = block[2][1] - block[3][0]
            half = 0.5 * scale
            turn_cos = half * turn_ref[moment, 0]
            turn_sin = half * turn_ref[moment, 1]
            back_real = cos_real - sin_imag
            back_imag = cos_imag + sin_real
            real = half * (cos_real + sin_imag) - (turn_cos * back_real - turn_sin * back_imag).T
            imag = half * (cos_imag - sin_real) + (turn_cos * back_imag + turn_sin * back_real).T
            target[place, 0] = real.astype(target.dtype)
            target[place, 1] = imag.astype(target.dtype)

    @pl.loop(0, sites)
    def _(place):
        for core, target in enumerate((keep_ref, send_ref)):
            one(target, place, rows_ref[2 * place + core, slot, 0])


def layer_items(slot, rows, item, own, ahead, phase, turn, scale):
    slices, _, _, nvec, width = own.shape
    devices = rows.shape[0]
    shape = jax.ShapeDtypeStruct((devices // 2, 2, nvec, nvec), jnp.bfloat16)
    whole = pl.BlockSpec(memory_space=pltpu.VMEM)
    scalar = pl.BlockSpec(memory_space=pltpu.SMEM)
    return pl.pallas_call(
        functools.partial(layer_kernel, slot, scale),
        in_specs=[scalar] + [whole] * 5,
        out_specs=[whole, whole],
        out_shape=[shape, shape],
        scratch_shapes=[pltpu.VMEM((4 * nvec, NCOL * width), jnp.bfloat16)],
        compiler_params=pltpu.CompilerParams(vmem_limit_bytes=VMEM_LIMIT),
        cost_estimate=pl.CostEstimate(
            flops=devices * 4 * nvec * nvec * NCOL * width,
            bytes_accessed=2 * own.size,
            transcendentals=0,
        ),
        name="layer_items",
    )(rows, item, own, ahead, phase, turn)


def rounded_sum(values):
    total = values[0].astype(jnp.float32)
    for value in values[1:]:
        total = total + value.astype(jnp.float32)
    return total.astype(jnp.bfloat16)


def halved(keep, send, order):
    entries = list(range(keep.shape[0]))
    terms = [(entries, keep), (entries, exchanged(send, 1))]
    for bit in order[:-2]:
        far = [r for r in entries if r >> (bit - 1) & 1]
        entries = [r for r in entries if r not in far]
        terms.append((entries, exchanged(rounded_sum([picked(term, far) for term in terms]), 1 << bit)))
    return terms


def picked(term, wanted):
    entries, value = term
    at = [entries.index(r) for r in wanted]
    run = 1
    while run < len(at) and at[run] == at[0] + run:
        run += 1
    step = at[run] - at[0] if run < len(at) else value.shape[0]
    tail = value.shape[1:]
    if len(at) == run:
        return lax.slice_in_dim(value, at[0], at[0] + run)
    blocks = value.reshape((value.shape[0] // step, step) + tail)
    return lax.slice_in_dim(blocks, at[0] % step, at[0] % step + run, axis=1).reshape((len(at),) + tail)


def outgoing(terms):
    return {r: rounded_sum([picked(term, [r]) for term in terms]) for r in terms[-1][0] if r}


def mix_kernel(slot_ref, structure_ref, weight_ref, tau_ref, out_ref):
    spins, _, nvec, width = tau_ref.shape[1:]
    base = structure_ref[pl.program_id(0)] * spins * spins
    weight = [[weight_ref[base + r * spins + s] for s in range(spins)] for r in range(spins)]

    @pl.loop(0, 2 * nvec // ROWS)
    def _(index):
        part = index // (nvec // ROWS)
        rows = pl.ds(pl.multiple_of(index % (nvec // ROWS) * ROWS, ROWS), ROWS)
        tau = [tau_ref[0, s, part, rows, :].astype(jnp.float32) for s in range(spins)]
        for r in range(spins):
            mixed = weight[r][0] * tau[0]
            for s in range(1, spins):
                mixed = mixed + weight[r][s] * tau[s]
            out_ref[0, r, part, rows, :] = mixed.astype(jnp.bfloat16)


def mixed_perambulators(slots, structures, weights, perambulators):
    block = (1,) + perambulators.shape[1:]
    count = slots.shape[0]
    return pl.pallas_call(
        mix_kernel,
        grid_spec=pltpu.PrefetchScalarGridSpec(
            num_scalar_prefetch=3,
            grid=(count,),
            in_specs=[pl.BlockSpec(block, lambda j, slot, *_: (slot[j], 0, 0, 0, 0))],
            out_specs=pl.BlockSpec(block, lambda j, *_: (j, 0, 0, 0, 0)),
        ),
        out_shape=jax.ShapeDtypeStruct((count,) + perambulators.shape[1:], jnp.bfloat16),
        compiler_params=pltpu.CompilerParams(vmem_limit_bytes=VMEM_LIMIT),
        cost_estimate=pl.CostEstimate(
            flops=8 * perambulators.size, bytes_accessed=4 * perambulators.size, transcendentals=0
        ),
        name="mixed_perambulators",
    )(slots, structures, weights, perambulators)


def diagram_kernel(count, *refs):
    terms = refs[: -4]
    tau_ref, out_ref, block_ref, sems = refs[-4:]
    spins, _, nvec, width = tau_ref.shape[1:]
    each = len(terms) // count

    def copy(index, r):
        return pltpu.make_async_copy(block_ref.at[index, r], out_ref.at[index, r], sems.at[index, r])

    for index in range(count):
        real, imag = (
            sum(ref[0, part].astype(jnp.float32) for ref in terms[index * each : (index + 1) * each])
            for part in range(2)
        )
        square = jnp.concatenate(
            [jnp.concatenate([real, -imag], 1), jnp.concatenate([imag, real], 1)], 0
        ).astype(jnp.bfloat16)
        for r in range(spins):
            tau = tau_ref[index, r].reshape(2 * nvec, width)
            block = jnp.dot(square, tau, preferred_element_type=jnp.float32)
            block_ref[index, r] = block.astype(jnp.bfloat16).reshape(2, nvec, width)
            copy(index, r).start()
    for index in range(count):
        for r in range(spins):
            copy(index, r).wait()


def diagrams(terms, tau):
    count, spins, _, nvec, width = tau.shape
    whole = pl.BlockSpec(memory_space=pltpu.VMEM)
    flat = [value for group in terms for value in group]
    return pl.pallas_call(
        functools.partial(diagram_kernel, count),
        in_specs=[whole] * (len(flat) + 1),
        out_specs=pl.BlockSpec(memory_space=pltpu.HBM),
        out_shape=jax.ShapeDtypeStruct(tau.shape, jnp.bfloat16),
        scratch_shapes=[
            pltpu.VMEM(tau.shape, jnp.bfloat16),
            pltpu.SemaphoreType.DMA((count, spins)),
        ],
        compiler_params=pltpu.CompilerParams(vmem_limit_bytes=VMEM_LIMIT),
        cost_estimate=pl.CostEstimate(
            flops=8 * nvec * nvec * width * spins * count, bytes_accessed=4 * tau.size, transcendentals=0
        ),
        name="diagrams",
    )(*flat, tau)


def body(eigvecs, gauge_links, momenta, spin_mix, perambulators, contraction_list):
    slices, _, _, nvec, depth, plane = eigvecs.shape
    devices = lax.axis_size(SITES)
    position = lax.axis_index(SITES)
    bits = devices.bit_length() - 1
    total_z = depth * devices
    width = depth * plane
    scale = 1.0 / math.sqrt(NCOL * plane * total_z)
    place = position.reshape(1)
    rows, (after, place) = gathered(contraction_list, (eigvecs, place))
    upper = shifted(after[:, :, :, :, :1, :], SITES, -1)
    vectors = eigvecs.reshape(slices, 2, NCOL, nvec, width)
    links = gauge_links.reshape(slices, 3, 2, NCOL, NCOL, 1, width)
    item, own, phase, turn = plane_items(place, momenta, vectors, links, total_z, plane, scale)
    ahead = jnp.concatenate([eigvecs[:, :, :, :, 1:, :], upper], 4).reshape(vectors.shape)
    slots = contraction_list[:, 2] - position * perambulators.shape[0]
    tau = mixed_perambulators(slots, contraction_list[:, 1], spin_mix.reshape(-1), perambulators)
    terms = []
    for slot in range(contraction_list.shape[0]):
        keep, send = layer_items(slot, rows, item, own, ahead, phase, turn, scale)
        order = [1 + (slot + step) % (bits - 1) for step in range(bits - 1)]
        terms.append(halved(keep, send, order))
    parts = []
    for group in terms:
        leaving = outgoing(group)
        if group is terms[-1]:
            leaving, tau = lax.optimization_barrier((leaving, tau))
        parts.append([value for _, value in group] + [exchanged(value, 2 * r) for r, value in leaving.items()])
    return diagrams(parts, tau)


def solution(mesh):
    placed = (
        P("cfg", None, None, None, ("space", "diag"), None),
        P("cfg", None, None, None, None, ("space", "diag"), None),
        P(),
        P(),
        P(("cfg", "space", "diag"), None, None, None, None),
        P(("space", "diag"), None),
    )
    return jax.shard_map(
        body,
        mesh=mesh,
        in_specs=placed,
        out_specs=P(("cfg", "space", "diag"), None, None, None, None),
        check_vma=False,
    )
```

```python
import functools
import math

import jax
import jax.numpy as jnp
from jax import lax
from jax.experimental import pallas as pl
from jax.experimental.pallas import tpu as pltpu
from jax.sharding import PartitionSpec as P

NCOL = 3
NMOM = 4
NDISP = 4
LX = 16
LY = 16
LANES = 128
ROWS = 16
SITES = ("space", "diag")
MIB = 1024 * 1024


def shifted(value, axis, by):
    size = lax.axis_size(axis)
    return lax.ppermute(value, axis, [(i, (i + by) % size) for i in range(size)])


def exchanged(value, mask):
    size = lax.axis_size(SITES)
    return lax.ppermute(value, SITES, [(i, i ^ mask) for i in range(size)])


def gathered(rows, token):
    bits = lax.axis_size(SITES).bit_length() - 1
    value = rows[None]
    for low in range(0, bits, 2):
        if low:
            value, token = lax.optimization_barrier((value, token)) if low == 2 else (value, token)
        steps = range(1, 1 << min(2, bits - low))
        value = jnp.concatenate([value] + [exchanged(value, step << low) for step in steps])
    return value, token


def color_product(matrix, real, imag, adjoint):
    rows = []
    for row in range(NCOL):
        real_part = imag_part = None
        for col in range(NCOL):
            if adjoint:
                mreal, mimag = matrix[0][col][row], matrix[1][col][row]
                one = mreal * real[col] + mimag * imag[col]
                two = mreal * imag[col] - mimag * real[col]
            else:
                mreal, mimag = matrix[0][row][col], matrix[1][row][col]
                one = mreal * real[col] - mimag * imag[col]
                two = mreal * imag[col] + mimag * real[col]
            real_part = one if real_part is None else real_part + one
            imag_part = two if imag_part is None else imag_part + two
        rows.append((real_part, imag_part))
    return rows


def color_loop(link, nvec, width, load, store, adjoint):
    height = math.gcd(nvec, 2 * ROWS)
    for lane in range(0, width, LANES):
        lanes = pl.ds(lane, LANES)
        matrix = [
            [[link(part, row, col, lanes) for col in range(NCOL)] for row in range(NCOL)] for part in range(2)
        ]
        for start in range(0, nvec, height):
            rows = pl.ds(start, height)
            real = [load(0, color, rows, lanes) for color in range(NCOL)]
            imag = [load(1, color, rows, lanes) for color in range(NCOL)]
            for color, (one, two) in enumerate(color_product(matrix, real, imag, adjoint)):
                store(0, color, rows, lanes, one)
                store(1, color, rows, lanes, two)


def fill_tables(position, total_z, plane, momenta_ref, phase_ref, turn_ref):
    width = phase_ref.shape[-1]
    flat = lax.broadcasted_iota(jnp.int32, (1, width), 1)
    xcoord = (flat % LX).astype(jnp.float32)
    ycoord = (flat % plane // LX).astype(jnp.float32)
    zcoord = (position * (width // plane) + flat // plane).astype(jnp.float32)
    for moment in range(NMOM):
        along_x = momenta_ref[moment, 0].astype(jnp.float32)
        along_y = momenta_ref[moment, 1].astype(jnp.float32)
        along_z = momenta_ref[moment, 2].astype(jnp.float32)
        angle = (
            2.0 * math.pi * (along_x * xcoord / LX + along_y * ycoord / LY + along_z * zcoord / total_z)
        )
        phase_ref[moment, 0] = jnp.cos(angle)
        phase_ref[moment, 1] = jnp.sin(angle)
        turn = jnp.full((1, turn_ref.shape[-1]), 2.0 * math.pi / total_z, jnp.float32) * along_z
        turn_ref[moment, 0] = jnp.cos(turn)
        turn_ref[moment, 1] = jnp.sin(turn)


def fill_moves(move_ref):
    width = move_ref.shape[-1]
    source = lax.broadcasted_iota(jnp.int32, (width, width), 0)
    site = lax.broadcasted_iota(jnp.int32, (width, width), 1)
    xcoord = site % LX
    ycoord = site // LX % LY
    for sign, by in enumerate((1, -1)):
        along_x = site - xcoord + (xcoord + LX + by) % LX
        along_y = site + ((ycoord + LY + by) % LY - ycoord) * LX
        move_ref[0, sign] = (source == along_x).astype(jnp.float32).astype(jnp.bfloat16)
        move_ref[1, sign] = (source == along_y).astype(jnp.float32).astype(jnp.bfloat16)


def adjoint_kernel(vector_ref, link_ref, out_ref):
    nvec, width = vector_ref.shape[3:]

    def link(part, row, col, lanes):
        return link_ref[0, 0, part, row, col, :, lanes]

    def vector(part, color, rows, lanes):
        return vector_ref[0, part, color, rows, lanes].astype(jnp.float32)

    def store(part, color, rows, lanes, value):
        out_ref[0, part, color, rows, lanes] = value

    color_loop(link, nvec, width, vector, store, True)


def adjoint_products(vectors, links, direction):
    slices, _, _, nvec, width = vectors.shape
    block = pl.BlockSpec((1, 2, NCOL, nvec, width), lambda t: (t, 0, 0, 0, 0))
    return pl.pallas_call(
        adjoint_kernel,
        grid=(slices,),
        in_specs=[
            block,
            pl.BlockSpec((1, 1, 2, NCOL, NCOL, 1, width), lambda t: (t, direction, 0, 0, 0, 0, 0)),
        ],
        out_specs=block,
        out_shape=jax.ShapeDtypeStruct(vectors.shape, jnp.float32),
        compiler_params=pltpu.CompilerParams(vmem_limit_bytes=8 * MIB),
        cost_estimate=pl.CostEstimate(
            flops=72 * slices * nvec * width, bytes_accessed=6 * vectors.size, transcendentals=0
        ),
        name="adjoint_products",
    )(vectors, links)


def plane_kernel(
    total_z, plane, scale,
    position_ref, momenta_in, vector_in, link_in,
    item_ref, phase_ref, turn_ref,
    momenta_ref, vector_ref, link_ref,
    ahead_x_ref, ahead_y_ref, behind_x_ref, behind_y_ref, adjoint_x_ref, adjoint_y_ref,
    phased_ref, still_ref, moved_x_ref, moved_y_ref, move_ref, momenta_sem, sems,
):
    now = pl.program_id(0)
    slices, _, _, nvec, width = vector_ref.shape

    def copies(index):
        return (
            pltpu.make_async_copy(vector_in.at[index], vector_ref.at[index], sems.at[0, index]),
            pltpu.make_async_copy(link_in.at[index], link_ref.at[index], sems.at[1, index]),
        )

    @pl.when(now == 0)
    def _():
        moments = pltpu.make_async_copy(momenta_in, momenta_ref, momenta_sem)
        moments.start()
        for index in range(slices):
            for copy in copies(index):
                copy.start()
        fill_moves(move_ref)
        moments.wait()
        fill_tables(position_ref[0], total_z, plane, momenta_ref, phase_ref, turn_ref)

    for copy in copies(now):
        copy.wait()

    def linker(direction):
        return lambda part, row, col, lanes: link_ref[now, direction, part, row, col, :, lanes]

    def vector(part, color, rows, lanes):
        return vector_ref[now, part, color, rows, lanes].astype(jnp.float32)

    def gram(moved_ref, disp):
        product = lax.dot_general(
            phased_ref[...], moved_ref[...], (((1,), (1,)), ((), ())), preferred_element_type=jnp.float32
        )
        for moment in range(NMOM):
            start = 2 * moment * nvec
            upper = product[start : start + nvec]
            lower = product[start + nvec : start + 2 * nvec]
            factor = scale if disp == 0 else 0.5 * scale
            item_ref[0, moment, disp, 0] = (factor * (upper[:, :nvec] + lower[:, nvec:])).astype(item_ref.dtype)
            item_ref[0, moment, disp, 1] = (factor * (upper[:, nvec:] - lower[:, :nvec])).astype(item_ref.dtype)

    flat = vector_ref[now].reshape(2 * NCOL * nvec, width)
    for direction, ahead_ref in enumerate((ahead_x_ref, ahead_y_ref)):
        ahead_ref[...] = jnp.dot(
            flat, move_ref[direction, 0], preferred_element_type=jnp.float32
        ).reshape(ahead_ref.shape)

    for color in range(NCOL):
        span = pl.ds(color * width, width)
        for part in range(2):
            still_ref[pl.ds(part * nvec, nvec), span] = vector_ref[now, part, color]
        for start in range(0, nvec, ROWS):
            real = vector_ref[now, 0, color, pl.ds(start, ROWS), :].astype(jnp.float32)
            imag = vector_ref[now, 1, color, pl.ds(start, ROWS), :].astype(jnp.float32)
            for moment in range(NMOM):
                cosine = phase_ref[moment, 0]
                sine = phase_ref[moment, 1]
                first = 2 * moment * nvec + start
                phased_ref[pl.ds(first, ROWS), span] = (cosine * real - sine * imag).astype(jnp.bfloat16)
                phased_ref[pl.ds(first + nvec, ROWS), span] = (sine * real + cosine * imag).astype(jnp.bfloat16)
    gram(still_ref, 0)

    for direction, (adjoint_ref, behind_ref) in enumerate(
        ((adjoint_x_ref, behind_x_ref), (adjoint_y_ref, behind_y_ref))
    ):

        def adjoint(part, color, rows, lanes, value):
            adjoint_ref[part, color, rows, lanes] = value.astype(jnp.bfloat16)

        color_loop(linker(direction), nvec, width, vector, adjoint, True)
        behind_ref[...] = jnp.dot(
            adjoint_ref[...].reshape(2 * NCOL * nvec, width),
            move_ref[direction, 1],
            preferred_element_type=jnp.float32,
        ).reshape(behind_ref.shape)

    for direction, (ahead_ref, behind_ref, moved_ref) in enumerate(
        ((ahead_x_ref, behind_x_ref, moved_x_ref), (ahead_y_ref, behind_y_ref, moved_y_ref))
    ):

        def ahead(part, color, rows, lanes):
            return ahead_ref[part, color, rows, lanes]

        def forward(part, color, rows, lanes, value):
            moved_ref[
                pl.ds(part * nvec + rows.start, rows.size), pl.ds(color * width + lanes.start, lanes.size)
            ] = (value - behind_ref[part, color, rows, lanes]).astype(jnp.bfloat16)

        color_loop(linker(direction), nvec, width, ahead, forward, False)
        gram(moved_ref, direction + 1)


def plane_items(position, momenta, vectors, links, total_z, plane, scale):
    slices, _, _, nvec, width = vectors.shape
    color_block = (2, NCOL, nvec, width)
    return pl.pallas_call(
        functools.partial(plane_kernel, total_z, plane, scale),
        grid=(slices,),
        in_specs=[pl.BlockSpec(memory_space=pltpu.SMEM)] + [pl.BlockSpec(memory_space=pltpu.HBM)] * 3,
        out_specs=[
            pl.BlockSpec((1, NMOM, NDISP - 1, 2, nvec, nvec), lambda t: (t, 0, 0, 0, 0, 0)),
            pl.BlockSpec((NMOM, 2, 1, width), lambda t: (0, 0, 0, 0)),
            pl.BlockSpec((NMOM, 2, 1, nvec), lambda t: (0, 0, 0, 0)),
        ],
        out_shape=[
            jax.ShapeDtypeStruct((slices, NMOM, NDISP - 1, 2, nvec, nvec), jnp.bfloat16),
            jax.ShapeDtypeStruct((NMOM, 2, 1, width), jnp.float32),
            jax.ShapeDtypeStruct((NMOM, 2, 1, nvec), jnp.float32),
        ],
        scratch_shapes=[
            pltpu.SMEM(momenta.shape, jnp.int32),
            pltpu.VMEM(vectors.shape, jnp.bfloat16),
            pltpu.VMEM(links.shape, jnp.float32),
        ]
        + [pltpu.VMEM(color_block, jnp.float32)] * 4
        + [pltpu.VMEM(color_block, jnp.bfloat16)] * 2
        + [pltpu.VMEM((NMOM * 2 * nvec, NCOL * width), jnp.bfloat16)]
        + [pltpu.VMEM((2 * nvec, NCOL * width), jnp.bfloat16)] * 3
        + [
            pltpu.VMEM((2, 2, width, width), jnp.bfloat16),
            pltpu.SemaphoreType.DMA,
            pltpu.SemaphoreType.DMA((2, slices)),
        ],
        compiler_params=pltpu.CompilerParams(vmem_limit_bytes=24 * MIB),
        cost_estimate=pl.CostEstimate(
            flops=slices * 16 * NMOM * nvec * nvec * NCOL * width,
            bytes_accessed=6 * vectors.size + 4 * links.size,
            transcendentals=0,
        ),
        name="plane_items",
    )(position, momenta, vectors, links)


def layer_kernel(
    slot, scale, rows_ref, item_ref, own_ref, ahead_ref, phase_ref, turn_ref,
    keep_ref, send_ref, lhs_ref, listed_ref,
):
    nvec, width = own_ref.shape[3:]
    devices = 2 * keep_ref.shape[0]
    targets = (keep_ref, send_ref)

    def bond(row, lhs):
        item = rows_ref[row, slot, 0]
        slice_index = item // (NMOM * NDISP)
        moment = item // NDISP % NMOM
        cosine = phase_ref[moment, 0]
        sine = phase_ref[moment, 1]
        for color in range(NCOL):
            span = pl.ds(color * width, width)
            for part in range(2):
                value = own_ref[slice_index, part, color]
                lhs[pl.ds(part * nvec, nvec), span] = (cosine * value).astype(jnp.bfloat16)
                lhs[pl.ds((2 + part) * nvec, nvec), span] = (sine * value).astype(jnp.bfloat16)
        rhs = jnp.concatenate(
            [
                jnp.concatenate([ahead_ref[slice_index, part, color] for color in range(NCOL)], 1)
                for part in range(2)
            ],
            0,
        )
        gram = lax.dot_general(lhs[...], rhs, (((1,), (1,)), ((), ())), preferred_element_type=jnp.float32)
        block = [
            [gram[i * nvec : (i + 1) * nvec, j * nvec : (j + 1) * nvec] for j in range(2)] for i in range(4)
        ]
        cos_real = block[0][0] + block[1][1]
        cos_imag = block[0][1] - block[1][0]
        sin_real = block[2][0] + block[3][1]
        sin_imag = block[2][1] - block[3][0]
        half = 0.5 * scale
        turn_cos = half * turn_ref[moment, 0]
        turn_sin = half * turn_ref[moment, 1]
        back_real = cos_real - sin_imag
        back_imag = cos_imag + sin_real
        real = half * (cos_real + sin_imag) - (turn_cos * back_real - turn_sin * back_imag).T
        imag = half * (cos_imag - sin_real) + (turn_cos * back_imag + turn_sin * back_real).T
        return real.astype(keep_ref.dtype), imag.astype(keep_ref.dtype)

    def note(row, found):
        item = rows_ref[row, slot, 0]
        disp = item % NDISP
        layer = disp == NDISP - 1

        @pl.when(layer)
        def _():
            listed_ref[found] = row

        for core in range(2):

            @pl.when(jnp.logical_not(layer) & (row % 2 == core))
            def _():
                targets[core][row // 2] = item_ref[item // (NMOM * NDISP), item // NDISP % NMOM, disp]

        return found + layer.astype(jnp.int32)

    found = lax.fori_loop(0, devices, note, jnp.int32(0))

    @pl.loop(0, (found + 1) // 2)
    def _(pair):
        both = [listed_ref[2 * pair], listed_ref[jnp.minimum(2 * pair + 1, found - 1)]]
        results = [bond(row, lhs_ref.at[index]) for index, row in enumerate(both)]
        for row, (real, imag) in zip(both, results):
            for core in range(2):

                @pl.when(row % 2 == core)
                def _():
                    targets[core][row // 2, 0] = real
                    targets[core][row // 2, 1] = imag


def layer_items(slot, rows, item, own, ahead, phase, turn, scale):
    slices, _, _, nvec, width = own.shape
    devices = rows.shape[0]
    shape = jax.ShapeDtypeStruct((devices // 2, 2, nvec, nvec), jnp.bfloat16)
    whole = pl.BlockSpec(memory_space=pltpu.VMEM)
    scalar = pl.BlockSpec(memory_space=pltpu.SMEM)
    return pl.pallas_call(
        functools.partial(layer_kernel, slot, scale),
        in_specs=[scalar] + [whole] * 5,
        out_specs=[whole, whole],
        out_shape=[shape, shape],
        scratch_shapes=[
            pltpu.VMEM((2, 4 * nvec, NCOL * width), jnp.bfloat16),
            pltpu.SMEM((devices,), jnp.int32),
        ],
        compiler_params=pltpu.CompilerParams(vmem_limit_bytes=12 * MIB),
        cost_estimate=pl.CostEstimate(
            flops=devices * 4 * nvec * nvec * NCOL * width,
            bytes_accessed=2 * own.size,
            transcendentals=0,
        ),
        name="layer_items",
    )(rows, item, own, ahead, phase, turn)


def add_kernel(places, *refs):
    terms, outs = refs[: len(places[0][0])], refs[len(places[0][0]) :]
    for out_ref, wanted in zip(outs, places):
        for entry, at in enumerate(wanted):
            total = terms[0][at[0]].astype(jnp.float32)
            for ref, index in zip(terms[1:], at[1:]):
                total = total + ref[index].astype(jnp.float32)
            out_ref[entry] = total.astype(out_ref.dtype)


def added(terms, groups):
    places = [[tuple(entries.index(r) for entries, _ in terms) for r in group] for group in groups]
    values = [value for _, value in terms]
    tail = values[0].shape[1:]
    whole = pl.BlockSpec(memory_space=pltpu.VMEM)
    size = sum(len(group) for group in groups) * math.prod(tail)
    return pl.pallas_call(
        functools.partial(add_kernel, places),
        in_specs=[whole] * len(values),
        out_specs=[whole] * len(groups),
        out_shape=[jax.ShapeDtypeStruct((len(group),) + tail, jnp.bfloat16) for group in groups],
        compiler_params=pltpu.CompilerParams(vmem_limit_bytes=8 * MIB),
        cost_estimate=pl.CostEstimate(
            flops=len(values) * size, bytes_accessed=2 * (len(values) + 1) * size, transcendentals=0
        ),
        name="added",
    )(*values)


def halved(keep, send, order):
    entries = list(range(keep.shape[0]))
    terms = [(entries, keep), (entries, exchanged(send, 1))]
    for bit in order[:-2]:
        far = [r for r in entries if r >> (bit - 1) & 1]
        entries = [r for r in entries if r not in far]
        (leaving,) = added(terms, [far])
        terms.append((entries, exchanged(leaving, 1 << bit)))
    return terms


def mix_kernel(slot_ref, structure_ref, weight_ref, tau_ref, out_ref):
    spins, _, nvec, width = tau_ref.shape[1:]
    base = structure_ref[pl.program_id(0)] * spins * spins
    weight = [[weight_ref[base + r * spins + s] for s in range(spins)] for r in range(spins)]

    @pl.loop(0, 2 * nvec // ROWS)
    def _(index):
        part = index // (nvec // ROWS)
        rows = pl.ds(pl.multiple_of(index % (nvec // ROWS) * ROWS, ROWS), ROWS)
        tau = [tau_ref[0, s, part, rows, :].astype(jnp.float32) for s in range(spins)]
        for r in range(spins):
            mixed = weight[r][0] * tau[0]
            for s in range(1, spins):
                mixed = mixed + weight[r][s] * tau[s]
            out_ref[0, r, part, rows, :] = mixed.astype(jnp.bfloat16)


def mixed_perambulators(slots, structures, weights, perambulators):
    block = (1,) + perambulators.shape[1:]
    count = slots.shape[0]
    return pl.pallas_call(
        mix_kernel,
        grid_spec=pltpu.PrefetchScalarGridSpec(
            num_scalar_prefetch=3,
            grid=(count,),
            in_specs=[pl.BlockSpec(block, lambda j, slot, *_: (slot[j], 0, 0, 0, 0))],
            out_specs=pl.BlockSpec(block, lambda j, *_: (j, 0, 0, 0, 0)),
        ),
        out_shape=jax.ShapeDtypeStruct((count,) + perambulators.shape[1:], jnp.bfloat16),
        compiler_params=pltpu.CompilerParams(vmem_limit_bytes=8 * MIB),
        cost_estimate=pl.CostEstimate(
            flops=8 * perambulators.size, bytes_accessed=4 * perambulators.size, transcendentals=0
        ),
        name="mixed_perambulators",
    )(slots, structures, weights, perambulators)


def diagram_kernel(count, *refs):
    terms = refs[: -4]
    tau_ref, out_ref, block_ref, sems = refs[-4:]
    spins, _, nvec, width = tau_ref.shape[1:]
    each = len(terms) // count

    def copy(index, r):
        return pltpu.make_async_copy(block_ref.at[index, r], out_ref.at[index, r], sems.at[index, r])

    for index in range(count):
        real, imag = (
            sum(ref[0, part].astype(jnp.float32) for ref in terms[index * each : (index + 1) * each])
            for part in range(2)
        )
        square = jnp.concatenate(
            [jnp.concatenate([real, -imag], 1), jnp.concatenate([imag, real], 1)], 0
        ).astype(jnp.bfloat16)
        for r in range(spins):
            tau = tau_ref[index, r].reshape(2 * nvec, width)
            block = jnp.dot(square, tau, preferred_element_type=jnp.float32)
            block_ref[index, r] = block.astype(jnp.bfloat16).reshape(2, nvec, width)
            copy(index, r).start()
    for index in range(count):
        for r in range(spins):
            copy(index, r).wait()


def diagrams(terms, tau):
    count, spins, _, nvec, width = tau.shape
    whole = pl.BlockSpec(memory_space=pltpu.VMEM)
    flat = [value for group in terms for value in group]
    return pl.pallas_call(
        functools.partial(diagram_kernel, count),
        in_specs=[whole] * (len(flat) + 1),
        out_specs=pl.BlockSpec(memory_space=pltpu.HBM),
        out_shape=jax.ShapeDtypeStruct(tau.shape, jnp.bfloat16),
        scratch_shapes=[
            pltpu.VMEM(tau.shape, jnp.bfloat16),
            pltpu.SemaphoreType.DMA((count, spins)),
        ],
        compiler_params=pltpu.CompilerParams(vmem_limit_bytes=12 * MIB),
        cost_estimate=pl.CostEstimate(
            flops=8 * nvec * nvec * width * spins * count, bytes_accessed=4 * tau.size, transcendentals=0
        ),
        name="diagrams",
    )(*flat, tau)


def body(eigvecs, gauge_links, momenta, spin_mix, perambulators, contraction_list):
    slices, _, _, nvec, depth, plane = eigvecs.shape
    devices = lax.axis_size(SITES)
    position = lax.axis_index(SITES)
    bits = devices.bit_length() - 1
    total_z = depth * devices
    width = depth * plane
    scale = 1.0 / math.sqrt(NCOL * plane * total_z)
    place = position.reshape(1)
    rows, (after, place) = gathered(contraction_list, (eigvecs, place))
    upper = shifted(after[:, :, :, :, :1, :], SITES, -1)
    vectors = eigvecs.reshape(slices, 2, NCOL, nvec, width)
    links = gauge_links.reshape(slices, 3, 2, NCOL, NCOL, 1, width)
    own = adjoint_products(vectors, links, 2)
    item, phase, turn = plane_items(place, momenta, vectors, links, total_z, plane, scale)
    ahead = jnp.concatenate([eigvecs[:, :, :, :, 1:, :], upper], 4).reshape(vectors.shape)
    slots = contraction_list[:, 2] - position * perambulators.shape[0]
    tau = mixed_perambulators(slots, contraction_list[:, 1], spin_mix.reshape(-1), perambulators)
    terms = []
    for slot in range(contraction_list.shape[0]):
        keep, send = layer_items(slot, rows, item, own, ahead, phase, turn, scale)
        order = [1 + (slot + step) % (bits - 1) for step in range(bits - 1)]
        terms.append(halved(keep, send, order))
    parts = []
    for group in terms:
        others = [r for r in group[-1][0] if r]
        leaving = added(group, [[r] for r in others])
        parts.append([value for _, value in group] + [exchanged(value, 2 * r) for r, value in zip(others, leaving)])
    return diagrams(parts, tau)


def solution(mesh):
    placed = (
        P("cfg", None, None, None, ("space", "diag"), None),
        P("cfg", None, None, None, None, ("space", "diag"), None),
        P(),
        P(),
        P(("cfg", "space", "diag"), None, None, None, None),
        P(("space", "diag"), None),
    )
    return jax.shard_map(
        body,
        mesh=mesh,
        in_specs=placed,
        out_specs=P(("cfg", "space", "diag"), None, None, None, None),
        check_vma=False,
    )
```

```python
import functools
import math

import jax
import jax.numpy as jnp
from jax import lax
from jax.experimental import pallas as pl
from jax.experimental.pallas import tpu as pltpu
from jax.sharding import PartitionSpec as P

NCOL = 3
NMOM = 4
NDISP = 4
LX = 16
LY = 16
LANES = 128
ROWS = 16
SITES = ("space", "diag")
MIB = 1024 * 1024
PLANE_LIMIT = 24 * MIB


def shifted(value, axis, by):
    size = lax.axis_size(axis)
    return lax.ppermute(value, axis, [(i, (i + by) % size) for i in range(size)])


def in_hbm(value):
    return pltpu.with_memory_space_constraint(value, pltpu.HBM)


def exchanged(value, mask):
    size = lax.axis_size(SITES)
    return lax.ppermute(value, SITES, [(i, i ^ mask) for i in range(size)])


def gathered(rows, token):
    parts = [rows[None]]
    for step in range(1, min(4, lax.axis_size(SITES))):
        parts.append(exchanged(parts[0], step))
        if step == 1:
            parts[1], token = lax.optimization_barrier((parts[1], token))
    return parts, token


def gathered_rest(parts):
    bits = lax.axis_size(SITES).bit_length() - 1
    value = jnp.concatenate(parts)
    for low in range(2, bits, 2):
        steps = range(1, 1 << min(2, bits - low))
        value = jnp.concatenate([value] + [exchanged(value, step << low) for step in steps])
    return value


def color_product(matrix, real, imag, adjoint):
    rows = []
    for row in range(NCOL):
        real_part = imag_part = None
        for col in range(NCOL):
            if adjoint:
                mreal, mimag = matrix[0][col][row], matrix[1][col][row]
                one = mreal * real[col] + mimag * imag[col]
                two = mreal * imag[col] - mimag * real[col]
            else:
                mreal, mimag = matrix[0][row][col], matrix[1][row][col]
                one = mreal * real[col] - mimag * imag[col]
                two = mreal * imag[col] + mimag * real[col]
            real_part = one if real_part is None else real_part + one
            imag_part = two if imag_part is None else imag_part + two
        rows.append((real_part, imag_part))
    return rows


def color_loop(link, nvec, width, load, store, adjoint):
    height = math.gcd(nvec, 2 * ROWS)
    for lane in range(0, width, LANES):
        lanes = pl.ds(lane, LANES)
        matrix = [
            [[link(part, row, col, lanes) for col in range(NCOL)] for row in range(NCOL)] for part in range(2)
        ]
        for start in range(0, nvec, height):
            rows = pl.ds(start, height)
            real = [load(0, color, rows, lanes) for color in range(NCOL)]
            imag = [load(1, color, rows, lanes) for color in range(NCOL)]
            for color, (one, two) in enumerate(color_product(matrix, real, imag, adjoint)):
                store(0, color, rows, lanes, one)
                store(1, color, rows, lanes, two)


def fill_tables(position, total_z, plane, momenta_ref, phase_ref, turn_ref):
    width = phase_ref.shape[-1]
    flat = lax.broadcasted_iota(jnp.int32, (1, width), 1)
    xcoord = (flat % LX).astype(jnp.float32)
    ycoord = (flat % plane // LX).astype(jnp.float32)
    zcoord = (position * (width // plane) + flat // plane).astype(jnp.float32)
    for moment in range(NMOM):
        along_x = momenta_ref[moment, 0].astype(jnp.float32)
        along_y = momenta_ref[moment, 1].astype(jnp.float32)
        along_z = momenta_ref[moment, 2].astype(jnp.float32)
        angle = (
            2.0 * math.pi * (along_x * xcoord / LX + along_y * ycoord / LY + along_z * zcoord / total_z)
        )
        phase_ref[moment, 0] = jnp.cos(angle)
        phase_ref[moment, 1] = jnp.sin(angle)
        turn = jnp.full((1, turn_ref.shape[-1]), 2.0 * math.pi / total_z, jnp.float32) * along_z
        turn_ref[moment, 0] = jnp.cos(turn)
        turn_ref[moment, 1] = jnp.sin(turn)


def fill_moves(move_ref):
    width = move_ref.shape[-1]
    source = lax.broadcasted_iota(jnp.int32, (width, width), 0)
    site = lax.broadcasted_iota(jnp.int32, (width, width), 1)
    xcoord = site % LX
    ycoord = site // LX % LY
    for sign, by in enumerate((1, -1)):
        along_x = site - xcoord + (xcoord + LX + by) % LX
        along_y = site + ((ycoord + LY + by) % LY - ycoord) * LX
        move_ref[0, sign] = (source == along_x).astype(jnp.float32).astype(jnp.bfloat16)
        move_ref[1, sign] = (source == along_y).astype(jnp.float32).astype(jnp.bfloat16)


def plane_kernel(
    total_z, plane, scale,
    position_ref, momenta_in, vector_in, link_in,
    item_ref, own_ref, phase_ref, turn_ref,
    momenta_ref, vector_ref, link_ref,
    ahead_x_ref, ahead_y_ref, behind_x_ref, behind_y_ref, adjoint_x_ref, adjoint_y_ref,
    phased_ref, still_ref, moved_x_ref, moved_y_ref, move_ref, momenta_sem, sems,
):
    now = pl.program_id(0)
    slices, _, _, nvec, width = vector_ref.shape

    def copies(index):
        return (
            pltpu.make_async_copy(vector_in.at[index], vector_ref.at[index], sems.at[0, index]),
            pltpu.make_async_copy(link_in.at[index], link_ref.at[index], sems.at[1, index]),
        )

    @pl.when(now == 0)
    def _():
        moments = pltpu.make_async_copy(momenta_in, momenta_ref, momenta_sem)
        moments.start()
        for index in range(slices):
            for copy in copies(index):
                copy.start()
        fill_moves(move_ref)
        moments.wait()
        fill_tables(position_ref[0], total_z, plane, momenta_ref, phase_ref, turn_ref)

    for copy in copies(now):
        copy.wait()

    def linker(direction):
        return lambda part, row, col, lanes: link_ref[now, direction, part, row, col, :, lanes]

    def vector(part, color, rows, lanes):
        return vector_ref[now, part, color, rows, lanes].astype(jnp.float32)

    def gram(moved_ref, disp):
        product = lax.dot_general(
            phased_ref[...], moved_ref[...], (((1,), (1,)), ((), ())), preferred_element_type=jnp.float32
        )
        for moment in range(NMOM):
            start = 2 * moment * nvec
            upper = product[start : start + nvec]
            lower = product[start + nvec : start + 2 * nvec]
            factor = scale if disp == 0 else 0.5 * scale
            item_ref[0, moment, disp, 0] = (factor * (upper[:, :nvec] + lower[:, nvec:])).astype(item_ref.dtype)
            item_ref[0, moment, disp, 1] = (factor * (upper[:, nvec:] - lower[:, :nvec])).astype(item_ref.dtype)

    flat = vector_ref[now].reshape(2 * NCOL * nvec, width)
    for direction, ahead_ref in enumerate((ahead_x_ref, ahead_y_ref)):
        ahead_ref[...] = jnp.dot(
            flat, move_ref[direction, 0], preferred_element_type=jnp.float32
        ).reshape(ahead_ref.shape)

    for color in range(NCOL):
        span = pl.ds(color * width, width)
        for part in range(2):
            still_ref[pl.ds(part * nvec, nvec), span] = vector_ref[now, part, color]
        for start in range(0, nvec, ROWS):
            real = vector_ref[now, 0, color, pl.ds(start, ROWS), :].astype(jnp.float32)
            imag = vector_ref[now, 1, color, pl.ds(start, ROWS), :].astype(jnp.float32)
            for moment in range(NMOM):
                cosine = phase_ref[moment, 0]
                sine = phase_ref[moment, 1]
                first = 2 * moment * nvec + start
                phased_ref[pl.ds(first, ROWS), span] = (cosine * real - sine * imag).astype(jnp.bfloat16)
                phased_ref[pl.ds(first + nvec, ROWS), span] = (sine * real + cosine * imag).astype(jnp.bfloat16)
    gram(still_ref, 0)

    for direction, (adjoint_ref, behind_ref) in enumerate(
        ((adjoint_x_ref, behind_x_ref), (adjoint_y_ref, behind_y_ref))
    ):

        def adjoint(part, color, rows, lanes, value):
            adjoint_ref[part, color, rows, lanes] = value.astype(jnp.bfloat16)

        color_loop(linker(direction), nvec, width, vector, adjoint, True)
        behind_ref[...] = jnp.dot(
            adjoint_ref[...].reshape(2 * NCOL * nvec, width),
            move_ref[direction, 1],
            preferred_element_type=jnp.float32,
        ).reshape(behind_ref.shape)

    for direction, (ahead_ref, behind_ref, moved_ref) in enumerate(
        ((ahead_x_ref, behind_x_ref, moved_x_ref), (ahead_y_ref, behind_y_ref, moved_y_ref))
    ):

        def ahead(part, color, rows, lanes):
            return ahead_ref[part, color, rows, lanes]

        def forward(part, color, rows, lanes, value):
            moved_ref[
                pl.ds(part * nvec + rows.start, rows.size), pl.ds(color * width + lanes.start, lanes.size)
            ] = (value - behind_ref[part, color, rows, lanes]).astype(jnp.bfloat16)

        color_loop(linker(direction), nvec, width, ahead, forward, False)
        gram(moved_ref, direction + 1)

    def own(part, color, rows, lanes, value):
        own_ref[0, part, color, rows, lanes] = value

    color_loop(linker(2), nvec, width, vector, own, True)


def plane_items(position, momenta, vectors, links, total_z, plane, scale):
    slices, _, _, nvec, width = vectors.shape
    color_block = (2, NCOL, nvec, width)
    return pl.pallas_call(
        functools.partial(plane_kernel, total_z, plane, scale),
        grid=(slices,),
        in_specs=[pl.BlockSpec(memory_space=pltpu.SMEM)] + [pl.BlockSpec(memory_space=pltpu.HBM)] * 3,
        out_specs=[
            pl.BlockSpec((1, NMOM, NDISP - 1, 2, nvec, nvec), lambda t: (t, 0, 0, 0, 0, 0)),
            pl.BlockSpec((1,) + color_block, lambda t: (t, 0, 0, 0, 0)),
            pl.BlockSpec((NMOM, 2, 1, width), lambda t: (0, 0, 0, 0)),
            pl.BlockSpec((NMOM, 2, 1, nvec), lambda t: (0, 0, 0, 0)),
        ],
        out_shape=[
            jax.ShapeDtypeStruct((slices, NMOM, NDISP - 1, 2, nvec, nvec), jnp.bfloat16),
            jax.ShapeDtypeStruct(vectors.shape, jnp.float32),
            jax.ShapeDtypeStruct((NMOM, 2, 1, width), jnp.float32),
            jax.ShapeDtypeStruct((NMOM, 2, 1, nvec), jnp.float32),
        ],
        scratch_shapes=[
            pltpu.SMEM(momenta.shape, jnp.int32),
            pltpu.VMEM(vectors.shape, jnp.bfloat16),
            pltpu.VMEM(links.shape, jnp.float32),
        ]
        + [pltpu.VMEM(color_block, jnp.float32)] * 4
        + [pltpu.VMEM(color_block, jnp.bfloat16)] * 2
        + [pltpu.VMEM((NMOM * 2 * nvec, NCOL * width), jnp.bfloat16)]
        + [pltpu.VMEM((2 * nvec, NCOL * width), jnp.bfloat16)] * 3
        + [
            pltpu.VMEM((2, 2, width, width), jnp.bfloat16),
            pltpu.SemaphoreType.DMA,
            pltpu.SemaphoreType.DMA((2, slices)),
        ],
        compiler_params=pltpu.CompilerParams(vmem_limit_bytes=PLANE_LIMIT),
        cost_estimate=pl.CostEstimate(
            flops=slices * 16 * NMOM * nvec * nvec * NCOL * width,
            bytes_accessed=6 * vectors.size + 4 * links.size,
            transcendentals=0,
        ),
        name="plane_items",
    )(position, in_hbm(momenta), in_hbm(vectors), in_hbm(links))


def layer_kernel(
    slot, core, scale, rows_ref, item_ref, own_ref, ahead_ref, phase_ref, turn_ref, out_ref, lhs_ref, listed_ref
):
    nvec, width = own_ref.shape[3:]
    sites = out_ref.shape[0]

    def parts_of(place):
        item = rows_ref[2 * place + core, slot, 0]
        rest = lax.rem(item, NMOM * NDISP)
        return lax.div(item, NMOM * NDISP), lax.div(rest, NDISP), lax.rem(rest, NDISP)

    def bond(place, lhs):
        slice_index, moment, _ = parts_of(place)
        cosine = phase_ref[moment, 0]
        sine = phase_ref[moment, 1]
        for color in range(NCOL):
            span = pl.ds(color * width, width)
            for part in range(2):
                value = own_ref[slice_index, part, color]
                lhs[pl.ds(part * nvec, nvec), span] = (cosine * value).astype(jnp.bfloat16)
                lhs[pl.ds((2 + part) * nvec, nvec), span] = (sine * value).astype(jnp.bfloat16)
        rhs = jnp.concatenate(
            [
                jnp.concatenate([ahead_ref[slice_index, part, color] for color in range(NCOL)], 1)
                for part in range(2)
            ],
            0,
        )
        gram = lax.dot_general(lhs[...], rhs, (((1,), (1,)), ((), ())), preferred_element_type=jnp.float32)
        block = [
            [gram[i * nvec : (i + 1) * nvec, j * nvec : (j + 1) * nvec] for j in range(2)] for i in range(4)
        ]
        cos_real = block[0][0] + block[1][1]
        cos_imag = block[0][1] - block[1][0]
        sin_real = block[2][0] + block[3][1]
        sin_imag = block[2][1] - block[3][0]
        half = 0.5 * scale
        turn_cos = half * turn_ref[moment, 0]
        turn_sin = half * turn_ref[moment, 1]
        back_real = cos_real - sin_imag
        back_imag = cos_imag + sin_real
        real = half * (cos_real + sin_imag) - (turn_cos * back_real - turn_sin * back_imag).T
        imag = half * (cos_imag - sin_real) + (turn_cos * back_imag + turn_sin * back_real).T
        return real.astype(out_ref.dtype), imag.astype(out_ref.dtype)

    found = jnp.int32(0)
    for place in range(sites):
        slice_index, moment, disp = parts_of(place)
        out_ref[place] = item_ref[slice_index, moment, jnp.minimum(disp, NDISP - 2)]
        listed_ref[found] = place
        found = found + (disp == NDISP - 1).astype(jnp.int32)

    @pl.loop(0, lax.div(found + 1, 2))
    def _(pair):
        both = [listed_ref[2 * pair], listed_ref[jnp.minimum(2 * pair + 1, found - 1)]]
        results = [bond(place, lhs_ref.at[index]) for index, place in enumerate(both)]
        for place, (real, imag) in zip(both, results):
            out_ref[place, 0] = real
            out_ref[place, 1] = imag


def layer_items(slot, core, rows, item, own, ahead, phase, turn, scale):
    slices, _, _, nvec, width = own.shape
    sites = rows.shape[0] // 2
    whole = pl.BlockSpec(memory_space=pltpu.VMEM)
    return pl.pallas_call(
        functools.partial(layer_kernel, slot, core, scale),
        in_specs=[pl.BlockSpec(memory_space=pltpu.SMEM)] + [whole] * 5,
        out_specs=whole,
        out_shape=jax.ShapeDtypeStruct((sites, 2, nvec, nvec), jnp.bfloat16),
        scratch_shapes=[
            pltpu.VMEM((2, 4 * nvec, NCOL * width), jnp.bfloat16),
            pltpu.SMEM((sites,), jnp.int32),
        ],
        compiler_params=pltpu.CompilerParams(vmem_limit_bytes=12 * MIB),
        cost_estimate=pl.CostEstimate(
            flops=sites * 4 * nvec * nvec * NCOL * width,
            bytes_accessed=2 * own.size,
            transcendentals=0,
        ),
        name="layer_items",
    )(rows, item, own, ahead, phase, turn)


def add_kernel(places, *refs):
    terms, outs = refs[: len(places[0][0])], refs[len(places[0][0]) :]
    for out_ref, wanted in zip(outs, places):
        for entry, at in enumerate(wanted):
            total = terms[0][at[0]].astype(jnp.float32)
            for ref, index in zip(terms[1:], at[1:]):
                total = total + ref[index].astype(jnp.float32)
            out_ref[entry] = total.astype(out_ref.dtype)


def added(terms, groups):
    places = [[tuple(entries.index(r) for entries, _ in terms) for r in group] for group in groups]
    values = [value for _, value in terms]
    tail = values[0].shape[1:]
    whole = pl.BlockSpec(memory_space=pltpu.VMEM)
    size = sum(len(group) for group in groups) * math.prod(tail)
    return pl.pallas_call(
        functools.partial(add_kernel, places),
        in_specs=[whole] * len(values),
        out_specs=[whole] * len(groups),
        out_shape=[jax.ShapeDtypeStruct((len(group),) + tail, jnp.bfloat16) for group in groups],
        compiler_params=pltpu.CompilerParams(vmem_limit_bytes=8 * MIB),
        cost_estimate=pl.CostEstimate(
            flops=len(values) * size, bytes_accessed=2 * (len(values) + 1) * size, transcendentals=0
        ),
        name="added",
    )(*values)


def halved(keep, send, order):
    entries = list(range(keep.shape[0]))
    terms = [(entries, keep), (entries, exchanged(send, 1))]
    for bit in order[:-2]:
        far = [r for r in entries if r >> (bit - 1) & 1]
        entries = [r for r in entries if r not in far]
        (leaving,) = added(terms, [far])
        terms.append((entries, exchanged(leaving, 1 << bit)))
    return terms


def mix_kernel(slot_ref, structure_ref, weight_ref, tau_ref, out_ref):
    spins, _, nvec, width = tau_ref.shape[1:]
    base = structure_ref[pl.program_id(0)] * spins * spins
    weight = [[weight_ref[base + r * spins + s] for s in range(spins)] for r in range(spins)]

    @pl.loop(0, 2 * nvec // ROWS)
    def _(index):
        part = index // (nvec // ROWS)
        rows = pl.ds(pl.multiple_of(index % (nvec // ROWS) * ROWS, ROWS), ROWS)
        tau = [tau_ref[0, s, part, rows, :].astype(jnp.float32) for s in range(spins)]
        for r in range(spins):
            mixed = weight[r][0] * tau[0]
            for s in range(1, spins):
                mixed = mixed + weight[r][s] * tau[s]
            out_ref[0, r, part, rows, :] = mixed.astype(jnp.bfloat16)


def mixed_perambulators(slots, structures, weights, perambulators):
    block = (1,) + perambulators.shape[1:]
    count = slots.shape[0]
    return pl.pallas_call(
        mix_kernel,
        grid_spec=pltpu.PrefetchScalarGridSpec(
            num_scalar_prefetch=3,
            grid=(count,),
            in_specs=[pl.BlockSpec(block, lambda j, slot, *_: (slot[j], 0, 0, 0, 0))],
            out_specs=pl.BlockSpec(block, lambda j, *_: (j, 0, 0, 0, 0)),
        ),
        out_shape=jax.ShapeDtypeStruct((count,) + perambulators.shape[1:], jnp.bfloat16),
        compiler_params=pltpu.CompilerParams(vmem_limit_bytes=8 * MIB),
        cost_estimate=pl.CostEstimate(
            flops=8 * perambulators.size, bytes_accessed=4 * perambulators.size, transcendentals=0
        ),
        name="mixed_perambulators",
    )(slots, structures, weights, in_hbm(perambulators))


def diagram_kernel(count, *refs):
    terms = refs[: -4]
    tau_ref, out_ref, block_ref, sems = refs[-4:]
    spins, _, nvec, width = tau_ref.shape[1:]
    each = len(terms) // count

    def copy(index, r):
        return pltpu.make_async_copy(block_ref.at[index, r], out_ref.at[index, r], sems.at[index, r])

    for index in range(count):
        real, imag = (
            sum(ref[0, part].astype(jnp.float32) for ref in terms[index * each : (index + 1) * each])
            for part in range(2)
        )
        square = jnp.concatenate(
            [jnp.concatenate([real, -imag], 1), jnp.concatenate([imag, real], 1)], 0
        ).astype(jnp.bfloat16)
        for r in range(spins):
            tau = tau_ref[index, r].reshape(2 * nvec, width)
            block = jnp.dot(square, tau, preferred_element_type=jnp.float32)
            block_ref[index, r] = block.astype(jnp.bfloat16).reshape(2, nvec, width)
            copy(index, r).start()
    for index in range(count):
        for r in range(spins):
            copy(index, r).wait()


def diagrams(terms, tau):
    count, spins, _, nvec, width = tau.shape
    whole = pl.BlockSpec(memory_space=pltpu.VMEM)
    flat = [value for group in terms for value in group]
    return pl.pallas_call(
        functools.partial(diagram_kernel, count),
        in_specs=[whole] * (len(flat) + 1),
        out_specs=pl.BlockSpec(memory_space=pltpu.HBM),
        out_shape=jax.ShapeDtypeStruct(tau.shape, jnp.bfloat16),
        scratch_shapes=[
            pltpu.VMEM(tau.shape, jnp.bfloat16),
            pltpu.SemaphoreType.DMA((count, spins)),
        ],
        compiler_params=pltpu.CompilerParams(vmem_limit_bytes=12 * MIB),
        cost_estimate=pl.CostEstimate(
            flops=8 * nvec * nvec * width * spins * count, bytes_accessed=4 * tau.size, transcendentals=0
        ),
        name="diagrams",
    )(*flat, tau)


def body(eigvecs, gauge_links, momenta, spin_mix, perambulators, contraction_list):
    slices, _, _, nvec, depth, plane = eigvecs.shape
    devices = lax.axis_size(SITES)
    position = lax.axis_index(SITES)
    bits = devices.bit_length() - 1
    total_z = depth * devices
    width = depth * plane
    scale = 1.0 / math.sqrt(NCOL * plane * total_z)
    place = position.reshape(1)
    near, after = gathered(contraction_list, eigvecs)
    upper = shifted(after[:, :, :, :, :1, :], SITES, -1)
    vectors = eigvecs.reshape(slices, 2, NCOL, nvec, width)
    links = gauge_links.reshape(slices, 3, 2, NCOL, NCOL, 1, width)
    item, own, phase, turn = plane_items(place, momenta, vectors, links, total_z, plane, scale)
    near, item = lax.optimization_barrier((near, item))
    rows = gathered_rest(near)
    slots = contraction_list[:, 2] - position * perambulators.shape[0]
    tau = mixed_perambulators(slots, contraction_list[:, 1], spin_mix.reshape(-1), perambulators)
    ahead = jnp.concatenate([eigvecs[:, :, :, :, 1:, :], upper], 4).reshape(vectors.shape)
    terms = []
    for slot in range(contraction_list.shape[0]):
        send = layer_items(slot, 1, rows, item, own, ahead, phase, turn, scale)
        keep = layer_items(slot, 0, rows, item, own, ahead, phase, turn, scale)
        terms.append(halved(keep, send, list(range(1, bits))))
    parts = []
    for group in terms:
        others = [r for r in group[-1][0] if r]
        leaving = added(group, [[r] for r in others])
        parts.append([value for _, value in group] + [exchanged(value, 2 * r) for r, value in zip(others, leaving)])
    return diagrams(parts, tau)


def solution(mesh):
    placed = (
        P("cfg", None, None, None, ("space", "diag"), None),
        P("cfg", None, None, None, None, ("space", "diag"), None),
        P(),
        P(),
        P(("cfg", "space", "diag"), None, None, None, None),
        P(("space", "diag"), None),
    )
    return jax.shard_map(
        body,
        mesh=mesh,
        in_specs=placed,
        out_specs=P(("cfg", "space", "diag"), None, None, None, None),
        check_vma=False,
    )
```

```python
import functools
import math

import jax
import jax.numpy as jnp
from jax import lax
from jax.experimental import pallas as pl
from jax.experimental.pallas import tpu as pltpu
from jax.sharding import PartitionSpec as P

NCOL = 3
NMOM = 4
NDISP = 4
LX = 16
LY = 16
LANES = 128
ROWS = 16
SITES = ("space", "diag")
MIB = 1024 * 1024
PLANE_LIMIT = 24 * MIB


def shifted(value, axis, by):
    size = lax.axis_size(axis)
    return lax.ppermute(value, axis, [(i, (i + by) % size) for i in range(size)])


def in_hbm(value):
    return pltpu.with_memory_space_constraint(value, pltpu.HBM)


def exchanged(value, mask):
    size = lax.axis_size(SITES)
    return lax.ppermute(value, SITES, [(i, i ^ mask) for i in range(size)])


def gathered(rows, token):
    bits = lax.axis_size(SITES).bit_length() - 1
    value = rows[None]
    for low in range(0, bits, 2):
        if low == 2:
            value, token = lax.optimization_barrier((value, token))
        steps = range(1, 1 << min(2, bits - low))
        value = jnp.concatenate([value] + [exchanged(value, step << low) for step in steps])
    return value, token


def color_product(matrix, real, imag, adjoint):
    rows = []
    for row in range(NCOL):
        real_part = imag_part = None
        for col in range(NCOL):
            if adjoint:
                mreal, mimag = matrix[0][col][row], matrix[1][col][row]
                one = mreal * real[col] + mimag * imag[col]
                two = mreal * imag[col] - mimag * real[col]
            else:
                mreal, mimag = matrix[0][row][col], matrix[1][row][col]
                one = mreal * real[col] - mimag * imag[col]
                two = mreal * imag[col] + mimag * real[col]
            real_part = one if real_part is None else real_part + one
            imag_part = two if imag_part is None else imag_part + two
        rows.append((real_part, imag_part))
    return rows


def color_loop(link, nvec, width, load, store, adjoint):
    height = math.gcd(nvec, 2 * ROWS)
    for lane in range(0, width, LANES):
        lanes = pl.ds(lane, LANES)
        matrix = [
            [[link(part, row, col, lanes) for col in range(NCOL)] for row in range(NCOL)] for part in range(2)
        ]
        for start in range(0, nvec, height):
            rows = pl.ds(start, height)
            real = [load(0, color, rows, lanes) for color in range(NCOL)]
            imag = [load(1, color, rows, lanes) for color in range(NCOL)]
            for color, (one, two) in enumerate(color_product(matrix, real, imag, adjoint)):
                store(0, color, rows, lanes, one)
                store(1, color, rows, lanes, two)


def fill_tables(position, total_z, plane, momenta_ref, phase_ref, turn_ref):
    width = phase_ref.shape[-1]
    flat = lax.broadcasted_iota(jnp.int32, (1, width), 1)
    xcoord = (flat % LX).astype(jnp.float32)
    ycoord = (flat % plane // LX).astype(jnp.float32)
    zcoord = (position * (width // plane) + flat // plane).astype(jnp.float32)
    for moment in range(NMOM):
        along_x = momenta_ref[moment, 0].astype(jnp.float32)
        along_y = momenta_ref[moment, 1].astype(jnp.float32)
        along_z = momenta_ref[moment, 2].astype(jnp.float32)
        angle = (
            2.0 * math.pi * (along_x * xcoord / LX + along_y * ycoord / LY + along_z * zcoord / total_z)
        )
        phase_ref[moment, 0] = jnp.cos(angle)
        phase_ref[moment, 1] = jnp.sin(angle)
        turn = jnp.full((1, turn_ref.shape[-1]), 2.0 * math.pi / total_z, jnp.float32) * along_z
        turn_ref[moment, 0] = jnp.cos(turn)
        turn_ref[moment, 1] = jnp.sin(turn)


def fill_moves(move_ref):
    width = move_ref.shape[-1]
    source = lax.broadcasted_iota(jnp.int32, (width, width), 0)
    site = lax.broadcasted_iota(jnp.int32, (width, width), 1)
    xcoord = site % LX
    ycoord = site // LX % LY
    for sign, by in enumerate((1, -1)):
        along_x = site - xcoord + (xcoord + LX + by) % LX
        along_y = site + ((ycoord + LY + by) % LY - ycoord) * LX
        move_ref[0, sign] = (source == along_x).astype(jnp.float32).astype(jnp.bfloat16)
        move_ref[1, sign] = (source == along_y).astype(jnp.float32).astype(jnp.bfloat16)


def plane_kernel(
    total_z, plane, scale,
    position_ref, momenta_in, vector_in, link_in,
    item_ref, own_ref, phase_ref, turn_ref,
    momenta_ref, vector_ref, link_ref,
    ahead_x_ref, ahead_y_ref, behind_x_ref, behind_y_ref, adjoint_x_ref, adjoint_y_ref,
    phased_ref, still_ref, moved_x_ref, moved_y_ref, move_ref, momenta_sem, sems,
):
    now = pl.program_id(0)
    slices, _, _, nvec, width = vector_ref.shape

    def copies(index):
        return (
            pltpu.make_async_copy(vector_in.at[index], vector_ref.at[index], sems.at[0, index]),
            pltpu.make_async_copy(link_in.at[index], link_ref.at[index], sems.at[1, index]),
        )

    @pl.when(now == 0)
    def _():
        moments = pltpu.make_async_copy(momenta_in, momenta_ref, momenta_sem)
        moments.start()
        for index in range(slices):
            for copy in copies(index):
                copy.start()
        fill_moves(move_ref)
        moments.wait()
        fill_tables(position_ref[0], total_z, plane, momenta_ref, phase_ref, turn_ref)

    for copy in copies(now):
        copy.wait()

    def linker(direction):
        return lambda part, row, col, lanes: link_ref[now, direction, part, row, col, :, lanes]

    def vector(part, color, rows, lanes):
        return vector_ref[now, part, color, rows, lanes].astype(jnp.float32)

    def gram(moved_ref, disp):
        product = lax.dot_general(
            phased_ref[...], moved_ref[...], (((1,), (1,)), ((), ())), preferred_element_type=jnp.float32
        )
        for moment in range(NMOM):
            start = 2 * moment * nvec
            upper = product[start : start + nvec]
            lower = product[start + nvec : start + 2 * nvec]
            factor = scale if disp == 0 else 0.5 * scale
            item_ref[0, moment, disp, 0] = (factor * (upper[:, :nvec] + lower[:, nvec:])).astype(item_ref.dtype)
            item_ref[0, moment, disp, 1] = (factor * (upper[:, nvec:] - lower[:, :nvec])).astype(item_ref.dtype)

    flat = vector_ref[now].reshape(2 * NCOL * nvec, width)
    for direction, ahead_ref in enumerate((ahead_x_ref, ahead_y_ref)):
        ahead_ref[...] = jnp.dot(
            flat, move_ref[direction, 0], preferred_element_type=jnp.float32
        ).reshape(ahead_ref.shape)

    for color in range(NCOL):
        span = pl.ds(color * width, width)
        for part in range(2):
            still_ref[pl.ds(part * nvec, nvec), span] = vector_ref[now, part, color]
        for start in range(0, nvec, ROWS):
            real = vector_ref[now, 0, color, pl.ds(start, ROWS), :].astype(jnp.float32)
            imag = vector_ref[now, 1, color, pl.ds(start, ROWS), :].astype(jnp.float32)
            for moment in range(NMOM):
                cosine = phase_ref[moment, 0]
                sine = phase_ref[moment, 1]
                first = 2 * moment * nvec + start
                phased_ref[pl.ds(first, ROWS), span] = (cosine * real - sine * imag).astype(jnp.bfloat16)
                phased_ref[pl.ds(first + nvec, ROWS), span] = (sine * real + cosine * imag).astype(jnp.bfloat16)
    gram(still_ref, 0)

    for direction, (adjoint_ref, behind_ref) in enumerate(
        ((adjoint_x_ref, behind_x_ref), (adjoint_y_ref, behind_y_ref))
    ):

        def adjoint(part, color, rows, lanes, value):
            adjoint_ref[part, color, rows, lanes] = value.astype(jnp.bfloat16)

        color_loop(linker(direction), nvec, width, vector, adjoint, True)
        behind_ref[...] = jnp.dot(
            adjoint_ref[...].reshape(2 * NCOL * nvec, width),
            move_ref[direction, 1],
            preferred_element_type=jnp.float32,
        ).reshape(behind_ref.shape)

    for direction, (ahead_ref, behind_ref, moved_ref) in enumerate(
        ((ahead_x_ref, behind_x_ref, moved_x_ref), (ahead_y_ref, behind_y_ref, moved_y_ref))
    ):

        def ahead(part, color, rows, lanes):
            return ahead_ref[part, color, rows, lanes]

        def forward(part, color, rows, lanes, value):
            moved_ref[
                pl.ds(part * nvec + rows.start, rows.size), pl.ds(color * width + lanes.start, lanes.size)
            ] = (value - behind_ref[part, color, rows, lanes]).astype(jnp.bfloat16)

        color_loop(linker(direction), nvec, width, ahead, forward, False)
        gram(moved_ref, direction + 1)

    def own(part, color, rows, lanes, value):
        own_ref[0, part, color, rows, lanes] = value

    color_loop(linker(2), nvec, width, vector, own, True)


def plane_items(position, momenta, vectors, links, total_z, plane, scale):
    slices, _, _, nvec, width = vectors.shape
    color_block = (2, NCOL, nvec, width)
    return pl.pallas_call(
        functools.partial(plane_kernel, total_z, plane, scale),
        grid=(slices,),
        in_specs=[pl.BlockSpec(memory_space=pltpu.SMEM)] + [pl.BlockSpec(memory_space=pltpu.HBM)] * 3,
        out_specs=[
            pl.BlockSpec((1, NMOM, NDISP - 1, 2, nvec, nvec), lambda t: (t, 0, 0, 0, 0, 0)),
            pl.BlockSpec((1,) + color_block, lambda t: (t, 0, 0, 0, 0)),
            pl.BlockSpec((NMOM, 2, 1, width), lambda t: (0, 0, 0, 0)),
            pl.BlockSpec((NMOM, 2, 1, nvec), lambda t: (0, 0, 0, 0)),
        ],
        out_shape=[
            jax.ShapeDtypeStruct((slices, NMOM, NDISP - 1, 2, nvec, nvec), jnp.bfloat16),
            jax.ShapeDtypeStruct(vectors.shape, jnp.float32),
            jax.ShapeDtypeStruct((NMOM, 2, 1, width), jnp.float32),
            jax.ShapeDtypeStruct((NMOM, 2, 1, nvec), jnp.float32),
        ],
        scratch_shapes=[
            pltpu.SMEM(momenta.shape, jnp.int32),
            pltpu.VMEM(vectors.shape, jnp.bfloat16),
            pltpu.VMEM(links.shape, jnp.float32),
        ]
        + [pltpu.VMEM(color_block, jnp.float32)] * 4
        + [pltpu.VMEM(color_block, jnp.bfloat16)] * 2
        + [pltpu.VMEM((NMOM * 2 * nvec, NCOL * width), jnp.bfloat16)]
        + [pltpu.VMEM((2 * nvec, NCOL * width), jnp.bfloat16)] * 3
        + [
            pltpu.VMEM((2, 2, width, width), jnp.bfloat16),
            pltpu.SemaphoreType.DMA,
            pltpu.SemaphoreType.DMA((2, slices)),
        ],
        compiler_params=pltpu.CompilerParams(vmem_limit_bytes=PLANE_LIMIT),
        cost_estimate=pl.CostEstimate(
            flops=slices * 16 * NMOM * nvec * nvec * NCOL * width,
            bytes_accessed=6 * vectors.size + 4 * links.size,
            transcendentals=0,
        ),
        name="plane_items",
    )(position, in_hbm(momenta), in_hbm(vectors), in_hbm(links))


def layer_kernel(
    slot, core, scale, rows_ref, item_ref, own_ref, ahead_ref, phase_ref, turn_ref, out_ref, lhs_ref, listed_ref
):
    nvec, width = own_ref.shape[3:]
    sites = out_ref.shape[0]

    def parts_of(place):
        item = rows_ref[2 * place + core, slot, 0]
        rest = lax.rem(item, NMOM * NDISP)
        return lax.div(item, NMOM * NDISP), lax.div(rest, NDISP), lax.rem(rest, NDISP)

    def bond(place, lhs):
        slice_index, moment, _ = parts_of(place)
        cosine = phase_ref[moment, 0]
        sine = phase_ref[moment, 1]
        for color in range(NCOL):
            span = pl.ds(color * width, width)
            for part in range(2):
                value = own_ref[slice_index, part, color]
                lhs[pl.ds(part * nvec, nvec), span] = (cosine * value).astype(jnp.bfloat16)
                lhs[pl.ds((2 + part) * nvec, nvec), span] = (sine * value).astype(jnp.bfloat16)
        rhs = jnp.concatenate(
            [
                jnp.concatenate([ahead_ref[slice_index, part, color] for color in range(NCOL)], 1)
                for part in range(2)
            ],
            0,
        )
        gram = lax.dot_general(lhs[...], rhs, (((1,), (1,)), ((), ())), preferred_element_type=jnp.float32)
        block = [
            [gram[i * nvec : (i + 1) * nvec, j * nvec : (j + 1) * nvec] for j in range(2)] for i in range(4)
        ]
        cos_real = block[0][0] + block[1][1]
        cos_imag = block[0][1] - block[1][0]
        sin_real = block[2][0] + block[3][1]
        sin_imag = block[2][1] - block[3][0]
        half = 0.5 * scale
        turn_cos = half * turn_ref[moment, 0]
        turn_sin = half * turn_ref[moment, 1]
        back_real = cos_real - sin_imag
        back_imag = cos_imag + sin_real
        real = half * (cos_real + sin_imag) - (turn_cos * back_real - turn_sin * back_imag).T
        imag = half * (cos_imag - sin_real) + (turn_cos * back_imag + turn_sin * back_real).T
        return real.astype(out_ref.dtype), imag.astype(out_ref.dtype)

    found = jnp.int32(0)
    for place in range(sites):
        slice_index, moment, disp = parts_of(place)
        out_ref[place] = item_ref[slice_index, moment, jnp.minimum(disp, NDISP - 2)]
        listed_ref[found] = place
        found = found + (disp == NDISP - 1).astype(jnp.int32)

    @pl.loop(0, lax.div(found + 1, 2))
    def _(pair):
        both = [listed_ref[2 * pair], listed_ref[jnp.minimum(2 * pair + 1, found - 1)]]
        results = [bond(place, lhs_ref.at[index]) for index, place in enumerate(both)]
        for place, (real, imag) in zip(both, results):
            out_ref[place, 0] = real
            out_ref[place, 1] = imag


def layer_items(slot, core, rows, item, own, ahead, phase, turn, scale):
    slices, _, _, nvec, width = own.shape
    sites = rows.shape[0] // 2
    whole = pl.BlockSpec(memory_space=pltpu.VMEM)
    return pl.pallas_call(
        functools.partial(layer_kernel, slot, core, scale),
        in_specs=[pl.BlockSpec(memory_space=pltpu.SMEM)] + [whole] * 5,
        out_specs=whole,
        out_shape=jax.ShapeDtypeStruct((sites, 2, nvec, nvec), jnp.bfloat16),
        scratch_shapes=[
            pltpu.VMEM((2, 4 * nvec, NCOL * width), jnp.bfloat16),
            pltpu.SMEM((sites,), jnp.int32),
        ],
        compiler_params=pltpu.CompilerParams(vmem_limit_bytes=12 * MIB),
        cost_estimate=pl.CostEstimate(
            flops=sites * 4 * nvec * nvec * NCOL * width,
            bytes_accessed=2 * own.size,
            transcendentals=0,
        ),
        name="layer_items",
    )(rows, item, own, ahead, phase, turn)


def add_kernel(places, *refs):
    terms, outs = refs[: len(places[0][0])], refs[len(places[0][0]) :]
    for out_ref, wanted in zip(outs, places):
        for entry, at in enumerate(wanted):
            total = terms[0][at[0]].astype(jnp.float32)
            for ref, index in zip(terms[1:], at[1:]):
                total = total + ref[index].astype(jnp.float32)
            out_ref[entry] = total.astype(out_ref.dtype)


def added(terms, sent, kept=()):
    groups = [(sent, jnp.bfloat16)] + [(kept, jnp.float32)] * bool(kept)
    places = [[tuple(entries.index(r) for entries, _ in terms) for r in group] for group, _ in groups]
    values = [value for _, value in terms]
    tail = values[0].shape[1:]
    whole = pl.BlockSpec(memory_space=pltpu.VMEM)
    size = (len(sent) + len(kept)) * math.prod(tail)
    return pl.pallas_call(
        functools.partial(add_kernel, places),
        in_specs=[whole] * len(values),
        out_specs=[whole] * len(groups),
        out_shape=[jax.ShapeDtypeStruct((len(group),) + tail, dtype) for group, dtype in groups],
        compiler_params=pltpu.CompilerParams(vmem_limit_bytes=8 * MIB),
        cost_estimate=pl.CostEstimate(
            flops=len(values) * size, bytes_accessed=2 * (len(values) + 1) * size, transcendentals=0
        ),
        name="added",
    )(*values)


def halved(keep, send, order):
    entries = list(range(keep.shape[0]))
    terms = [(entries, keep), (entries, exchanged(send, 1))]
    for bit in order[:-2]:
        far = [r for r in entries if r >> (bit - 1) & 1]
        entries = [r for r in entries if r not in far]
        leaving, left = added(terms, far, entries)
        terms = [(entries, left), (entries, exchanged(leaving, 1 << bit))]
    return terms


def finished(terms):
    entries = terms[0][0]
    arrived = []
    for r in sorted(entries, reverse=True)[:-1]:
        last = r == min(r for r in entries if r)
        outs = added(terms, [r], [0] if last else [])
        values = [value for _, value in terms]
        leaving, values = lax.optimization_barrier((outs[0], values))
        terms = [(left, value) for (left, _), value in zip(terms, values)]
        arrived.append(exchanged(leaving, 2 * r))
    return [outs[1]] + arrived


def mix_kernel(slot_ref, structure_ref, weight_ref, tau_ref, out_ref):
    spins, _, nvec, width = tau_ref.shape[1:]
    base = structure_ref[pl.program_id(0)] * spins * spins
    weight = [[weight_ref[base + r * spins + s] for s in range(spins)] for r in range(spins)]

    @pl.loop(0, 2 * nvec // ROWS)
    def _(index):
        part = index // (nvec // ROWS)
        rows = pl.ds(pl.multiple_of(index % (nvec // ROWS) * ROWS, ROWS), ROWS)
        tau = [tau_ref[0, s, part, rows, :].astype(jnp.float32) for s in range(spins)]
        for r in range(spins):
            mixed = weight[r][0] * tau[0]
            for s in range(1, spins):
                mixed = mixed + weight[r][s] * tau[s]
            out_ref[0, r, part, rows, :] = mixed.astype(jnp.bfloat16)


def mixed_perambulators(slots, structures, weights, perambulators):
    block = (1,) + perambulators.shape[1:]
    count = slots.shape[0]
    return pl.pallas_call(
        mix_kernel,
        grid_spec=pltpu.PrefetchScalarGridSpec(
            num_scalar_prefetch=3,
            grid=(count,),
            in_specs=[pl.BlockSpec(block, lambda j, slot, *_: (slot[j], 0, 0, 0, 0))],
            out_specs=pl.BlockSpec(block, lambda j, *_: (j, 0, 0, 0, 0)),
        ),
        out_shape=jax.ShapeDtypeStruct((count,) + perambulators.shape[1:], jnp.bfloat16),
        compiler_params=pltpu.CompilerParams(vmem_limit_bytes=8 * MIB),
        cost_estimate=pl.CostEstimate(
            flops=8 * perambulators.size, bytes_accessed=4 * perambulators.size, transcendentals=0
        ),
        name="mixed_perambulators",
    )(slots, structures, weights, in_hbm(perambulators))


def diagram_kernel(count, *refs):
    terms = refs[: -4]
    tau_ref, out_ref, block_ref, sems = refs[-4:]
    spins, _, nvec, width = tau_ref.shape[1:]
    each = len(terms) // count

    def copy(index, r):
        return pltpu.make_async_copy(block_ref.at[index, r], out_ref.at[index, r], sems.at[index, r])

    for index in range(count):
        real, imag = (
            sum(ref[0, part].astype(jnp.float32) for ref in terms[index * each : (index + 1) * each])
            for part in range(2)
        )
        square = jnp.concatenate(
            [jnp.concatenate([real, -imag], 1), jnp.concatenate([imag, real], 1)], 0
        ).astype(jnp.bfloat16)
        for r in range(spins):
            tau = tau_ref[index, r].reshape(2 * nvec, width)
            block = jnp.dot(square, tau, preferred_element_type=jnp.float32)
            block_ref[index, r] = block.astype(jnp.bfloat16).reshape(2, nvec, width)
            copy(index, r).start()
    for index in range(count):
        for r in range(spins):
            copy(index, r).wait()


def diagrams(terms, tau):
    count, spins, _, nvec, width = tau.shape
    whole = pl.BlockSpec(memory_space=pltpu.VMEM)
    flat = [value for group in terms for value in group]
    return pl.pallas_call(
        functools.partial(diagram_kernel, count),
        in_specs=[whole] * (len(flat) + 1),
        out_specs=pl.BlockSpec(memory_space=pltpu.HBM),
        out_shape=jax.ShapeDtypeStruct(tau.shape, jnp.bfloat16),
        scratch_shapes=[
            pltpu.VMEM(tau.shape, jnp.bfloat16),
            pltpu.SemaphoreType.DMA((count, spins)),
        ],
        compiler_params=pltpu.CompilerParams(vmem_limit_bytes=12 * MIB),
        cost_estimate=pl.CostEstimate(
            flops=8 * nvec * nvec * width * spins * count, bytes_accessed=4 * tau.size, transcendentals=0
        ),
        name="diagrams",
    )(*flat, tau)


def body(eigvecs, gauge_links, momenta, spin_mix, perambulators, contraction_list):
    slices, _, _, nvec, depth, plane = eigvecs.shape
    devices = lax.axis_size(SITES)
    position = lax.axis_index(SITES)
    bits = devices.bit_length() - 1
    total_z = depth * devices
    width = depth * plane
    scale = 1.0 / math.sqrt(NCOL * plane * total_z)
    place = position.reshape(1)
    rows, (after, place) = gathered(contraction_list, (eigvecs, place))
    upper = shifted(after[:, :, :, :, :1, :], SITES, -1)
    vectors = eigvecs.reshape(slices, 2, NCOL, nvec, width)
    links = gauge_links.reshape(slices, 3, 2, NCOL, NCOL, 1, width)
    item, own, phase, turn = plane_items(place, momenta, vectors, links, total_z, plane, scale)
    slots = contraction_list[:, 2] - position * perambulators.shape[0]
    tau = mixed_perambulators(slots, contraction_list[:, 1], spin_mix.reshape(-1), perambulators)
    ahead = jnp.concatenate([eigvecs[:, :, :, :, 1:, :], upper], 4).reshape(vectors.shape)
    terms = []
    for slot in range(contraction_list.shape[0]):
        send = layer_items(slot, 1, rows, item, own, ahead, phase, turn, scale)
        keep = layer_items(slot, 0, rows, item, own, ahead, phase, turn, scale)
        terms.append(halved(keep, send, list(range(1, bits))))
    parts = [finished(group) for group in terms]
    return diagrams(parts, tau)


def solution(mesh):
    placed = (
        P("cfg", None, None, None, ("space", "diag"), None),
        P("cfg", None, None, None, None, ("space", "diag"), None),
        P(),
        P(),
        P(("cfg", "space", "diag"), None, None, None, None),
        P(("space", "diag"), None),
    )
    return jax.shard_map(
        body,
        mesh=mesh,
        in_specs=placed,
        out_specs=P(("cfg", "space", "diag"), None, None, None, None),
        check_vma=False,
    )
```

```python
import functools
import math

import jax
import jax.numpy as jnp
from jax import lax
from jax.experimental import pallas as pl
from jax.experimental.pallas import tpu as pltpu
from jax.sharding import PartitionSpec as P

NCOL = 3
NMOM = 4
NDISP = 4
LX = 16
LY = 16
LANES = 128
ROWS = 16
SITES = ("space", "diag")
MIB = 1024 * 1024
PLANE_LIMIT = 24 * MIB


def shifted(value, axis, by):
    size = lax.axis_size(axis)
    return lax.ppermute(value, axis, [(i, (i + by) % size) for i in range(size)])


def in_hbm(value):
    return pltpu.with_memory_space_constraint(value, pltpu.HBM)


def exchanged(value, mask):
    size = lax.axis_size(SITES)
    return lax.ppermute(value, SITES, [(i, i ^ mask) for i in range(size)])


def gathered(rows, token):
    bits = lax.axis_size(SITES).bit_length() - 1
    value = rows[None]
    for low in range(0, bits, 2):
        if low == 2:
            value, token = lax.optimization_barrier((value, token))
        steps = range(1, 1 << min(2, bits - low))
        value = jnp.concatenate([value] + [exchanged(value, step << low) for step in steps])
    return value, token


def color_product(matrix, real, imag, adjoint):
    rows = []
    for row in range(NCOL):
        real_part = imag_part = None
        for col in range(NCOL):
            if adjoint:
                mreal, mimag = matrix[0][col][row], matrix[1][col][row]
                one = mreal * real[col] + mimag * imag[col]
                two = mreal * imag[col] - mimag * real[col]
            else:
                mreal, mimag = matrix[0][row][col], matrix[1][row][col]
                one = mreal * real[col] - mimag * imag[col]
                two = mreal * imag[col] + mimag * real[col]
            real_part = one if real_part is None else real_part + one
            imag_part = two if imag_part is None else imag_part + two
        rows.append((real_part, imag_part))
    return rows


def color_loop(link, nvec, width, load, store, adjoint):
    height = math.gcd(nvec, 2 * ROWS)
    for lane in range(0, width, LANES):
        lanes = pl.ds(lane, LANES)
        matrix = [
            [[link(part, row, col, lanes) for col in range(NCOL)] for row in range(NCOL)] for part in range(2)
        ]
        for start in range(0, nvec, height):
            rows = pl.ds(start, height)
            real = [load(0, color, rows, lanes) for color in range(NCOL)]
            imag = [load(1, color, rows, lanes) for color in range(NCOL)]
            for color, (one, two) in enumerate(color_product(matrix, real, imag, adjoint)):
                store(0, color, rows, lanes, one)
                store(1, color, rows, lanes, two)


def fill_tables(position, total_z, plane, momenta_ref, phase_ref, turn_ref):
    width = phase_ref.shape[-1]
    flat = lax.broadcasted_iota(jnp.int32, (1, width), 1)
    xcoord = (flat % LX).astype(jnp.float32)
    ycoord = (flat % plane // LX).astype(jnp.float32)
    zcoord = (position * (width // plane) + flat // plane).astype(jnp.float32)
    for moment in range(NMOM):
        along_x = momenta_ref[moment, 0].astype(jnp.float32)
        along_y = momenta_ref[moment, 1].astype(jnp.float32)
        along_z = momenta_ref[moment, 2].astype(jnp.float32)
        angle = (
            2.0 * math.pi * (along_x * xcoord / LX + along_y * ycoord / LY + along_z * zcoord / total_z)
        )
        phase_ref[moment, 0] = jnp.cos(angle)
        phase_ref[moment, 1] = jnp.sin(angle)
        turn = jnp.full((1, turn_ref.shape[-1]), 2.0 * math.pi / total_z, jnp.float32) * along_z
        turn_ref[moment, 0] = jnp.cos(turn)
        turn_ref[moment, 1] = jnp.sin(turn)


def fill_moves(move_ref):
    width = move_ref.shape[-1]
    source = lax.broadcasted_iota(jnp.int32, (width, width), 0)
    site = lax.broadcasted_iota(jnp.int32, (width, width), 1)
    xcoord = site % LX
    ycoord = site // LX % LY
    for sign, by in enumerate((1, -1)):
        along_x = site - xcoord + (xcoord + LX + by) % LX
        along_y = site + ((ycoord + LY + by) % LY - ycoord) * LX
        move_ref[0, sign] = (source == along_x).astype(jnp.float32).astype(jnp.bfloat16)
        move_ref[1, sign] = (source == along_y).astype(jnp.float32).astype(jnp.bfloat16)


def plane_kernel(
    total_z, plane, scale,
    position_ref, momenta_in, vector_in, link_in,
    item_ref, own_ref, phase_ref, turn_ref,
    momenta_ref, vector_ref, link_ref,
    ahead_x_ref, ahead_y_ref, behind_x_ref, behind_y_ref, adjoint_x_ref, adjoint_y_ref,
    phased_ref, still_ref, moved_x_ref, moved_y_ref, move_ref, momenta_sem, sems,
):
    now = pl.program_id(0)
    slices, _, _, nvec, width = vector_ref.shape

    def copies(index):
        return (
            pltpu.make_async_copy(vector_in.at[index], vector_ref.at[index], sems.at[0, index]),
            pltpu.make_async_copy(link_in.at[index], link_ref.at[index], sems.at[1, index]),
        )

    @pl.when(now == 0)
    def _():
        moments = pltpu.make_async_copy(momenta_in, momenta_ref, momenta_sem)
        moments.start()
        for index in range(slices):
            for copy in copies(index):
                copy.start()
        fill_moves(move_ref)
        moments.wait()
        fill_tables(position_ref[0], total_z, plane, momenta_ref, phase_ref, turn_ref)

    for copy in copies(now):
        copy.wait()

    def linker(direction):
        return lambda part, row, col, lanes: link_ref[now, direction, part, row, col, :, lanes]

    def vector(part, color, rows, lanes):
        return vector_ref[now, part, color, rows, lanes].astype(jnp.float32)

    def gram(moved_ref, disp):
        product = lax.dot_general(
            phased_ref[...], moved_ref[...], (((1,), (1,)), ((), ())), preferred_element_type=jnp.float32
        )
        for moment in range(NMOM):
            start = 2 * moment * nvec
            upper = product[start : start + nvec]
            lower = product[start + nvec : start + 2 * nvec]
            factor = scale if disp == 0 else 0.5 * scale
            item_ref[0, moment, disp, 0] = (factor * (upper[:, :nvec] + lower[:, nvec:])).astype(item_ref.dtype)
            item_ref[0, moment, disp, 1] = (factor * (upper[:, nvec:] - lower[:, :nvec])).astype(item_ref.dtype)

    flat = vector_ref[now].reshape(2 * NCOL * nvec, width)
    for direction, ahead_ref in enumerate((ahead_x_ref, ahead_y_ref)):
        ahead_ref[...] = jnp.dot(
            flat, move_ref[direction, 0], preferred_element_type=jnp.float32
        ).reshape(ahead_ref.shape)

    for color in range(NCOL):
        span = pl.ds(color * width, width)
        for part in range(2):
            still_ref[pl.ds(part * nvec, nvec), span] = vector_ref[now, part, color]
        for start in range(0, nvec, ROWS):
            real = vector_ref[now, 0, color, pl.ds(start, ROWS), :].astype(jnp.float32)
            imag = vector_ref[now, 1, color, pl.ds(start, ROWS), :].astype(jnp.float32)
            for moment in range(NMOM):
                cosine = phase_ref[moment, 0]
                sine = phase_ref[moment, 1]
                first = 2 * moment * nvec + start
                phased_ref[pl.ds(first, ROWS), span] = (cosine * real - sine * imag).astype(jnp.bfloat16)
                phased_ref[pl.ds(first + nvec, ROWS), span] = (sine * real + cosine * imag).astype(jnp.bfloat16)
    gram(still_ref, 0)

    for direction, (adjoint_ref, behind_ref) in enumerate(
        ((adjoint_x_ref, behind_x_ref), (adjoint_y_ref, behind_y_ref))
    ):

        def adjoint(part, color, rows, lanes, value):
            adjoint_ref[part, color, rows, lanes] = value.astype(jnp.bfloat16)

        color_loop(linker(direction), nvec, width, vector, adjoint, True)
        behind_ref[...] = jnp.dot(
            adjoint_ref[...].reshape(2 * NCOL * nvec, width),
            move_ref[direction, 1],
            preferred_element_type=jnp.float32,
        ).reshape(behind_ref.shape)

    for direction, (ahead_ref, behind_ref, moved_ref) in enumerate(
        ((ahead_x_ref, behind_x_ref, moved_x_ref), (ahead_y_ref, behind_y_ref, moved_y_ref))
    ):

        def ahead(part, color, rows, lanes):
            return ahead_ref[part, color, rows, lanes]

        def forward(part, color, rows, lanes, value):
            moved_ref[
                pl.ds(part * nvec + rows.start, rows.size), pl.ds(color * width + lanes.start, lanes.size)
            ] = (value - behind_ref[part, color, rows, lanes]).astype(jnp.bfloat16)

        color_loop(linker(direction), nvec, width, ahead, forward, False)
        gram(moved_ref, direction + 1)

    def own(part, color, rows, lanes, value):
        own_ref[0, part, color, rows, lanes] = value

    color_loop(linker(2), nvec, width, vector, own, True)


def plane_items(position, momenta, vectors, links, total_z, plane, scale):
    slices, _, _, nvec, width = vectors.shape
    color_block = (2, NCOL, nvec, width)
    return pl.pallas_call(
        functools.partial(plane_kernel, total_z, plane, scale),
        grid=(slices,),
        in_specs=[pl.BlockSpec(memory_space=pltpu.SMEM)] + [pl.BlockSpec(memory_space=pltpu.HBM)] * 3,
        out_specs=[
            pl.BlockSpec((1, NMOM, NDISP - 1, 2, nvec, nvec), lambda t: (t, 0, 0, 0, 0, 0)),
            pl.BlockSpec((1,) + color_block, lambda t: (t, 0, 0, 0, 0)),
            pl.BlockSpec((NMOM, 2, 1, width), lambda t: (0, 0, 0, 0)),
            pl.BlockSpec((NMOM, 2, 1, nvec), lambda t: (0, 0, 0, 0)),
        ],
        out_shape=[
            jax.ShapeDtypeStruct((slices, NMOM, NDISP - 1, 2, nvec, nvec), jnp.bfloat16),
            jax.ShapeDtypeStruct(vectors.shape, jnp.float32),
            jax.ShapeDtypeStruct((NMOM, 2, 1, width), jnp.float32),
            jax.ShapeDtypeStruct((NMOM, 2, 1, nvec), jnp.float32),
        ],
        scratch_shapes=[
            pltpu.SMEM(momenta.shape, jnp.int32),
            pltpu.VMEM(vectors.shape, jnp.bfloat16),
            pltpu.VMEM(links.shape, jnp.float32),
        ]
        + [pltpu.VMEM(color_block, jnp.float32)] * 4
        + [pltpu.VMEM(color_block, jnp.bfloat16)] * 2
        + [pltpu.VMEM((NMOM * 2 * nvec, NCOL * width), jnp.bfloat16)]
        + [pltpu.VMEM((2 * nvec, NCOL * width), jnp.bfloat16)] * 3
        + [
            pltpu.VMEM((2, 2, width, width), jnp.bfloat16),
            pltpu.SemaphoreType.DMA,
            pltpu.SemaphoreType.DMA((2, slices)),
        ],
        compiler_params=pltpu.CompilerParams(vmem_limit_bytes=PLANE_LIMIT),
        cost_estimate=pl.CostEstimate(
            flops=slices * 16 * NMOM * nvec * nvec * NCOL * width,
            bytes_accessed=6 * vectors.size + 4 * links.size,
            transcendentals=0,
        ),
        name="plane_items",
    )(position, in_hbm(momenta), in_hbm(vectors), in_hbm(links))


def layer_kernel(
    core, scale, rows_ref, item_ref, own_ref, ahead_ref, phase_ref, turn_ref, out_ref, lhs_ref, listed_ref
):
    nvec, width = own_ref.shape[3:]
    total = out_ref.shape[0]
    sites = rows_ref.shape[0] // 2

    def parts_of(place):
        item = rows_ref[2 * lax.rem(place, sites) + core, lax.div(place, sites), 0]
        rest = lax.rem(item, NMOM * NDISP)
        return lax.div(item, NMOM * NDISP), lax.div(rest, NDISP), lax.rem(rest, NDISP)

    def bond(place, lhs):
        slice_index, moment, _ = parts_of(place)
        cosine = phase_ref[moment, 0]
        sine = phase_ref[moment, 1]
        for color in range(NCOL):
            span = pl.ds(color * width, width)
            for part in range(2):
                value = own_ref[slice_index, part, color]
                lhs[pl.ds(part * nvec, nvec), span] = (cosine * value).astype(jnp.bfloat16)
                lhs[pl.ds((2 + part) * nvec, nvec), span] = (sine * value).astype(jnp.bfloat16)
        rhs = jnp.concatenate(
            [
                jnp.concatenate([ahead_ref[slice_index, part, color] for color in range(NCOL)], 1)
                for part in range(2)
            ],
            0,
        )
        gram = lax.dot_general(lhs[...], rhs, (((1,), (1,)), ((), ())), preferred_element_type=jnp.float32)
        block = [
            [gram[i * nvec : (i + 1) * nvec, j * nvec : (j + 1) * nvec] for j in range(2)] for i in range(4)
        ]
        cos_real = block[0][0] + block[1][1]
        cos_imag = block[0][1] - block[1][0]
        sin_real = block[2][0] + block[3][1]
        sin_imag = block[2][1] - block[3][0]
        half = 0.5 * scale
        turn_cos = half * turn_ref[moment, 0]
        turn_sin = half * turn_ref[moment, 1]
        back_real = cos_real - sin_imag
        back_imag = cos_imag + sin_real
        real = half * (cos_real + sin_imag) - (turn_cos * back_real - turn_sin * back_imag).T
        imag = half * (cos_imag - sin_real) + (turn_cos * back_imag + turn_sin * back_real).T
        return real.astype(out_ref.dtype), imag.astype(out_ref.dtype)

    found = jnp.int32(0)
    for place in range(total):
        slice_index, moment, disp = parts_of(jnp.int32(place))
        out_ref[place] = item_ref[slice_index, moment, jnp.minimum(disp, NDISP - 2)]
        listed_ref[found] = place
        found = found + (disp == NDISP - 1).astype(jnp.int32)

    @pl.loop(0, lax.div(found + 1, 2))
    def _(pair):
        both = [listed_ref[2 * pair], listed_ref[jnp.minimum(2 * pair + 1, found - 1)]]
        results = [bond(place, lhs_ref.at[index]) for index, place in enumerate(both)]
        for place, (real, imag) in zip(both, results):
            out_ref[place, 0] = real
            out_ref[place, 1] = imag


def layer_items(core, rows, item, own, ahead, phase, turn, scale):
    slices, _, _, nvec, width = own.shape
    devices, slots, _ = rows.shape
    total = slots * devices // 2
    whole = pl.BlockSpec(memory_space=pltpu.VMEM)
    return pl.pallas_call(
        functools.partial(layer_kernel, core, scale),
        in_specs=[pl.BlockSpec(memory_space=pltpu.SMEM)] + [whole] * 5,
        out_specs=whole,
        out_shape=jax.ShapeDtypeStruct((total, 2, nvec, nvec), jnp.bfloat16),
        scratch_shapes=[
            pltpu.VMEM((2, 4 * nvec, NCOL * width), jnp.bfloat16),
            pltpu.SMEM((total,), jnp.int32),
        ],
        compiler_params=pltpu.CompilerParams(vmem_limit_bytes=12 * MIB),
        cost_estimate=pl.CostEstimate(
            flops=total * 4 * nvec * nvec * NCOL * width,
            bytes_accessed=2 * own.size,
            transcendentals=0,
        ),
        name="layer_items",
    )(rows, item, own, ahead, phase, turn)


def add_kernel(places, *refs):
    terms, outs = refs[: len(places[0][0])], refs[len(places[0][0]) :]
    for out_ref, wanted in zip(outs, places):
        for entry, at in enumerate(wanted):
            total = terms[0][at[0]].astype(jnp.float32)
            for ref, index in zip(terms[1:], at[1:]):
                total = total + ref[index].astype(jnp.float32)
            out_ref[entry] = total.astype(out_ref.dtype)


def added(terms, sent, kept=()):
    groups = [(sent, jnp.bfloat16)] + [(kept, jnp.float32)] * bool(kept)
    places = [[tuple(entries.index(r) for entries, _ in terms) for r in group] for group, _ in groups]
    values = [value for _, value in terms]
    tail = values[0].shape[1:]
    whole = pl.BlockSpec(memory_space=pltpu.VMEM)
    size = (len(sent) + len(kept)) * math.prod(tail)
    return pl.pallas_call(
        functools.partial(add_kernel, places),
        in_specs=[whole] * len(values),
        out_specs=[whole] * len(groups),
        out_shape=[jax.ShapeDtypeStruct((len(group),) + tail, dtype) for group, dtype in groups],
        compiler_params=pltpu.CompilerParams(vmem_limit_bytes=8 * MIB),
        cost_estimate=pl.CostEstimate(
            flops=len(values) * size, bytes_accessed=2 * (len(values) + 1) * size, transcendentals=0
        ),
        name="added",
    )(*values)


def halved(terms, slot, order):
    entries = [entry for entry in terms[0][0] if entry[0] == slot]
    for bit in order[:-2]:
        far = [entry for entry in entries if entry[1] >> (bit - 1) & 1]
        entries = [entry for entry in entries if entry not in far]
        leaving, left = added(terms, far, entries)
        terms = [(entries, left), (entries, exchanged(leaving, 1 << bit))]
    return terms


def finished(terms, slot):
    others = sorted(r for _, r in terms[0][0] if r)
    arrived = []
    for r in others:
        outs = added(terms, [(slot, r)], [(slot, 0)] if r == others[-1] else [])
        arrived.append(exchanged(outs[0], 2 * r))
    return [outs[1]] + arrived


def mix_kernel(slot_ref, structure_ref, weight_ref, tau_ref, out_ref):
    spins, _, nvec, width = tau_ref.shape[1:]
    base = structure_ref[pl.program_id(0)] * spins * spins
    weight = [[weight_ref[base + r * spins + s] for s in range(spins)] for r in range(spins)]

    @pl.loop(0, 2 * nvec // ROWS)
    def _(index):
        part = index // (nvec // ROWS)
        rows = pl.ds(pl.multiple_of(index % (nvec // ROWS) * ROWS, ROWS), ROWS)
        tau = [tau_ref[0, s, part, rows, :].astype(jnp.float32) for s in range(spins)]
        for r in range(spins):
            mixed = weight[r][0] * tau[0]
            for s in range(1, spins):
                mixed = mixed + weight[r][s] * tau[s]
            out_ref[0, r, part, rows, :] = mixed.astype(jnp.bfloat16)


def mixed_perambulators(slots, structures, weights, perambulators):
    block = (1,) + perambulators.shape[1:]
    count = slots.shape[0]
    return pl.pallas_call(
        mix_kernel,
        grid_spec=pltpu.PrefetchScalarGridSpec(
            num_scalar_prefetch=3,
            grid=(count,),
            in_specs=[pl.BlockSpec(block, lambda j, slot, *_: (slot[j], 0, 0, 0, 0))],
            out_specs=pl.BlockSpec(block, lambda j, *_: (j, 0, 0, 0, 0)),
        ),
        out_shape=jax.ShapeDtypeStruct((count,) + perambulators.shape[1:], jnp.bfloat16),
        compiler_params=pltpu.CompilerParams(vmem_limit_bytes=8 * MIB),
        cost_estimate=pl.CostEstimate(
            flops=8 * perambulators.size, bytes_accessed=4 * perambulators.size, transcendentals=0
        ),
        name="mixed_perambulators",
    )(slots, structures, weights, in_hbm(perambulators))


def diagram_kernel(count, *refs):
    terms = refs[: -4]
    tau_ref, out_ref, block_ref, sems = refs[-4:]
    spins, _, nvec, width = tau_ref.shape[1:]
    each = len(terms) // count

    def copy(index, r):
        return pltpu.make_async_copy(block_ref.at[index, r], out_ref.at[index, r], sems.at[index, r])

    for index in range(count):
        real, imag = (
            sum(ref[0, part].astype(jnp.float32) for ref in terms[index * each : (index + 1) * each])
            for part in range(2)
        )
        square = jnp.concatenate(
            [jnp.concatenate([real, -imag], 1), jnp.concatenate([imag, real], 1)], 0
        ).astype(jnp.bfloat16)
        for r in range(spins):
            tau = tau_ref[index, r].reshape(2 * nvec, width)
            block = jnp.dot(square, tau, preferred_element_type=jnp.float32)
            block_ref[index, r] = block.astype(jnp.bfloat16).reshape(2, nvec, width)
            copy(index, r).start()
    for index in range(count):
        for r in range(spins):
            copy(index, r).wait()


def diagrams(terms, tau):
    count, spins, _, nvec, width = tau.shape
    whole = pl.BlockSpec(memory_space=pltpu.VMEM)
    flat = [value for group in terms for value in group]
    return pl.pallas_call(
        functools.partial(diagram_kernel, count),
        in_specs=[whole] * (len(flat) + 1),
        out_specs=pl.BlockSpec(memory_space=pltpu.HBM),
        out_shape=jax.ShapeDtypeStruct(tau.shape, jnp.bfloat16),
        scratch_shapes=[
            pltpu.VMEM(tau.shape, jnp.bfloat16),
            pltpu.SemaphoreType.DMA((count, spins)),
        ],
        compiler_params=pltpu.CompilerParams(vmem_limit_bytes=12 * MIB),
        cost_estimate=pl.CostEstimate(
            flops=8 * nvec * nvec * width * spins * count, bytes_accessed=4 * tau.size, transcendentals=0
        ),
        name="diagrams",
    )(*flat, tau)


def body(eigvecs, gauge_links, momenta, spin_mix, perambulators, contraction_list):
    slices, _, _, nvec, depth, plane = eigvecs.shape
    devices = lax.axis_size(SITES)
    position = lax.axis_index(SITES)
    bits = devices.bit_length() - 1
    total_z = depth * devices
    width = depth * plane
    scale = 1.0 / math.sqrt(NCOL * plane * total_z)
    place = position.reshape(1)
    rows, (after, place) = gathered(contraction_list, (eigvecs, place))
    upper = shifted(after[:, :, :, :, :1, :], SITES, -1)
    vectors = eigvecs.reshape(slices, 2, NCOL, nvec, width)
    links = gauge_links.reshape(slices, 3, 2, NCOL, NCOL, 1, width)
    item, own, phase, turn = plane_items(place, momenta, vectors, links, total_z, plane, scale)
    chosen = contraction_list[:, 2] - position * perambulators.shape[0]
    tau = mixed_perambulators(chosen, contraction_list[:, 1], spin_mix.reshape(-1), perambulators)
    ahead = jnp.concatenate([eigvecs[:, :, :, :, 1:, :], upper], 4).reshape(vectors.shape)
    send = layer_items(1, rows, item, own, ahead, phase, turn, scale)
    keep = layer_items(0, rows, item, own, ahead, phase, turn, scale)
    slots = range(contraction_list.shape[0])
    entries = [(slot, r) for slot in slots for r in range(devices // 2)]
    terms = [(entries, keep), (entries, exchanged(send, 1))]
    groups = [
        halved(terms, slot, [1 + (slot + step) % (bits - 1) for step in range(bits - 1)]) for slot in slots
    ]
    values, tau = lax.optimization_barrier(([value for _, value in groups[0]], tau))
    groups[0] = [(left, value) for (left, _), value in zip(groups[0], values)]
    parts = [finished(group, slot) for slot, group in zip(slots, groups)]
    return diagrams(parts, tau)


def solution(mesh):
    placed = (
        P("cfg", None, None, None, ("space", "diag"), None),
        P("cfg", None, None, None, None, ("space", "diag"), None),
        P(),
        P(),
        P(("cfg", "space", "diag"), None, None, None, None),
        P(("space", "diag"), None),
    )
    return jax.shard_map(
        body,
        mesh=mesh,
        in_specs=placed,
        out_specs=P(("cfg", "space", "diag"), None, None, None, None),
        check_vma=False,
    )
```

```python
import functools
import math

import jax
import jax.numpy as jnp
from jax import lax
from jax.experimental import pallas as pl
from jax.experimental.pallas import tpu as pltpu
from jax.sharding import PartitionSpec as P

NCOL = 3
NMOM = 4
NDISP = 4
LX = 16
LY = 16
LANES = 128
ROWS = 16
SITES = ("space", "diag")
MIB = 1024 * 1024
PLANE_LIMIT = 24 * MIB


def shifted(value, axis, by):
    size = lax.axis_size(axis)
    return lax.ppermute(value, axis, [(i, (i + by) % size) for i in range(size)])


def in_hbm(value):
    return pltpu.with_memory_space_constraint(value, pltpu.HBM)


def exchanged(value, mask):
    size = lax.axis_size(SITES)
    return lax.ppermute(value, SITES, [(i, i ^ mask) for i in range(size)])


def gathered(rows, early, late):
    bits = lax.axis_size(SITES).bit_length() - 1
    value = rows[None]
    for low in range(0, bits, 2):
        if low == 2:
            value, late = lax.optimization_barrier((value, late))
        arrived = [exchanged(value, step << low) for step in range(1, 1 << min(2, bits - low))]
        if low == 0:
            arrived[-1], early = lax.optimization_barrier((arrived[-1], early))
        value = jnp.concatenate([value] + arrived)
    return value, early, late


def color_product(matrix, real, imag, adjoint):
    rows = []
    for row in range(NCOL):
        real_part = imag_part = None
        for col in range(NCOL):
            if adjoint:
                mreal, mimag = matrix[0][col][row], matrix[1][col][row]
                one = mreal * real[col] + mimag * imag[col]
                two = mreal * imag[col] - mimag * real[col]
            else:
                mreal, mimag = matrix[0][row][col], matrix[1][row][col]
                one = mreal * real[col] - mimag * imag[col]
                two = mreal * imag[col] + mimag * real[col]
            real_part = one if real_part is None else real_part + one
            imag_part = two if imag_part is None else imag_part + two
        rows.append((real_part, imag_part))
    return rows


def color_loop(link, nvec, width, load, store, adjoint):
    height = math.gcd(nvec, 2 * ROWS)
    for lane in range(0, width, LANES):
        lanes = pl.ds(lane, LANES)
        matrix = [
            [[link(part, row, col, lanes) for col in range(NCOL)] for row in range(NCOL)] for part in range(2)
        ]
        for start in range(0, nvec, height):
            rows = pl.ds(start, height)
            real = [load(0, color, rows, lanes) for color in range(NCOL)]
            imag = [load(1, color, rows, lanes) for color in range(NCOL)]
            for color, (one, two) in enumerate(color_product(matrix, real, imag, adjoint)):
                store(0, color, rows, lanes, one)
                store(1, color, rows, lanes, two)


def fill_tables(position, total_z, plane, momenta_ref, phase_ref, turn_ref):
    width = phase_ref.shape[-1]
    flat = lax.broadcasted_iota(jnp.int32, (1, width), 1)
    xcoord = (flat % LX).astype(jnp.float32)
    ycoord = (flat % plane // LX).astype(jnp.float32)
    zcoord = (position * (width // plane) + flat // plane).astype(jnp.float32)
    for moment in range(NMOM):
        along_x = momenta_ref[moment, 0].astype(jnp.float32)
        along_y = momenta_ref[moment, 1].astype(jnp.float32)
        along_z = momenta_ref[moment, 2].astype(jnp.float32)
        angle = (
            2.0 * math.pi * (along_x * xcoord / LX + along_y * ycoord / LY + along_z * zcoord / total_z)
        )
        phase_ref[moment, 0] = jnp.cos(angle)
        phase_ref[moment, 1] = jnp.sin(angle)
        turn = jnp.full((1, turn_ref.shape[-1]), 2.0 * math.pi / total_z, jnp.float32) * along_z
        turn_ref[moment, 0] = jnp.cos(turn)
        turn_ref[moment, 1] = jnp.sin(turn)


def fill_moves(move_ref):
    width = move_ref.shape[-1]
    source = lax.broadcasted_iota(jnp.int32, (width, width), 0)
    site = lax.broadcasted_iota(jnp.int32, (width, width), 1)
    xcoord = site % LX
    ycoord = site // LX % LY
    for sign, by in enumerate((1, -1)):
        along_x = site - xcoord + (xcoord + LX + by) % LX
        along_y = site + ((ycoord + LY + by) % LY - ycoord) * LX
        move_ref[0, sign] = (source == along_x).astype(jnp.float32).astype(jnp.bfloat16)
        move_ref[1, sign] = (source == along_y).astype(jnp.float32).astype(jnp.bfloat16)


def plane_kernel(
    total_z, plane, scale,
    position_ref, momenta_in, vector_in, link_in,
    item_ref, own_ref, phase_ref, turn_ref,
    momenta_ref, vector_ref, link_ref,
    ahead_x_ref, ahead_y_ref, behind_x_ref, behind_y_ref, adjoint_x_ref, adjoint_y_ref,
    phased_ref, still_ref, moved_x_ref, moved_y_ref, move_ref, momenta_sem, sems,
):
    now = pl.program_id(0)
    slices, _, _, nvec, width = vector_ref.shape

    def copies(index):
        return (
            pltpu.make_async_copy(vector_in.at[index], vector_ref.at[index], sems.at[0, index]),
            pltpu.make_async_copy(link_in.at[index], link_ref.at[index], sems.at[1, index]),
        )

    @pl.when(now == 0)
    def _():
        moments = pltpu.make_async_copy(momenta_in, momenta_ref, momenta_sem)
        moments.start()
        for index in range(slices):
            for copy in copies(index):
                copy.start()
        fill_moves(move_ref)
        moments.wait()
        fill_tables(position_ref[0], total_z, plane, momenta_ref, phase_ref, turn_ref)

    for copy in copies(now):
        copy.wait()

    def linker(direction):
        return lambda part, row, col, lanes: link_ref[now, direction, part, row, col, :, lanes]

    def vector(part, color, rows, lanes):
        return vector_ref[now, part, color, rows, lanes].astype(jnp.float32)

    def gram(moved_ref, disp):
        product = lax.dot_general(
            phased_ref[...], moved_ref[...], (((1,), (1,)), ((), ())), preferred_element_type=jnp.float32
        )
        for moment in range(NMOM):
            start = 2 * moment * nvec
            upper = product[start : start + nvec]
            lower = product[start + nvec : start + 2 * nvec]
            factor = scale if disp == 0 else 0.5 * scale
            item_ref[0, moment, disp, 0] = (factor * (upper[:, :nvec] + lower[:, nvec:])).astype(item_ref.dtype)
            item_ref[0, moment, disp, 1] = (factor * (upper[:, nvec:] - lower[:, :nvec])).astype(item_ref.dtype)

    flat = vector_ref[now].reshape(2 * NCOL * nvec, width)
    for direction, ahead_ref in enumerate((ahead_x_ref, ahead_y_ref)):
        ahead_ref[...] = jnp.dot(
            flat, move_ref[direction, 0], preferred_element_type=jnp.float32
        ).reshape(ahead_ref.shape)

    for color in range(NCOL):
        span = pl.ds(color * width, width)
        for part in range(2):
            still_ref[pl.ds(part * nvec, nvec), span] = vector_ref[now, part, color]
        for start in range(0, nvec, ROWS):
            real = vector_ref[now, 0, color, pl.ds(start, ROWS), :].astype(jnp.float32)
            imag = vector_ref[now, 1, color, pl.ds(start, ROWS), :].astype(jnp.float32)
            for moment in range(NMOM):
                cosine = phase_ref[moment, 0]
                sine = phase_ref[moment, 1]
                first = 2 * moment * nvec + start
                phased_ref[pl.ds(first, ROWS), span] = (cosine * real - sine * imag).astype(jnp.bfloat16)
                phased_ref[pl.ds(first + nvec, ROWS), span] = (sine * real + cosine * imag).astype(jnp.bfloat16)
    gram(still_ref, 0)

    for direction, (adjoint_ref, behind_ref) in enumerate(
        ((adjoint_x_ref, behind_x_ref), (adjoint_y_ref, behind_y_ref))
    ):

        def adjoint(part, color, rows, lanes, value):
            adjoint_ref[part, color, rows, lanes] = value.astype(jnp.bfloat16)

        color_loop(linker(direction), nvec, width, vector, adjoint, True)
        behind_ref[...] = jnp.dot(
            adjoint_ref[...].reshape(2 * NCOL * nvec, width),
            move_ref[direction, 1],
            preferred_element_type=jnp.float32,
        ).reshape(behind_ref.shape)

    for direction, (ahead_ref, behind_ref, moved_ref) in enumerate(
        ((ahead_x_ref, behind_x_ref, moved_x_ref), (ahead_y_ref, behind_y_ref, moved_y_ref))
    ):

        def ahead(part, color, rows, lanes):
            return ahead_ref[part, color, rows, lanes]

        def forward(part, color, rows, lanes, value):
            moved_ref[
                pl.ds(part * nvec + rows.start, rows.size), pl.ds(color * width + lanes.start, lanes.size)
            ] = (value - behind_ref[part, color, rows, lanes]).astype(jnp.bfloat16)

        color_loop(linker(direction), nvec, width, ahead, forward, False)
        gram(moved_ref, direction + 1)

    def own(part, color, rows, lanes, value):
        own_ref[0, part, color, rows, lanes] = value

    color_loop(linker(2), nvec, width, vector, own, True)


def plane_items(position, momenta, vectors, links, total_z, plane, scale):
    slices, _, _, nvec, width = vectors.shape
    color_block = (2, NCOL, nvec, width)
    return pl.pallas_call(
        functools.partial(plane_kernel, total_z, plane, scale),
        grid=(slices,),
        in_specs=[pl.BlockSpec(memory_space=pltpu.SMEM)] + [pl.BlockSpec(memory_space=pltpu.HBM)] * 3,
        out_specs=[
            pl.BlockSpec((1, NMOM, NDISP - 1, 2, nvec, nvec), lambda t: (t, 0, 0, 0, 0, 0)),
            pl.BlockSpec((1,) + color_block, lambda t: (t, 0, 0, 0, 0)),
            pl.BlockSpec((NMOM, 2, 1, width), lambda t: (0, 0, 0, 0)),
            pl.BlockSpec((NMOM, 2, 1, nvec), lambda t: (0, 0, 0, 0)),
        ],
        out_shape=[
            jax.ShapeDtypeStruct((slices, NMOM, NDISP - 1, 2, nvec, nvec), jnp.bfloat16),
            jax.ShapeDtypeStruct(vectors.shape, jnp.float32),
            jax.ShapeDtypeStruct((NMOM, 2, 1, width), jnp.float32),
            jax.ShapeDtypeStruct((NMOM, 2, 1, nvec), jnp.float32),
        ],
        scratch_shapes=[
            pltpu.SMEM(momenta.shape, jnp.int32),
            pltpu.VMEM(vectors.shape, jnp.bfloat16),
            pltpu.VMEM(links.shape, jnp.float32),
        ]
        + [pltpu.VMEM(color_block, jnp.float32)] * 4
        + [pltpu.VMEM(color_block, jnp.bfloat16)] * 2
        + [pltpu.VMEM((NMOM * 2 * nvec, NCOL * width), jnp.bfloat16)]
        + [pltpu.VMEM((2 * nvec, NCOL * width), jnp.bfloat16)] * 3
        + [
            pltpu.VMEM((2, 2, width, width), jnp.bfloat16),
            pltpu.SemaphoreType.DMA,
            pltpu.SemaphoreType.DMA((2, slices)),
        ],
        compiler_params=pltpu.CompilerParams(vmem_limit_bytes=PLANE_LIMIT),
        cost_estimate=pl.CostEstimate(
            flops=slices * 16 * NMOM * nvec * nvec * NCOL * width,
            bytes_accessed=6 * vectors.size + 4 * links.size,
            transcendentals=0,
        ),
        name="plane_items",
    )(position, in_hbm(momenta), in_hbm(vectors), in_hbm(links))


def layer_kernel(
    core, scale, rows_ref, item_ref, own_ref, ahead_ref, phase_ref, turn_ref, out_ref, lhs_ref, listed_ref
):
    nvec, width = own_ref.shape[3:]
    total = out_ref.shape[0]
    sites = rows_ref.shape[0] // 2

    def parts_of(place):
        item = rows_ref[2 * lax.rem(place, sites) + core, lax.div(place, sites), 0]
        rest = lax.rem(item, NMOM * NDISP)
        return lax.div(item, NMOM * NDISP), lax.div(rest, NDISP), lax.rem(rest, NDISP)

    def bond(place, lhs):
        slice_index, moment, _ = parts_of(place)
        cosine = phase_ref[moment, 0]
        sine = phase_ref[moment, 1]
        for color in range(NCOL):
            span = pl.ds(color * width, width)
            for part in range(2):
                value = own_ref[slice_index, part, color]
                lhs[pl.ds(part * nvec, nvec), span] = (cosine * value).astype(jnp.bfloat16)
                lhs[pl.ds((2 + part) * nvec, nvec), span] = (sine * value).astype(jnp.bfloat16)
        rhs = jnp.concatenate(
            [
                jnp.concatenate([ahead_ref[slice_index, part, color] for color in range(NCOL)], 1)
                for part in range(2)
            ],
            0,
        )
        gram = lax.dot_general(lhs[...], rhs, (((1,), (1,)), ((), ())), preferred_element_type=jnp.float32)
        block = [
            [gram[i * nvec : (i + 1) * nvec, j * nvec : (j + 1) * nvec] for j in range(2)] for i in range(4)
        ]
        cos_real = block[0][0] + block[1][1]
        cos_imag = block[0][1] - block[1][0]
        sin_real = block[2][0] + block[3][1]
        sin_imag = block[2][1] - block[3][0]
        half = 0.5 * scale
        turn_cos = half * turn_ref[moment, 0]
        turn_sin = half * turn_ref[moment, 1]
        back_real = cos_real - sin_imag
        back_imag = cos_imag + sin_real
        real = half * (cos_real + sin_imag) - (turn_cos * back_real - turn_sin * back_imag).T
        imag = half * (cos_imag - sin_real) + (turn_cos * back_imag + turn_sin * back_real).T
        return real.astype(out_ref.dtype), imag.astype(out_ref.dtype)

    found = jnp.int32(0)
    for place in range(total):
        slice_index, moment, disp = parts_of(jnp.int32(place))
        out_ref[place] = item_ref[slice_index, moment, jnp.minimum(disp, NDISP - 2)]
        listed_ref[found] = place
        found = found + (disp == NDISP - 1).astype(jnp.int32)

    @pl.loop(0, lax.div(found + 1, 2))
    def _(pair):
        both = [listed_ref[2 * pair], listed_ref[jnp.minimum(2 * pair + 1, found - 1)]]
        results = [bond(place, lhs_ref.at[index]) for index, place in enumerate(both)]
        for place, (real, imag) in zip(both, results):
            out_ref[place, 0] = real
            out_ref[place, 1] = imag


def layer_items(core, rows, item, own, ahead, phase, turn, scale):
    slices, _, _, nvec, width = own.shape
    devices, slots, _ = rows.shape
    total = slots * devices // 2
    whole = pl.BlockSpec(memory_space=pltpu.VMEM)
    return pl.pallas_call(
        functools.partial(layer_kernel, core, scale),
        in_specs=[pl.BlockSpec(memory_space=pltpu.SMEM)] + [whole] * 5,
        out_specs=whole,
        out_shape=jax.ShapeDtypeStruct((total, 2, nvec, nvec), jnp.bfloat16),
        scratch_shapes=[
            pltpu.VMEM((2, 4 * nvec, NCOL * width), jnp.bfloat16),
            pltpu.SMEM((total,), jnp.int32),
        ],
        compiler_params=pltpu.CompilerParams(vmem_limit_bytes=12 * MIB),
        cost_estimate=pl.CostEstimate(
            flops=total * 4 * nvec * nvec * NCOL * width,
            bytes_accessed=2 * own.size,
            transcendentals=0,
        ),
        name="layer_items",
    )(rows, item, own, ahead, phase, turn)


def add_kernel(places, *refs):
    terms, outs = refs[: len(places[0][0])], refs[len(places[0][0]) :]
    for out_ref, wanted in zip(outs, places):
        for entry, at in enumerate(wanted):
            total = terms[0][at[0]].astype(jnp.float32)
            for ref, index in zip(terms[1:], at[1:]):
                total = total + ref[index].astype(jnp.float32)
            out_ref[entry] = total.astype(out_ref.dtype)


def added(terms, sent, kept=()):
    groups = [(sent, jnp.bfloat16)] + [(kept, jnp.float32)] * bool(kept)
    places = [[tuple(entries.index(r) for entries, _ in terms) for r in group] for group, _ in groups]
    values = [value for _, value in terms]
    tail = values[0].shape[1:]
    whole = pl.BlockSpec(memory_space=pltpu.VMEM)
    size = (len(sent) + len(kept)) * math.prod(tail)
    return pl.pallas_call(
        functools.partial(add_kernel, places),
        in_specs=[whole] * len(values),
        out_specs=[whole] * len(groups),
        out_shape=[jax.ShapeDtypeStruct((len(group),) + tail, dtype) for group, dtype in groups],
        compiler_params=pltpu.CompilerParams(vmem_limit_bytes=8 * MIB),
        cost_estimate=pl.CostEstimate(
            flops=len(values) * size, bytes_accessed=2 * (len(values) + 1) * size, transcendentals=0
        ),
        name="added",
    )(*values)


def halved(terms, slot, order):
    entries = [entry for entry in terms[0][0] if entry[0] == slot]
    for bit in order:
        far = [entry for entry in entries if entry[1] >> (bit - 1) & 1]
        entries = [entry for entry in entries if entry not in far]
        leaving, left = added(terms, far, entries)
        terms = [(entries, left), (entries, exchanged(leaving, 1 << bit))]
    return terms


def finished(terms, slot):
    others = sorted(r for _, r in terms[0][0] if r)
    if not others:
        return [value for _, value in terms]
    arrived = []
    for r in others:
        outs = added(terms, [(slot, r)], [(slot, 0)] if r == others[-1] else [])
        arrived.append(exchanged(outs[0], 2 * r))
    return [outs[1]] + arrived


def mix_kernel(slot_ref, structure_ref, weight_ref, tau_ref, out_ref):
    spins, _, nvec, width = tau_ref.shape[1:]
    base = structure_ref[pl.program_id(0)] * spins * spins
    weight = [[weight_ref[base + r * spins + s] for s in range(spins)] for r in range(spins)]

    @pl.loop(0, 2 * nvec // ROWS)
    def _(index):
        part = index // (nvec // ROWS)
        rows = pl.ds(pl.multiple_of(index % (nvec // ROWS) * ROWS, ROWS), ROWS)
        tau = [tau_ref[0, s, part, rows, :].astype(jnp.float32) for s in range(spins)]
        for r in range(spins):
            mixed = weight[r][0] * tau[0]
            for s in range(1, spins):
                mixed = mixed + weight[r][s] * tau[s]
            out_ref[0, r, part, rows, :] = mixed.astype(jnp.bfloat16)


def mixed_perambulators(slots, structures, weights, perambulators):
    block = (1,) + perambulators.shape[1:]
    count = slots.shape[0]
    return pl.pallas_call(
        mix_kernel,
        grid_spec=pltpu.PrefetchScalarGridSpec(
            num_scalar_prefetch=3,
            grid=(count,),
            in_specs=[pl.BlockSpec(block, lambda j, slot, *_: (slot[j], 0, 0, 0, 0))],
            out_specs=pl.BlockSpec(block, lambda j, *_: (j, 0, 0, 0, 0)),
        ),
        out_shape=jax.ShapeDtypeStruct((count,) + perambulators.shape[1:], jnp.bfloat16),
        compiler_params=pltpu.CompilerParams(vmem_limit_bytes=8 * MIB),
        cost_estimate=pl.CostEstimate(
            flops=8 * perambulators.size, bytes_accessed=4 * perambulators.size, transcendentals=0
        ),
        name="mixed_perambulators",
    )(slots, structures, weights, in_hbm(perambulators))


def diagram_kernel(counts, *refs):
    terms = refs[:-4]
    tau_ref, out_ref, block_ref, sems = refs[-4:]
    spins, _, nvec, width = tau_ref.shape[1:]
    count = len(counts)

    def copy(index, r):
        return pltpu.make_async_copy(block_ref.at[index, r], out_ref.at[index, r], sems.at[index, r])

    for index in range(count):
        real, imag = (
            sum(ref[0, part].astype(jnp.float32) for ref in terms[sum(counts[:index]) : sum(counts[: index + 1])])
            for part in range(2)
        )
        square = jnp.concatenate(
            [jnp.concatenate([real, -imag], 1), jnp.concatenate([imag, real], 1)], 0
        ).astype(jnp.bfloat16)
        for r in range(spins):
            tau = tau_ref[index, r].reshape(2 * nvec, width)
            block = jnp.dot(square, tau, preferred_element_type=jnp.float32)
            block_ref[index, r] = block.astype(jnp.bfloat16).reshape(2, nvec, width)
            copy(index, r).start()
    for index in range(count):
        for r in range(spins):
            copy(index, r).wait()


def diagrams(terms, tau):
    count, spins, _, nvec, width = tau.shape
    whole = pl.BlockSpec(memory_space=pltpu.VMEM)
    flat = [value for group in terms for value in group]
    return pl.pallas_call(
        functools.partial(diagram_kernel, [len(group) for group in terms]),
        in_specs=[whole] * (len(flat) + 1),
        out_specs=pl.BlockSpec(memory_space=pltpu.HBM),
        out_shape=jax.ShapeDtypeStruct(tau.shape, jnp.bfloat16),
        scratch_shapes=[
            pltpu.VMEM(tau.shape, jnp.bfloat16),
            pltpu.SemaphoreType.DMA((count, spins)),
        ],
        compiler_params=pltpu.CompilerParams(vmem_limit_bytes=12 * MIB),
        cost_estimate=pl.CostEstimate(
            flops=8 * nvec * nvec * width * spins * count, bytes_accessed=4 * tau.size, transcendentals=0
        ),
        name="diagrams",
    )(*flat, tau)


def body(eigvecs, gauge_links, momenta, spin_mix, perambulators, contraction_list):
    slices, _, _, nvec, depth, plane = eigvecs.shape
    devices = lax.axis_size(SITES)
    position = lax.axis_index(SITES)
    bits = devices.bit_length() - 1
    total_z = depth * devices
    width = depth * plane
    scale = 1.0 / math.sqrt(NCOL * plane * total_z)
    place = position.reshape(1)
    rows, after, place = gathered(contraction_list, eigvecs, place)
    upper = shifted(after[:, :, :, :, :1, :], SITES, -1)
    vectors = eigvecs.reshape(slices, 2, NCOL, nvec, width)
    links = gauge_links.reshape(slices, 3, 2, NCOL, NCOL, 1, width)
    item, own, phase, turn = plane_items(place, momenta, vectors, links, total_z, plane, scale)
    chosen = contraction_list[:, 2] - position * perambulators.shape[0]
    tau = mixed_perambulators(chosen, contraction_list[:, 1], spin_mix.reshape(-1), perambulators)
    ahead = jnp.concatenate([eigvecs[:, :, :, :, 1:, :], upper], 4).reshape(vectors.shape)
    send = layer_items(1, rows, item, own, ahead, phase, turn, scale)
    keep = layer_items(0, rows, item, own, ahead, phase, turn, scale)
    slots = range(contraction_list.shape[0])
    entries = [(slot, r) for slot in slots for r in range(devices // 2)]
    terms = [(entries, keep), (entries, exchanged(send, 1))]
    groups = []
    for slot in slots:
        order = [1 + (slot + step) % (bits - 1) for step in range(bits - 1)]
        if slot % 2:
            groups.append(halved(terms, slot, order[:-2]))
            continue
        group = halved(terms, slot, order[:1])
        values, tau = lax.optimization_barrier(([value for _, value in group], tau))
        group = [(left, value) for (left, _), value in zip(group, values)]
        groups.append(halved(group, slot, order[1:]))
    parts = [finished(group, slot) for slot, group in zip(slots, groups)]
    return diagrams(parts, tau)


def solution(mesh):
    placed = (
        P("cfg", None, None, None, ("space", "diag"), None),
        P("cfg", None, None, None, None, ("space", "diag"), None),
        P(),
        P(),
        P(("cfg", "space", "diag"), None, None, None, None),
        P(("space", "diag"), None),
    )
    return jax.shard_map(
        body,
        mesh=mesh,
        in_specs=placed,
        out_specs=P(("cfg", "space", "diag"), None, None, None, None),
        check_vma=False,
    )
```

```python
import functools
import math

import jax
import jax.numpy as jnp
from jax import lax
from jax.experimental import pallas as pl
from jax.experimental.pallas import tpu as pltpu
from jax.sharding import PartitionSpec as P

NCOL = 3
NMOM = 4
NDISP = 4
LX = 16
LY = 16
LANES = 128
ROWS = 16
SITES = ("space", "diag")
MIB = 1024 * 1024
PLANE_LIMIT = 24 * MIB


def shifted(value, axis, by):
    size = lax.axis_size(axis)
    return lax.ppermute(value, axis, [(i, (i + by) % size) for i in range(size)])


def in_hbm(value):
    return pltpu.with_memory_space_constraint(value, pltpu.HBM)


def exchanged(value, mask):
    size = lax.axis_size(SITES)
    return lax.ppermute(value, SITES, [(i, i ^ mask) for i in range(size)])


def gathered(rows, early, late):
    bits = lax.axis_size(SITES).bit_length() - 1
    value = rows[None]
    for low in range(0, bits, 2):
        if low == 2:
            value, late = lax.optimization_barrier((value, late))
        arrived = [exchanged(value, step << low) for step in range(1, 1 << min(2, bits - low))]
        if low == 0:
            arrived, early = lax.optimization_barrier((arrived, early))
        value = jnp.concatenate([value] + arrived)
    return value, early, late


def color_product(matrix, real, imag, adjoint):
    rows = []
    for row in range(NCOL):
        real_part = imag_part = None
        for col in range(NCOL):
            if adjoint:
                mreal, mimag = matrix[0][col][row], matrix[1][col][row]
                one = mreal * real[col] + mimag * imag[col]
                two = mreal * imag[col] - mimag * real[col]
            else:
                mreal, mimag = matrix[0][row][col], matrix[1][row][col]
                one = mreal * real[col] - mimag * imag[col]
                two = mreal * imag[col] + mimag * real[col]
            real_part = one if real_part is None else real_part + one
            imag_part = two if imag_part is None else imag_part + two
        rows.append((real_part, imag_part))
    return rows


def color_loop(link, nvec, width, load, store, adjoint):
    height = math.gcd(nvec, 2 * ROWS)
    for lane in range(0, width, LANES):
        lanes = pl.ds(lane, LANES)
        matrix = [
            [[link(part, row, col, lanes) for col in range(NCOL)] for row in range(NCOL)] for part in range(2)
        ]
        for start in range(0, nvec, height):
            rows = pl.ds(start, height)
            real = [load(0, color, rows, lanes) for color in range(NCOL)]
            imag = [load(1, color, rows, lanes) for color in range(NCOL)]
            for color, (one, two) in enumerate(color_product(matrix, real, imag, adjoint)):
                store(0, color, rows, lanes, one)
                store(1, color, rows, lanes, two)


def fill_tables(position, total_z, plane, momenta_ref, phase_ref, turn_ref):
    width = phase_ref.shape[-1]
    flat = lax.broadcasted_iota(jnp.int32, (1, width), 1)
    xcoord = (flat % LX).astype(jnp.float32)
    ycoord = (flat % plane // LX).astype(jnp.float32)
    zcoord = (position * (width // plane) + flat // plane).astype(jnp.float32)
    for moment in range(NMOM):
        along_x = momenta_ref[moment, 0].astype(jnp.float32)
        along_y = momenta_ref[moment, 1].astype(jnp.float32)
        along_z = momenta_ref[moment, 2].astype(jnp.float32)
        angle = (
            2.0 * math.pi * (along_x * xcoord / LX + along_y * ycoord / LY + along_z * zcoord / total_z)
        )
        phase_ref[moment, 0] = jnp.cos(angle)
        phase_ref[moment, 1] = jnp.sin(angle)
        turn = jnp.full((1, turn_ref.shape[-1]), 2.0 * math.pi / total_z, jnp.float32) * along_z
        turn_ref[moment, 0] = jnp.cos(turn)
        turn_ref[moment, 1] = jnp.sin(turn)


def fill_moves(move_ref):
    width = move_ref.shape[-1]
    source = lax.broadcasted_iota(jnp.int32, (width, width), 0)
    site = lax.broadcasted_iota(jnp.int32, (width, width), 1)
    xcoord = site % LX
    ycoord = site // LX % LY
    for sign, by in enumerate((1, -1)):
        along_x = site - xcoord + (xcoord + LX + by) % LX
        along_y = site + ((ycoord + LY + by) % LY - ycoord) * LX
        move_ref[0, sign] = (source == along_x).astype(jnp.float32).astype(jnp.bfloat16)
        move_ref[1, sign] = (source == along_y).astype(jnp.float32).astype(jnp.bfloat16)


def plane_kernel(
    total_z, plane, scale,
    position_ref, momenta_in, vector_in, link_in,
    item_ref, own_ref, phase_ref, turn_ref,
    momenta_ref, vector_ref, link_ref,
    ahead_x_ref, ahead_y_ref, behind_x_ref, behind_y_ref, adjoint_x_ref, adjoint_y_ref,
    phased_ref, still_ref, moved_x_ref, moved_y_ref, move_ref, momenta_sem, sems,
):
    now = pl.program_id(0)
    slices, _, _, nvec, width = vector_ref.shape

    def copies(index):
        return (
            pltpu.make_async_copy(vector_in.at[index], vector_ref.at[index], sems.at[0, index]),
            pltpu.make_async_copy(link_in.at[index], link_ref.at[index], sems.at[1, index]),
        )

    @pl.when(now == 0)
    def _():
        moments = pltpu.make_async_copy(momenta_in, momenta_ref, momenta_sem)
        moments.start()
        for index in range(slices):
            for copy in copies(index):
                copy.start()
        fill_moves(move_ref)
        moments.wait()
        fill_tables(position_ref[0], total_z, plane, momenta_ref, phase_ref, turn_ref)

    for copy in copies(now):
        copy.wait()

    def linker(direction):
        return lambda part, row, col, lanes: link_ref[now, direction, part, row, col, :, lanes]

    def vector(part, color, rows, lanes):
        return vector_ref[now, part, color, rows, lanes].astype(jnp.float32)

    def gram(moved_ref, disp):
        product = lax.dot_general(
            phased_ref[...], moved_ref[...], (((1,), (1,)), ((), ())), preferred_element_type=jnp.float32
        )
        for moment in range(NMOM):
            start = 2 * moment * nvec
            upper = product[start : start + nvec]
            lower = product[start + nvec : start + 2 * nvec]
            factor = scale if disp == 0 else 0.5 * scale
            item_ref[0, moment, disp, 0] = (factor * (upper[:, :nvec] + lower[:, nvec:])).astype(item_ref.dtype)
            item_ref[0, moment, disp, 1] = (factor * (upper[:, nvec:] - lower[:, :nvec])).astype(item_ref.dtype)

    flat = vector_ref[now].reshape(2 * NCOL * nvec, width)
    for direction, ahead_ref in enumerate((ahead_x_ref, ahead_y_ref)):
        ahead_ref[...] = jnp.dot(
            flat, move_ref[direction, 0], preferred_element_type=jnp.float32
        ).reshape(ahead_ref.shape)

    for color in range(NCOL):
        span = pl.ds(color * width, width)
        for part in range(2):
            still_ref[pl.ds(part * nvec, nvec), span] = vector_ref[now, part, color]
        for start in range(0, nvec, ROWS):
            real = vector_ref[now, 0, color, pl.ds(start, ROWS), :].astype(jnp.float32)
            imag = vector_ref[now, 1, color, pl.ds(start, ROWS), :].astype(jnp.float32)
            for moment in range(NMOM):
                cosine = phase_ref[moment, 0]
                sine = phase_ref[moment, 1]
                first = 2 * moment * nvec + start
                phased_ref[pl.ds(first, ROWS), span] = (cosine * real - sine * imag).astype(jnp.bfloat16)
                phased_ref[pl.ds(first + nvec, ROWS), span] = (sine * real + cosine * imag).astype(jnp.bfloat16)
    gram(still_ref, 0)

    for direction, (adjoint_ref, behind_ref) in enumerate(
        ((adjoint_x_ref, behind_x_ref), (adjoint_y_ref, behind_y_ref))
    ):

        def adjoint(part, color, rows, lanes, value):
            adjoint_ref[part, color, rows, lanes] = value.astype(jnp.bfloat16)

        color_loop(linker(direction), nvec, width, vector, adjoint, True)
        behind_ref[...] = jnp.dot(
            adjoint_ref[...].reshape(2 * NCOL * nvec, width),
            move_ref[direction, 1],
            preferred_element_type=jnp.float32,
        ).reshape(behind_ref.shape)

    for direction, (ahead_ref, behind_ref, moved_ref) in enumerate(
        ((ahead_x_ref, behind_x_ref, moved_x_ref), (ahead_y_ref, behind_y_ref, moved_y_ref))
    ):

        def ahead(part, color, rows, lanes):
            return ahead_ref[part, color, rows, lanes]

        def forward(part, color, rows, lanes, value):
            moved_ref[
                pl.ds(part * nvec + rows.start, rows.size), pl.ds(color * width + lanes.start, lanes.size)
            ] = (value - behind_ref[part, color, rows, lanes]).astype(jnp.bfloat16)

        color_loop(linker(direction), nvec, width, ahead, forward, False)
        gram(moved_ref, direction + 1)

    def own(part, color, rows, lanes, value):
        own_ref[0, part, color, rows, lanes] = value

    color_loop(linker(2), nvec, width, vector, own, True)


def plane_items(position, momenta, vectors, links, total_z, plane, scale):
    slices, _, _, nvec, width = vectors.shape
    color_block = (2, NCOL, nvec, width)
    return pl.pallas_call(
        functools.partial(plane_kernel, total_z, plane, scale),
        grid=(slices,),
        in_specs=[pl.BlockSpec(memory_space=pltpu.SMEM)] + [pl.BlockSpec(memory_space=pltpu.HBM)] * 3,
        out_specs=[
            pl.BlockSpec((1, NMOM, NDISP - 1, 2, nvec, nvec), lambda t: (t, 0, 0, 0, 0, 0)),
            pl.BlockSpec((1,) + color_block, lambda t: (t, 0, 0, 0, 0)),
            pl.BlockSpec((NMOM, 2, 1, width), lambda t: (0, 0, 0, 0)),
            pl.BlockSpec((NMOM, 2, 1, nvec), lambda t: (0, 0, 0, 0)),
        ],
        out_shape=[
            jax.ShapeDtypeStruct((slices, NMOM, NDISP - 1, 2, nvec, nvec), jnp.bfloat16),
            jax.ShapeDtypeStruct(vectors.shape, jnp.float32),
            jax.ShapeDtypeStruct((NMOM, 2, 1, width), jnp.float32),
            jax.ShapeDtypeStruct((NMOM, 2, 1, nvec), jnp.float32),
        ],
        scratch_shapes=[
            pltpu.SMEM(momenta.shape, jnp.int32),
            pltpu.VMEM(vectors.shape, jnp.bfloat16),
            pltpu.VMEM(links.shape, jnp.float32),
        ]
        + [pltpu.VMEM(color_block, jnp.float32)] * 4
        + [pltpu.VMEM(color_block, jnp.bfloat16)] * 2
        + [pltpu.VMEM((NMOM * 2 * nvec, NCOL * width), jnp.bfloat16)]
        + [pltpu.VMEM((2 * nvec, NCOL * width), jnp.bfloat16)] * 3
        + [
            pltpu.VMEM((2, 2, width, width), jnp.bfloat16),
            pltpu.SemaphoreType.DMA,
            pltpu.SemaphoreType.DMA((2, slices)),
        ],
        compiler_params=pltpu.CompilerParams(vmem_limit_bytes=PLANE_LIMIT),
        cost_estimate=pl.CostEstimate(
            flops=slices * 16 * NMOM * nvec * nvec * NCOL * width,
            bytes_accessed=6 * vectors.size + 4 * links.size,
            transcendentals=0,
        ),
        name="plane_items",
    )(position, in_hbm(momenta), in_hbm(vectors), in_hbm(links))


def layer_kernel(
    core, scale, rows_ref, item_ref, own_ref, ahead_ref, phase_ref, turn_ref, out_ref, lhs_ref, listed_ref
):
    nvec, width = own_ref.shape[3:]
    total = out_ref.shape[0]
    sites = rows_ref.shape[0] // 2

    def parts_of(place):
        item = rows_ref[2 * lax.rem(place, sites) + core, lax.div(place, sites), 0]
        rest = lax.rem(item, NMOM * NDISP)
        return lax.div(item, NMOM * NDISP), lax.div(rest, NDISP), lax.rem(rest, NDISP)

    def bond(place, lhs):
        slice_index, moment, _ = parts_of(place)
        cosine = phase_ref[moment, 0]
        sine = phase_ref[moment, 1]
        for color in range(NCOL):
            span = pl.ds(color * width, width)
            for part in range(2):
                value = own_ref[slice_index, part, color]
                lhs[pl.ds(part * nvec, nvec), span] = (cosine * value).astype(jnp.bfloat16)
                lhs[pl.ds((2 + part) * nvec, nvec), span] = (sine * value).astype(jnp.bfloat16)
        rhs = jnp.concatenate(
            [
                jnp.concatenate([ahead_ref[slice_index, part, color] for color in range(NCOL)], 1)
                for part in range(2)
            ],
            0,
        )
        gram = lax.dot_general(lhs[...], rhs, (((1,), (1,)), ((), ())), preferred_element_type=jnp.float32)
        block = [
            [gram[i * nvec : (i + 1) * nvec, j * nvec : (j + 1) * nvec] for j in range(2)] for i in range(4)
        ]
        cos_real = block[0][0] + block[1][1]
        cos_imag = block[0][1] - block[1][0]
        sin_real = block[2][0] + block[3][1]
        sin_imag = block[2][1] - block[3][0]
        half = 0.5 * scale
        turn_cos = half * turn_ref[moment, 0]
        turn_sin = half * turn_ref[moment, 1]
        back_real = cos_real - sin_imag
        back_imag = cos_imag + sin_real
        real = half * (cos_real + sin_imag) - (turn_cos * back_real - turn_sin * back_imag).T
        imag = half * (cos_imag - sin_real) + (turn_cos * back_imag + turn_sin * back_real).T
        return real.astype(out_ref.dtype), imag.astype(out_ref.dtype)

    found = jnp.int32(0)
    for place in range(total):
        slice_index, moment, disp = parts_of(jnp.int32(place))
        out_ref[place] = item_ref[slice_index, moment, jnp.minimum(disp, NDISP - 2)]
        listed_ref[found] = place
        found = found + (disp == NDISP - 1).astype(jnp.int32)

    @pl.loop(0, lax.div(found + 1, 2))
    def _(pair):
        both = [listed_ref[2 * pair], listed_ref[jnp.minimum(2 * pair + 1, found - 1)]]
        results = [bond(place, lhs_ref.at[index]) for index, place in enumerate(both)]
        for place, (real, imag) in zip(both, results):
            out_ref[place, 0] = real
            out_ref[place, 1] = imag


def layer_items(core, rows, item, own, ahead, phase, turn, scale):
    slices, _, _, nvec, width = own.shape
    devices, slots, _ = rows.shape
    total = slots * devices // 2
    whole = pl.BlockSpec(memory_space=pltpu.VMEM)
    return pl.pallas_call(
        functools.partial(layer_kernel, core, scale),
        in_specs=[pl.BlockSpec(memory_space=pltpu.SMEM)] + [whole] * 5,
        out_specs=whole,
        out_shape=jax.ShapeDtypeStruct((total, 2, nvec, nvec), jnp.bfloat16),
        scratch_shapes=[
            pltpu.VMEM((2, 4 * nvec, NCOL * width), jnp.bfloat16),
            pltpu.SMEM((total,), jnp.int32),
        ],
        compiler_params=pltpu.CompilerParams(vmem_limit_bytes=12 * MIB),
        cost_estimate=pl.CostEstimate(
            flops=total * 4 * nvec * nvec * NCOL * width,
            bytes_accessed=2 * own.size,
            transcendentals=0,
        ),
        name="layer_items",
    )(rows, item, own, ahead, phase, turn)


def add_kernel(places, *refs):
    terms, outs = refs[: len(places[0][0])], refs[len(places[0][0]) :]
    for out_ref, wanted in zip(outs, places):
        for entry, at in enumerate(wanted):
            total = terms[0][at[0]].astype(jnp.float32)
            for ref, index in zip(terms[1:], at[1:]):
                total = total + ref[index].astype(jnp.float32)
            out_ref[entry] = total.astype(out_ref.dtype)


def added(terms, sent, kept=()):
    groups = [(sent, jnp.bfloat16)] + [(kept, jnp.float32)] * bool(kept)
    places = [[tuple(entries.index(r) for entries, _ in terms) for r in group] for group, _ in groups]
    values = [value for _, value in terms]
    tail = values[0].shape[1:]
    whole = pl.BlockSpec(memory_space=pltpu.VMEM)
    size = (len(sent) + len(kept)) * math.prod(tail)
    return pl.pallas_call(
        functools.partial(add_kernel, places),
        in_specs=[whole] * len(values),
        out_specs=[whole] * len(groups),
        out_shape=[jax.ShapeDtypeStruct((len(group),) + tail, dtype) for group, dtype in groups],
        compiler_params=pltpu.CompilerParams(vmem_limit_bytes=8 * MIB),
        cost_estimate=pl.CostEstimate(
            flops=len(values) * size, bytes_accessed=2 * (len(values) + 1) * size, transcendentals=0
        ),
        name="added",
    )(*values)


def halved(terms, wanted, bit):
    far = [(slot, r ^ (1 << (bit - 1))) for slot, r in wanted]
    leaving, left = added(terms, far, wanted)
    return [(wanted, left), (wanted, exchanged(leaving, 1 << bit))]


def chunked(terms, slot, order):
    entries = [entry for entry in terms[0][0] if entry[0] == slot]
    for place, bit in enumerate(order[:-2]):
        entries = [(slot, r) for _, r in entries if not r >> (bit - 1) & 1]
        if place < len(order) - 3:
            terms = halved(terms, entries, bit)
    middle = len(entries) // 2
    return [functools.partial(halved, terms, chunk, order[-3]) for chunk in (entries[middle:], entries[:middle])]


def sent(terms):
    entries = terms[0][0]
    arrived = []
    for slot, r in reversed(entries):
        if r == 0:
            break
        own = [(slot, 0)] if entries[0][1] == 0 and (slot, r) == entries[1] else []
        outs = added(terms, [(slot, r)], own)
        arrived.append(exchanged(outs[0], 2 * r))
    return arrived + list(outs[1:])


def mix_kernel(slot_ref, structure_ref, weight_ref, tau_ref, out_ref):
    spins, _, nvec, width = tau_ref.shape[1:]
    base = structure_ref[pl.program_id(0)] * spins * spins
    weight = [[weight_ref[base + r * spins + s] for s in range(spins)] for r in range(spins)]

    @pl.loop(0, 2 * nvec // ROWS)
    def _(index):
        part = index // (nvec // ROWS)
        rows = pl.ds(pl.multiple_of(index % (nvec // ROWS) * ROWS, ROWS), ROWS)
        tau = [tau_ref[0, s, part, rows, :].astype(jnp.float32) for s in range(spins)]
        for r in range(spins):
            mixed = weight[r][0] * tau[0]
            for s in range(1, spins):
                mixed = mixed + weight[r][s] * tau[s]
            out_ref[0, r, part, rows, :] = mixed.astype(jnp.bfloat16)


def mixed_perambulators(slots, structures, weights, perambulators):
    block = (1,) + perambulators.shape[1:]
    count = slots.shape[0]
    return pl.pallas_call(
        mix_kernel,
        grid_spec=pltpu.PrefetchScalarGridSpec(
            num_scalar_prefetch=3,
            grid=(count,),
            in_specs=[pl.BlockSpec(block, lambda j, slot, *_: (slot[j], 0, 0, 0, 0))],
            out_specs=pl.BlockSpec(block, lambda j, *_: (j, 0, 0, 0, 0)),
        ),
        out_shape=jax.ShapeDtypeStruct((count,) + perambulators.shape[1:], jnp.bfloat16),
        compiler_params=pltpu.CompilerParams(vmem_limit_bytes=8 * MIB),
        cost_estimate=pl.CostEstimate(
            flops=8 * perambulators.size, bytes_accessed=4 * perambulators.size, transcendentals=0
        ),
        name="mixed_perambulators",
    )(slots, structures, weights, in_hbm(perambulators))


def diagram_kernel(owners, *refs):
    terms = refs[:-4]
    tau_ref, out_ref, block_ref, sems = refs[-4:]
    spins, _, nvec, width = tau_ref.shape[1:]
    count = tau_ref.shape[0]

    def copy(index, r):
        return pltpu.make_async_copy(block_ref.at[index, r], out_ref.at[index, r], sems.at[index, r])

    for index in range(count):
        real, imag = (
            sum(ref[0, part].astype(jnp.float32) for ref, owner in zip(terms, owners) if owner == index)
            for part in range(2)
        )
        square = jnp.concatenate(
            [jnp.concatenate([real, -imag], 1), jnp.concatenate([imag, real], 1)], 0
        ).astype(jnp.bfloat16)
        for r in range(spins):
            tau = tau_ref[index, r].reshape(2 * nvec, width)
            block = jnp.dot(square, tau, preferred_element_type=jnp.float32)
            block_ref[index, r] = block.astype(jnp.bfloat16).reshape(2, nvec, width)
            copy(index, r).start()
    for index in range(count):
        for r in range(spins):
            copy(index, r).wait()


def diagrams(owners, terms, tau):
    count, spins, _, nvec, width = tau.shape
    whole = pl.BlockSpec(memory_space=pltpu.VMEM)
    return pl.pallas_call(
        functools.partial(diagram_kernel, owners),
        in_specs=[whole] * (len(terms) + 1),
        out_specs=pl.BlockSpec(memory_space=pltpu.HBM),
        out_shape=jax.ShapeDtypeStruct(tau.shape, jnp.bfloat16),
        scratch_shapes=[
            pltpu.VMEM(tau.shape, jnp.bfloat16),
            pltpu.SemaphoreType.DMA((count, spins)),
        ],
        compiler_params=pltpu.CompilerParams(vmem_limit_bytes=12 * MIB),
        cost_estimate=pl.CostEstimate(
            flops=8 * nvec * nvec * width * spins * count, bytes_accessed=4 * tau.size, transcendentals=0
        ),
        name="diagrams",
    )(*terms, tau)


def body(eigvecs, gauge_links, momenta, spin_mix, perambulators, contraction_list):
    slices, _, _, nvec, depth, plane = eigvecs.shape
    devices = lax.axis_size(SITES)
    position = lax.axis_index(SITES)
    bits = devices.bit_length() - 1
    total_z = depth * devices
    width = depth * plane
    scale = 1.0 / math.sqrt(NCOL * plane * total_z)
    place = position.reshape(1)
    rows, after, place = gathered(contraction_list, eigvecs, place)
    upper = shifted(after[:, :, :, :, :1, :], SITES, -1)
    vectors = eigvecs.reshape(slices, 2, NCOL, nvec, width)
    links = gauge_links.reshape(slices, 3, 2, NCOL, NCOL, 1, width)
    item, own, phase, turn = plane_items(place, momenta, vectors, links, total_z, plane, scale)
    chosen = contraction_list[:, 2] - position * perambulators.shape[0]
    tau = mixed_perambulators(chosen, contraction_list[:, 1], spin_mix.reshape(-1), perambulators)
    ahead = jnp.concatenate([eigvecs[:, :, :, :, 1:, :], upper], 4).reshape(vectors.shape)
    send = layer_items(1, rows, item, own, ahead, phase, turn, scale)
    keep = layer_items(0, rows, item, own, ahead, phase, turn, scale)
    slots = range(contraction_list.shape[0])
    entries = [(slot, r) for slot in slots for r in range(devices // 2)]
    terms = [(entries, keep), (entries, exchanged(send, 1))]
    chunks = [
        chunked(terms, slot, [1 + (slot + step) % (bits - 1) for step in range(bits - 1)]) for slot in slots
    ]
    chunks = list(zip(*[[chunks[slot][half]() for slot in slots] for half in range(2)]))
    chunks = [list(pair) for pair in chunks]
    first = chunks[0][0]
    values, tau = lax.optimization_barrier(([value for _, value in first], tau))
    chunks[0][0] = [(left, value) for (left, _), value in zip(first, values)]
    owners = []
    parts = []
    for half in range(2):
        for slot in slots:
            values = sent(chunks[slot][half])
            owners += [slot] * len(values)
            parts += values
    return diagrams(owners, parts, tau)


def solution(mesh):
    placed = (
        P("cfg", None, None, None, ("space", "diag"), None),
        P("cfg", None, None, None, None, ("space", "diag"), None),
        P(),
        P(),
        P(("cfg", "space", "diag"), None, None, None, None),
        P(("space", "diag"), None),
    )
    return jax.shard_map(
        body,
        mesh=mesh,
        in_specs=placed,
        out_specs=P(("cfg", "space", "diag"), None, None, None, None),
        check_vma=False,
    )
```

```python
import functools
import math

import jax
import jax.numpy as jnp
from jax import lax
from jax.experimental import pallas as pl
from jax.experimental.pallas import tpu as pltpu
from jax.sharding import PartitionSpec as P

NCOL = 3
NMOM = 4
NDISP = 4
LX = 16
LY = 16
LANES = 128
ROWS = 16
SITES = ("space", "diag")
MIB = 1024 * 1024
PLANE_LIMIT = 20 * MIB


def shifted(value, axis, by):
    size = lax.axis_size(axis)
    return lax.ppermute(value, axis, [(i, (i + by) % size) for i in range(size)])


def in_hbm(value):
    return pltpu.with_memory_space_constraint(value, pltpu.HBM)


def exchanged(value, mask):
    size = lax.axis_size(SITES)
    return lax.ppermute(value, SITES, [(i, i ^ mask) for i in range(size)])


def gathered(rows, early, late):
    bits = lax.axis_size(SITES).bit_length() - 1
    value = rows[None]
    for low in range(0, bits, 2):
        if low == 2:
            value, late = lax.optimization_barrier((value, late))
        arrived = [exchanged(value, step << low) for step in range(1, 1 << min(2, bits - low))]
        if low == 0:
            arrived, early = lax.optimization_barrier((arrived, early))
        value = jnp.concatenate([value] + arrived)
    return value, early, late


def color_product(matrix, real, imag, adjoint):
    rows = []
    for row in range(NCOL):
        real_part = imag_part = None
        for col in range(NCOL):
            if adjoint:
                mreal, mimag = matrix[0][col][row], matrix[1][col][row]
                one = mreal * real[col] + mimag * imag[col]
                two = mreal * imag[col] - mimag * real[col]
            else:
                mreal, mimag = matrix[0][row][col], matrix[1][row][col]
                one = mreal * real[col] - mimag * imag[col]
                two = mreal * imag[col] + mimag * real[col]
            real_part = one if real_part is None else real_part + one
            imag_part = two if imag_part is None else imag_part + two
        rows.append((real_part, imag_part))
    return rows


def color_loop(link, nvec, width, load, store, adjoint):
    height = math.gcd(nvec, 2 * ROWS)
    for lane in range(0, width, LANES):
        lanes = pl.ds(lane, LANES)
        matrix = [
            [[link(part, row, col, lanes) for col in range(NCOL)] for row in range(NCOL)] for part in range(2)
        ]
        for start in range(0, nvec, height):
            rows = pl.ds(start, height)
            real = [load(0, color, rows, lanes) for color in range(NCOL)]
            imag = [load(1, color, rows, lanes) for color in range(NCOL)]
            for color, (one, two) in enumerate(color_product(matrix, real, imag, adjoint)):
                store(0, color, rows, lanes, one)
                store(1, color, rows, lanes, two)


def fill_tables(position, total_z, plane, momenta_ref, phase_ref, turn_ref):
    width = phase_ref.shape[-1]
    flat = lax.broadcasted_iota(jnp.int32, (1, width), 1)
    xcoord = (flat % LX).astype(jnp.float32)
    ycoord = (flat % plane // LX).astype(jnp.float32)
    zcoord = (position * (width // plane) + flat // plane).astype(jnp.float32)
    for moment in range(NMOM):
        along_x = momenta_ref[moment, 0].astype(jnp.float32)
        along_y = momenta_ref[moment, 1].astype(jnp.float32)
        along_z = momenta_ref[moment, 2].astype(jnp.float32)
        angle = (
            2.0 * math.pi * (along_x * xcoord / LX + along_y * ycoord / LY + along_z * zcoord / total_z)
        )
        phase_ref[moment, 0] = jnp.cos(angle)
        phase_ref[moment, 1] = jnp.sin(angle)
        turn = jnp.full((1, turn_ref.shape[-1]), 2.0 * math.pi / total_z, jnp.float32) * along_z
        turn_ref[moment, 0] = jnp.cos(turn)
        turn_ref[moment, 1] = jnp.sin(turn)


def fill_moves(move_ref):
    width = move_ref.shape[-1]
    source = lax.broadcasted_iota(jnp.int32, (width, width), 0)
    site = lax.broadcasted_iota(jnp.int32, (width, width), 1)
    xcoord = site % LX
    ycoord = site // LX % LY
    for sign, by in enumerate((1, -1)):
        along_x = site - xcoord + (xcoord + LX + by) % LX
        along_y = site + ((ycoord + LY + by) % LY - ycoord) * LX
        move_ref[0, sign] = (source == along_x).astype(jnp.float32).astype(jnp.bfloat16)
        move_ref[1, sign] = (source == along_y).astype(jnp.float32).astype(jnp.bfloat16)


def plane_kernel(
    total_z, plane, scale,
    position_ref, momenta_in, vector_in, link_in,
    item_ref, own_ref, phase_ref, turn_ref,
    momenta_ref, vector_ref, link_ref,
    ahead_x_ref, ahead_y_ref, behind_x_ref, behind_y_ref, adjoint_x_ref, adjoint_y_ref,
    phased_ref, still_ref, moved_x_ref, moved_y_ref, move_ref, momenta_sem, sems,
):
    now = pl.program_id(0)
    slices, _, _, nvec, width = vector_ref.shape

    def copies(index):
        return (
            pltpu.make_async_copy(vector_in.at[index], vector_ref.at[index], sems.at[0, index]),
            pltpu.make_async_copy(link_in.at[index], link_ref.at[index], sems.at[1, index]),
        )

    @pl.when(now == 0)
    def _():
        moments = pltpu.make_async_copy(momenta_in, momenta_ref, momenta_sem)
        moments.start()
        for index in range(slices):
            for copy in copies(index):
                copy.start()
        fill_moves(move_ref)
        moments.wait()
        fill_tables(position_ref[0], total_z, plane, momenta_ref, phase_ref, turn_ref)

    for copy in copies(now):
        copy.wait()

    def linker(direction):
        return lambda part, row, col, lanes: link_ref[now, direction, part, row, col, :, lanes]

    def vector(part, color, rows, lanes):
        return vector_ref[now, part, color, rows, lanes].astype(jnp.float32)

    def gram(moved_ref, disp):
        product = lax.dot_general(
            phased_ref[...], moved_ref[...], (((1,), (1,)), ((), ())), preferred_element_type=jnp.float32
        )
        for moment in range(NMOM):
            start = 2 * moment * nvec
            upper = product[start : start + nvec]
            lower = product[start + nvec : start + 2 * nvec]
            factor = scale if disp == 0 else 0.5 * scale
            item_ref[0, moment, disp, 0] = (factor * (upper[:, :nvec] + lower[:, nvec:])).astype(item_ref.dtype)
            item_ref[0, moment, disp, 1] = (factor * (upper[:, nvec:] - lower[:, :nvec])).astype(item_ref.dtype)

    flat = vector_ref[now].reshape(2 * NCOL * nvec, width)
    for direction, ahead_ref in enumerate((ahead_x_ref, ahead_y_ref)):
        ahead_ref[...] = jnp.dot(
            flat, move_ref[direction, 0], preferred_element_type=jnp.float32
        ).reshape(ahead_ref.shape)

    for color in range(NCOL):
        span = pl.ds(color * width, width)
        for part in range(2):
            still_ref[pl.ds(part * nvec, nvec), span] = vector_ref[now, part, color]
        for start in range(0, nvec, ROWS):
            real = vector_ref[now, 0, color, pl.ds(start, ROWS), :].astype(jnp.float32)
            imag = vector_ref[now, 1, color, pl.ds(start, ROWS), :].astype(jnp.float32)
            for moment in range(NMOM):
                cosine = phase_ref[moment, 0]
                sine = phase_ref[moment, 1]
                first = 2 * moment * nvec + start
                phased_ref[pl.ds(first, ROWS), span] = (cosine * real - sine * imag).astype(jnp.bfloat16)
                phased_ref[pl.ds(first + nvec, ROWS), span] = (sine * real + cosine * imag).astype(jnp.bfloat16)
    gram(still_ref, 0)

    for direction, (adjoint_ref, behind_ref) in enumerate(
        ((adjoint_x_ref, behind_x_ref), (adjoint_y_ref, behind_y_ref))
    ):

        def adjoint(part, color, rows, lanes, value):
            adjoint_ref[part, color, rows, lanes] = value.astype(jnp.bfloat16)

        color_loop(linker(direction), nvec, width, vector, adjoint, True)
        behind_ref[...] = jnp.dot(
            adjoint_ref[...].reshape(2 * NCOL * nvec, width),
            move_ref[direction, 1],
            preferred_element_type=jnp.float32,
        ).reshape(behind_ref.shape)

    for direction, (ahead_ref, behind_ref, moved_ref) in enumerate(
        ((ahead_x_ref, behind_x_ref, moved_x_ref), (ahead_y_ref, behind_y_ref, moved_y_ref))
    ):

        def ahead(part, color, rows, lanes):
            return ahead_ref[part, color, rows, lanes]

        def forward(part, color, rows, lanes, value):
            moved_ref[
                pl.ds(part * nvec + rows.start, rows.size), pl.ds(color * width + lanes.start, lanes.size)
            ] = (value - behind_ref[part, color, rows, lanes]).astype(jnp.bfloat16)

        color_loop(linker(direction), nvec, width, ahead, forward, False)
        gram(moved_ref, direction + 1)

    def own(part, color, rows, lanes, value):
        own_ref[0, part, color, rows, lanes] = value

    color_loop(linker(2), nvec, width, vector, own, True)


def plane_items(position, momenta, vectors, links, total_z, plane, scale):
    slices, _, _, nvec, width = vectors.shape
    color_block = (2, NCOL, nvec, width)
    return pl.pallas_call(
        functools.partial(plane_kernel, total_z, plane, scale),
        grid=(slices,),
        in_specs=[pl.BlockSpec(memory_space=pltpu.SMEM)] + [pl.BlockSpec(memory_space=pltpu.HBM)] * 3,
        out_specs=[
            pl.BlockSpec((1, NMOM, NDISP - 1, 2, nvec, nvec), lambda t: (t, 0, 0, 0, 0, 0)),
            pl.BlockSpec((1,) + color_block, lambda t: (t, 0, 0, 0, 0)),
            pl.BlockSpec((NMOM, 2, 1, width), lambda t: (0, 0, 0, 0)),
            pl.BlockSpec((NMOM, 2, 1, nvec), lambda t: (0, 0, 0, 0)),
        ],
        out_shape=[
            jax.ShapeDtypeStruct((slices, NMOM, NDISP - 1, 2, nvec, nvec), jnp.bfloat16),
            jax.ShapeDtypeStruct(vectors.shape, jnp.float32),
            jax.ShapeDtypeStruct((NMOM, 2, 1, width), jnp.float32),
            jax.ShapeDtypeStruct((NMOM, 2, 1, nvec), jnp.float32),
        ],
        scratch_shapes=[
            pltpu.SMEM(momenta.shape, jnp.int32),
            pltpu.VMEM(vectors.shape, jnp.bfloat16),
            pltpu.VMEM(links.shape, jnp.float32),
        ]
        + [pltpu.VMEM(color_block, jnp.float32)] * 4
        + [pltpu.VMEM(color_block, jnp.bfloat16)] * 2
        + [pltpu.VMEM((NMOM * 2 * nvec, NCOL * width), jnp.bfloat16)]
        + [pltpu.VMEM((2 * nvec, NCOL * width), jnp.bfloat16)] * 3
        + [
            pltpu.VMEM((2, 2, width, width), jnp.bfloat16),
            pltpu.SemaphoreType.DMA,
            pltpu.SemaphoreType.DMA((2, slices)),
        ],
        compiler_params=pltpu.CompilerParams(vmem_limit_bytes=PLANE_LIMIT),
        cost_estimate=pl.CostEstimate(
            flops=slices * 16 * NMOM * nvec * nvec * NCOL * width,
            bytes_accessed=6 * vectors.size + 4 * links.size,
            transcendentals=0,
        ),
        name="plane_items",
    )(position, in_hbm(momenta), in_hbm(vectors), in_hbm(links))


def layer_kernel(
    core, scale, rows_ref, item_ref, own_ref, ahead_ref, phase_ref, turn_ref, out_ref, lhs_ref, listed_ref
):
    nvec, width = own_ref.shape[3:]
    total = out_ref.shape[0]
    sites = rows_ref.shape[0] // 2

    def parts_of(place):
        item = rows_ref[2 * lax.rem(place, sites) + core, lax.div(place, sites), 0]
        rest = lax.rem(item, NMOM * NDISP)
        return lax.div(item, NMOM * NDISP), lax.div(rest, NDISP), lax.rem(rest, NDISP)

    def bond(place, lhs):
        slice_index, moment, _ = parts_of(place)
        cosine = phase_ref[moment, 0]
        sine = phase_ref[moment, 1]
        for color in range(NCOL):
            span = pl.ds(color * width, width)
            for part in range(2):
                value = own_ref[slice_index, part, color]
                lhs[pl.ds(part * nvec, nvec), span] = (cosine * value).astype(jnp.bfloat16)
                lhs[pl.ds((2 + part) * nvec, nvec), span] = (sine * value).astype(jnp.bfloat16)
        rhs = jnp.concatenate(
            [
                jnp.concatenate([ahead_ref[slice_index, part, color] for color in range(NCOL)], 1)
                for part in range(2)
            ],
            0,
        )
        gram = lax.dot_general(lhs[...], rhs, (((1,), (1,)), ((), ())), preferred_element_type=jnp.float32)
        block = [
            [gram[i * nvec : (i + 1) * nvec, j * nvec : (j + 1) * nvec] for j in range(2)] for i in range(4)
        ]
        cos_real = block[0][0] + block[1][1]
        cos_imag = block[0][1] - block[1][0]
        sin_real = block[2][0] + block[3][1]
        sin_imag = block[2][1] - block[3][0]
        half = 0.5 * scale
        turn_cos = half * turn_ref[moment, 0]
        turn_sin = half * turn_ref[moment, 1]
        back_real = cos_real - sin_imag
        back_imag = cos_imag + sin_real
        real = half * (cos_real + sin_imag) - (turn_cos * back_real - turn_sin * back_imag).T
        imag = half * (cos_imag - sin_real) + (turn_cos * back_imag + turn_sin * back_real).T
        return real.astype(out_ref.dtype), imag.astype(out_ref.dtype)

    found = jnp.int32(0)
    for place in range(total):
        slice_index, moment, disp = parts_of(jnp.int32(place))
        out_ref[place] = item_ref[slice_index, moment, jnp.minimum(disp, NDISP - 2)]
        listed_ref[found] = place
        found = found + (disp == NDISP - 1).astype(jnp.int32)

    @pl.loop(0, lax.div(found + 1, 2))
    def _(pair):
        both = [listed_ref[2 * pair], listed_ref[jnp.minimum(2 * pair + 1, found - 1)]]
        results = [bond(place, lhs_ref.at[index]) for index, place in enumerate(both)]
        for place, (real, imag) in zip(both, results):
            out_ref[place, 0] = real
            out_ref[place, 1] = imag


def layer_items(core, rows, item, own, ahead, phase, turn, scale):
    slices, _, _, nvec, width = own.shape
    devices, slots, _ = rows.shape
    total = slots * devices // 2
    whole = pl.BlockSpec(memory_space=pltpu.VMEM)
    return pl.pallas_call(
        functools.partial(layer_kernel, core, scale),
        in_specs=[pl.BlockSpec(memory_space=pltpu.SMEM)] + [whole] * 5,
        out_specs=whole,
        out_shape=jax.ShapeDtypeStruct((total, 2, nvec, nvec), jnp.bfloat16),
        scratch_shapes=[
            pltpu.VMEM((2, 4 * nvec, NCOL * width), jnp.bfloat16),
            pltpu.SMEM((total,), jnp.int32),
        ],
        compiler_params=pltpu.CompilerParams(vmem_limit_bytes=8 * MIB),
        cost_estimate=pl.CostEstimate(
            flops=total * 4 * nvec * nvec * NCOL * width,
            bytes_accessed=2 * own.size,
            transcendentals=0,
        ),
        name="layer_items",
    )(rows, item, own, ahead, phase, turn)


def add_kernel(places, *refs):
    terms, outs = refs[: len(places[0][0])], refs[len(places[0][0]) :]
    for out_ref, wanted in zip(outs, places):
        for entry, at in enumerate(wanted):
            total = terms[0][at[0]].astype(jnp.float32)
            for ref, index in zip(terms[1:], at[1:]):
                total = total + ref[index].astype(jnp.float32)
            out_ref[entry] = total.astype(out_ref.dtype)


def added(terms, sent, kept=()):
    groups = [(sent, jnp.bfloat16)] + [(kept, jnp.float32)] * bool(kept)
    places = [[tuple(entries.index(r) for entries, _ in terms) for r in group] for group, _ in groups]
    values = [value for _, value in terms]
    tail = values[0].shape[1:]
    whole = pl.BlockSpec(memory_space=pltpu.VMEM)
    size = (len(sent) + len(kept)) * math.prod(tail)
    return pl.pallas_call(
        functools.partial(add_kernel, places),
        in_specs=[whole] * len(values),
        out_specs=[whole] * len(groups),
        out_shape=[jax.ShapeDtypeStruct((len(group),) + tail, dtype) for group, dtype in groups],
        compiler_params=pltpu.CompilerParams(vmem_limit_bytes=8 * MIB),
        cost_estimate=pl.CostEstimate(
            flops=len(values) * size, bytes_accessed=2 * (len(values) + 1) * size, transcendentals=0
        ),
        name="added",
    )(*values)


def halved(terms, wanted, bit):
    far = [(slot, r ^ (1 << (bit - 1))) for slot, r in wanted]
    leaving, left = added(terms, far, wanted)
    return [(wanted, left), (wanted, exchanged(leaving, 1 << bit))]


def chunked(terms, slot, order):
    entries = [entry for entry in terms[0][0] if entry[0] == slot]
    for place, bit in enumerate(order[:-2]):
        entries = [(slot, r) for _, r in entries if not r >> (bit - 1) & 1]
        if place < len(order) - 3:
            terms = halved(terms, entries, bit)
    middle = len(entries) // 2
    return [functools.partial(halved, terms, chunk, order[-3]) for chunk in (entries[middle:], entries[:middle])]


def sent(terms):
    entries = terms[0][0]
    arrived = []
    for slot, r in reversed(entries):
        if r == 0:
            break
        own = [(slot, 0)] if entries[0][1] == 0 and (slot, r) == entries[1] else []
        outs = added(terms, [(slot, r)], own)
        arrived.append(exchanged(outs[0], 2 * r))
    return arrived + list(outs[1:])


def mix_kernel(slot_ref, structure_ref, weight_ref, tau_ref, out_ref):
    spins, _, nvec, width = tau_ref.shape[1:]
    base = structure_ref[pl.program_id(0)] * spins * spins
    weight = [[weight_ref[base + r * spins + s] for s in range(spins)] for r in range(spins)]

    @pl.loop(0, 2 * nvec // ROWS)
    def _(index):
        part = index // (nvec // ROWS)
        rows = pl.ds(pl.multiple_of(index % (nvec // ROWS) * ROWS, ROWS), ROWS)
        tau = [tau_ref[0, s, part, rows, :].astype(jnp.float32) for s in range(spins)]
        for r in range(spins):
            mixed = weight[r][0] * tau[0]
            for s in range(1, spins):
                mixed = mixed + weight[r][s] * tau[s]
            out_ref[0, r, part, rows, :] = mixed.astype(jnp.bfloat16)


def mixed_perambulators(slots, structures, weights, perambulators):
    block = (1,) + perambulators.shape[1:]
    count = slots.shape[0]
    return pl.pallas_call(
        mix_kernel,
        grid_spec=pltpu.PrefetchScalarGridSpec(
            num_scalar_prefetch=3,
            grid=(count,),
            in_specs=[pl.BlockSpec(block, lambda j, slot, *_: (slot[j], 0, 0, 0, 0))],
            out_specs=pl.BlockSpec(block, lambda j, *_: (j, 0, 0, 0, 0)),
        ),
        out_shape=jax.ShapeDtypeStruct((count,) + perambulators.shape[1:], jnp.bfloat16),
        compiler_params=pltpu.CompilerParams(vmem_limit_bytes=8 * MIB),
        cost_estimate=pl.CostEstimate(
            flops=8 * perambulators.size, bytes_accessed=4 * perambulators.size, transcendentals=0
        ),
        name="mixed_perambulators",
    )(slots, structures, weights, in_hbm(perambulators))


def diagram_kernel(owners, *refs):
    terms = refs[:-4]
    tau_ref, out_ref, block_ref, sems = refs[-4:]
    spins, _, nvec, width = tau_ref.shape[1:]
    count = tau_ref.shape[0]

    def copy(index, r):
        return pltpu.make_async_copy(block_ref.at[index, r], out_ref.at[index, r], sems.at[index, r])

    for index in range(count):
        real, imag = (
            sum(ref[0, part].astype(jnp.float32) for ref, owner in zip(terms, owners) if owner == index)
            for part in range(2)
        )
        square = jnp.concatenate(
            [jnp.concatenate([real, -imag], 1), jnp.concatenate([imag, real], 1)], 0
        ).astype(jnp.bfloat16)
        for r in range(spins):
            tau = tau_ref[index, r].reshape(2 * nvec, width)
            block = jnp.dot(square, tau, preferred_element_type=jnp.float32)
            block_ref[index, r] = block.astype(jnp.bfloat16).reshape(2, nvec, width)
            copy(index, r).start()
    for index in range(count):
        for r in range(spins):
            copy(index, r).wait()


def diagrams(owners, terms, tau):
    count, spins, _, nvec, width = tau.shape
    whole = pl.BlockSpec(memory_space=pltpu.VMEM)
    return pl.pallas_call(
        functools.partial(diagram_kernel, owners),
        in_specs=[whole] * (len(terms) + 1),
        out_specs=pl.BlockSpec(memory_space=pltpu.HBM),
        out_shape=jax.ShapeDtypeStruct(tau.shape, jnp.bfloat16),
        scratch_shapes=[
            pltpu.VMEM(tau.shape, jnp.bfloat16),
            pltpu.SemaphoreType.DMA((count, spins)),
        ],
        compiler_params=pltpu.CompilerParams(vmem_limit_bytes=8 * MIB),
        cost_estimate=pl.CostEstimate(
            flops=8 * nvec * nvec * width * spins * count, bytes_accessed=4 * tau.size, transcendentals=0
        ),
        name="diagrams",
    )(*terms, tau)


def body(eigvecs, gauge_links, momenta, spin_mix, perambulators, contraction_list):
    slices, _, _, nvec, depth, plane = eigvecs.shape
    devices = lax.axis_size(SITES)
    position = lax.axis_index(SITES)
    bits = devices.bit_length() - 1
    total_z = depth * devices
    width = depth * plane
    scale = 1.0 / math.sqrt(NCOL * plane * total_z)
    place = position.reshape(1)
    rows, after, place = gathered(contraction_list, eigvecs, place)
    upper = shifted(after[:, :, :, :, :1, :], SITES, -1)
    vectors = eigvecs.reshape(slices, 2, NCOL, nvec, width)
    links = gauge_links.reshape(slices, 3, 2, NCOL, NCOL, 1, width)
    item, own, phase, turn = plane_items(place, momenta, vectors, links, total_z, plane, scale)
    chosen = contraction_list[:, 2] - position * perambulators.shape[0]
    tau = mixed_perambulators(chosen, contraction_list[:, 1], spin_mix.reshape(-1), perambulators)
    ahead = jnp.concatenate([eigvecs[:, :, :, :, 1:, :], upper], 4).reshape(vectors.shape)
    send = layer_items(1, rows, item, own, ahead, phase, turn, scale)
    keep = layer_items(0, rows, item, own, ahead, phase, turn, scale)
    slots = range(contraction_list.shape[0])
    entries = [(slot, r) for slot in slots for r in range(devices // 2)]
    terms = [(entries, keep), (entries, exchanged(send, 1))]
    chunks = [
        chunked(terms, slot, [1 + (slot + step) % (bits - 1) for step in range(bits - 1)]) for slot in slots
    ]
    chunks = list(zip(*[[chunks[slot][half]() for slot in slots] for half in range(2)]))
    chunks = [list(pair) for pair in chunks]
    owners = []
    parts = []
    for half in range(2):
        for slot in slots:
            values = sent(chunks[slot][half])
            owners += [slot] * len(values)
            parts += values
    return diagrams(owners, parts, tau)


def solution(mesh):
    placed = (
        P("cfg", None, None, None, ("space", "diag"), None),
        P("cfg", None, None, None, None, ("space", "diag"), None),
        P(),
        P(),
        P(("cfg", "space", "diag"), None, None, None, None),
        P(("space", "diag"), None),
    )
    return jax.shard_map(
        body,
        mesh=mesh,
        in_specs=placed,
        out_specs=P(("cfg", "space", "diag"), None, None, None, None),
        check_vma=False,
    )
```

```python
import functools
import math

import jax
import jax.numpy as jnp
from jax import lax
from jax.experimental import pallas as pl
from jax.experimental.pallas import tpu as pltpu
from jax.sharding import PartitionSpec as P

NCOL = 3
NMOM = 4
NDISP = 4
LX = 16
LY = 16
LANES = 128
ROWS = 16
SITES = ("space", "diag")
MIB = 1024 * 1024
PLANE_LIMIT = 20 * MIB


def shifted(value, axis, by):
    size = lax.axis_size(axis)
    return lax.ppermute(value, axis, [(i, (i + by) % size) for i in range(size)])


def in_hbm(value):
    return pltpu.with_memory_space_constraint(value, pltpu.HBM)


def exchanged(value, mask):
    size = lax.axis_size(SITES)
    return lax.ppermute(value, SITES, [(i, i ^ mask) for i in range(size)])


def join_kernel(*refs):
    size = refs[0].shape[0]
    for index, ref in enumerate(refs[:-1]):
        refs[-1][pl.ds(index * size, size)] = ref[...]


def joined(parts):
    whole = pl.BlockSpec(memory_space=pltpu.VMEM)
    return pl.pallas_call(
        join_kernel,
        in_specs=[whole] * len(parts),
        out_specs=whole,
        out_shape=jax.ShapeDtypeStruct((len(parts) * parts[0].shape[0],) + parts[0].shape[1:], parts[0].dtype),
        name="joined",
    )(*parts)


def gathered(rows, early, late):
    bits = lax.axis_size(SITES).bit_length() - 1
    value = rows[None]
    for low in range(0, bits, 2):
        if low == 2:
            value, late = lax.optimization_barrier((value, late))
        arrived = [exchanged(value, step << low) for step in reversed(range(1, 1 << min(2, bits - low)))]
        if low == 0:
            arrived, early = lax.optimization_barrier((arrived, early))
        value = joined([value] + arrived[::-1])
    return value, early, late


def diagonal(value):
    size = value.shape[0]
    same = lax.broadcasted_iota(jnp.int32, value.shape, 0) == lax.broadcasted_iota(jnp.int32, value.shape, 1)
    return jnp.sum(jnp.where(same, value, 0.0), 0, keepdims=True).reshape(1, size)


def rounded(real, imag, left=None):
    planes = [value.astype(jnp.bfloat16) for value in (real, imag)]
    lost = [diagonal(value - plane.astype(jnp.float32)) for value, plane in zip((real, imag), planes)]
    tile = jnp.concatenate(lost + [jnp.zeros((ROWS - 2, real.shape[1]), jnp.float32)], 0)
    if left is not None:
        tile = tile + left
    return planes, tile.astype(jnp.bfloat16)


def store_rounded(ref, index, real, imag, left=None):
    nvec = real.shape[0]
    planes, tile = rounded(real, imag, left)
    ref[(*index, pl.ds(0, nvec))] = planes[0]
    ref[(*index, pl.ds(nvec, nvec))] = planes[1]
    ref[(*index, pl.ds(2 * nvec, ROWS))] = tile


def restored(total):
    nvec = total.shape[1]
    shape = (nvec, nvec)
    same = lax.broadcasted_iota(jnp.int32, shape, 0) == lax.broadcasted_iota(jnp.int32, shape, 1)
    return [
        total[part * nvec : (part + 1) * nvec] + jnp.where(same, total[2 * nvec + part : 2 * nvec + part + 1], 0.0)
        for part in range(2)
    ]


def color_product(matrix, real, imag, adjoint):
    rows = []
    for row in range(NCOL):
        real_part = imag_part = None
        for col in range(NCOL):
            if adjoint:
                mreal, mimag = matrix[0][col][row], matrix[1][col][row]
                one = mreal * real[col] + mimag * imag[col]
                two = mreal * imag[col] - mimag * real[col]
            else:
                mreal, mimag = matrix[0][row][col], matrix[1][row][col]
                one = mreal * real[col] - mimag * imag[col]
                two = mreal * imag[col] + mimag * real[col]
            real_part = one if real_part is None else real_part + one
            imag_part = two if imag_part is None else imag_part + two
        rows.append((real_part, imag_part))
    return rows


def color_loop(link, nvec, width, load, store, adjoint):
    height = math.gcd(nvec, 2 * ROWS)
    for lane in range(0, width, LANES):
        lanes = pl.ds(lane, LANES)
        matrix = [
            [[link(part, row, col, lanes) for col in range(NCOL)] for row in range(NCOL)] for part in range(2)
        ]
        for start in range(0, nvec, height):
            rows = pl.ds(start, height)
            real = [load(0, color, rows, lanes) for color in range(NCOL)]
            imag = [load(1, color, rows, lanes) for color in range(NCOL)]
            for color, (one, two) in enumerate(color_product(matrix, real, imag, adjoint)):
                store(0, color, rows, lanes, one)
                store(1, color, rows, lanes, two)


def fill_tables(position, total_z, plane, momenta_ref, phase_ref, turn_ref):
    width = phase_ref.shape[-1]
    flat = lax.broadcasted_iota(jnp.int32, (1, width), 1)
    xcoord = (flat % LX).astype(jnp.float32)
    ycoord = (flat % plane // LX).astype(jnp.float32)
    zcoord = (position * (width // plane) + flat // plane).astype(jnp.float32)
    for moment in range(NMOM):
        along_x = momenta_ref[moment, 0].astype(jnp.float32)
        along_y = momenta_ref[moment, 1].astype(jnp.float32)
        along_z = momenta_ref[moment, 2].astype(jnp.float32)
        angle = (
            2.0 * math.pi * (along_x * xcoord / LX + along_y * ycoord / LY + along_z * zcoord / total_z)
        )
        phase_ref[moment, 0] = jnp.cos(angle)
        phase_ref[moment, 1] = jnp.sin(angle)
        turn = jnp.full((1, turn_ref.shape[-1]), 2.0 * math.pi / total_z, jnp.float32) * along_z
        turn_ref[moment, 0] = jnp.cos(turn)
        turn_ref[moment, 1] = jnp.sin(turn)


def fill_moves(move_ref):
    width = move_ref.shape[-1]
    source = lax.broadcasted_iota(jnp.int32, (width, width), 0)
    site = lax.broadcasted_iota(jnp.int32, (width, width), 1)
    xcoord = site % LX
    ycoord = site // LX % LY
    for sign, by in enumerate((1, -1)):
        along_x = site - xcoord + (xcoord + LX + by) % LX
        along_y = site + ((ycoord + LY + by) % LY - ycoord) * LX
        move_ref[0, sign] = (source == along_x).astype(jnp.float32).astype(jnp.bfloat16)
        move_ref[1, sign] = (source == along_y).astype(jnp.float32).astype(jnp.bfloat16)


def plane_kernel(
    total_z, plane, scale,
    position_ref, momenta_in, vector_in, link_in,
    item_ref, own_ref, phase_ref, turn_ref,
    momenta_ref, vector_ref, link_ref,
    ahead_x_ref, ahead_y_ref, behind_x_ref, behind_y_ref, adjoint_x_ref, adjoint_y_ref,
    phased_ref, still_ref, moved_x_ref, moved_y_ref, move_ref, momenta_sem, sems,
):
    now = pl.program_id(0)
    slices, _, _, nvec, width = vector_ref.shape

    def copies(index):
        return (
            pltpu.make_async_copy(vector_in.at[index], vector_ref.at[index], sems.at[0, index]),
            pltpu.make_async_copy(link_in.at[index], link_ref.at[index], sems.at[1, index]),
        )

    @pl.when(now == 0)
    def _():
        moments = pltpu.make_async_copy(momenta_in, momenta_ref, momenta_sem)
        moments.start()
        for index in range(slices):
            for copy in copies(index):
                copy.start()
        fill_moves(move_ref)
        moments.wait()
        fill_tables(position_ref[0], total_z, plane, momenta_ref, phase_ref, turn_ref)

    for copy in copies(now):
        copy.wait()

    def linker(direction):
        return lambda part, row, col, lanes: link_ref[now, direction, part, row, col, :, lanes]

    def vector(part, color, rows, lanes):
        return vector_ref[now, part, color, rows, lanes].astype(jnp.float32)

    def gram(moved_ref, disp):
        product = lax.dot_general(
            phased_ref[...], moved_ref[...], (((1,), (1,)), ((), ())), preferred_element_type=jnp.float32
        )
        for moment in range(NMOM):
            start = 2 * moment * nvec
            upper = product[start : start + nvec]
            lower = product[start + nvec : start + 2 * nvec]
            factor = scale if disp == 0 else 0.5 * scale
            real = factor * (upper[:, :nvec] + lower[:, nvec:])
            imag = factor * (upper[:, nvec:] - lower[:, :nvec])
            store_rounded(item_ref, (0, moment, disp), real, imag)

    flat = vector_ref[now].reshape(2 * NCOL * nvec, width)
    for direction, ahead_ref in enumerate((ahead_x_ref, ahead_y_ref)):
        ahead_ref[...] = jnp.dot(
            flat, move_ref[direction, 0], preferred_element_type=jnp.float32
        ).reshape(ahead_ref.shape)

    for color in range(NCOL):
        span = pl.ds(color * width, width)
        for part in range(2):
            still_ref[pl.ds(part * nvec, nvec), span] = vector_ref[now, part, color]
        for start in range(0, nvec, ROWS):
            real = vector_ref[now, 0, color, pl.ds(start, ROWS), :].astype(jnp.float32)
            imag = vector_ref[now, 1, color, pl.ds(start, ROWS), :].astype(jnp.float32)
            for moment in range(NMOM):
                cosine = phase_ref[moment, 0]
                sine = phase_ref[moment, 1]
                first = 2 * moment * nvec + start
                phased_ref[pl.ds(first, ROWS), span] = (cosine * real - sine * imag).astype(jnp.bfloat16)
                phased_ref[pl.ds(first + nvec, ROWS), span] = (sine * real + cosine * imag).astype(jnp.bfloat16)
    gram(still_ref, 0)

    for direction, (adjoint_ref, behind_ref) in enumerate(
        ((adjoint_x_ref, behind_x_ref), (adjoint_y_ref, behind_y_ref))
    ):

        def adjoint(part, color, rows, lanes, value):
            adjoint_ref[part, color, rows, lanes] = value.astype(jnp.bfloat16)

        color_loop(linker(direction), nvec, width, vector, adjoint, True)
        behind_ref[...] = jnp.dot(
            adjoint_ref[...].reshape(2 * NCOL * nvec, width),
            move_ref[direction, 1],
            preferred_element_type=jnp.float32,
        ).reshape(behind_ref.shape)

    for direction, (ahead_ref, behind_ref, moved_ref) in enumerate(
        ((ahead_x_ref, behind_x_ref, moved_x_ref), (ahead_y_ref, behind_y_ref, moved_y_ref))
    ):

        def ahead(part, color, rows, lanes):
            return ahead_ref[part, color, rows, lanes]

        def forward(part, color, rows, lanes, value):
            moved_ref[
                pl.ds(part * nvec + rows.start, rows.size), pl.ds(color * width + lanes.start, lanes.size)
            ] = (value - behind_ref[part, color, rows, lanes]).astype(jnp.bfloat16)

        color_loop(linker(direction), nvec, width, ahead, forward, False)
        gram(moved_ref, direction + 1)

    def own(part, color, rows, lanes, value):
        own_ref[0, part, color, rows, lanes] = value

    color_loop(linker(2), nvec, width, vector, own, True)


def plane_items(position, momenta, vectors, links, total_z, plane, scale):
    slices, _, _, nvec, width = vectors.shape
    color_block = (2, NCOL, nvec, width)
    return pl.pallas_call(
        functools.partial(plane_kernel, total_z, plane, scale),
        grid=(slices,),
        in_specs=[pl.BlockSpec(memory_space=pltpu.SMEM)] + [pl.BlockSpec(memory_space=pltpu.HBM)] * 3,
        out_specs=[
            pl.BlockSpec((1, NMOM, NDISP - 1, 2 * nvec + ROWS, nvec), lambda t: (t, 0, 0, 0, 0)),
            pl.BlockSpec((1,) + color_block, lambda t: (t, 0, 0, 0, 0)),
            pl.BlockSpec((NMOM, 2, 1, width), lambda t: (0, 0, 0, 0)),
            pl.BlockSpec((NMOM, 2, 1, nvec), lambda t: (0, 0, 0, 0)),
        ],
        out_shape=[
            jax.ShapeDtypeStruct((slices, NMOM, NDISP - 1, 2 * nvec + ROWS, nvec), jnp.bfloat16),
            jax.ShapeDtypeStruct(vectors.shape, jnp.float32),
            jax.ShapeDtypeStruct((NMOM, 2, 1, width), jnp.float32),
            jax.ShapeDtypeStruct((NMOM, 2, 1, nvec), jnp.float32),
        ],
        scratch_shapes=[
            pltpu.SMEM(momenta.shape, jnp.int32),
            pltpu.VMEM(vectors.shape, jnp.bfloat16),
            pltpu.VMEM(links.shape, jnp.float32),
        ]
        + [pltpu.VMEM(color_block, jnp.float32)] * 4
        + [pltpu.VMEM(color_block, jnp.bfloat16)] * 2
        + [pltpu.VMEM((NMOM * 2 * nvec, NCOL * width), jnp.bfloat16)]
        + [pltpu.VMEM((2 * nvec, NCOL * width), jnp.bfloat16)] * 3
        + [
            pltpu.VMEM((2, 2, width, width), jnp.bfloat16),
            pltpu.SemaphoreType.DMA,
            pltpu.SemaphoreType.DMA((2, slices)),
        ],
        compiler_params=pltpu.CompilerParams(vmem_limit_bytes=PLANE_LIMIT),
        cost_estimate=pl.CostEstimate(
            flops=slices * 16 * NMOM * nvec * nvec * NCOL * width,
            bytes_accessed=6 * vectors.size + 4 * links.size,
            transcendentals=0,
        ),
        name="plane_items",
    )(position, in_hbm(momenta), in_hbm(vectors), in_hbm(links))


def layer_kernel(
    core, scale, rows_ref, item_ref, own_ref, ahead_ref, phase_ref, turn_ref, out_ref, lhs_ref, listed_ref
):
    nvec, width = own_ref.shape[3:]
    total = out_ref.shape[0]
    sites = rows_ref.shape[0] // 2

    def parts_of(place):
        item = rows_ref[2 * lax.rem(place, sites) + core, lax.div(place, sites), 0]
        rest = lax.rem(item, NMOM * NDISP)
        return lax.div(item, NMOM * NDISP), lax.div(rest, NDISP), lax.rem(rest, NDISP)

    def bond(place, lhs):
        slice_index, moment, _ = parts_of(place)
        cosine = phase_ref[moment, 0]
        sine = phase_ref[moment, 1]
        for color in range(NCOL):
            span = pl.ds(color * width, width)
            for part in range(2):
                value = own_ref[slice_index, part, color]
                lhs[pl.ds(part * nvec, nvec), span] = (cosine * value).astype(jnp.bfloat16)
                lhs[pl.ds((2 + part) * nvec, nvec), span] = (sine * value).astype(jnp.bfloat16)
        rhs = jnp.concatenate(
            [
                jnp.concatenate([ahead_ref[slice_index, part, color] for color in range(NCOL)], 1)
                for part in range(2)
            ],
            0,
        )
        gram = lax.dot_general(lhs[...], rhs, (((1,), (1,)), ((), ())), preferred_element_type=jnp.float32)
        block = [
            [gram[i * nvec : (i + 1) * nvec, j * nvec : (j + 1) * nvec] for j in range(2)] for i in range(4)
        ]
        cos_real = block[0][0] + block[1][1]
        cos_imag = block[0][1] - block[1][0]
        sin_real = block[2][0] + block[3][1]
        sin_imag = block[2][1] - block[3][0]
        half = 0.5 * scale
        turn_cos = half * turn_ref[moment, 0]
        turn_sin = half * turn_ref[moment, 1]
        back_real = cos_real - sin_imag
        back_imag = cos_imag + sin_real
        real = half * (cos_real + sin_imag) - (turn_cos * back_real - turn_sin * back_imag).T
        imag = half * (cos_imag - sin_real) + (turn_cos * back_imag + turn_sin * back_real).T
        return real, imag

    found = jnp.int32(0)
    for place in range(total):
        slice_index, moment, disp = parts_of(jnp.int32(place))
        out_ref[place] = item_ref[slice_index, moment, jnp.minimum(disp, NDISP - 2)]
        listed_ref[found] = place
        found = found + (disp == NDISP - 1).astype(jnp.int32)

    @pl.loop(0, lax.div(found + 1, 2))
    def _(pair):
        both = [listed_ref[2 * pair], listed_ref[jnp.minimum(2 * pair + 1, found - 1)]]
        results = [bond(place, lhs_ref.at[index]) for index, place in enumerate(both)]
        for place, (real, imag) in zip(both, results):
            store_rounded(out_ref, (place,), real, imag)


def layer_items(core, rows, item, own, ahead, phase, turn, scale):
    slices, _, _, nvec, width = own.shape
    devices, slots, _ = rows.shape
    total = slots * devices // 2
    whole = pl.BlockSpec(memory_space=pltpu.VMEM)
    return pl.pallas_call(
        functools.partial(layer_kernel, core, scale),
        in_specs=[pl.BlockSpec(memory_space=pltpu.SMEM)] + [whole] * 5,
        out_specs=whole,
        out_shape=jax.ShapeDtypeStruct((total, 2 * nvec + ROWS, nvec), jnp.bfloat16),
        scratch_shapes=[
            pltpu.VMEM((2, 4 * nvec, NCOL * width), jnp.bfloat16),
            pltpu.SMEM((total,), jnp.int32),
        ],
        compiler_params=pltpu.CompilerParams(vmem_limit_bytes=8 * MIB),
        cost_estimate=pl.CostEstimate(
            flops=total * 4 * nvec * nvec * NCOL * width,
            bytes_accessed=2 * own.size,
            transcendentals=0,
        ),
        name="layer_items",
    )(rows, item, own, ahead, phase, turn)


def add_kernel(places, *refs):
    for out_ref, entries in zip(refs[len(refs) - len(places) :], places):
        for index, entry in enumerate(entries):
            total = sum(refs[number][at].astype(jnp.float32) for number, at in entry)
            nvec = total.shape[1]
            if out_ref.dtype == jnp.float32:
                out_ref[index] = total
            else:
                left = total[2 * nvec :]
                store_rounded(out_ref, (index,), total[:nvec], total[nvec : 2 * nvec], left)


def added(groups):
    arrays = []

    def number(array):
        found = [place for place, other in enumerate(arrays) if other is array]
        if not found:
            arrays.append(array)
        return found[0] if found else len(arrays) - 1

    places = [[[(number(array), at) for array, at in entry] for entry in entries] for entries, _ in groups]
    tail = arrays[0].shape[1:]
    whole = pl.BlockSpec(memory_space=pltpu.VMEM)
    size = sum(len(entry) for entries in places for entry in entries) * math.prod(tail)
    return pl.pallas_call(
        functools.partial(add_kernel, places),
        in_specs=[whole] * len(arrays),
        out_specs=[whole] * len(groups),
        out_shape=[jax.ShapeDtypeStruct((len(entries),) + tail, dtype) for entries, dtype in groups],
        compiler_params=pltpu.CompilerParams(vmem_limit_bytes=8 * MIB),
        cost_estimate=pl.CostEstimate(flops=size, bytes_accessed=4 * size, transcendentals=0),
        name="added",
    )(*arrays)


class Chain:
    def __init__(self, entries, order):
        self.entries = entries
        self.order = order

    def chunks(self, step):
        far = [r for r in self.entries if r >> (self.order[step] - 1) & 1]
        if step + 1 == len(self.order):
            return [far]
        split = [[], []]
        for r in far:
            split[r >> (self.order[step + 1] - 1) & 1].append(r)
        return [split[1], split[0]]

    def send(self, step, far):
        bit = self.order[step]
        near = [r ^ (1 << (bit - 1)) for r in far]
        groups = [([self.entries[r] for r in far], jnp.bfloat16)]
        last = step + 1 == len(self.order)
        if step == 0 or last:
            kept = [self.entries[r] if step == 0 else self.entries[r][:2] for r in near]
            groups.append((kept, jnp.float32))
        outs = added(groups)
        arrived = exchanged(outs[0], 1 << bit)
        for at, r in enumerate(near):
            if step == 0:
                self.entries[r] = [(outs[1], at)]
            elif last:
                self.entries[r][:2] = [(outs[1], at)]
            self.entries[r].append((arrived, at))
        for r in far:
            del self.entries[r]


def mix_kernel(slot_ref, structure_ref, weight_ref, tau_ref, out_ref):
    spins, _, nvec, width = tau_ref.shape[1:]
    base = structure_ref[pl.program_id(0)] * spins * spins
    weight = [[weight_ref[base + r * spins + s] for s in range(spins)] for r in range(spins)]

    @pl.loop(0, 2 * nvec // ROWS)
    def _(index):
        part = index // (nvec // ROWS)
        rows = pl.ds(pl.multiple_of(index % (nvec // ROWS) * ROWS, ROWS), ROWS)
        tau = [tau_ref[0, s, part, rows, :].astype(jnp.float32) for s in range(spins)]
        for r in range(spins):
            mixed = weight[r][0] * tau[0]
            for s in range(1, spins):
                mixed = mixed + weight[r][s] * tau[s]
            out_ref[0, r, part, rows, :] = mixed.astype(jnp.bfloat16)


def mixed_perambulators(slots, structures, weights, perambulators):
    block = (1,) + perambulators.shape[1:]
    count = slots.shape[0]
    return pl.pallas_call(
        mix_kernel,
        grid_spec=pltpu.PrefetchScalarGridSpec(
            num_scalar_prefetch=3,
            grid=(count,),
            in_specs=[pl.BlockSpec(block, lambda j, slot, *_: (slot[j], 0, 0, 0, 0))],
            out_specs=pl.BlockSpec(block, lambda j, *_: (j, 0, 0, 0, 0)),
        ),
        out_shape=jax.ShapeDtypeStruct((count,) + perambulators.shape[1:], jnp.bfloat16),
        compiler_params=pltpu.CompilerParams(vmem_limit_bytes=8 * MIB),
        cost_estimate=pl.CostEstimate(
            flops=8 * perambulators.size, bytes_accessed=4 * perambulators.size, transcendentals=0
        ),
        name="mixed_perambulators",
    )(slots, structures, weights, in_hbm(perambulators))


def diagram_kernel(places, *refs):
    tau_ref, out_ref, block_ref, sems = refs[-4:]
    count, spins, _, nvec, width = tau_ref.shape

    def copy(index, r):
        return pltpu.make_async_copy(block_ref.at[index, r], out_ref.at[index, r], sems.at[index, r])

    for index, entry in enumerate(places):
        real, imag = restored(sum(refs[number][at].astype(jnp.float32) for number, at in entry))
        square = jnp.concatenate(
            [jnp.concatenate([real, -imag], 1), jnp.concatenate([imag, real], 1)], 0
        ).astype(jnp.bfloat16)
        for r in range(spins):
            tau = tau_ref[index, r].reshape(2 * nvec, width)
            block = jnp.dot(square, tau, preferred_element_type=jnp.float32)
            block_ref[index, r] = block.astype(jnp.bfloat16).reshape(2, nvec, width)
            copy(index, r).start()
    for index in range(count):
        for r in range(spins):
            copy(index, r).wait()


def diagrams(entries, tau):
    count, spins, _, nvec, width = tau.shape
    whole = pl.BlockSpec(memory_space=pltpu.VMEM)
    arrays = [array for entry in entries for array, _ in entry]
    places = []
    for entry in entries:
        start = sum(len(one) for one in places)
        places.append([(start + number, at) for number, (_, at) in enumerate(entry)])
    return pl.pallas_call(
        functools.partial(diagram_kernel, places),
        in_specs=[whole] * (len(arrays) + 1),
        out_specs=pl.BlockSpec(memory_space=pltpu.HBM),
        out_shape=jax.ShapeDtypeStruct(tau.shape, jnp.bfloat16),
        scratch_shapes=[
            pltpu.VMEM(tau.shape, jnp.bfloat16),
            pltpu.SemaphoreType.DMA((count, spins)),
        ],
        compiler_params=pltpu.CompilerParams(vmem_limit_bytes=8 * MIB),
        cost_estimate=pl.CostEstimate(
            flops=8 * nvec * nvec * width * spins * count, bytes_accessed=4 * tau.size, transcendentals=0
        ),
        name="diagrams",
    )(*arrays, tau)


def body(eigvecs, gauge_links, momenta, spin_mix, perambulators, contraction_list):
    slices, _, _, nvec, depth, plane = eigvecs.shape
    devices = lax.axis_size(SITES)
    position = lax.axis_index(SITES)
    bits = devices.bit_length() - 1
    total_z = depth * devices
    width = depth * plane
    scale = 1.0 / math.sqrt(NCOL * plane * total_z)
    place = position.reshape(1)
    rows, after, place = gathered(contraction_list, eigvecs, place)
    upper = shifted(after[:, :, :, :, :1, :], SITES, -1)
    vectors = eigvecs.reshape(slices, 2, NCOL, nvec, width)
    links = gauge_links.reshape(slices, 3, 2, NCOL, NCOL, 1, width)
    item, own, phase, turn = plane_items(place, momenta, vectors, links, total_z, plane, scale)
    chosen = contraction_list[:, 2] - position * perambulators.shape[0]
    tau = mixed_perambulators(chosen, contraction_list[:, 1], spin_mix.reshape(-1), perambulators)
    ahead = jnp.concatenate([eigvecs[:, :, :, :, 1:, :], upper], 4).reshape(vectors.shape)
    send = layer_items(1, rows, item, own, ahead, phase, turn, scale)
    keep = layer_items(0, rows, item, own, ahead, phase, turn, scale)
    slots = range(contraction_list.shape[0])
    other = exchanged(send, 1)
    sites = devices // 2
    chains = [
        Chain(
            {r: [(keep, slot * sites + r), (other, slot * sites + r)] for r in range(sites)},
            [1 + (slot + step) % (bits - 2) for step in range(bits - 2)] + [bits - 1],
        )
        for slot in slots
    ]
    for step in range(bits - 1):
        messages = [chain.chunks(step) for chain in chains]
        for part in range(len(messages[0])):
            for chain, far in zip(chains, messages):
                chain.send(step, far[part])
    return diagrams([chain.entries[0] for chain in chains], tau)


def solution(mesh):
    placed = (
        P("cfg", None, None, None, ("space", "diag"), None),
        P("cfg", None, None, None, None, ("space", "diag"), None),
        P(),
        P(),
        P(("cfg", "space", "diag"), None, None, None, None),
        P(("space", "diag"), None),
    )
    return jax.shard_map(
        body,
        mesh=mesh,
        in_specs=placed,
        out_specs=P(("cfg", "space", "diag"), None, None, None, None),
        check_vma=False,
    )
```

```python
import functools
import math

import jax
import jax.numpy as jnp
from jax import lax
from jax.experimental import pallas as pl
from jax.experimental.pallas import tpu as pltpu
from jax.sharding import PartitionSpec as P

NCOL = 3
NMOM = 4
NDISP = 4
LX = 16
LY = 16
LANES = 128
ROWS = 16
SITES = ("space", "diag")
MIB = 1024 * 1024
PLANE_LIMIT = 20 * MIB


def shifted(value, axis, by):
    size = lax.axis_size(axis)
    return lax.ppermute(value, axis, [(i, (i + by) % size) for i in range(size)])


def in_hbm(value):
    return pltpu.with_memory_space_constraint(value, pltpu.HBM)


def exchanged(value, mask):
    size = lax.axis_size(SITES)
    return lax.ppermute(value, SITES, [(i, i ^ mask) for i in range(size)])


def gathered(rows, early, late):
    bits = lax.axis_size(SITES).bit_length() - 1
    value = rows[None]
    for low in range(0, bits, 2):
        if low == 2:
            value, late = lax.optimization_barrier((value, late))
        arrived = [exchanged(value, step << low) for step in reversed(range(1, 1 << min(2, bits - low)))]
        if low == 0:
            arrived, early = lax.optimization_barrier((arrived, early))
        value = jnp.concatenate([value] + arrived[::-1])
    return value, early, late


def diagonal(value):
    size = value.shape[0]
    same = lax.broadcasted_iota(jnp.int32, value.shape, 0) == lax.broadcasted_iota(jnp.int32, value.shape, 1)
    return jnp.sum(jnp.where(same, value, 0.0), 0, keepdims=True).reshape(1, size)


def rounded(real, imag, left=None):
    planes = [value.astype(jnp.bfloat16) for value in (real, imag)]
    lost = [diagonal(value - plane.astype(jnp.float32)) for value, plane in zip((real, imag), planes)]
    tile = jnp.concatenate(lost + [jnp.zeros((ROWS - 2, real.shape[1]), jnp.float32)], 0)
    if left is not None:
        tile = tile + left
    return planes, tile.astype(jnp.bfloat16)


def store_rounded(ref, index, real, imag, left=None):
    nvec = real.shape[0]
    planes, tile = rounded(real, imag, left)
    ref[(*index, pl.ds(0, nvec))] = planes[0]
    ref[(*index, pl.ds(nvec, nvec))] = planes[1]
    ref[(*index, pl.ds(2 * nvec, ROWS))] = tile


def restored(total):
    nvec = total.shape[1]
    shape = (nvec, nvec)
    same = lax.broadcasted_iota(jnp.int32, shape, 0) == lax.broadcasted_iota(jnp.int32, shape, 1)
    return [
        total[part * nvec : (part + 1) * nvec] + jnp.where(same, total[2 * nvec + part : 2 * nvec + part + 1], 0.0)
        for part in range(2)
    ]


def color_product(matrix, real, imag, adjoint):
    rows = []
    for row in range(NCOL):
        real_part = imag_part = None
        for col in range(NCOL):
            if adjoint:
                mreal, mimag = matrix[0][col][row], matrix[1][col][row]
                one = mreal * real[col] + mimag * imag[col]
                two = mreal * imag[col] - mimag * real[col]
            else:
                mreal, mimag = matrix[0][row][col], matrix[1][row][col]
                one = mreal * real[col] - mimag * imag[col]
                two = mreal * imag[col] + mimag * real[col]
            real_part = one if real_part is None else real_part + one
            imag_part = two if imag_part is None else imag_part + two
        rows.append((real_part, imag_part))
    return rows


def color_loop(link, nvec, width, load, store, adjoint):
    height = math.gcd(nvec, 2 * ROWS)
    for lane in range(0, width, LANES):
        lanes = pl.ds(lane, LANES)
        matrix = [
            [[link(part, row, col, lanes) for col in range(NCOL)] for row in range(NCOL)] for part in range(2)
        ]
        for start in range(0, nvec, height):
            rows = pl.ds(start, height)
            real = [load(0, color, rows, lanes) for color in range(NCOL)]
            imag = [load(1, color, rows, lanes) for color in range(NCOL)]
            for color, (one, two) in enumerate(color_product(matrix, real, imag, adjoint)):
                store(0, color, rows, lanes, one)
                store(1, color, rows, lanes, two)


def fill_tables(position, total_z, plane, momenta_ref, phase_ref, turn_ref):
    width = phase_ref.shape[-1]
    flat = lax.broadcasted_iota(jnp.int32, (1, width), 1)
    xcoord = (flat % LX).astype(jnp.float32)
    ycoord = (flat % plane // LX).astype(jnp.float32)
    zcoord = (position * (width // plane) + flat // plane).astype(jnp.float32)
    for moment in range(NMOM):
        along_x = momenta_ref[moment, 0].astype(jnp.float32)
        along_y = momenta_ref[moment, 1].astype(jnp.float32)
        along_z = momenta_ref[moment, 2].astype(jnp.float32)
        angle = (
            2.0 * math.pi * (along_x * xcoord / LX + along_y * ycoord / LY + along_z * zcoord / total_z)
        )
        phase_ref[moment, 0] = jnp.cos(angle)
        phase_ref[moment, 1] = jnp.sin(angle)
        turn = jnp.full((1, turn_ref.shape[-1]), 2.0 * math.pi / total_z, jnp.float32) * along_z
        turn_ref[moment, 0] = jnp.cos(turn)
        turn_ref[moment, 1] = jnp.sin(turn)


def fill_moves(move_ref):
    width = move_ref.shape[-1]
    source = lax.broadcasted_iota(jnp.int32, (width, width), 0)
    site = lax.broadcasted_iota(jnp.int32, (width, width), 1)
    xcoord = site % LX
    ycoord = site // LX % LY
    for sign, by in enumerate((1, -1)):
        along_x = site - xcoord + (xcoord + LX + by) % LX
        along_y = site + ((ycoord + LY + by) % LY - ycoord) * LX
        move_ref[0, sign] = (source == along_x).astype(jnp.float32).astype(jnp.bfloat16)
        move_ref[1, sign] = (source == along_y).astype(jnp.float32).astype(jnp.bfloat16)


def plane_kernel(
    total_z, plane, scale,
    position_ref, momenta_in, vector_in, link_in,
    item_ref, own_ref, phase_ref, turn_ref,
    momenta_ref, vector_ref, link_ref,
    ahead_x_ref, ahead_y_ref, behind_x_ref, behind_y_ref, adjoint_x_ref, adjoint_y_ref,
    phased_ref, still_ref, moved_x_ref, moved_y_ref, move_ref, momenta_sem, sems,
):
    now = pl.program_id(0)
    slices, _, _, nvec, width = vector_ref.shape

    def copies(index):
        return (
            pltpu.make_async_copy(vector_in.at[index], vector_ref.at[index], sems.at[0, index]),
            pltpu.make_async_copy(link_in.at[index], link_ref.at[index], sems.at[1, index]),
        )

    @pl.when(now == 0)
    def _():
        moments = pltpu.make_async_copy(momenta_in, momenta_ref, momenta_sem)
        moments.start()
        for index in range(slices):
            for copy in copies(index):
                copy.start()
        fill_moves(move_ref)
        moments.wait()
        fill_tables(position_ref[0], total_z, plane, momenta_ref, phase_ref, turn_ref)

    for copy in copies(now):
        copy.wait()

    def linker(direction):
        return lambda part, row, col, lanes: link_ref[now, direction, part, row, col, :, lanes]

    def vector(part, color, rows, lanes):
        return vector_ref[now, part, color, rows, lanes].astype(jnp.float32)

    def gram(moved_ref, disp):
        product = lax.dot_general(
            phased_ref[...], moved_ref[...], (((1,), (1,)), ((), ())), preferred_element_type=jnp.float32
        )
        for moment in range(NMOM):
            start = 2 * moment * nvec
            upper = product[start : start + nvec]
            lower = product[start + nvec : start + 2 * nvec]
            factor = scale if disp == 0 else 0.5 * scale
            real = factor * (upper[:, :nvec] + lower[:, nvec:])
            imag = factor * (upper[:, nvec:] - lower[:, :nvec])
            store_rounded(item_ref, (0, moment, disp), real, imag)

    flat = vector_ref[now].reshape(2 * NCOL * nvec, width)
    for direction, ahead_ref in enumerate((ahead_x_ref, ahead_y_ref)):
        ahead_ref[...] = jnp.dot(
            flat, move_ref[direction, 0], preferred_element_type=jnp.float32
        ).reshape(ahead_ref.shape)

    for color in range(NCOL):
        span = pl.ds(color * width, width)
        for part in range(2):
            still_ref[pl.ds(part * nvec, nvec), span] = vector_ref[now, part, color]
        for start in range(0, nvec, ROWS):
            real = vector_ref[now, 0, color, pl.ds(start, ROWS), :].astype(jnp.float32)
            imag = vector_ref[now, 1, color, pl.ds(start, ROWS), :].astype(jnp.float32)
            for moment in range(NMOM):
                cosine = phase_ref[moment, 0]
                sine = phase_ref[moment, 1]
                first = 2 * moment * nvec + start
                phased_ref[pl.ds(first, ROWS), span] = (cosine * real - sine * imag).astype(jnp.bfloat16)
                phased_ref[pl.ds(first + nvec, ROWS), span] = (sine * real + cosine * imag).astype(jnp.bfloat16)
    gram(still_ref, 0)

    for direction, (adjoint_ref, behind_ref) in enumerate(
        ((adjoint_x_ref, behind_x_ref), (adjoint_y_ref, behind_y_ref))
    ):

        def adjoint(part, color, rows, lanes, value):
            adjoint_ref[part, color, rows, lanes] = value.astype(jnp.bfloat16)

        color_loop(linker(direction), nvec, width, vector, adjoint, True)
        behind_ref[...] = jnp.dot(
            adjoint_ref[...].reshape(2 * NCOL * nvec, width),
            move_ref[direction, 1],
            preferred_element_type=jnp.float32,
        ).reshape(behind_ref.shape)

    for direction, (ahead_ref, behind_ref, moved_ref) in enumerate(
        ((ahead_x_ref, behind_x_ref, moved_x_ref), (ahead_y_ref, behind_y_ref, moved_y_ref))
    ):

        def ahead(part, color, rows, lanes):
            return ahead_ref[part, color, rows, lanes]

        def forward(part, color, rows, lanes, value):
            moved_ref[
                pl.ds(part * nvec + rows.start, rows.size), pl.ds(color * width + lanes.start, lanes.size)
            ] = (value - behind_ref[part, color, rows, lanes]).astype(jnp.bfloat16)

        color_loop(linker(direction), nvec, width, ahead, forward, False)
        gram(moved_ref, direction + 1)

    def own(part, color, rows, lanes, value):
        own_ref[0, part, color, rows, lanes] = value

    color_loop(linker(2), nvec, width, vector, own, True)


def plane_items(position, momenta, vectors, links, total_z, plane, scale):
    slices, _, _, nvec, width = vectors.shape
    color_block = (2, NCOL, nvec, width)
    return pl.pallas_call(
        functools.partial(plane_kernel, total_z, plane, scale),
        grid=(slices,),
        in_specs=[pl.BlockSpec(memory_space=pltpu.SMEM)] + [pl.BlockSpec(memory_space=pltpu.HBM)] * 3,
        out_specs=[
            pl.BlockSpec((1, NMOM, NDISP - 1, 2 * nvec + ROWS, nvec), lambda t: (t, 0, 0, 0, 0)),
            pl.BlockSpec((1,) + color_block, lambda t: (t, 0, 0, 0, 0)),
            pl.BlockSpec((NMOM, 2, 1, width), lambda t: (0, 0, 0, 0)),
            pl.BlockSpec((NMOM, 2, 1, nvec), lambda t: (0, 0, 0, 0)),
        ],
        out_shape=[
            jax.ShapeDtypeStruct((slices, NMOM, NDISP - 1, 2 * nvec + ROWS, nvec), jnp.bfloat16),
            jax.ShapeDtypeStruct(vectors.shape, jnp.float32),
            jax.ShapeDtypeStruct((NMOM, 2, 1, width), jnp.float32),
            jax.ShapeDtypeStruct((NMOM, 2, 1, nvec), jnp.float32),
        ],
        scratch_shapes=[
            pltpu.SMEM(momenta.shape, jnp.int32),
            pltpu.VMEM(vectors.shape, jnp.bfloat16),
            pltpu.VMEM(links.shape, jnp.float32),
        ]
        + [pltpu.VMEM(color_block, jnp.float32)] * 4
        + [pltpu.VMEM(color_block, jnp.bfloat16)] * 2
        + [pltpu.VMEM((NMOM * 2 * nvec, NCOL * width), jnp.bfloat16)]
        + [pltpu.VMEM((2 * nvec, NCOL * width), jnp.bfloat16)] * 3
        + [
            pltpu.VMEM((2, 2, width, width), jnp.bfloat16),
            pltpu.SemaphoreType.DMA,
            pltpu.SemaphoreType.DMA((2, slices)),
        ],
        compiler_params=pltpu.CompilerParams(vmem_limit_bytes=PLANE_LIMIT),
        cost_estimate=pl.CostEstimate(
            flops=slices * 16 * NMOM * nvec * nvec * NCOL * width,
            bytes_accessed=6 * vectors.size + 4 * links.size,
            transcendentals=0,
        ),
        name="plane_items",
    )(position, in_hbm(momenta), in_hbm(vectors), in_hbm(links))


def layer_kernel(
    core, scale, rows_ref, item_ref, own_ref, ahead_ref, phase_ref, turn_ref, out_ref, lhs_ref, listed_ref
):
    nvec, width = own_ref.shape[3:]
    total = out_ref.shape[0]
    sites = rows_ref.shape[0] // 2

    def parts_of(place):
        item = rows_ref[2 * lax.rem(place, sites) + core, lax.div(place, sites), 0]
        rest = lax.rem(item, NMOM * NDISP)
        return lax.div(item, NMOM * NDISP), lax.div(rest, NDISP), lax.rem(rest, NDISP)

    def bond(place, lhs):
        slice_index, moment, _ = parts_of(place)
        cosine = phase_ref[moment, 0]
        sine = phase_ref[moment, 1]
        for color in range(NCOL):
            span = pl.ds(color * width, width)
            for part in range(2):
                value = own_ref[slice_index, part, color]
                lhs[pl.ds(part * nvec, nvec), span] = (cosine * value).astype(jnp.bfloat16)
                lhs[pl.ds((2 + part) * nvec, nvec), span] = (sine * value).astype(jnp.bfloat16)
        rhs = jnp.concatenate(
            [
                jnp.concatenate([ahead_ref[slice_index, part, color] for color in range(NCOL)], 1)
                for part in range(2)
            ],
            0,
        )
        gram = lax.dot_general(lhs[...], rhs, (((1,), (1,)), ((), ())), preferred_element_type=jnp.float32)
        block = [
            [gram[i * nvec : (i + 1) * nvec, j * nvec : (j + 1) * nvec] for j in range(2)] for i in range(4)
        ]
        cos_real = block[0][0] + block[1][1]
        cos_imag = block[0][1] - block[1][0]
        sin_real = block[2][0] + block[3][1]
        sin_imag = block[2][1] - block[3][0]
        half = 0.5 * scale
        turn_cos = half * turn_ref[moment, 0]
        turn_sin = half * turn_ref[moment, 1]
        back_real = cos_real - sin_imag
        back_imag = cos_imag + sin_real
        real = half * (cos_real + sin_imag) - (turn_cos * back_real - turn_sin * back_imag).T
        imag = half * (cos_imag - sin_real) + (turn_cos * back_imag + turn_sin * back_real).T
        return real, imag

    found = jnp.int32(0)
    for place in range(total):
        slice_index, moment, disp = parts_of(jnp.int32(place))
        out_ref[place] = item_ref[slice_index, moment, jnp.minimum(disp, NDISP - 2)]
        listed_ref[found] = place
        found = found + (disp == NDISP - 1).astype(jnp.int32)

    @pl.loop(0, lax.div(found + 1, 2))
    def _(pair):
        both = [listed_ref[2 * pair], listed_ref[jnp.minimum(2 * pair + 1, found - 1)]]
        results = [bond(place, lhs_ref.at[index]) for index, place in enumerate(both)]
        for place, (real, imag) in zip(both, results):
            store_rounded(out_ref, (place,), real, imag)


def layer_items(core, rows, item, own, ahead, phase, turn, scale):
    slices, _, _, nvec, width = own.shape
    devices, slots, _ = rows.shape
    total = slots * devices // 2
    whole = pl.BlockSpec(memory_space=pltpu.VMEM)
    return pl.pallas_call(
        functools.partial(layer_kernel, core, scale),
        in_specs=[pl.BlockSpec(memory_space=pltpu.SMEM)] + [whole] * 5,
        out_specs=whole,
        out_shape=jax.ShapeDtypeStruct((total, 2 * nvec + ROWS, nvec), jnp.bfloat16),
        scratch_shapes=[
            pltpu.VMEM((2, 4 * nvec, NCOL * width), jnp.bfloat16),
            pltpu.SMEM((total,), jnp.int32),
        ],
        compiler_params=pltpu.CompilerParams(vmem_limit_bytes=8 * MIB),
        cost_estimate=pl.CostEstimate(
            flops=total * 4 * nvec * nvec * NCOL * width,
            bytes_accessed=2 * own.size,
            transcendentals=0,
        ),
        name="layer_items",
    )(rows, item, own, ahead, phase, turn)


def add_kernel(places, *refs):
    for out_ref, entries in zip(refs[len(refs) - len(places) :], places):
        for index, entry in enumerate(entries):
            total = sum(refs[number][at].astype(jnp.float32) for number, at in entry)
            nvec = total.shape[1]
            if out_ref.dtype == jnp.float32:
                out_ref[index] = total
            else:
                left = total[2 * nvec :]
                store_rounded(out_ref, (index,), total[:nvec], total[nvec : 2 * nvec], left)


def added(groups):
    arrays = []

    def number(array):
        found = [place for place, other in enumerate(arrays) if other is array]
        if not found:
            arrays.append(array)
        return found[0] if found else len(arrays) - 1

    places = [[[(number(array), at) for array, at in entry] for entry in entries] for entries, _ in groups]
    tail = arrays[0].shape[1:]
    whole = pl.BlockSpec(memory_space=pltpu.VMEM)
    size = sum(len(entry) for entries in places for entry in entries) * math.prod(tail)
    return pl.pallas_call(
        functools.partial(add_kernel, places),
        in_specs=[whole] * len(arrays),
        out_specs=[whole] * len(groups),
        out_shape=[jax.ShapeDtypeStruct((len(entries),) + tail, dtype) for entries, dtype in groups],
        compiler_params=pltpu.CompilerParams(vmem_limit_bytes=8 * MIB),
        cost_estimate=pl.CostEstimate(flops=size, bytes_accessed=4 * size, transcendentals=0),
        name="added",
    )(*arrays)


class Chain:
    def __init__(self, entries, order):
        self.entries = entries
        self.order = order

    def chunks(self, step):
        far = [r for r in self.entries if r >> (self.order[step] - 1) & 1]
        if step + 1 == len(self.order):
            return [far]
        split = [[], []]
        for r in far:
            split[r >> (self.order[step + 1] - 1) & 1].append(r)
        return [split[1], split[0]]

    def send(self, step, far):
        bit = self.order[step]
        near = [r ^ (1 << (bit - 1)) for r in far]
        groups = [([self.entries[r] for r in far], jnp.bfloat16)]
        last = step + 1 == len(self.order)
        if step == 0 or last:
            kept = [self.entries[r] if step == 0 else self.entries[r][:2] for r in near]
            groups.append((kept, jnp.float32))
        outs = added(groups)
        arrived = exchanged(outs[0], 1 << bit)
        for at, r in enumerate(near):
            if step == 0:
                self.entries[r] = [(outs[1], at)]
            elif last:
                self.entries[r][:2] = [(outs[1], at)]
            self.entries[r].append((arrived, at))
        for r in far:
            del self.entries[r]


def mix_kernel(slot_ref, structure_ref, weight_ref, tau_ref, out_ref):
    spins, _, nvec, width = tau_ref.shape[1:]
    base = structure_ref[pl.program_id(0)] * spins * spins
    weight = [[weight_ref[base + r * spins + s] for s in range(spins)] for r in range(spins)]

    @pl.loop(0, 2 * nvec // ROWS)
    def _(index):
        part = index // (nvec // ROWS)
        rows = pl.ds(pl.multiple_of(index % (nvec // ROWS) * ROWS, ROWS), ROWS)
        tau = [tau_ref[0, s, part, rows, :].astype(jnp.float32) for s in range(spins)]
        for r in range(spins):
            mixed = weight[r][0] * tau[0]
            for s in range(1, spins):
                mixed = mixed + weight[r][s] * tau[s]
            out_ref[0, r, part, rows, :] = mixed.astype(jnp.bfloat16)


def mixed_perambulators(slots, structures, weights, perambulators):
    block = (1,) + perambulators.shape[1:]
    count = slots.shape[0]
    return pl.pallas_call(
        mix_kernel,
        grid_spec=pltpu.PrefetchScalarGridSpec(
            num_scalar_prefetch=3,
            grid=(count,),
            in_specs=[pl.BlockSpec(block, lambda j, slot, *_: (slot[j], 0, 0, 0, 0))],
            out_specs=pl.BlockSpec(block, lambda j, *_: (j, 0, 0, 0, 0)),
        ),
        out_shape=jax.ShapeDtypeStruct((count,) + perambulators.shape[1:], jnp.bfloat16),
        compiler_params=pltpu.CompilerParams(vmem_limit_bytes=8 * MIB),
        cost_estimate=pl.CostEstimate(
            flops=8 * perambulators.size, bytes_accessed=4 * perambulators.size, transcendentals=0
        ),
        name="mixed_perambulators",
    )(slots, structures, weights, in_hbm(perambulators))


def diagram_kernel(places, *refs):
    tau_ref, out_ref, block_ref, sems = refs[-4:]
    count, spins, _, nvec, width = tau_ref.shape

    def copy(index, r):
        return pltpu.make_async_copy(block_ref.at[index, r], out_ref.at[index, r], sems.at[index, r])

    for index, entry in enumerate(places):
        real, imag = restored(sum(refs[number][at].astype(jnp.float32) for number, at in entry))
        square = jnp.concatenate(
            [jnp.concatenate([real, -imag], 1), jnp.concatenate([imag, real], 1)], 0
        ).astype(jnp.bfloat16)
        for r in range(spins):
            tau = tau_ref[index, r].reshape(2 * nvec, width)
            block = jnp.dot(square, tau, preferred_element_type=jnp.float32)
            block_ref[index, r] = block.astype(jnp.bfloat16).reshape(2, nvec, width)
            copy(index, r).start()
    for index in range(count):
        for r in range(spins):
            copy(index, r).wait()


def diagrams(entries, tau):
    count, spins, _, nvec, width = tau.shape
    whole = pl.BlockSpec(memory_space=pltpu.VMEM)
    arrays = [array for entry in entries for array, _ in entry]
    places = []
    for entry in entries:
        start = sum(len(one) for one in places)
        places.append([(start + number, at) for number, (_, at) in enumerate(entry)])
    return pl.pallas_call(
        functools.partial(diagram_kernel, places),
        in_specs=[whole] * (len(arrays) + 1),
        out_specs=pl.BlockSpec(memory_space=pltpu.HBM),
        out_shape=jax.ShapeDtypeStruct(tau.shape, jnp.bfloat16),
        scratch_shapes=[
            pltpu.VMEM(tau.shape, jnp.bfloat16),
            pltpu.SemaphoreType.DMA((count, spins)),
        ],
        compiler_params=pltpu.CompilerParams(vmem_limit_bytes=8 * MIB),
        cost_estimate=pl.CostEstimate(
            flops=8 * nvec * nvec * width * spins * count, bytes_accessed=4 * tau.size, transcendentals=0
        ),
        name="diagrams",
    )(*arrays, tau)


def body(eigvecs, gauge_links, momenta, spin_mix, perambulators, contraction_list):
    slices, _, _, nvec, depth, plane = eigvecs.shape
    devices = lax.axis_size(SITES)
    position = lax.axis_index(SITES)
    bits = devices.bit_length() - 1
    total_z = depth * devices
    width = depth * plane
    scale = 1.0 / math.sqrt(NCOL * plane * total_z)
    place = position.reshape(1)
    rows, after, place = gathered(contraction_list, eigvecs, place)
    upper = shifted(after[:, :, :, :, :1, :], SITES, -1)
    vectors = eigvecs.reshape(slices, 2, NCOL, nvec, width)
    links = gauge_links.reshape(slices, 3, 2, NCOL, NCOL, 1, width)
    item, own, phase, turn = plane_items(place, momenta, vectors, links, total_z, plane, scale)
    chosen = contraction_list[:, 2] - position * perambulators.shape[0]
    tau = mixed_perambulators(chosen, contraction_list[:, 1], spin_mix.reshape(-1), perambulators)
    ahead = jnp.concatenate([eigvecs[:, :, :, :, 1:, :], upper], 4).reshape(vectors.shape)
    send = layer_items(1, rows, item, own, ahead, phase, turn, scale)
    keep = layer_items(0, rows, item, own, ahead, phase, turn, scale)
    slots = range(contraction_list.shape[0])
    other = exchanged(send, 1)
    sites = devices // 2
    chains = [
        Chain(
            {r: [(keep, slot * sites + r), (other, slot * sites + r)] for r in range(sites)},
            [1 + (slot + step) % (bits - 2) for step in range(bits - 2)] + [bits - 1],
        )
        for slot in slots
    ]
    for step in range(bits - 1):
        messages = [chain.chunks(step) for chain in chains]
        for part in range(len(messages[0])):
            for chain, far in zip(chains, messages):
                chain.send(step, far[part])
    return diagrams([chain.entries[0] for chain in chains], tau)


def solution(mesh):
    placed = (
        P("cfg", None, None, None, ("space", "diag"), None),
        P("cfg", None, None, None, None, ("space", "diag"), None),
        P(),
        P(),
        P(("cfg", "space", "diag"), None, None, None, None),
        P(("space", "diag"), None),
    )
    return jax.shard_map(
        body,
        mesh=mesh,
        in_specs=placed,
        out_specs=P(("cfg", "space", "diag"), None, None, None, None),
        check_vma=False,
    )
```

```python
import functools
import math

import jax
import jax.numpy as jnp
from jax import lax
from jax.experimental import pallas as pl
from jax.experimental.pallas import tpu as pltpu
from jax.sharding import PartitionSpec as P

NCOL = 3
NMOM = 4
NDISP = 4
LX = 16
LY = 16
LANES = 128
ROWS = 16
SITES = ("space", "diag")
MIB = 1024 * 1024
PLANE_LIMIT = 20 * MIB


def shifted(value, axis, by):
    size = lax.axis_size(axis)
    return lax.ppermute(value, axis, [(i, (i + by) % size) for i in range(size)])


def in_hbm(value):
    return pltpu.with_memory_space_constraint(value, pltpu.HBM)


def exchanged(value, mask):
    size = lax.axis_size(SITES)
    return lax.ppermute(value, SITES, [(i, i ^ mask) for i in range(size)])


def gathered(rows, early, late):
    bits = lax.axis_size(SITES).bit_length() - 1
    value = rows[None]
    for low in range(0, bits, 2):
        if low == 2:
            value, late = lax.optimization_barrier((value, late))
        arrived = [exchanged(value, step << low) for step in reversed(range(1, 1 << min(2, bits - low)))]
        if low == 0:
            arrived, early = lax.optimization_barrier((arrived, early))
        value = jnp.concatenate([value] + arrived[::-1])
    return value, early, late


def diagonal(value):
    size = value.shape[0]
    same = lax.broadcasted_iota(jnp.int32, value.shape, 0) == lax.broadcasted_iota(jnp.int32, value.shape, 1)
    return jnp.sum(jnp.where(same, value, 0.0), 0, keepdims=True).reshape(1, size)


def rounded(real, imag, left=None):
    planes = [value.astype(jnp.bfloat16) for value in (real, imag)]
    lost = [diagonal(value - plane.astype(jnp.float32)) for value, plane in zip((real, imag), planes)]
    tile = jnp.concatenate(lost + [jnp.zeros((ROWS - 2, real.shape[1]), jnp.float32)], 0)
    if left is not None:
        tile = tile + left
    return planes, tile.astype(jnp.bfloat16)


def store_rounded(ref, index, real, imag, left=None):
    nvec = real.shape[0]
    planes, tile = rounded(real, imag, left)
    ref[(*index, pl.ds(0, nvec))] = planes[0]
    ref[(*index, pl.ds(nvec, nvec))] = planes[1]
    ref[(*index, pl.ds(2 * nvec, ROWS))] = tile


def restored(total):
    nvec = total.shape[1]
    shape = (nvec, nvec)
    same = lax.broadcasted_iota(jnp.int32, shape, 0) == lax.broadcasted_iota(jnp.int32, shape, 1)
    return [
        total[part * nvec : (part + 1) * nvec] + jnp.where(same, total[2 * nvec + part : 2 * nvec + part + 1], 0.0)
        for part in range(2)
    ]


def color_product(matrix, real, imag, adjoint):
    rows = []
    for row in range(NCOL):
        real_part = imag_part = None
        for col in range(NCOL):
            if adjoint:
                mreal, mimag = matrix[0][col][row], matrix[1][col][row]
                one = mreal * real[col] + mimag * imag[col]
                two = mreal * imag[col] - mimag * real[col]
            else:
                mreal, mimag = matrix[0][row][col], matrix[1][row][col]
                one = mreal * real[col] - mimag * imag[col]
                two = mreal * imag[col] + mimag * real[col]
            real_part = one if real_part is None else real_part + one
            imag_part = two if imag_part is None else imag_part + two
        rows.append((real_part, imag_part))
    return rows


def color_loop(link, nvec, width, load, store, adjoint):
    height = math.gcd(nvec, 2 * ROWS)
    for lane in range(0, width, LANES):
        lanes = pl.ds(lane, LANES)
        matrix = [
            [[link(part, row, col, lanes) for col in range(NCOL)] for row in range(NCOL)] for part in range(2)
        ]
        for start in range(0, nvec, height):
            rows = pl.ds(start, height)
            real = [load(0, color, rows, lanes) for color in range(NCOL)]
            imag = [load(1, color, rows, lanes) for color in range(NCOL)]
            for color, (one, two) in enumerate(color_product(matrix, real, imag, adjoint)):
                store(0, color, rows, lanes, one)
                store(1, color, rows, lanes, two)


def fill_tables(position, total_z, plane, momenta_ref, phase_ref, turn_ref):
    width = phase_ref.shape[-1]
    flat = lax.broadcasted_iota(jnp.int32, (1, width), 1)
    xcoord = (flat % LX).astype(jnp.float32)
    ycoord = (flat % plane // LX).astype(jnp.float32)
    zcoord = (position * (width // plane) + flat // plane).astype(jnp.float32)
    for moment in range(NMOM):
        along_x = momenta_ref[moment, 0].astype(jnp.float32)
        along_y = momenta_ref[moment, 1].astype(jnp.float32)
        along_z = momenta_ref[moment, 2].astype(jnp.float32)
        angle = (
            2.0 * math.pi * (along_x * xcoord / LX + along_y * ycoord / LY + along_z * zcoord / total_z)
        )
        phase_ref[moment, 0] = jnp.cos(angle)
        phase_ref[moment, 1] = jnp.sin(angle)
        turn = jnp.full((1, turn_ref.shape[-1]), 2.0 * math.pi / total_z, jnp.float32) * along_z
        turn_ref[moment, 0] = jnp.cos(turn)
        turn_ref[moment, 1] = jnp.sin(turn)


def fill_moves(move_ref):
    width = move_ref.shape[-1]
    source = lax.broadcasted_iota(jnp.int32, (width, width), 0)
    site = lax.broadcasted_iota(jnp.int32, (width, width), 1)
    xcoord = site % LX
    ycoord = site // LX % LY
    for sign, by in enumerate((1, -1)):
        along_x = site - xcoord + (xcoord + LX + by) % LX
        along_y = site + ((ycoord + LY + by) % LY - ycoord) * LX
        move_ref[0, sign] = (source == along_x).astype(jnp.float32).astype(jnp.bfloat16)
        move_ref[1, sign] = (source == along_y).astype(jnp.float32).astype(jnp.bfloat16)


def plane_kernel(
    total_z, plane, scale,
    position_ref, momenta_in, vector_in, link_in,
    item_ref, own_ref, phase_ref, turn_ref,
    momenta_ref, vector_ref, link_ref,
    ahead_x_ref, ahead_y_ref, behind_x_ref, behind_y_ref, adjoint_x_ref, adjoint_y_ref,
    phased_ref, still_ref, moved_x_ref, moved_y_ref, move_ref, momenta_sem, sems,
):
    now = pl.program_id(0)
    slices, _, _, nvec, width = vector_ref.shape

    def copies(index):
        return (
            pltpu.make_async_copy(vector_in.at[index], vector_ref.at[index], sems.at[0, index]),
            pltpu.make_async_copy(link_in.at[index], link_ref.at[index], sems.at[1, index]),
        )

    @pl.when(now == 0)
    def _():
        moments = pltpu.make_async_copy(momenta_in, momenta_ref, momenta_sem)
        moments.start()
        for index in range(slices):
            for copy in copies(index):
                copy.start()
        fill_moves(move_ref)
        moments.wait()
        fill_tables(position_ref[0], total_z, plane, momenta_ref, phase_ref, turn_ref)

    for copy in copies(now):
        copy.wait()

    def linker(direction):
        return lambda part, row, col, lanes: link_ref[now, direction, part, row, col, :, lanes]

    def vector(part, color, rows, lanes):
        return vector_ref[now, part, color, rows, lanes].astype(jnp.float32)

    def gram(moved_ref, disp):
        product = lax.dot_general(
            phased_ref[...], moved_ref[...], (((1,), (1,)), ((), ())), preferred_element_type=jnp.float32
        )
        for moment in range(NMOM):
            start = 2 * moment * nvec
            upper = product[start : start + nvec]
            lower = product[start + nvec : start + 2 * nvec]
            factor = scale if disp == 0 else 0.5 * scale
            real = factor * (upper[:, :nvec] + lower[:, nvec:])
            imag = factor * (upper[:, nvec:] - lower[:, :nvec])
            store_rounded(item_ref, (0, moment, disp), real, imag)

    flat = vector_ref[now].reshape(2 * NCOL * nvec, width)
    for direction, ahead_ref in enumerate((ahead_x_ref, ahead_y_ref)):
        ahead_ref[...] = jnp.dot(
            flat, move_ref[direction, 0], preferred_element_type=jnp.float32
        ).reshape(ahead_ref.shape)

    for color in range(NCOL):
        span = pl.ds(color * width, width)
        for part in range(2):
            still_ref[pl.ds(part * nvec, nvec), span] = vector_ref[now, part, color]
        for start in range(0, nvec, ROWS):
            real = vector_ref[now, 0, color, pl.ds(start, ROWS), :].astype(jnp.float32)
            imag = vector_ref[now, 1, color, pl.ds(start, ROWS), :].astype(jnp.float32)
            for moment in range(NMOM):
                cosine = phase_ref[moment, 0]
                sine = phase_ref[moment, 1]
                first = 2 * moment * nvec + start
                phased_ref[pl.ds(first, ROWS), span] = (cosine * real - sine * imag).astype(jnp.bfloat16)
                phased_ref[pl.ds(first + nvec, ROWS), span] = (sine * real + cosine * imag).astype(jnp.bfloat16)
    gram(still_ref, 0)

    for direction, (adjoint_ref, behind_ref) in enumerate(
        ((adjoint_x_ref, behind_x_ref), (adjoint_y_ref, behind_y_ref))
    ):

        def adjoint(part, color, rows, lanes, value):
            adjoint_ref[part, color, rows, lanes] = value.astype(jnp.bfloat16)

        color_loop(linker(direction), nvec, width, vector, adjoint, True)
        behind_ref[...] = jnp.dot(
            adjoint_ref[...].reshape(2 * NCOL * nvec, width),
            move_ref[direction, 1],
            preferred_element_type=jnp.float32,
        ).reshape(behind_ref.shape)

    for direction, (ahead_ref, behind_ref, moved_ref) in enumerate(
        ((ahead_x_ref, behind_x_ref, moved_x_ref), (ahead_y_ref, behind_y_ref, moved_y_ref))
    ):

        def ahead(part, color, rows, lanes):
            return ahead_ref[part, color, rows, lanes]

        def forward(part, color, rows, lanes, value):
            moved_ref[
                pl.ds(part * nvec + rows.start, rows.size), pl.ds(color * width + lanes.start, lanes.size)
            ] = (value - behind_ref[part, color, rows, lanes]).astype(jnp.bfloat16)

        color_loop(linker(direction), nvec, width, ahead, forward, False)
        gram(moved_ref, direction + 1)

    def own(part, color, rows, lanes, value):
        own_ref[0, part, color, rows, lanes] = value

    color_loop(linker(2), nvec, width, vector, own, True)


def plane_items(position, momenta, vectors, links, total_z, plane, scale):
    slices, _, _, nvec, width = vectors.shape
    color_block = (2, NCOL, nvec, width)
    return pl.pallas_call(
        functools.partial(plane_kernel, total_z, plane, scale),
        grid=(slices,),
        in_specs=[pl.BlockSpec(memory_space=pltpu.SMEM)] + [pl.BlockSpec(memory_space=pltpu.HBM)] * 3,
        out_specs=[
            pl.BlockSpec((1, NMOM, NDISP - 1, 2 * nvec + ROWS, nvec), lambda t: (t, 0, 0, 0, 0)),
            pl.BlockSpec((1,) + color_block, lambda t: (t, 0, 0, 0, 0)),
            pl.BlockSpec((NMOM, 2, 1, width), lambda t: (0, 0, 0, 0)),
            pl.BlockSpec((NMOM, 2, 1, nvec), lambda t: (0, 0, 0, 0)),
        ],
        out_shape=[
            jax.ShapeDtypeStruct((slices, NMOM, NDISP - 1, 2 * nvec + ROWS, nvec), jnp.bfloat16),
            jax.ShapeDtypeStruct(vectors.shape, jnp.float32),
            jax.ShapeDtypeStruct((NMOM, 2, 1, width), jnp.float32),
            jax.ShapeDtypeStruct((NMOM, 2, 1, nvec), jnp.float32),
        ],
        scratch_shapes=[
            pltpu.SMEM(momenta.shape, jnp.int32),
            pltpu.VMEM(vectors.shape, jnp.bfloat16),
            pltpu.VMEM(links.shape, jnp.float32),
        ]
        + [pltpu.VMEM(color_block, jnp.float32)] * 4
        + [pltpu.VMEM(color_block, jnp.bfloat16)] * 2
        + [pltpu.VMEM((NMOM * 2 * nvec, NCOL * width), jnp.bfloat16)]
        + [pltpu.VMEM((2 * nvec, NCOL * width), jnp.bfloat16)] * 3
        + [
            pltpu.VMEM((2, 2, width, width), jnp.bfloat16),
            pltpu.SemaphoreType.DMA,
            pltpu.SemaphoreType.DMA((2, slices)),
        ],
        compiler_params=pltpu.CompilerParams(vmem_limit_bytes=PLANE_LIMIT),
        cost_estimate=pl.CostEstimate(
            flops=slices * 16 * NMOM * nvec * nvec * NCOL * width,
            bytes_accessed=6 * vectors.size + 4 * links.size,
            transcendentals=0,
        ),
        name="plane_items",
    )(position, in_hbm(momenta), in_hbm(vectors), in_hbm(links))


def layer_kernel(
    core, scale, rows_ref, item_ref, own_ref, ahead_ref, phase_ref, turn_ref, out_ref, lhs_ref, listed_ref
):
    nvec, width = own_ref.shape[3:]
    total = out_ref.shape[0]
    sites = rows_ref.shape[0] // 2

    def parts_of(place):
        item = rows_ref[2 * lax.rem(place, sites) + core, lax.div(place, sites), 0]
        rest = lax.rem(item, NMOM * NDISP)
        return lax.div(item, NMOM * NDISP), lax.div(rest, NDISP), lax.rem(rest, NDISP)

    def bond(place, lhs):
        slice_index, moment, _ = parts_of(place)
        cosine = phase_ref[moment, 0]
        sine = phase_ref[moment, 1]
        for color in range(NCOL):
            span = pl.ds(color * width, width)
            for part in range(2):
                value = own_ref[slice_index, part, color]
                lhs[pl.ds(part * nvec, nvec), span] = (cosine * value).astype(jnp.bfloat16)
                lhs[pl.ds((2 + part) * nvec, nvec), span] = (sine * value).astype(jnp.bfloat16)
        rhs = jnp.concatenate(
            [
                jnp.concatenate([ahead_ref[slice_index, part, color] for color in range(NCOL)], 1)
                for part in range(2)
            ],
            0,
        )
        gram = lax.dot_general(lhs[...], rhs, (((1,), (1,)), ((), ())), preferred_element_type=jnp.float32)
        block = [
            [gram[i * nvec : (i + 1) * nvec, j * nvec : (j + 1) * nvec] for j in range(2)] for i in range(4)
        ]
        cos_real = block[0][0] + block[1][1]
        cos_imag = block[0][1] - block[1][0]
        sin_real = block[2][0] + block[3][1]
        sin_imag = block[2][1] - block[3][0]
        half = 0.5 * scale
        turn_cos = half * turn_ref[moment, 0]
        turn_sin = half * turn_ref[moment, 1]
        back_real = cos_real - sin_imag
        back_imag = cos_imag + sin_real
        real = half * (cos_real + sin_imag) - (turn_cos * back_real - turn_sin * back_imag).T
        imag = half * (cos_imag - sin_real) + (turn_cos * back_imag + turn_sin * back_real).T
        return real, imag

    found = jnp.int32(0)
    for place in range(total):
        slice_index, moment, disp = parts_of(jnp.int32(place))
        out_ref[place] = item_ref[slice_index, moment, jnp.minimum(disp, NDISP - 2)]
        listed_ref[found] = place
        found = found + (disp == NDISP - 1).astype(jnp.int32)

    @pl.loop(0, lax.div(found + 1, 2))
    def _(pair):
        both = [listed_ref[2 * pair], listed_ref[jnp.minimum(2 * pair + 1, found - 1)]]
        results = [bond(place, lhs_ref.at[index]) for index, place in enumerate(both)]
        for place, (real, imag) in zip(both, results):
            store_rounded(out_ref, (place,), real, imag)


def layer_items(core, rows, item, own, ahead, phase, turn, scale):
    slices, _, _, nvec, width = own.shape
    devices, slots, _ = rows.shape
    total = slots * devices // 2
    whole = pl.BlockSpec(memory_space=pltpu.VMEM)
    return pl.pallas_call(
        functools.partial(layer_kernel, core, scale),
        in_specs=[pl.BlockSpec(memory_space=pltpu.SMEM)] + [whole] * 5,
        out_specs=whole,
        out_shape=jax.ShapeDtypeStruct((total, 2 * nvec + ROWS, nvec), jnp.bfloat16),
        scratch_shapes=[
            pltpu.VMEM((2, 4 * nvec, NCOL * width), jnp.bfloat16),
            pltpu.SMEM((total,), jnp.int32),
        ],
        compiler_params=pltpu.CompilerParams(vmem_limit_bytes=8 * MIB),
        cost_estimate=pl.CostEstimate(
            flops=total * 4 * nvec * nvec * NCOL * width,
            bytes_accessed=2 * own.size,
            transcendentals=0,
        ),
        name="layer_items",
    )(rows, item, own, ahead, phase, turn)


def add_kernel(places, *refs):
    for out_ref, entries in zip(refs[len(refs) - len(places) :], places):
        for index, entry in enumerate(entries):
            total = sum(refs[number][at].astype(jnp.float32) for number, at in entry)
            nvec = total.shape[1]
            if out_ref.dtype == jnp.float32:
                out_ref[index] = total
            else:
                left = total[2 * nvec :]
                store_rounded(out_ref, (index,), total[:nvec], total[nvec : 2 * nvec], left)


def added(groups):
    arrays = []

    def number(array):
        found = [place for place, other in enumerate(arrays) if other is array]
        if not found:
            arrays.append(array)
        return found[0] if found else len(arrays) - 1

    places = [[[(number(array), at) for array, at in entry] for entry in entries] for entries, _ in groups]
    tail = arrays[0].shape[1:]
    whole = pl.BlockSpec(memory_space=pltpu.VMEM)
    size = sum(len(entry) for entries in places for entry in entries) * math.prod(tail)
    return pl.pallas_call(
        functools.partial(add_kernel, places),
        in_specs=[whole] * len(arrays),
        out_specs=[whole] * len(groups),
        out_shape=[jax.ShapeDtypeStruct((len(entries),) + tail, dtype) for entries, dtype in groups],
        compiler_params=pltpu.CompilerParams(vmem_limit_bytes=8 * MIB),
        cost_estimate=pl.CostEstimate(flops=size, bytes_accessed=4 * size, transcendentals=0),
        name="added",
    )(*arrays)


class Chain:
    def __init__(self, entries, order):
        self.entries = entries
        self.order = order

    def chunks(self, step):
        far = [r for r in self.entries if r >> (self.order[step] - 1) & 1]
        if step + 1 == len(self.order):
            return [far]
        split = [[], []]
        for r in far:
            split[r >> (self.order[step + 1] - 1) & 1].append(r)
        return [split[1], split[0]]

    def send(self, step, far):
        bit = self.order[step]
        near = [r ^ (1 << (bit - 1)) for r in far]
        groups = [([self.entries[r] for r in far], jnp.bfloat16)]
        last = step + 1 == len(self.order)
        if step == 0 or last:
            kept = [self.entries[r] if step == 0 else self.entries[r][:2] for r in near]
            groups.append((kept, jnp.float32))
        outs = added(groups)
        arrived = exchanged(outs[0], 1 << bit)
        for at, r in enumerate(near):
            if step == 0:
                self.entries[r] = [(outs[1], at)]
            elif last:
                self.entries[r][:2] = [(outs[1], at)]
            self.entries[r].append((arrived, at))
        for r in far:
            del self.entries[r]


def mix_kernel(slot_ref, structure_ref, weight_ref, tau_ref, out_ref):
    spins, _, nvec, width = tau_ref.shape[1:]
    base = structure_ref[pl.program_id(0)] * spins * spins
    weight = [[weight_ref[base + r * spins + s] for s in range(spins)] for r in range(spins)]

    @pl.loop(0, 2 * nvec // ROWS)
    def _(index):
        part = index // (nvec // ROWS)
        rows = pl.ds(pl.multiple_of(index % (nvec // ROWS) * ROWS, ROWS), ROWS)
        tau = [tau_ref[0, s, part, rows, :].astype(jnp.float32) for s in range(spins)]
        for r in range(spins):
            mixed = weight[r][0] * tau[0]
            for s in range(1, spins):
                mixed = mixed + weight[r][s] * tau[s]
            out_ref[0, r, part, rows, :] = mixed.astype(jnp.bfloat16)


def mixed_perambulators(slots, structures, weights, perambulators):
    block = (1,) + perambulators.shape[1:]
    count = slots.shape[0]
    return pl.pallas_call(
        mix_kernel,
        grid_spec=pltpu.PrefetchScalarGridSpec(
            num_scalar_prefetch=3,
            grid=(count,),
            in_specs=[pl.BlockSpec(block, lambda j, slot, *_: (slot[j], 0, 0, 0, 0))],
            out_specs=pl.BlockSpec(block, lambda j, *_: (j, 0, 0, 0, 0)),
        ),
        out_shape=jax.ShapeDtypeStruct((count,) + perambulators.shape[1:], jnp.bfloat16),
        compiler_params=pltpu.CompilerParams(vmem_limit_bytes=8 * MIB),
        cost_estimate=pl.CostEstimate(
            flops=8 * perambulators.size, bytes_accessed=4 * perambulators.size, transcendentals=0
        ),
        name="mixed_perambulators",
    )(slots, structures, weights, in_hbm(perambulators))


def diagram_kernel(places, *refs):
    tau_ref, out_ref, block_ref, sems = refs[-4:]
    count, spins, _, nvec, width = tau_ref.shape

    def copy(index, r):
        return pltpu.make_async_copy(block_ref.at[index, r], out_ref.at[index, r], sems.at[index, r])

    for index, entry in enumerate(places):
        real, imag = restored(sum(refs[number][at].astype(jnp.float32) for number, at in entry))
        square = jnp.concatenate(
            [jnp.concatenate([real, -imag], 1), jnp.concatenate([imag, real], 1)], 0
        ).astype(jnp.bfloat16)
        for r in range(spins):
            tau = tau_ref[index, r].reshape(2 * nvec, width)
            block = jnp.dot(square, tau, preferred_element_type=jnp.float32)
            block_ref[index, r] = block.astype(jnp.bfloat16).reshape(2, nvec, width)
            copy(index, r).start()
    for index in range(count):
        for r in range(spins):
            copy(index, r).wait()


def diagrams(entries, tau):
    count, spins, _, nvec, width = tau.shape
    whole = pl.BlockSpec(memory_space=pltpu.VMEM)
    arrays = [array for entry in entries for array, _ in entry]
    places = []
    for entry in entries:
        start = sum(len(one) for one in places)
        places.append([(start + number, at) for number, (_, at) in enumerate(entry)])
    return pl.pallas_call(
        functools.partial(diagram_kernel, places),
        in_specs=[whole] * (len(arrays) + 1),
        out_specs=pl.BlockSpec(memory_space=pltpu.HBM),
        out_shape=jax.ShapeDtypeStruct(tau.shape, jnp.bfloat16),
        scratch_shapes=[
            pltpu.VMEM(tau.shape, jnp.bfloat16),
            pltpu.SemaphoreType.DMA((count, spins)),
        ],
        compiler_params=pltpu.CompilerParams(vmem_limit_bytes=8 * MIB),
        cost_estimate=pl.CostEstimate(
            flops=8 * nvec * nvec * width * spins * count, bytes_accessed=4 * tau.size, transcendentals=0
        ),
        name="diagrams",
    )(*arrays, tau)


def body(eigvecs, gauge_links, momenta, spin_mix, perambulators, contraction_list):
    slices, _, _, nvec, depth, plane = eigvecs.shape
    devices = lax.axis_size(SITES)
    position = lax.axis_index(SITES)
    bits = devices.bit_length() - 1
    total_z = depth * devices
    width = depth * plane
    scale = 1.0 / math.sqrt(NCOL * plane * total_z)
    place = position.reshape(1)
    rows, after, place = gathered(contraction_list, eigvecs, place)
    upper = shifted(after[:, :, :, :, :1, :], SITES, -1)
    vectors = eigvecs.reshape(slices, 2, NCOL, nvec, width)
    links = gauge_links.reshape(slices, 3, 2, NCOL, NCOL, 1, width)
    item, own, phase, turn = plane_items(place, momenta, vectors, links, total_z, plane, scale)
    chosen = contraction_list[:, 2] - position * perambulators.shape[0]
    tau = mixed_perambulators(chosen, contraction_list[:, 1], spin_mix.reshape(-1), perambulators)
    ahead = jnp.concatenate([eigvecs[:, :, :, :, 1:, :], upper], 4).reshape(vectors.shape)
    send = layer_items(1, rows, item, own, ahead, phase, turn, scale)
    keep = layer_items(0, rows, item, own, ahead, phase, turn, scale)
    slots = range(contraction_list.shape[0])
    other = exchanged(send, 1)
    sites = devices // 2
    chains = [
        Chain(
            {r: [(keep, slot * sites + r), (other, slot * sites + r)] for r in range(sites)},
            [2, 1, *range(3, bits)] if slot % 2 else [1, bits - 1, *range(2, bits - 1)],
        )
        for slot in slots
    ]
    for step in range(bits - 1):
        messages = [chain.chunks(step) for chain in chains]
        for part in range(len(messages[0])):
            for chain, far in zip(chains, messages):
                chain.send(step, far[part])
    return diagrams([chain.entries[0] for chain in chains], tau)


def solution(mesh):
    placed = (
        P("cfg", None, None, None, ("space", "diag"), None),
        P("cfg", None, None, None, None, ("space", "diag"), None),
        P(),
        P(),
        P(("cfg", "space", "diag"), None, None, None, None),
        P(("space", "diag"), None),
    )
    return jax.shard_map(
        body,
        mesh=mesh,
        in_specs=placed,
        out_specs=P(("cfg", "space", "diag"), None, None, None, None),
        check_vma=False,
    )
```

```python
import functools
import math

import jax
import jax.numpy as jnp
from jax import lax
from jax.experimental import pallas as pl
from jax.experimental.pallas import tpu as pltpu
from jax.sharding import PartitionSpec as P

NCOL = 3
NMOM = 4
NDISP = 4
LX = 16
LY = 16
LANES = 128
ROWS = 16
SITES = ("space", "diag")
MIB = 1024 * 1024
PLANE_LIMIT = 20 * MIB


def shifted(value, axis, by):
    size = lax.axis_size(axis)
    return lax.ppermute(value, axis, [(i, (i + by) % size) for i in range(size)])


def in_hbm(value):
    return pltpu.with_memory_space_constraint(value, pltpu.HBM)


def exchanged(value, mask):
    size = lax.axis_size(SITES)
    return lax.ppermute(value, SITES, [(i, i ^ mask) for i in range(size)])


def gathered(rows, early, late):
    bits = lax.axis_size(SITES).bit_length() - 1
    value = rows[None]
    for low in range(0, bits, 2):
        if low == 2:
            value, late = lax.optimization_barrier((value, late))
        arrived = [exchanged(value, step << low) for step in reversed(range(1, 1 << min(2, bits - low)))]
        if low == 0:
            arrived, early = lax.optimization_barrier((arrived, early))
        value = jnp.concatenate([value] + arrived[::-1])
    return value, early, late


def diagonal(value):
    size = value.shape[0]
    same = lax.broadcasted_iota(jnp.int32, value.shape, 0) == lax.broadcasted_iota(jnp.int32, value.shape, 1)
    return jnp.sum(jnp.where(same, value, 0.0), 0, keepdims=True).reshape(1, size)


def rounded(real, imag, left=None):
    planes = [value.astype(jnp.bfloat16) for value in (real, imag)]
    lost = [diagonal(value - plane.astype(jnp.float32)) for value, plane in zip((real, imag), planes)]
    tile = jnp.concatenate(lost + [jnp.zeros((ROWS - 2, real.shape[1]), jnp.float32)], 0)
    if left is not None:
        tile = tile + left
    return planes, tile.astype(jnp.bfloat16)


def store_rounded(ref, index, real, imag, left=None):
    nvec = real.shape[0]
    planes, tile = rounded(real, imag, left)
    ref[(*index, pl.ds(0, nvec))] = planes[0]
    ref[(*index, pl.ds(nvec, nvec))] = planes[1]
    ref[(*index, pl.ds(2 * nvec, ROWS))] = tile


def restored(total):
    nvec = total.shape[1]
    shape = (nvec, nvec)
    same = lax.broadcasted_iota(jnp.int32, shape, 0) == lax.broadcasted_iota(jnp.int32, shape, 1)
    return [
        total[part * nvec : (part + 1) * nvec] + jnp.where(same, total[2 * nvec + part : 2 * nvec + part + 1], 0.0)
        for part in range(2)
    ]


def color_product(matrix, real, imag, adjoint):
    rows = []
    for row in range(NCOL):
        real_part = imag_part = None
        for col in range(NCOL):
            if adjoint:
                mreal, mimag = matrix[0][col][row], matrix[1][col][row]
                one = mreal * real[col] + mimag * imag[col]
                two = mreal * imag[col] - mimag * real[col]
            else:
                mreal, mimag = matrix[0][row][col], matrix[1][row][col]
                one = mreal * real[col] - mimag * imag[col]
                two = mreal * imag[col] + mimag * real[col]
            real_part = one if real_part is None else real_part + one
            imag_part = two if imag_part is None else imag_part + two
        rows.append((real_part, imag_part))
    return rows


def color_loop(link, nvec, width, load, store, adjoint):
    height = math.gcd(nvec, 2 * ROWS)
    for lane in range(0, width, LANES):
        lanes = pl.ds(lane, LANES)
        matrix = [
            [[link(part, row, col, lanes) for col in range(NCOL)] for row in range(NCOL)] for part in range(2)
        ]
        for start in range(0, nvec, height):
            rows = pl.ds(start, height)
            real = [load(0, color, rows, lanes) for color in range(NCOL)]
            imag = [load(1, color, rows, lanes) for color in range(NCOL)]
            for color, (one, two) in enumerate(color_product(matrix, real, imag, adjoint)):
                store(0, color, rows, lanes, one)
                store(1, color, rows, lanes, two)


def fill_tables(position, total_z, plane, momenta_ref, phase_ref, turn_ref):
    width = phase_ref.shape[-1]
    flat = lax.broadcasted_iota(jnp.int32, (1, width), 1)
    xcoord = (flat % LX).astype(jnp.float32)
    ycoord = (flat % plane // LX).astype(jnp.float32)
    zcoord = (position * (width // plane) + flat // plane).astype(jnp.float32)
    for moment in range(NMOM):
        along_x = momenta_ref[moment, 0].astype(jnp.float32)
        along_y = momenta_ref[moment, 1].astype(jnp.float32)
        along_z = momenta_ref[moment, 2].astype(jnp.float32)
        angle = (
            2.0 * math.pi * (along_x * xcoord / LX + along_y * ycoord / LY + along_z * zcoord / total_z)
        )
        phase_ref[moment, 0] = jnp.cos(angle)
        phase_ref[moment, 1] = jnp.sin(angle)
        turn = jnp.full((1, turn_ref.shape[-1]), 2.0 * math.pi / total_z, jnp.float32) * along_z
        turn_ref[moment, 0] = jnp.cos(turn)
        turn_ref[moment, 1] = jnp.sin(turn)


def fill_moves(move_ref):
    width = move_ref.shape[-1]
    source = lax.broadcasted_iota(jnp.int32, (width, width), 0)
    site = lax.broadcasted_iota(jnp.int32, (width, width), 1)
    xcoord = site % LX
    ycoord = site // LX % LY
    for sign, by in enumerate((1, -1)):
        along_x = site - xcoord + (xcoord + LX + by) % LX
        along_y = site + ((ycoord + LY + by) % LY - ycoord) * LX
        move_ref[0, sign] = (source == along_x).astype(jnp.float32).astype(jnp.bfloat16)
        move_ref[1, sign] = (source == along_y).astype(jnp.float32).astype(jnp.bfloat16)


def plane_kernel(
    total_z, plane, scale,
    position_ref, momenta_in, vector_in, link_in,
    item_ref, own_ref, phase_ref, turn_ref,
    momenta_ref, vector_ref, link_ref,
    ahead_x_ref, ahead_y_ref, behind_x_ref, behind_y_ref, adjoint_x_ref, adjoint_y_ref,
    phased_ref, still_ref, moved_x_ref, moved_y_ref, move_ref, momenta_sem, sems,
):
    now = pl.program_id(0)
    slices, _, _, nvec, width = vector_ref.shape

    def copies(index):
        return (
            pltpu.make_async_copy(vector_in.at[index], vector_ref.at[index], sems.at[0, index]),
            pltpu.make_async_copy(link_in.at[index], link_ref.at[index], sems.at[1, index]),
        )

    @pl.when(now == 0)
    def _():
        moments = pltpu.make_async_copy(momenta_in, momenta_ref, momenta_sem)
        moments.start()
        for index in range(slices):
            for copy in copies(index):
                copy.start()
        fill_moves(move_ref)
        moments.wait()
        fill_tables(position_ref[0], total_z, plane, momenta_ref, phase_ref, turn_ref)

    for copy in copies(now):
        copy.wait()

    def linker(direction):
        return lambda part, row, col, lanes: link_ref[now, direction, part, row, col, :, lanes]

    def vector(part, color, rows, lanes):
        return vector_ref[now, part, color, rows, lanes].astype(jnp.float32)

    def gram(moved_ref, disp):
        product = lax.dot_general(
            phased_ref[...], moved_ref[...], (((1,), (1,)), ((), ())), preferred_element_type=jnp.float32
        )
        for moment in range(NMOM):
            start = 2 * moment * nvec
            upper = product[start : start + nvec]
            lower = product[start + nvec : start + 2 * nvec]
            factor = scale if disp == 0 else 0.5 * scale
            real = factor * (upper[:, :nvec] + lower[:, nvec:])
            imag = factor * (upper[:, nvec:] - lower[:, :nvec])
            store_rounded(item_ref, (0, moment, disp), real, imag)

    flat = vector_ref[now].reshape(2 * NCOL * nvec, width)
    for direction, ahead_ref in enumerate((ahead_x_ref, ahead_y_ref)):
        ahead_ref[...] = jnp.dot(
            flat, move_ref[direction, 0], preferred_element_type=jnp.float32
        ).reshape(ahead_ref.shape)

    for color in range(NCOL):
        span = pl.ds(color * width, width)
        for part in range(2):
            still_ref[pl.ds(part * nvec, nvec), span] = vector_ref[now, part, color]
        for start in range(0, nvec, ROWS):
            real = vector_ref[now, 0, color, pl.ds(start, ROWS), :].astype(jnp.float32)
            imag = vector_ref[now, 1, color, pl.ds(start, ROWS), :].astype(jnp.float32)
            for moment in range(NMOM):
                cosine = phase_ref[moment, 0]
                sine = phase_ref[moment, 1]
                first = 2 * moment * nvec + start
                phased_ref[pl.ds(first, ROWS), span] = (cosine * real - sine * imag).astype(jnp.bfloat16)
                phased_ref[pl.ds(first + nvec, ROWS), span] = (sine * real + cosine * imag).astype(jnp.bfloat16)
    gram(still_ref, 0)

    for direction, (adjoint_ref, behind_ref) in enumerate(
        ((adjoint_x_ref, behind_x_ref), (adjoint_y_ref, behind_y_ref))
    ):

        def adjoint(part, color, rows, lanes, value):
            adjoint_ref[part, color, rows, lanes] = value.astype(jnp.bfloat16)

        color_loop(linker(direction), nvec, width, vector, adjoint, True)
        behind_ref[...] = jnp.dot(
            adjoint_ref[...].reshape(2 * NCOL * nvec, width),
            move_ref[direction, 1],
            preferred_element_type=jnp.float32,
        ).reshape(behind_ref.shape)

    for direction, (ahead_ref, behind_ref, moved_ref) in enumerate(
        ((ahead_x_ref, behind_x_ref, moved_x_ref), (ahead_y_ref, behind_y_ref, moved_y_ref))
    ):

        def ahead(part, color, rows, lanes):
            return ahead_ref[part, color, rows, lanes]

        def forward(part, color, rows, lanes, value):
            moved_ref[
                pl.ds(part * nvec + rows.start, rows.size), pl.ds(color * width + lanes.start, lanes.size)
            ] = (value - behind_ref[part, color, rows, lanes]).astype(jnp.bfloat16)

        color_loop(linker(direction), nvec, width, ahead, forward, False)
        gram(moved_ref, direction + 1)

    def own(part, color, rows, lanes, value):
        own_ref[0, part, color, rows, lanes] = value

    color_loop(linker(2), nvec, width, vector, own, True)


def plane_items(position, momenta, vectors, links, total_z, plane, scale):
    slices, _, _, nvec, width = vectors.shape
    color_block = (2, NCOL, nvec, width)
    return pl.pallas_call(
        functools.partial(plane_kernel, total_z, plane, scale),
        grid=(slices,),
        in_specs=[pl.BlockSpec(memory_space=pltpu.SMEM)] + [pl.BlockSpec(memory_space=pltpu.HBM)] * 3,
        out_specs=[
            pl.BlockSpec((1, NMOM, NDISP - 1, 2 * nvec + ROWS, nvec), lambda t: (t, 0, 0, 0, 0)),
            pl.BlockSpec((1,) + color_block, lambda t: (t, 0, 0, 0, 0)),
            pl.BlockSpec((NMOM, 2, 1, width), lambda t: (0, 0, 0, 0)),
            pl.BlockSpec((NMOM, 2, 1, nvec), lambda t: (0, 0, 0, 0)),
        ],
        out_shape=[
            jax.ShapeDtypeStruct((slices, NMOM, NDISP - 1, 2 * nvec + ROWS, nvec), jnp.bfloat16),
            jax.ShapeDtypeStruct(vectors.shape, jnp.float32),
            jax.ShapeDtypeStruct((NMOM, 2, 1, width), jnp.float32),
            jax.ShapeDtypeStruct((NMOM, 2, 1, nvec), jnp.float32),
        ],
        scratch_shapes=[
            pltpu.SMEM(momenta.shape, jnp.int32),
            pltpu.VMEM(vectors.shape, jnp.bfloat16),
            pltpu.VMEM(links.shape, jnp.float32),
        ]
        + [pltpu.VMEM(color_block, jnp.float32)] * 4
        + [pltpu.VMEM(color_block, jnp.bfloat16)] * 2
        + [pltpu.VMEM((NMOM * 2 * nvec, NCOL * width), jnp.bfloat16)]
        + [pltpu.VMEM((2 * nvec, NCOL * width), jnp.bfloat16)] * 3
        + [
            pltpu.VMEM((2, 2, width, width), jnp.bfloat16),
            pltpu.SemaphoreType.DMA,
            pltpu.SemaphoreType.DMA((2, slices)),
        ],
        compiler_params=pltpu.CompilerParams(vmem_limit_bytes=PLANE_LIMIT),
        cost_estimate=pl.CostEstimate(
            flops=slices * 16 * NMOM * nvec * nvec * NCOL * width,
            bytes_accessed=6 * vectors.size + 4 * links.size,
            transcendentals=0,
        ),
        name="plane_items",
    )(position, in_hbm(momenta), in_hbm(vectors), in_hbm(links))


def layer_kernel(
    core, scale, rows_ref, item_ref, own_ref, ahead_ref, phase_ref, turn_ref, out_ref, lhs_ref, listed_ref
):
    nvec, width = own_ref.shape[3:]
    total = out_ref.shape[0]
    sites = rows_ref.shape[0] // 2

    def parts_of(place):
        item = rows_ref[2 * lax.rem(place, sites) + core, lax.div(place, sites), 0]
        rest = lax.rem(item, NMOM * NDISP)
        return lax.div(item, NMOM * NDISP), lax.div(rest, NDISP), lax.rem(rest, NDISP)

    def bond(place, lhs):
        slice_index, moment, _ = parts_of(place)
        cosine = phase_ref[moment, 0]
        sine = phase_ref[moment, 1]
        for color in range(NCOL):
            span = pl.ds(color * width, width)
            for part in range(2):
                value = own_ref[slice_index, part, color]
                lhs[pl.ds(part * nvec, nvec), span] = (cosine * value).astype(jnp.bfloat16)
                lhs[pl.ds((2 + part) * nvec, nvec), span] = (sine * value).astype(jnp.bfloat16)
        rhs = jnp.concatenate(
            [
                jnp.concatenate([ahead_ref[slice_index, part, color] for color in range(NCOL)], 1)
                for part in range(2)
            ],
            0,
        )
        gram = lax.dot_general(lhs[...], rhs, (((1,), (1,)), ((), ())), preferred_element_type=jnp.float32)
        block = [
            [gram[i * nvec : (i + 1) * nvec, j * nvec : (j + 1) * nvec] for j in range(2)] for i in range(4)
        ]
        cos_real = block[0][0] + block[1][1]
        cos_imag = block[0][1] - block[1][0]
        sin_real = block[2][0] + block[3][1]
        sin_imag = block[2][1] - block[3][0]
        half = 0.5 * scale
        turn_cos = half * turn_ref[moment, 0]
        turn_sin = half * turn_ref[moment, 1]
        back_real = cos_real - sin_imag
        back_imag = cos_imag + sin_real
        real = half * (cos_real + sin_imag) - (turn_cos * back_real - turn_sin * back_imag).T
        imag = half * (cos_imag - sin_real) + (turn_cos * back_imag + turn_sin * back_real).T
        return real, imag

    found = jnp.int32(0)
    for place in range(total):
        slice_index, moment, disp = parts_of(jnp.int32(place))
        out_ref[place] = item_ref[slice_index, moment, jnp.minimum(disp, NDISP - 2)]
        listed_ref[found] = place
        found = found + (disp == NDISP - 1).astype(jnp.int32)

    @pl.loop(0, lax.div(found + 1, 2))
    def _(pair):
        both = [listed_ref[2 * pair], listed_ref[jnp.minimum(2 * pair + 1, found - 1)]]
        results = [bond(place, lhs_ref.at[index]) for index, place in enumerate(both)]
        for place, (real, imag) in zip(both, results):
            store_rounded(out_ref, (place,), real, imag)


def layer_items(core, rows, item, own, ahead, phase, turn, scale):
    slices, _, _, nvec, width = own.shape
    devices, slots, _ = rows.shape
    total = slots * devices // 2
    whole = pl.BlockSpec(memory_space=pltpu.VMEM)
    return pl.pallas_call(
        functools.partial(layer_kernel, core, scale),
        in_specs=[pl.BlockSpec(memory_space=pltpu.SMEM)] + [whole] * 5,
        out_specs=whole,
        out_shape=jax.ShapeDtypeStruct((total, 2 * nvec + ROWS, nvec), jnp.bfloat16),
        scratch_shapes=[
            pltpu.VMEM((2, 4 * nvec, NCOL * width), jnp.bfloat16),
            pltpu.SMEM((total,), jnp.int32),
        ],
        compiler_params=pltpu.CompilerParams(vmem_limit_bytes=8 * MIB),
        cost_estimate=pl.CostEstimate(
            flops=total * 4 * nvec * nvec * NCOL * width,
            bytes_accessed=2 * own.size,
            transcendentals=0,
        ),
        name="layer_items",
    )(rows, item, own, ahead, phase, turn)


def add_kernel(places, *refs):
    for out_ref, entries in zip(refs[len(refs) - len(places) :], places):
        for index, entry in enumerate(entries):
            total = sum(refs[number][at].astype(jnp.float32) for number, at in entry)
            nvec = total.shape[1]
            if out_ref.dtype == jnp.float32:
                out_ref[index] = total
            else:
                left = total[2 * nvec :]
                store_rounded(out_ref, (index,), total[:nvec], total[nvec : 2 * nvec], left)


def added(groups):
    arrays = []

    def number(array):
        found = [place for place, other in enumerate(arrays) if other is array]
        if not found:
            arrays.append(array)
        return found[0] if found else len(arrays) - 1

    places = [[[(number(array), at) for array, at in entry] for entry in entries] for entries, _ in groups]
    tail = arrays[0].shape[1:]
    whole = pl.BlockSpec(memory_space=pltpu.VMEM)
    size = sum(len(entry) for entries in places for entry in entries) * math.prod(tail)
    return pl.pallas_call(
        functools.partial(add_kernel, places),
        in_specs=[whole] * len(arrays),
        out_specs=[whole] * len(groups),
        out_shape=[jax.ShapeDtypeStruct((len(entries),) + tail, dtype) for entries, dtype in groups],
        compiler_params=pltpu.CompilerParams(vmem_limit_bytes=8 * MIB),
        cost_estimate=pl.CostEstimate(flops=size, bytes_accessed=4 * size, transcendentals=0),
        name="added",
    )(*arrays)


class Chain:
    def __init__(self, entries, order):
        self.entries = entries
        self.order = order

    def chunks(self, step):
        far = [r for r in self.entries if r >> (self.order[step] - 1) & 1]
        if step + 1 == len(self.order):
            return [far]
        split = [[], []]
        for r in far:
            split[r >> (self.order[step + 1] - 1) & 1].append(r)
        return [split[1], split[0]]

    def send(self, step, far):
        bit = self.order[step]
        near = [r ^ (1 << (bit - 1)) for r in far]
        groups = [([self.entries[r] for r in far], jnp.bfloat16)]
        last = step + 1 == len(self.order)
        if step == 0 or last:
            kept = [self.entries[r] if step == 0 else self.entries[r][:2] for r in near]
            groups.append((kept, jnp.float32))
        outs = added(groups)
        arrived = exchanged(outs[0], 1 << bit)
        for at, r in enumerate(near):
            if step == 0:
                self.entries[r] = [(outs[1], at)]
            elif last:
                self.entries[r][:2] = [(outs[1], at)]
            self.entries[r].append((arrived, at))
        for r in far:
            del self.entries[r]


def mix_kernel(slot_ref, structure_ref, weight_ref, tau_in, out_ref, tau_ref, sems):
    count, spins, parts, nvec, width = out_ref.shape

    def copy(index, part):
        return pltpu.make_async_copy(
            tau_in.at[slot_ref[index], :, part], tau_ref.at[index, :, part], sems.at[index, part]
        )

    for index in range(count):
        for part in range(parts):
            copy(index, part).start()
    for index in range(count):
        base = structure_ref[index] * spins * spins
        weight = [[weight_ref[base + r * spins + s] for s in range(spins)] for r in range(spins)]
        for part in range(parts):
            copy(index, part).wait()

            @pl.loop(0, nvec // ROWS)
            def _(step):
                rows = pl.ds(pl.multiple_of(step * ROWS, ROWS), ROWS)
                tau = [tau_ref[index, s, part, rows, :].astype(jnp.float32) for s in range(spins)]
                for r in range(spins):
                    mixed = weight[r][0] * tau[0]
                    for s in range(1, spins):
                        mixed = mixed + weight[r][s] * tau[s]
                    out_ref[index, r, part, rows, :] = mixed.astype(jnp.bfloat16)


def mixed_perambulators(slots, structures, weights, perambulators):
    shape = (slots.shape[0],) + perambulators.shape[1:]
    scalar = pl.BlockSpec(memory_space=pltpu.SMEM)
    return pl.pallas_call(
        mix_kernel,
        in_specs=[scalar] * 3 + [pl.BlockSpec(memory_space=pltpu.HBM)],
        out_specs=pl.BlockSpec(memory_space=pltpu.VMEM),
        out_shape=jax.ShapeDtypeStruct(shape, jnp.bfloat16),
        scratch_shapes=[
            pltpu.VMEM(shape, jnp.bfloat16),
            pltpu.SemaphoreType.DMA(shape[::2][:2]),
        ],
        compiler_params=pltpu.CompilerParams(vmem_limit_bytes=8 * MIB),
        cost_estimate=pl.CostEstimate(
            flops=8 * math.prod(shape), bytes_accessed=4 * math.prod(shape), transcendentals=0
        ),
        name="mixed_perambulators",
    )(slots, structures, weights, in_hbm(perambulators))


def diagram_kernel(places, *refs):
    tau_ref, out_ref, block_ref, sems = refs[-4:]
    count, spins, _, nvec, width = tau_ref.shape

    def copy(index, r):
        return pltpu.make_async_copy(block_ref.at[index, r], out_ref.at[index, r], sems.at[index, r])

    for index, entry in enumerate(places):
        real, imag = restored(sum(refs[number][at].astype(jnp.float32) for number, at in entry))
        square = jnp.concatenate(
            [jnp.concatenate([real, -imag], 1), jnp.concatenate([imag, real], 1)], 0
        ).astype(jnp.bfloat16)
        for r in range(spins):
            tau = tau_ref[index, r].reshape(2 * nvec, width)
            block = jnp.dot(square, tau, preferred_element_type=jnp.float32)
            block_ref[index, r] = block.astype(jnp.bfloat16).reshape(2, nvec, width)
            copy(index, r).start()
    for index in range(count):
        for r in range(spins):
            copy(index, r).wait()


def diagrams(entries, tau):
    count, spins, _, nvec, width = tau.shape
    whole = pl.BlockSpec(memory_space=pltpu.VMEM)
    arrays = [array for entry in entries for array, _ in entry]
    places = []
    for entry in entries:
        start = sum(len(one) for one in places)
        places.append([(start + number, at) for number, (_, at) in enumerate(entry)])
    return pl.pallas_call(
        functools.partial(diagram_kernel, places),
        in_specs=[whole] * (len(arrays) + 1),
        out_specs=pl.BlockSpec(memory_space=pltpu.HBM),
        out_shape=jax.ShapeDtypeStruct(tau.shape, jnp.bfloat16),
        scratch_shapes=[
            pltpu.VMEM(tau.shape, jnp.bfloat16),
            pltpu.SemaphoreType.DMA((count, spins)),
        ],
        compiler_params=pltpu.CompilerParams(vmem_limit_bytes=8 * MIB),
        cost_estimate=pl.CostEstimate(
            flops=8 * nvec * nvec * width * spins * count, bytes_accessed=4 * tau.size, transcendentals=0
        ),
        name="diagrams",
    )(*arrays, tau)


def body(eigvecs, gauge_links, momenta, spin_mix, perambulators, contraction_list):
    slices, _, _, nvec, depth, plane = eigvecs.shape
    devices = lax.axis_size(SITES)
    position = lax.axis_index(SITES)
    bits = devices.bit_length() - 1
    total_z = depth * devices
    width = depth * plane
    scale = 1.0 / math.sqrt(NCOL * plane * total_z)
    place = position.reshape(1)
    rows, after, place = gathered(contraction_list, eigvecs, place)
    upper = shifted(after[:, :, :, :, :1, :], SITES, -1)
    vectors = eigvecs.reshape(slices, 2, NCOL, nvec, width)
    links = gauge_links.reshape(slices, 3, 2, NCOL, NCOL, 1, width)
    item, own, phase, turn = plane_items(place, momenta, vectors, links, total_z, plane, scale)
    chosen = contraction_list[:, 2] - position * perambulators.shape[0]
    tau = mixed_perambulators(chosen, contraction_list[:, 1], spin_mix.reshape(-1), perambulators)
    ahead = jnp.concatenate([eigvecs[:, :, :, :, 1:, :], upper], 4).reshape(vectors.shape)
    send = layer_items(1, rows, item, own, ahead, phase, turn, scale)
    keep = layer_items(0, rows, item, own, ahead, phase, turn, scale)
    slots = range(contraction_list.shape[0])
    other = exchanged(send, 1)
    sites = devices // 2
    chains = [
        Chain(
            {r: [(keep, slot * sites + r), (other, slot * sites + r)] for r in range(sites)},
            [2, 1, *range(3, bits)] if slot % 2 else [1, bits - 1, *range(2, bits - 1)],
        )
        for slot in slots
    ]
    for step in range(bits - 1):
        messages = [chain.chunks(step) for chain in chains]
        for part in range(len(messages[0])):
            for chain, far in zip(chains, messages):
                chain.send(step, far[part])
    return diagrams([chain.entries[0] for chain in chains], tau)


def solution(mesh):
    placed = (
        P("cfg", None, None, None, ("space", "diag"), None),
        P("cfg", None, None, None, None, ("space", "diag"), None),
        P(),
        P(),
        P(("cfg", "space", "diag"), None, None, None, None),
        P(("space", "diag"), None),
    )
    return jax.shard_map(
        body,
        mesh=mesh,
        in_specs=placed,
        out_specs=P(("cfg", "space", "diag"), None, None, None, None),
        check_vma=False,
    )
```

```python
import functools
import math

import jax
import jax.numpy as jnp
from jax import lax
from jax.experimental import pallas as pl
from jax.experimental.pallas import tpu as pltpu
from jax.sharding import PartitionSpec as P

NCOL = 3
NMOM = 4
NDISP = 4
LX = 16
LY = 16
LANES = 128
ROWS = 16
SITES = ("space", "diag")
MIB = 1024 * 1024
PLANE_LIMIT = 20 * MIB


def shifted(value, axis, by):
    size = lax.axis_size(axis)
    return lax.ppermute(value, axis, [(i, (i + by) % size) for i in range(size)])


def in_hbm(value):
    return pltpu.with_memory_space_constraint(value, pltpu.HBM)


def exchanged(value, mask):
    size = lax.axis_size(SITES)
    return lax.ppermute(value, SITES, [(i, i ^ mask) for i in range(size)])


def gathered(rows, early, late):
    bits = lax.axis_size(SITES).bit_length() - 1
    value = rows[None]
    for low in range(0, bits, 2):
        if low == 2:
            value, late = lax.optimization_barrier((value, late))
        arrived = [exchanged(value, step << low) for step in reversed(range(1, 1 << min(2, bits - low)))]
        if low == 0:
            arrived, early = lax.optimization_barrier((arrived, early))
        value = jnp.concatenate([value] + arrived[::-1])
    return value, early, late


def diagonal(value):
    size = value.shape[0]
    same = lax.broadcasted_iota(jnp.int32, value.shape, 0) == lax.broadcasted_iota(jnp.int32, value.shape, 1)
    return jnp.sum(jnp.where(same, value, 0.0), 0, keepdims=True).reshape(1, size)


def rounded(real, imag, left=None):
    planes = [value.astype(jnp.bfloat16) for value in (real, imag)]
    lost = [diagonal(value - plane.astype(jnp.float32)) for value, plane in zip((real, imag), planes)]
    tile = jnp.concatenate(lost + [jnp.zeros((ROWS - 2, real.shape[1]), jnp.float32)], 0)
    if left is not None:
        tile = tile + left
    return planes, tile.astype(jnp.bfloat16)


def store_rounded(ref, index, real, imag, left=None):
    nvec = real.shape[0]
    planes, tile = rounded(real, imag, left)
    ref[(*index, pl.ds(0, nvec))] = planes[0]
    ref[(*index, pl.ds(nvec, nvec))] = planes[1]
    ref[(*index, pl.ds(2 * nvec, ROWS))] = tile


def restored(total):
    nvec = total.shape[1]
    shape = (nvec, nvec)
    same = lax.broadcasted_iota(jnp.int32, shape, 0) == lax.broadcasted_iota(jnp.int32, shape, 1)
    return [
        total[part * nvec : (part + 1) * nvec] + jnp.where(same, total[2 * nvec + part : 2 * nvec + part + 1], 0.0)
        for part in range(2)
    ]


def color_product(matrix, real, imag, adjoint):
    rows = []
    for row in range(NCOL):
        real_part = imag_part = None
        for col in range(NCOL):
            if adjoint:
                mreal, mimag = matrix[0][col][row], matrix[1][col][row]
                one = mreal * real[col] + mimag * imag[col]
                two = mreal * imag[col] - mimag * real[col]
            else:
                mreal, mimag = matrix[0][row][col], matrix[1][row][col]
                one = mreal * real[col] - mimag * imag[col]
                two = mreal * imag[col] + mimag * real[col]
            real_part = one if real_part is None else real_part + one
            imag_part = two if imag_part is None else imag_part + two
        rows.append((real_part, imag_part))
    return rows


def color_loop(link, nvec, width, load, store, adjoint):
    height = math.gcd(nvec, 2 * ROWS)
    for lane in range(0, width, LANES):
        lanes = pl.ds(lane, LANES)
        matrix = [
            [[link(part, row, col, lanes) for col in range(NCOL)] for row in range(NCOL)] for part in range(2)
        ]
        for start in range(0, nvec, height):
            rows = pl.ds(start, height)
            real = [load(0, color, rows, lanes) for color in range(NCOL)]
            imag = [load(1, color, rows, lanes) for color in range(NCOL)]
            for color, (one, two) in enumerate(color_product(matrix, real, imag, adjoint)):
                store(0, color, rows, lanes, one)
                store(1, color, rows, lanes, two)


def fill_tables(position, total_z, plane, momenta_ref, phase_ref, turn_ref):
    width = phase_ref.shape[-1]
    flat = lax.broadcasted_iota(jnp.int32, (1, width), 1)
    xcoord = (flat % LX).astype(jnp.float32)
    ycoord = (flat % plane // LX).astype(jnp.float32)
    zcoord = (position * (width // plane) + flat // plane).astype(jnp.float32)
    for moment in range(NMOM):
        along_x = momenta_ref[moment, 0].astype(jnp.float32)
        along_y = momenta_ref[moment, 1].astype(jnp.float32)
        along_z = momenta_ref[moment, 2].astype(jnp.float32)
        angle = (
            2.0 * math.pi * (along_x * xcoord / LX + along_y * ycoord / LY + along_z * zcoord / total_z)
        )
        phase_ref[moment, 0] = jnp.cos(angle)
        phase_ref[moment, 1] = jnp.sin(angle)
        turn = jnp.full((1, turn_ref.shape[-1]), 2.0 * math.pi / total_z, jnp.float32) * along_z
        turn_ref[moment, 0] = jnp.cos(turn)
        turn_ref[moment, 1] = jnp.sin(turn)


def fill_moves(move_ref):
    width = move_ref.shape[-1]
    source = lax.broadcasted_iota(jnp.int32, (width, width), 0)
    site = lax.broadcasted_iota(jnp.int32, (width, width), 1)
    xcoord = site % LX
    ycoord = site // LX % LY
    for sign, by in enumerate((1, -1)):
        along_x = site - xcoord + (xcoord + LX + by) % LX
        along_y = site + ((ycoord + LY + by) % LY - ycoord) * LX
        move_ref[0, sign] = (source == along_x).astype(jnp.float32).astype(jnp.bfloat16)
        move_ref[1, sign] = (source == along_y).astype(jnp.float32).astype(jnp.bfloat16)


def plane_kernel(
    total_z, plane, scale,
    position_ref, momenta_in, vector_in, link_in,
    item_ref, own_ref, phase_ref, turn_ref,
    momenta_ref, vector_ref, link_ref,
    ahead_x_ref, ahead_y_ref, behind_x_ref, behind_y_ref, adjoint_x_ref, adjoint_y_ref,
    phased_ref, still_ref, moved_x_ref, moved_y_ref, move_ref, momenta_sem, sems,
):
    now = pl.program_id(0)
    slices, _, _, nvec, width = vector_ref.shape

    def copies(index):
        return (
            pltpu.make_async_copy(vector_in.at[index], vector_ref.at[index], sems.at[0, index]),
            pltpu.make_async_copy(link_in.at[index], link_ref.at[index], sems.at[1, index]),
        )

    @pl.when(now == 0)
    def _():
        moments = pltpu.make_async_copy(momenta_in, momenta_ref, momenta_sem)
        moments.start()
        for index in range(slices):
            for copy in copies(index):
                copy.start()
        fill_moves(move_ref)
        moments.wait()
        fill_tables(position_ref[0], total_z, plane, momenta_ref, phase_ref, turn_ref)

    for copy in copies(now):
        copy.wait()

    def linker(direction):
        return lambda part, row, col, lanes: link_ref[now, direction, part, row, col, :, lanes]

    def vector(part, color, rows, lanes):
        return vector_ref[now, part, color, rows, lanes].astype(jnp.float32)

    def gram(moved_ref, disp):
        product = lax.dot_general(
            phased_ref[...], moved_ref[...], (((1,), (1,)), ((), ())), preferred_element_type=jnp.float32
        )
        for moment in range(NMOM):
            start = 2 * moment * nvec
            upper = product[start : start + nvec]
            lower = product[start + nvec : start + 2 * nvec]
            factor = scale if disp == 0 else 0.5 * scale
            real = factor * (upper[:, :nvec] + lower[:, nvec:])
            imag = factor * (upper[:, nvec:] - lower[:, :nvec])
            store_rounded(item_ref, (0, moment, disp), real, imag)

    flat = vector_ref[now].reshape(2 * NCOL * nvec, width)
    for direction, ahead_ref in enumerate((ahead_x_ref, ahead_y_ref)):
        ahead_ref[...] = jnp.dot(
            flat, move_ref[direction, 0], preferred_element_type=jnp.float32
        ).reshape(ahead_ref.shape)

    for color in range(NCOL):
        span = pl.ds(color * width, width)
        for part in range(2):
            still_ref[pl.ds(part * nvec, nvec), span] = vector_ref[now, part, color]
        for start in range(0, nvec, ROWS):
            real = vector_ref[now, 0, color, pl.ds(start, ROWS), :].astype(jnp.float32)
            imag = vector_ref[now, 1, color, pl.ds(start, ROWS), :].astype(jnp.float32)
            for moment in range(NMOM):
                cosine = phase_ref[moment, 0]
                sine = phase_ref[moment, 1]
                first = 2 * moment * nvec + start
                phased_ref[pl.ds(first, ROWS), span] = (cosine * real - sine * imag).astype(jnp.bfloat16)
                phased_ref[pl.ds(first + nvec, ROWS), span] = (sine * real + cosine * imag).astype(jnp.bfloat16)
    gram(still_ref, 0)

    for direction, (adjoint_ref, behind_ref) in enumerate(
        ((adjoint_x_ref, behind_x_ref), (adjoint_y_ref, behind_y_ref))
    ):

        def adjoint(part, color, rows, lanes, value):
            adjoint_ref[part, color, rows, lanes] = value.astype(jnp.bfloat16)

        color_loop(linker(direction), nvec, width, vector, adjoint, True)
        behind_ref[...] = jnp.dot(
            adjoint_ref[...].reshape(2 * NCOL * nvec, width),
            move_ref[direction, 1],
            preferred_element_type=jnp.float32,
        ).reshape(behind_ref.shape)

    for direction, (ahead_ref, behind_ref, moved_ref) in enumerate(
        ((ahead_x_ref, behind_x_ref, moved_x_ref), (ahead_y_ref, behind_y_ref, moved_y_ref))
    ):

        def ahead(part, color, rows, lanes):
            return ahead_ref[part, color, rows, lanes]

        def forward(part, color, rows, lanes, value):
            moved_ref[
                pl.ds(part * nvec + rows.start, rows.size), pl.ds(color * width + lanes.start, lanes.size)
            ] = (value - behind_ref[part, color, rows, lanes]).astype(jnp.bfloat16)

        color_loop(linker(direction), nvec, width, ahead, forward, False)
        gram(moved_ref, direction + 1)

    def own(part, color, rows, lanes, value):
        own_ref[0, part, color, rows, lanes] = value

    color_loop(linker(2), nvec, width, vector, own, True)


def plane_items(position, momenta, vectors, links, total_z, plane, scale):
    slices, _, _, nvec, width = vectors.shape
    color_block = (2, NCOL, nvec, width)
    return pl.pallas_call(
        functools.partial(plane_kernel, total_z, plane, scale),
        grid=(slices,),
        in_specs=[pl.BlockSpec(memory_space=pltpu.SMEM)] + [pl.BlockSpec(memory_space=pltpu.HBM)] * 3,
        out_specs=[
            pl.BlockSpec((1, NMOM, NDISP - 1, 2 * nvec + ROWS, nvec), lambda t: (t, 0, 0, 0, 0)),
            pl.BlockSpec((1,) + color_block, lambda t: (t, 0, 0, 0, 0)),
            pl.BlockSpec((NMOM, 2, 1, width), lambda t: (0, 0, 0, 0)),
            pl.BlockSpec((NMOM, 2, 1, nvec), lambda t: (0, 0, 0, 0)),
        ],
        out_shape=[
            jax.ShapeDtypeStruct((slices, NMOM, NDISP - 1, 2 * nvec + ROWS, nvec), jnp.bfloat16),
            jax.ShapeDtypeStruct(vectors.shape, jnp.float32),
            jax.ShapeDtypeStruct((NMOM, 2, 1, width), jnp.float32),
            jax.ShapeDtypeStruct((NMOM, 2, 1, nvec), jnp.float32),
        ],
        scratch_shapes=[
            pltpu.SMEM(momenta.shape, jnp.int32),
            pltpu.VMEM(vectors.shape, jnp.bfloat16),
            pltpu.VMEM(links.shape, jnp.float32),
        ]
        + [pltpu.VMEM(color_block, jnp.float32)] * 4
        + [pltpu.VMEM(color_block, jnp.bfloat16)] * 2
        + [pltpu.VMEM((NMOM * 2 * nvec, NCOL * width), jnp.bfloat16)]
        + [pltpu.VMEM((2 * nvec, NCOL * width), jnp.bfloat16)] * 3
        + [
            pltpu.VMEM((2, 2, width, width), jnp.bfloat16),
            pltpu.SemaphoreType.DMA,
            pltpu.SemaphoreType.DMA((2, slices)),
        ],
        compiler_params=pltpu.CompilerParams(vmem_limit_bytes=PLANE_LIMIT),
        cost_estimate=pl.CostEstimate(
            flops=slices * 16 * NMOM * nvec * nvec * NCOL * width,
            bytes_accessed=6 * vectors.size + 4 * links.size,
            transcendentals=0,
        ),
        name="plane_items",
    )(position, in_hbm(momenta), in_hbm(vectors), in_hbm(links))


def layer_kernel(
    core, scale, rows_ref, item_ref, own_ref, ahead_ref, phase_ref, turn_ref, out_ref, lhs_ref, listed_ref
):
    nvec, width = own_ref.shape[3:]
    total = out_ref.shape[0]
    sites = rows_ref.shape[0] // 2

    def parts_of(place):
        item = rows_ref[2 * lax.rem(place, sites) + core, lax.div(place, sites), 0]
        rest = lax.rem(item, NMOM * NDISP)
        return lax.div(item, NMOM * NDISP), lax.div(rest, NDISP), lax.rem(rest, NDISP)

    def bond(place, lhs):
        slice_index, moment, _ = parts_of(place)
        cosine = phase_ref[moment, 0]
        sine = phase_ref[moment, 1]
        for color in range(NCOL):
            span = pl.ds(color * width, width)
            for part in range(2):
                value = own_ref[slice_index, part, color]
                lhs[pl.ds(part * nvec, nvec), span] = (cosine * value).astype(jnp.bfloat16)
                lhs[pl.ds((2 + part) * nvec, nvec), span] = (sine * value).astype(jnp.bfloat16)
        rhs = jnp.concatenate(
            [
                jnp.concatenate([ahead_ref[slice_index, part, color] for color in range(NCOL)], 1)
                for part in range(2)
            ],
            0,
        )
        gram = lax.dot_general(lhs[...], rhs, (((1,), (1,)), ((), ())), preferred_element_type=jnp.float32)
        block = [
            [gram[i * nvec : (i + 1) * nvec, j * nvec : (j + 1) * nvec] for j in range(2)] for i in range(4)
        ]
        cos_real = block[0][0] + block[1][1]
        cos_imag = block[0][1] - block[1][0]
        sin_real = block[2][0] + block[3][1]
        sin_imag = block[2][1] - block[3][0]
        half = 0.5 * scale
        turn_cos = half * turn_ref[moment, 0]
        turn_sin = half * turn_ref[moment, 1]
        back_real = cos_real - sin_imag
        back_imag = cos_imag + sin_real
        real = half * (cos_real + sin_imag) - (turn_cos * back_real - turn_sin * back_imag).T
        imag = half * (cos_imag - sin_real) + (turn_cos * back_imag + turn_sin * back_real).T
        return real, imag

    found = jnp.int32(0)
    for place in range(total):
        slice_index, moment, disp = parts_of(jnp.int32(place))
        out_ref[place] = item_ref[slice_index, moment, jnp.minimum(disp, NDISP - 2)]
        listed_ref[found] = place
        found = found + (disp == NDISP - 1).astype(jnp.int32)

    def finish(places):
        results = [bond(place, lhs_ref.at[index]) for index, place in enumerate(places)]
        for place, (real, imag) in zip(places, results):
            store_rounded(out_ref, (place,), real, imag)

    @pl.loop(0, lax.div(found, 2))
    def _(pair):
        finish([listed_ref[2 * pair], listed_ref[2 * pair + 1]])

    @pl.when(lax.rem(found, 2) == 1)
    def _():
        finish([listed_ref[found - 1]])


def layer_items(core, rows, item, own, ahead, phase, turn, scale):
    slices, _, _, nvec, width = own.shape
    devices, slots, _ = rows.shape
    total = slots * devices // 2
    whole = pl.BlockSpec(memory_space=pltpu.VMEM)
    return pl.pallas_call(
        functools.partial(layer_kernel, core, scale),
        in_specs=[pl.BlockSpec(memory_space=pltpu.SMEM)] + [whole] * 5,
        out_specs=whole,
        out_shape=jax.ShapeDtypeStruct((total, 2 * nvec + ROWS, nvec), jnp.bfloat16),
        scratch_shapes=[
            pltpu.VMEM((2, 4 * nvec, NCOL * width), jnp.bfloat16),
            pltpu.SMEM((total,), jnp.int32),
        ],
        compiler_params=pltpu.CompilerParams(vmem_limit_bytes=8 * MIB),
        cost_estimate=pl.CostEstimate(
            flops=total * 4 * nvec * nvec * NCOL * width,
            bytes_accessed=2 * own.size,
            transcendentals=0,
        ),
        name="layer_items",
    )(rows, item, own, ahead, phase, turn)


def add_kernel(places, *refs):
    for out_ref, entries in zip(refs[len(refs) - len(places) :], places):
        for index, entry in enumerate(entries):
            total = sum(refs[number][at].astype(jnp.float32) for number, at in entry)
            nvec = total.shape[1]
            if out_ref.dtype == jnp.float32:
                out_ref[index] = total
            else:
                left = total[2 * nvec :]
                store_rounded(out_ref, (index,), total[:nvec], total[nvec : 2 * nvec], left)


def added(groups):
    arrays = []

    def number(array):
        found = [place for place, other in enumerate(arrays) if other is array]
        if not found:
            arrays.append(array)
        return found[0] if found else len(arrays) - 1

    places = [[[(number(array), at) for array, at in entry] for entry in entries] for entries, _ in groups]
    tail = arrays[0].shape[1:]
    whole = pl.BlockSpec(memory_space=pltpu.VMEM)
    size = sum(len(entry) for entries in places for entry in entries) * math.prod(tail)
    return pl.pallas_call(
        functools.partial(add_kernel, places),
        in_specs=[whole] * len(arrays),
        out_specs=[whole] * len(groups),
        out_shape=[jax.ShapeDtypeStruct((len(entries),) + tail, dtype) for entries, dtype in groups],
        compiler_params=pltpu.CompilerParams(vmem_limit_bytes=8 * MIB),
        cost_estimate=pl.CostEstimate(flops=size, bytes_accessed=4 * size, transcendentals=0),
        name="added",
    )(*arrays)


class Chain:
    def __init__(self, entries, order):
        self.entries = entries
        self.order = order

    def chunks(self, step):
        far = [r for r in self.entries if r >> (self.order[step] - 1) & 1]
        if step + 1 == len(self.order):
            return [far]
        split = [[], []]
        for r in far:
            split[r >> (self.order[step + 1] - 1) & 1].append(r)
        return [split[1], split[0]]

    def send(self, step, far):
        bit = self.order[step]
        near = [r ^ (1 << (bit - 1)) for r in far]
        groups = [([self.entries[r] for r in far], jnp.bfloat16)]
        last = step + 1 == len(self.order)
        if step == 0 or last:
            kept = [self.entries[r] if step == 0 else self.entries[r][:2] for r in near]
            groups.append((kept, jnp.float32))
        outs = added(groups)
        arrived = exchanged(outs[0], 1 << bit)
        for at, r in enumerate(near):
            if step == 0:
                self.entries[r] = [(outs[1], at)]
            elif last:
                self.entries[r][:2] = [(outs[1], at)]
            self.entries[r].append((arrived, at))
        for r in far:
            del self.entries[r]


def mix_kernel(index, slot_ref, structure_ref, weight_ref, tau_in, out_ref, tau_ref, sems):
    spins, parts, nvec, width = out_ref.shape
    copies = [
        pltpu.make_async_copy(tau_in.at[slot_ref[index], :, part], tau_ref.at[:, part], sems.at[part])
        for part in range(parts)
    ]
    for copy in copies:
        copy.start()
    base = structure_ref[index] * spins * spins
    weight = [[weight_ref[base + r * spins + s] for s in range(spins)] for r in range(spins)]
    for part in range(parts):
        copies[part].wait()

        @pl.loop(0, nvec // ROWS)
        def _(step):
            rows = pl.ds(pl.multiple_of(step * ROWS, ROWS), ROWS)
            tau = [tau_ref[s, part, rows, :].astype(jnp.float32) for s in range(spins)]
            for r in range(spins):
                mixed = weight[r][0] * tau[0]
                for s in range(1, spins):
                    mixed = mixed + weight[r][s] * tau[s]
                out_ref[r, part, rows, :] = mixed.astype(jnp.bfloat16)


def mixed_perambulator(index, slots, structures, weights, perambulators):
    shape = perambulators.shape[1:]
    scalar = pl.BlockSpec(memory_space=pltpu.SMEM)
    return pl.pallas_call(
        functools.partial(mix_kernel, index),
        in_specs=[scalar] * 3 + [pl.BlockSpec(memory_space=pltpu.HBM)],
        out_specs=pl.BlockSpec(memory_space=pltpu.VMEM),
        out_shape=jax.ShapeDtypeStruct(shape, jnp.bfloat16),
        scratch_shapes=[pltpu.VMEM(shape, jnp.bfloat16), pltpu.SemaphoreType.DMA(shape[1:2])],
        compiler_params=pltpu.CompilerParams(vmem_limit_bytes=8 * MIB),
        cost_estimate=pl.CostEstimate(
            flops=8 * math.prod(shape), bytes_accessed=4 * math.prod(shape), transcendentals=0
        ),
        name="mixed_perambulator",
    )(slots, structures, weights, in_hbm(perambulators))


def diagram_kernel(index, places, *refs):
    tau_ref = refs[len(places)]
    out_ref, block_ref, sems = refs[-3:]
    spins, _, nvec, width = tau_ref.shape
    real, imag = restored(sum(ref[at].astype(jnp.float32) for ref, at in zip(refs, places)))
    square = jnp.concatenate(
        [jnp.concatenate([real, -imag], 1), jnp.concatenate([imag, real], 1)], 0
    ).astype(jnp.bfloat16)
    copies = [
        pltpu.make_async_copy(block_ref.at[r], out_ref.at[index, r], sems.at[r]) for r in range(spins)
    ]
    for r in range(spins):
        tau = tau_ref[r].reshape(2 * nvec, width)
        block = jnp.dot(square, tau, preferred_element_type=jnp.float32)
        block_ref[r] = block.astype(jnp.bfloat16).reshape(2, nvec, width)
        copies[r].start()
    for copy in copies:
        copy.wait()


def diagram(index, count, entry, tau, before):
    whole = pl.BlockSpec(memory_space=pltpu.VMEM)
    large = pl.BlockSpec(memory_space=pltpu.HBM)
    earlier = [] if before is None else [before]
    return pl.pallas_call(
        functools.partial(diagram_kernel, index, [at for _, at in entry]),
        in_specs=[whole] * (len(entry) + 1) + [large] * len(earlier),
        out_specs=large,
        out_shape=jax.ShapeDtypeStruct((count,) + tau.shape, jnp.bfloat16),
        scratch_shapes=[pltpu.VMEM(tau.shape, jnp.bfloat16), pltpu.SemaphoreType.DMA(tau.shape[:1])],
        input_output_aliases={len(entry) + 1: 0} if earlier else {},
        compiler_params=pltpu.CompilerParams(vmem_limit_bytes=8 * MIB),
        cost_estimate=pl.CostEstimate(
            flops=8 * tau.shape[2] * tau.size, bytes_accessed=4 * tau.size, transcendentals=0
        ),
        name="diagram",
    )(*[array for array, _ in entry], tau, *earlier)


def body(eigvecs, gauge_links, momenta, spin_mix, perambulators, contraction_list):
    slices, _, _, nvec, depth, plane = eigvecs.shape
    devices = lax.axis_size(SITES)
    position = lax.axis_index(SITES)
    bits = devices.bit_length() - 1
    total_z = depth * devices
    width = depth * plane
    scale = 1.0 / math.sqrt(NCOL * plane * total_z)
    place = position.reshape(1)
    rows, after, place = gathered(contraction_list, eigvecs, place)
    upper = shifted(after[:, :, :, :, :1, :], SITES, -1)
    vectors = eigvecs.reshape(slices, 2, NCOL, nvec, width)
    links = gauge_links.reshape(slices, 3, 2, NCOL, NCOL, 1, width)
    item, own, phase, turn = plane_items(place, momenta, vectors, links, total_z, plane, scale)
    chosen = contraction_list[:, 2] - position * perambulators.shape[0]
    weights = spin_mix.reshape(-1)
    taus = [
        mixed_perambulator(j, chosen, contraction_list[:, 1], weights, perambulators)
        for j in range(contraction_list.shape[0])
    ]
    ahead = jnp.concatenate([eigvecs[:, :, :, :, 1:, :], upper], 4).reshape(vectors.shape)
    send = layer_items(1, rows, item, own, ahead, phase, turn, scale)
    keep = layer_items(0, rows, item, own, ahead, phase, turn, scale)
    slots = range(contraction_list.shape[0])
    other = exchanged(send, 1)
    sites = devices // 2
    chains = [
        Chain(
            {r: [(keep, slot * sites + r), (other, slot * sites + r)] for r in range(sites)},
            [2, 1, *range(3, bits)] if slot % 2 else [1, bits - 1, *range(2, bits - 1)],
        )
        for slot in slots
    ]
    for step in range(bits - 1):
        messages = [chain.chunks(step) for chain in chains]
        if step == bits - 2:
            terms = chains[0].entries[messages[0][0][0]]
            (array, at) = terms[-1]
            array, taus[0] = lax.optimization_barrier((array, taus[0]))
            terms[-1] = (array, at)
        for part in range(len(messages[0])):
            for chain, far in zip(chains, messages):
                chain.send(step, far[part])
    out = None
    for slot, chain in enumerate(chains):
        out = diagram(slot, len(chains), chain.entries[0], taus[slot], out)
    return out


def solution(mesh):
    placed = (
        P("cfg", None, None, None, ("space", "diag"), None),
        P("cfg", None, None, None, None, ("space", "diag"), None),
        P(),
        P(),
        P(("cfg", "space", "diag"), None, None, None, None),
        P(("space", "diag"), None),
    )
    return jax.shard_map(
        body,
        mesh=mesh,
        in_specs=placed,
        out_specs=P(("cfg", "space", "diag"), None, None, None, None),
        check_vma=False,
    )
```

```python
import functools
import math

import jax
import jax.numpy as jnp
from jax import lax
from jax.experimental import pallas as pl
from jax.experimental.pallas import tpu as pltpu
from jax.sharding import PartitionSpec as P

NCOL = 3
NMOM = 4
NDISP = 4
LX = 16
LY = 16
LANES = 128
ROWS = 16
SITES = ("space", "diag")
MIB = 1024 * 1024
PLANE_LIMIT = 20 * MIB


def shifted(value, axis, by):
    size = lax.axis_size(axis)
    return lax.ppermute(value, axis, [(i, (i + by) % size) for i in range(size)])


def in_hbm(value):
    return pltpu.with_memory_space_constraint(value, pltpu.HBM)


def exchanged(value, mask):
    size = lax.axis_size(SITES)
    return lax.ppermute(value, SITES, [(i, i ^ mask) for i in range(size)])


def gathered(rows, early, late):
    bits = lax.axis_size(SITES).bit_length() - 1
    value = rows[None]
    for low in range(0, bits, 2):
        if low == 2:
            value, late = lax.optimization_barrier((value, late))
        arrived = [exchanged(value, step << low) for step in reversed(range(1, 1 << min(2, bits - low)))]
        if low == 0:
            arrived, early = lax.optimization_barrier((arrived, early))
        value = jnp.concatenate([value] + arrived[::-1])
    return value, early, late


def diagonal(value):
    size = value.shape[0]
    same = lax.broadcasted_iota(jnp.int32, value.shape, 0) == lax.broadcasted_iota(jnp.int32, value.shape, 1)
    return jnp.sum(jnp.where(same, value, 0.0), 0, keepdims=True).reshape(1, size)


def rounded(real, imag, left=None):
    planes = [value.astype(jnp.bfloat16) for value in (real, imag)]
    lost = [diagonal(value - plane.astype(jnp.float32)) for value, plane in zip((real, imag), planes)]
    tile = jnp.concatenate(lost + [jnp.zeros((ROWS - 2, real.shape[1]), jnp.float32)], 0)
    if left is not None:
        tile = tile + left
    return planes, tile.astype(jnp.bfloat16)


def store_rounded(ref, index, real, imag, left=None):
    nvec = real.shape[0]
    planes, tile = rounded(real, imag, left)
    ref[(*index, pl.ds(0, nvec))] = planes[0]
    ref[(*index, pl.ds(nvec, nvec))] = planes[1]
    ref[(*index, pl.ds(2 * nvec, ROWS))] = tile


def restored(total):
    nvec = total.shape[1]
    shape = (nvec, nvec)
    same = lax.broadcasted_iota(jnp.int32, shape, 0) == lax.broadcasted_iota(jnp.int32, shape, 1)
    return [
        total[part * nvec : (part + 1) * nvec] + jnp.where(same, total[2 * nvec + part : 2 * nvec + part + 1], 0.0)
        for part in range(2)
    ]


def color_product(matrix, real, imag, adjoint):
    rows = []
    for row in range(NCOL):
        real_part = imag_part = None
        for col in range(NCOL):
            if adjoint:
                mreal, mimag = matrix[0][col][row], matrix[1][col][row]
                one = mreal * real[col] + mimag * imag[col]
                two = mreal * imag[col] - mimag * real[col]
            else:
                mreal, mimag = matrix[0][row][col], matrix[1][row][col]
                one = mreal * real[col] - mimag * imag[col]
                two = mreal * imag[col] + mimag * real[col]
            real_part = one if real_part is None else real_part + one
            imag_part = two if imag_part is None else imag_part + two
        rows.append((real_part, imag_part))
    return rows


def color_loop(link, nvec, width, load, store, adjoint):
    height = math.gcd(nvec, 2 * ROWS)
    for lane in range(0, width, LANES):
        lanes = pl.ds(lane, LANES)
        matrix = [
            [[link(part, row, col, lanes) for col in range(NCOL)] for row in range(NCOL)] for part in range(2)
        ]
        for start in range(0, nvec, height):
            rows = pl.ds(start, height)
            real = [load(0, color, rows, lanes) for color in range(NCOL)]
            imag = [load(1, color, rows, lanes) for color in range(NCOL)]
            for color, (one, two) in enumerate(color_product(matrix, real, imag, adjoint)):
                store(0, color, rows, lanes, one)
                store(1, color, rows, lanes, two)


def fill_tables(position, total_z, plane, momenta_ref, phase_ref, turn_ref):
    width = phase_ref.shape[-1]
    flat = lax.broadcasted_iota(jnp.int32, (1, width), 1)
    xcoord = (flat % LX).astype(jnp.float32)
    ycoord = (flat % plane // LX).astype(jnp.float32)
    zcoord = (position * (width // plane) + flat // plane).astype(jnp.float32)
    for moment in range(NMOM):
        along_x = momenta_ref[moment, 0].astype(jnp.float32)
        along_y = momenta_ref[moment, 1].astype(jnp.float32)
        along_z = momenta_ref[moment, 2].astype(jnp.float32)
        angle = (
            2.0 * math.pi * (along_x * xcoord / LX + along_y * ycoord / LY + along_z * zcoord / total_z)
        )
        phase_ref[moment, 0] = jnp.cos(angle)
        phase_ref[moment, 1] = jnp.sin(angle)
        turn = jnp.full((1, turn_ref.shape[-1]), 2.0 * math.pi / total_z, jnp.float32) * along_z
        turn_ref[moment, 0] = jnp.cos(turn)
        turn_ref[moment, 1] = jnp.sin(turn)


def fill_moves(move_ref):
    width = move_ref.shape[-1]
    source = lax.broadcasted_iota(jnp.int32, (width, width), 0)
    site = lax.broadcasted_iota(jnp.int32, (width, width), 1)
    xcoord = site % LX
    ycoord = site // LX % LY
    for sign, by in enumerate((1, -1)):
        along_x = site - xcoord + (xcoord + LX + by) % LX
        along_y = site + ((ycoord + LY + by) % LY - ycoord) * LX
        move_ref[0, sign] = (source == along_x).astype(jnp.float32).astype(jnp.bfloat16)
        move_ref[1, sign] = (source == along_y).astype(jnp.float32).astype(jnp.bfloat16)


def plane_kernel(
    total_z, plane, scale,
    position_ref, momenta_in, vector_in, link_in,
    item_ref, own_ref, phase_ref, turn_ref,
    momenta_ref, vector_ref, link_ref,
    ahead_x_ref, ahead_y_ref, behind_x_ref, behind_y_ref, adjoint_x_ref, adjoint_y_ref,
    phased_ref, still_ref, moved_x_ref, moved_y_ref, move_ref, momenta_sem, sems,
):
    now = pl.program_id(0)
    slices, _, _, nvec, width = vector_ref.shape

    def copies(index):
        return (
            pltpu.make_async_copy(vector_in.at[index], vector_ref.at[index], sems.at[0, index]),
            pltpu.make_async_copy(link_in.at[index], link_ref.at[index], sems.at[1, index]),
        )

    @pl.when(now == 0)
    def _():
        moments = pltpu.make_async_copy(momenta_in, momenta_ref, momenta_sem)
        moments.start()
        for index in range(slices):
            for copy in copies(index):
                copy.start()
        fill_moves(move_ref)
        moments.wait()
        fill_tables(position_ref[0], total_z, plane, momenta_ref, phase_ref, turn_ref)

    for copy in copies(now):
        copy.wait()

    def linker(direction):
        return lambda part, row, col, lanes: link_ref[now, direction, part, row, col, :, lanes]

    def vector(part, color, rows, lanes):
        return vector_ref[now, part, color, rows, lanes].astype(jnp.float32)

    def gram(moved_ref, disp):
        product = lax.dot_general(
            phased_ref[...], moved_ref[...], (((1,), (1,)), ((), ())), preferred_element_type=jnp.float32
        )
        for moment in range(NMOM):
            start = 2 * moment * nvec
            upper = product[start : start + nvec]
            lower = product[start + nvec : start + 2 * nvec]
            factor = scale if disp == 0 else 0.5 * scale
            real = factor * (upper[:, :nvec] + lower[:, nvec:])
            imag = factor * (upper[:, nvec:] - lower[:, :nvec])
            store_rounded(item_ref, (0, moment, disp), real, imag)

    flat = vector_ref[now].reshape(2 * NCOL * nvec, width)
    for direction, ahead_ref in enumerate((ahead_x_ref, ahead_y_ref)):
        ahead_ref[...] = jnp.dot(
            flat, move_ref[direction, 0], preferred_element_type=jnp.float32
        ).reshape(ahead_ref.shape)

    for color in range(NCOL):
        span = pl.ds(color * width, width)
        for part in range(2):
            still_ref[pl.ds(part * nvec, nvec), span] = vector_ref[now, part, color]
        for start in range(0, nvec, ROWS):
            real = vector_ref[now, 0, color, pl.ds(start, ROWS), :].astype(jnp.float32)
            imag = vector_ref[now, 1, color, pl.ds(start, ROWS), :].astype(jnp.float32)
            for moment in range(NMOM):
                cosine = phase_ref[moment, 0]
                sine = phase_ref[moment, 1]
                first = 2 * moment * nvec + start
                phased_ref[pl.ds(first, ROWS), span] = (cosine * real - sine * imag).astype(jnp.bfloat16)
                phased_ref[pl.ds(first + nvec, ROWS), span] = (sine * real + cosine * imag).astype(jnp.bfloat16)
    gram(still_ref, 0)

    for direction, (adjoint_ref, behind_ref) in enumerate(
        ((adjoint_x_ref, behind_x_ref), (adjoint_y_ref, behind_y_ref))
    ):

        def adjoint(part, color, rows, lanes, value):
            adjoint_ref[part, color, rows, lanes] = value.astype(jnp.bfloat16)

        color_loop(linker(direction), nvec, width, vector, adjoint, True)
        behind_ref[...] = jnp.dot(
            adjoint_ref[...].reshape(2 * NCOL * nvec, width),
            move_ref[direction, 1],
            preferred_element_type=jnp.float32,
        ).reshape(behind_ref.shape)

    for direction, (ahead_ref, behind_ref, moved_ref) in enumerate(
        ((ahead_x_ref, behind_x_ref, moved_x_ref), (ahead_y_ref, behind_y_ref, moved_y_ref))
    ):

        def ahead(part, color, rows, lanes):
            return ahead_ref[part, color, rows, lanes]

        def forward(part, color, rows, lanes, value):
            moved_ref[
                pl.ds(part * nvec + rows.start, rows.size), pl.ds(color * width + lanes.start, lanes.size)
            ] = (value - behind_ref[part, color, rows, lanes]).astype(jnp.bfloat16)

        color_loop(linker(direction), nvec, width, ahead, forward, False)
        gram(moved_ref, direction + 1)

    def own(part, color, rows, lanes, value):
        own_ref[0, part, color, rows, lanes] = value

    color_loop(linker(2), nvec, width, vector, own, True)


def plane_items(position, momenta, vectors, links, total_z, plane, scale):
    slices, _, _, nvec, width = vectors.shape
    color_block = (2, NCOL, nvec, width)
    return pl.pallas_call(
        functools.partial(plane_kernel, total_z, plane, scale),
        grid=(slices,),
        in_specs=[pl.BlockSpec(memory_space=pltpu.SMEM)] + [pl.BlockSpec(memory_space=pltpu.HBM)] * 3,
        out_specs=[
            pl.BlockSpec((1, NMOM, NDISP - 1, 2 * nvec + ROWS, nvec), lambda t: (t, 0, 0, 0, 0)),
            pl.BlockSpec((1,) + color_block, lambda t: (t, 0, 0, 0, 0)),
            pl.BlockSpec((NMOM, 2, 1, width), lambda t: (0, 0, 0, 0)),
            pl.BlockSpec((NMOM, 2, 1, nvec), lambda t: (0, 0, 0, 0)),
        ],
        out_shape=[
            jax.ShapeDtypeStruct((slices, NMOM, NDISP - 1, 2 * nvec + ROWS, nvec), jnp.bfloat16),
            jax.ShapeDtypeStruct(vectors.shape, jnp.float32),
            jax.ShapeDtypeStruct((NMOM, 2, 1, width), jnp.float32),
            jax.ShapeDtypeStruct((NMOM, 2, 1, nvec), jnp.float32),
        ],
        scratch_shapes=[
            pltpu.SMEM(momenta.shape, jnp.int32),
            pltpu.VMEM(vectors.shape, jnp.bfloat16),
            pltpu.VMEM(links.shape, jnp.float32),
        ]
        + [pltpu.VMEM(color_block, jnp.float32)] * 4
        + [pltpu.VMEM(color_block, jnp.bfloat16)] * 2
        + [pltpu.VMEM((NMOM * 2 * nvec, NCOL * width), jnp.bfloat16)]
        + [pltpu.VMEM((2 * nvec, NCOL * width), jnp.bfloat16)] * 3
        + [
            pltpu.VMEM((2, 2, width, width), jnp.bfloat16),
            pltpu.SemaphoreType.DMA,
            pltpu.SemaphoreType.DMA((2, slices)),
        ],
        compiler_params=pltpu.CompilerParams(vmem_limit_bytes=PLANE_LIMIT),
        cost_estimate=pl.CostEstimate(
            flops=slices * 16 * NMOM * nvec * nvec * NCOL * width,
            bytes_accessed=6 * vectors.size + 4 * links.size,
            transcendentals=0,
        ),
        name="plane_items",
    )(position, in_hbm(momenta), in_hbm(vectors), in_hbm(links))


def layer_kernel(
    core, scale, rows_ref, item_ref, own_ref, ahead_ref, phase_ref, turn_ref, out_ref, lhs_ref, listed_ref
):
    nvec, width = own_ref.shape[3:]
    total = out_ref.shape[0]
    sites = rows_ref.shape[0] // 2

    def parts_of(place):
        item = rows_ref[2 * lax.rem(place, sites) + core, lax.div(place, sites), 0]
        rest = lax.rem(item, NMOM * NDISP)
        return lax.div(item, NMOM * NDISP), lax.div(rest, NDISP), lax.rem(rest, NDISP)

    def bond(place, lhs):
        slice_index, moment, _ = parts_of(place)
        cosine = phase_ref[moment, 0]
        sine = phase_ref[moment, 1]
        for color in range(NCOL):
            span = pl.ds(color * width, width)
            for part in range(2):
                value = own_ref[slice_index, part, color]
                lhs[pl.ds(part * nvec, nvec), span] = (cosine * value).astype(jnp.bfloat16)
                lhs[pl.ds((2 + part) * nvec, nvec), span] = (sine * value).astype(jnp.bfloat16)
        rhs = jnp.concatenate(
            [
                jnp.concatenate([ahead_ref[slice_index, part, color] for color in range(NCOL)], 1)
                for part in range(2)
            ],
            0,
        )
        gram = lax.dot_general(lhs[...], rhs, (((1,), (1,)), ((), ())), preferred_element_type=jnp.float32)
        block = [
            [gram[i * nvec : (i + 1) * nvec, j * nvec : (j + 1) * nvec] for j in range(2)] for i in range(4)
        ]
        cos_real = block[0][0] + block[1][1]
        cos_imag = block[0][1] - block[1][0]
        sin_real = block[2][0] + block[3][1]
        sin_imag = block[2][1] - block[3][0]
        half = 0.5 * scale
        turn_cos = half * turn_ref[moment, 0]
        turn_sin = half * turn_ref[moment, 1]
        back_real = cos_real - sin_imag
        back_imag = cos_imag + sin_real
        real = half * (cos_real + sin_imag) - (turn_cos * back_real - turn_sin * back_imag).T
        imag = half * (cos_imag - sin_real) + (turn_cos * back_imag + turn_sin * back_real).T
        return real, imag

    found = jnp.int32(0)
    for place in range(total):
        slice_index, moment, disp = parts_of(jnp.int32(place))
        out_ref[place] = item_ref[slice_index, moment, jnp.minimum(disp, NDISP - 2)]
        listed_ref[found] = place
        found = found + (disp == NDISP - 1).astype(jnp.int32)

    def finish(places):
        results = [bond(place, lhs_ref.at[index]) for index, place in enumerate(places)]
        for place, (real, imag) in zip(places, results):
            store_rounded(out_ref, (place,), real, imag)

    @pl.loop(0, lax.div(found, 2))
    def _(pair):
        finish([listed_ref[2 * pair], listed_ref[2 * pair + 1]])

    @pl.when(lax.rem(found, 2) == 1)
    def _():
        finish([listed_ref[found - 1]])


def layer_items(core, rows, item, own, ahead, phase, turn, scale):
    slices, _, _, nvec, width = own.shape
    devices, slots, _ = rows.shape
    total = slots * devices // 2
    whole = pl.BlockSpec(memory_space=pltpu.VMEM)
    return pl.pallas_call(
        functools.partial(layer_kernel, core, scale),
        in_specs=[pl.BlockSpec(memory_space=pltpu.SMEM)] + [whole] * 5,
        out_specs=whole,
        out_shape=jax.ShapeDtypeStruct((total, 2 * nvec + ROWS, nvec), jnp.bfloat16),
        scratch_shapes=[
            pltpu.VMEM((2, 4 * nvec, NCOL * width), jnp.bfloat16),
            pltpu.SMEM((total,), jnp.int32),
        ],
        compiler_params=pltpu.CompilerParams(vmem_limit_bytes=8 * MIB),
        cost_estimate=pl.CostEstimate(
            flops=total * 4 * nvec * nvec * NCOL * width,
            bytes_accessed=2 * own.size,
            transcendentals=0,
        ),
        name="layer_items",
    )(rows, item, own, ahead, phase, turn)


def add_kernel(places, *refs):
    for out_ref, entries in zip(refs[len(refs) - len(places) :], places):
        for index, entry in enumerate(entries):
            total = sum(refs[number][at].astype(jnp.float32) for number, at in entry)
            nvec = total.shape[1]
            if out_ref.dtype == jnp.float32:
                out_ref[index] = total
            else:
                left = total[2 * nvec :]
                store_rounded(out_ref, (index,), total[:nvec], total[nvec : 2 * nvec], left)


def added(groups):
    arrays = []

    def number(array):
        found = [place for place, other in enumerate(arrays) if other is array]
        if not found:
            arrays.append(array)
        return found[0] if found else len(arrays) - 1

    places = [[[(number(array), at) for array, at in entry] for entry in entries] for entries, _ in groups]
    tail = arrays[0].shape[1:]
    whole = pl.BlockSpec(memory_space=pltpu.VMEM)
    size = sum(len(entry) for entries in places for entry in entries) * math.prod(tail)
    return pl.pallas_call(
        functools.partial(add_kernel, places),
        in_specs=[whole] * len(arrays),
        out_specs=[whole] * len(groups),
        out_shape=[jax.ShapeDtypeStruct((len(entries),) + tail, dtype) for entries, dtype in groups],
        compiler_params=pltpu.CompilerParams(vmem_limit_bytes=8 * MIB),
        cost_estimate=pl.CostEstimate(flops=size, bytes_accessed=4 * size, transcendentals=0),
        name="added",
    )(*arrays)


class Chain:
    def __init__(self, entries, order):
        self.entries = entries
        self.order = order

    def chunks(self, step):
        far = [r for r in self.entries if r >> (self.order[step] - 1) & 1]
        if step + 1 == len(self.order):
            return [far]
        split = [[], []]
        for r in far:
            split[r >> (self.order[step + 1] - 1) & 1].append(r)
        return [split[1], split[0]]

    def send(self, step, far):
        bit = self.order[step]
        near = [r ^ (1 << (bit - 1)) for r in far]
        groups = [([self.entries[r] for r in far], jnp.bfloat16)]
        last = step + 1 == len(self.order)
        if step == 0 or last:
            kept = [self.entries[r] if step == 0 else self.entries[r][:2] for r in near]
            groups.append((kept, jnp.float32))
        outs = added(groups)
        arrived = exchanged(outs[0], 1 << bit)
        for at, r in enumerate(near):
            if step == 0:
                self.entries[r] = [(outs[1], at)]
            elif last:
                self.entries[r][:2] = [(outs[1], at)]
            self.entries[r].append((arrived, at))
        for r in far:
            del self.entries[r]


def mix_kernel(slot_ref, structure_ref, weight_ref, tau_in, out_ref, tau_ref, sems):
    count, spins, parts, nvec, width = out_ref.shape

    def copy(index, part):
        return pltpu.make_async_copy(
            tau_in.at[slot_ref[index], :, part], tau_ref.at[index, :, part], sems.at[index, part]
        )

    for index in range(count):
        for part in range(parts):
            copy(index, part).start()
    for index in range(count):
        base = structure_ref[index] * spins * spins
        weight = [[weight_ref[base + r * spins + s] for s in range(spins)] for r in range(spins)]
        for part in range(parts):
            copy(index, part).wait()

            @pl.loop(0, nvec // ROWS)
            def _(step):
                rows = pl.ds(pl.multiple_of(step * ROWS, ROWS), ROWS)
                tau = [tau_ref[index, s, part, rows, :].astype(jnp.float32) for s in range(spins)]
                for r in range(spins):
                    mixed = weight[r][0] * tau[0]
                    for s in range(1, spins):
                        mixed = mixed + weight[r][s] * tau[s]
                    out_ref[index, r, part, rows, :] = mixed.astype(jnp.bfloat16)


def mixed_perambulators(slots, structures, weights, perambulators):
    shape = (slots.shape[0],) + perambulators.shape[1:]
    scalar = pl.BlockSpec(memory_space=pltpu.SMEM)
    return pl.pallas_call(
        mix_kernel,
        in_specs=[scalar] * 3 + [pl.BlockSpec(memory_space=pltpu.HBM)],
        out_specs=pl.BlockSpec(memory_space=pltpu.VMEM),
        out_shape=jax.ShapeDtypeStruct(shape, jnp.bfloat16),
        scratch_shapes=[
            pltpu.VMEM(shape, jnp.bfloat16),
            pltpu.SemaphoreType.DMA(shape[::2][:2]),
        ],
        compiler_params=pltpu.CompilerParams(vmem_limit_bytes=8 * MIB),
        cost_estimate=pl.CostEstimate(
            flops=8 * math.prod(shape), bytes_accessed=4 * math.prod(shape), transcendentals=0
        ),
        name="mixed_perambulators",
    )(slots, structures, weights, in_hbm(perambulators))


def diagram_kernel(places, *refs):
    tau_ref, out_ref, block_ref, sems = refs[-4:]
    count, spins, _, nvec, width = tau_ref.shape

    def copy(index, r):
        return pltpu.make_async_copy(block_ref.at[index, r], out_ref.at[index, r], sems.at[index, r])

    for index, entry in enumerate(places):
        real, imag = restored(sum(refs[number][at].astype(jnp.float32) for number, at in entry))
        square = jnp.concatenate(
            [jnp.concatenate([real, -imag], 1), jnp.concatenate([imag, real], 1)], 0
        ).astype(jnp.bfloat16)
        for r in range(spins):
            tau = tau_ref[index, r].reshape(2 * nvec, width)
            block = jnp.dot(square, tau, preferred_element_type=jnp.float32)
            block_ref[index, r] = block.astype(jnp.bfloat16).reshape(2, nvec, width)
            copy(index, r).start()
    for index in range(count):
        for r in range(spins):
            copy(index, r).wait()


def diagrams(entries, tau):
    count, spins, _, nvec, width = tau.shape
    whole = pl.BlockSpec(memory_space=pltpu.VMEM)
    arrays = [array for entry in entries for array, _ in entry]
    places = []
    for entry in entries:
        start = sum(len(one) for one in places)
        places.append([(start + number, at) for number, (_, at) in enumerate(entry)])
    return pl.pallas_call(
        functools.partial(diagram_kernel, places),
        in_specs=[whole] * (len(arrays) + 1),
        out_specs=pl.BlockSpec(memory_space=pltpu.HBM),
        out_shape=jax.ShapeDtypeStruct(tau.shape, jnp.bfloat16),
        scratch_shapes=[
            pltpu.VMEM(tau.shape, jnp.bfloat16),
            pltpu.SemaphoreType.DMA((count, spins)),
        ],
        compiler_params=pltpu.CompilerParams(vmem_limit_bytes=8 * MIB),
        cost_estimate=pl.CostEstimate(
            flops=8 * nvec * nvec * width * spins * count, bytes_accessed=4 * tau.size, transcendentals=0
        ),
        name="diagrams",
    )(*arrays, tau)


def body(eigvecs, gauge_links, momenta, spin_mix, perambulators, contraction_list):
    slices, _, _, nvec, depth, plane = eigvecs.shape
    devices = lax.axis_size(SITES)
    position = lax.axis_index(SITES)
    bits = devices.bit_length() - 1
    total_z = depth * devices
    width = depth * plane
    scale = 1.0 / math.sqrt(NCOL * plane * total_z)
    place = position.reshape(1)
    rows, after, place = gathered(contraction_list, eigvecs, place)
    upper = shifted(after[:, :, :, :, :1, :], SITES, -1)
    vectors = eigvecs.reshape(slices, 2, NCOL, nvec, width)
    links = gauge_links.reshape(slices, 3, 2, NCOL, NCOL, 1, width)
    item, own, phase, turn = plane_items(place, momenta, vectors, links, total_z, plane, scale)
    chosen = contraction_list[:, 2] - position * perambulators.shape[0]
    tau = mixed_perambulators(chosen, contraction_list[:, 1], spin_mix.reshape(-1), perambulators)
    ahead = jnp.concatenate([eigvecs[:, :, :, :, 1:, :], upper], 4).reshape(vectors.shape)
    send = layer_items(1, rows, item, own, ahead, phase, turn, scale)
    keep = layer_items(0, rows, item, own, ahead, phase, turn, scale)
    slots = range(contraction_list.shape[0])
    other = exchanged(send, 1)
    sites = devices // 2
    chains = [
        Chain(
            {r: [(keep, slot * sites + r), (other, slot * sites + r)] for r in range(sites)},
            [2, 1, *range(3, bits)] if slot % 2 else [1, bits - 1, *range(2, bits - 1)],
        )
        for slot in slots
    ]
    for step in range(bits - 1):
        messages = [chain.chunks(step) for chain in chains]
        for part in range(len(messages[0])):
            for chain, far in zip(chains, messages):
                chain.send(step, far[part])
    return diagrams([chain.entries[0] for chain in chains], tau)


def solution(mesh):
    placed = (
        P("cfg", None, None, None, ("space", "diag"), None),
        P("cfg", None, None, None, None, ("space", "diag"), None),
        P(),
        P(),
        P(("cfg", "space", "diag"), None, None, None, None),
        P(("space", "diag"), None),
    )
    return jax.shard_map(
        body,
        mesh=mesh,
        in_specs=placed,
        out_specs=P(("cfg", "space", "diag"), None, None, None, None),
        check_vma=False,
    )
```

```python
import functools
import math

import jax
import jax.numpy as jnp
from jax import lax
from jax.experimental import pallas as pl
from jax.experimental.pallas import tpu as pltpu
from jax.sharding import PartitionSpec as P

NCOL = 3
NMOM = 4
NDISP = 4
LX = 16
LY = 16
LANES = 128
ROWS = 16
SITES = ("space", "diag")
MIB = 1024 * 1024
PLANE_LIMIT = 20 * MIB


def shifted(value, axis, by):
    size = lax.axis_size(axis)
    return lax.ppermute(value, axis, [(i, (i + by) % size) for i in range(size)])


def in_hbm(value):
    return pltpu.with_memory_space_constraint(value, pltpu.HBM)


def exchanged(value, mask):
    size = lax.axis_size(SITES)
    return lax.ppermute(value, SITES, [(i, i ^ mask) for i in range(size)])


def gathered(rows, early, late):
    bits = lax.axis_size(SITES).bit_length() - 1
    value = rows[None]
    for low in range(0, bits, 2):
        if low == 2:
            value, late = lax.optimization_barrier((value, late))
        arrived = [exchanged(value, step << low) for step in reversed(range(1, 1 << min(2, bits - low)))]
        if low == 0:
            arrived, early = lax.optimization_barrier((arrived, early))
        value = jnp.concatenate([value] + arrived[::-1])
    return value, early, late


def diagonal(value):
    size = value.shape[0]
    same = lax.broadcasted_iota(jnp.int32, value.shape, 0) == lax.broadcasted_iota(jnp.int32, value.shape, 1)
    return jnp.sum(jnp.where(same, value, 0.0), 0, keepdims=True).reshape(1, size)


def rounded(real, imag, left=None):
    planes = [value.astype(jnp.bfloat16) for value in (real, imag)]
    lost = [diagonal(value - plane.astype(jnp.float32)) for value, plane in zip((real, imag), planes)]
    tile = jnp.concatenate(lost + [jnp.zeros((ROWS - 2, real.shape[1]), jnp.float32)], 0)
    if left is not None:
        tile = tile + left
    return planes, tile.astype(jnp.bfloat16)


def store_rounded(ref, index, real, imag, left=None):
    nvec = real.shape[0]
    planes, tile = rounded(real, imag, left)
    ref[(*index, pl.ds(0, nvec))] = planes[0]
    ref[(*index, pl.ds(nvec, nvec))] = planes[1]
    ref[(*index, pl.ds(2 * nvec, ROWS))] = tile


def restored(total):
    nvec = total.shape[1]
    shape = (nvec, nvec)
    same = lax.broadcasted_iota(jnp.int32, shape, 0) == lax.broadcasted_iota(jnp.int32, shape, 1)
    return [
        total[part * nvec : (part + 1) * nvec] + jnp.where(same, total[2 * nvec + part : 2 * nvec + part + 1], 0.0)
        for part in range(2)
    ]


def color_product(matrix, real, imag, adjoint):
    rows = []
    for row in range(NCOL):
        real_part = imag_part = None
        for col in range(NCOL):
            if adjoint:
                mreal, mimag = matrix[0][col][row], matrix[1][col][row]
                one = mreal * real[col] + mimag * imag[col]
                two = mreal * imag[col] - mimag * real[col]
            else:
                mreal, mimag = matrix[0][row][col], matrix[1][row][col]
                one = mreal * real[col] - mimag * imag[col]
                two = mreal * imag[col] + mimag * real[col]
            real_part = one if real_part is None else real_part + one
            imag_part = two if imag_part is None else imag_part + two
        rows.append((real_part, imag_part))
    return rows


def color_loop(link, nvec, width, load, store, adjoint):
    height = math.gcd(nvec, 2 * ROWS)
    for lane in range(0, width, LANES):
        lanes = pl.ds(lane, LANES)
        matrix = [
            [[link(part, row, col, lanes) for col in range(NCOL)] for row in range(NCOL)] for part in range(2)
        ]
        for start in range(0, nvec, height):
            rows = pl.ds(start, height)
            real = [load(0, color, rows, lanes) for color in range(NCOL)]
            imag = [load(1, color, rows, lanes) for color in range(NCOL)]
            for color, (one, two) in enumerate(color_product(matrix, real, imag, adjoint)):
                store(0, color, rows, lanes, one)
                store(1, color, rows, lanes, two)


def fill_tables(position, total_z, plane, momenta_ref, phase_ref, turn_ref):
    width = phase_ref.shape[-1]
    flat = lax.broadcasted_iota(jnp.int32, (1, width), 1)
    xcoord = (flat % LX).astype(jnp.float32)
    ycoord = (flat % plane // LX).astype(jnp.float32)
    zcoord = (position * (width // plane) + flat // plane).astype(jnp.float32)
    for moment in range(NMOM):
        along_x = momenta_ref[moment, 0].astype(jnp.float32)
        along_y = momenta_ref[moment, 1].astype(jnp.float32)
        along_z = momenta_ref[moment, 2].astype(jnp.float32)
        angle = (
            2.0 * math.pi * (along_x * xcoord / LX + along_y * ycoord / LY + along_z * zcoord / total_z)
        )
        phase_ref[moment, 0] = jnp.cos(angle)
        phase_ref[moment, 1] = jnp.sin(angle)
        turn = jnp.full((1, turn_ref.shape[-1]), 2.0 * math.pi / total_z, jnp.float32) * along_z
        turn_ref[moment, 0] = jnp.cos(turn)
        turn_ref[moment, 1] = jnp.sin(turn)


def fill_moves(move_ref):
    width = move_ref.shape[-1]
    source = lax.broadcasted_iota(jnp.int32, (width, width), 0)
    site = lax.broadcasted_iota(jnp.int32, (width, width), 1)
    xcoord = site % LX
    ycoord = site // LX % LY
    for sign, by in enumerate((1, -1)):
        along_x = site - xcoord + (xcoord + LX + by) % LX
        along_y = site + ((ycoord + LY + by) % LY - ycoord) * LX
        move_ref[0, sign] = (source == along_x).astype(jnp.float32).astype(jnp.bfloat16)
        move_ref[1, sign] = (source == along_y).astype(jnp.float32).astype(jnp.bfloat16)


def plane_kernel(
    total_z, plane, scale,
    position_ref, momenta_in, vector_in, link_in,
    item_ref, own_ref, phase_ref, turn_ref,
    momenta_ref, vector_ref, link_ref,
    ahead_x_ref, ahead_y_ref, behind_x_ref, behind_y_ref, adjoint_x_ref, adjoint_y_ref,
    phased_ref, still_ref, moved_x_ref, moved_y_ref, move_ref, momenta_sem, sems,
):
    now = pl.program_id(0)
    slices, _, _, nvec, width = vector_ref.shape

    def copies(index):
        return (
            pltpu.make_async_copy(vector_in.at[index], vector_ref.at[index], sems.at[0, index]),
            pltpu.make_async_copy(link_in.at[index], link_ref.at[index], sems.at[1, index]),
        )

    @pl.when(now == 0)
    def _():
        moments = pltpu.make_async_copy(momenta_in, momenta_ref, momenta_sem)
        moments.start()
        for index in range(slices):
            for copy in copies(index):
                copy.start()
        fill_moves(move_ref)
        moments.wait()
        fill_tables(position_ref[0], total_z, plane, momenta_ref, phase_ref, turn_ref)

    for copy in copies(now):
        copy.wait()

    def linker(direction):
        return lambda part, row, col, lanes: link_ref[now, direction, part, row, col, :, lanes]

    def vector(part, color, rows, lanes):
        return vector_ref[now, part, color, rows, lanes].astype(jnp.float32)

    def gram(moved_ref, disp):
        product = lax.dot_general(
            phased_ref[...], moved_ref[...], (((1,), (1,)), ((), ())), preferred_element_type=jnp.float32
        )
        for moment in range(NMOM):
            start = 2 * moment * nvec
            upper = product[start : start + nvec]
            lower = product[start + nvec : start + 2 * nvec]
            factor = scale if disp == 0 else 0.5 * scale
            real = factor * (upper[:, :nvec] + lower[:, nvec:])
            imag = factor * (upper[:, nvec:] - lower[:, :nvec])
            store_rounded(item_ref, (0, moment, disp), real, imag)

    flat = vector_ref[now].reshape(2 * NCOL * nvec, width)
    for direction, ahead_ref in enumerate((ahead_x_ref, ahead_y_ref)):
        ahead_ref[...] = jnp.dot(
            flat, move_ref[direction, 0], preferred_element_type=jnp.float32
        ).reshape(ahead_ref.shape)

    for color in range(NCOL):
        span = pl.ds(color * width, width)
        for part in range(2):
            still_ref[pl.ds(part * nvec, nvec), span] = vector_ref[now, part, color]
        for start in range(0, nvec, ROWS):
            real = vector_ref[now, 0, color, pl.ds(start, ROWS), :].astype(jnp.float32)
            imag = vector_ref[now, 1, color, pl.ds(start, ROWS), :].astype(jnp.float32)
            for moment in range(NMOM):
                cosine = phase_ref[moment, 0]
                sine = phase_ref[moment, 1]
                first = 2 * moment * nvec + start
                phased_ref[pl.ds(first, ROWS), span] = (cosine * real - sine * imag).astype(jnp.bfloat16)
                phased_ref[pl.ds(first + nvec, ROWS), span] = (sine * real + cosine * imag).astype(jnp.bfloat16)
    gram(still_ref, 0)

    for direction, (adjoint_ref, behind_ref) in enumerate(
        ((adjoint_x_ref, behind_x_ref), (adjoint_y_ref, behind_y_ref))
    ):

        def adjoint(part, color, rows, lanes, value):
            adjoint_ref[part, color, rows, lanes] = value.astype(jnp.bfloat16)

        color_loop(linker(direction), nvec, width, vector, adjoint, True)
        behind_ref[...] = jnp.dot(
            adjoint_ref[...].reshape(2 * NCOL * nvec, width),
            move_ref[direction, 1],
            preferred_element_type=jnp.float32,
        ).reshape(behind_ref.shape)

    for direction, (ahead_ref, behind_ref, moved_ref) in enumerate(
        ((ahead_x_ref, behind_x_ref, moved_x_ref), (ahead_y_ref, behind_y_ref, moved_y_ref))
    ):

        def ahead(part, color, rows, lanes):
            return ahead_ref[part, color, rows, lanes]

        def forward(part, color, rows, lanes, value):
            moved_ref[
                pl.ds(part * nvec + rows.start, rows.size), pl.ds(color * width + lanes.start, lanes.size)
            ] = (value - behind_ref[part, color, rows, lanes]).astype(jnp.bfloat16)

        color_loop(linker(direction), nvec, width, ahead, forward, False)
        gram(moved_ref, direction + 1)

    def own(part, color, rows, lanes, value):
        own_ref[0, part, color, rows, lanes] = value

    color_loop(linker(2), nvec, width, vector, own, True)


def plane_items(position, momenta, vectors, links, total_z, plane, scale):
    slices, _, _, nvec, width = vectors.shape
    color_block = (2, NCOL, nvec, width)
    return pl.pallas_call(
        functools.partial(plane_kernel, total_z, plane, scale),
        grid=(slices,),
        in_specs=[pl.BlockSpec(memory_space=pltpu.SMEM)] + [pl.BlockSpec(memory_space=pltpu.HBM)] * 3,
        out_specs=[
            pl.BlockSpec((1, NMOM, NDISP - 1, 2 * nvec + ROWS, nvec), lambda t: (t, 0, 0, 0, 0)),
            pl.BlockSpec((1,) + color_block, lambda t: (t, 0, 0, 0, 0)),
            pl.BlockSpec((NMOM, 2, 1, width), lambda t: (0, 0, 0, 0)),
            pl.BlockSpec((NMOM, 2, 1, nvec), lambda t: (0, 0, 0, 0)),
        ],
        out_shape=[
            jax.ShapeDtypeStruct((slices, NMOM, NDISP - 1, 2 * nvec + ROWS, nvec), jnp.bfloat16),
            jax.ShapeDtypeStruct(vectors.shape, jnp.float32),
            jax.ShapeDtypeStruct((NMOM, 2, 1, width), jnp.float32),
            jax.ShapeDtypeStruct((NMOM, 2, 1, nvec), jnp.float32),
        ],
        scratch_shapes=[
            pltpu.SMEM(momenta.shape, jnp.int32),
            pltpu.VMEM(vectors.shape, jnp.bfloat16),
            pltpu.VMEM(links.shape, jnp.float32),
        ]
        + [pltpu.VMEM(color_block, jnp.float32)] * 4
        + [pltpu.VMEM(color_block, jnp.bfloat16)] * 2
        + [pltpu.VMEM((NMOM * 2 * nvec, NCOL * width), jnp.bfloat16)]
        + [pltpu.VMEM((2 * nvec, NCOL * width), jnp.bfloat16)] * 3
        + [
            pltpu.VMEM((2, 2, width, width), jnp.bfloat16),
            pltpu.SemaphoreType.DMA,
            pltpu.SemaphoreType.DMA((2, slices)),
        ],
        compiler_params=pltpu.CompilerParams(vmem_limit_bytes=PLANE_LIMIT),
        cost_estimate=pl.CostEstimate(
            flops=slices * 16 * NMOM * nvec * nvec * NCOL * width,
            bytes_accessed=6 * vectors.size + 4 * links.size,
            transcendentals=0,
        ),
        name="plane_items",
    )(position, in_hbm(momenta), in_hbm(vectors), in_hbm(links))


def layer_kernel(
    core, scale, rows_ref, item_ref, own_ref, ahead_ref, phase_ref, turn_ref, out_ref, lhs_ref, listed_ref
):
    nvec, width = own_ref.shape[3:]
    total = out_ref.shape[0]
    sites = rows_ref.shape[0] // 2

    def parts_of(place):
        item = rows_ref[2 * lax.rem(place, sites) + core, lax.div(place, sites), 0]
        rest = lax.rem(item, NMOM * NDISP)
        return lax.div(item, NMOM * NDISP), lax.div(rest, NDISP), lax.rem(rest, NDISP)

    def bond(place, lhs):
        slice_index, moment, _ = parts_of(place)
        cosine = phase_ref[moment, 0]
        sine = phase_ref[moment, 1]
        for color in range(NCOL):
            span = pl.ds(color * width, width)
            for part in range(2):
                value = own_ref[slice_index, part, color]
                lhs[pl.ds(part * nvec, nvec), span] = (cosine * value).astype(jnp.bfloat16)
                lhs[pl.ds((2 + part) * nvec, nvec), span] = (sine * value).astype(jnp.bfloat16)
        rhs = jnp.concatenate(
            [
                jnp.concatenate([ahead_ref[slice_index, part, color] for color in range(NCOL)], 1)
                for part in range(2)
            ],
            0,
        )
        gram = lax.dot_general(lhs[...], rhs, (((1,), (1,)), ((), ())), preferred_element_type=jnp.float32)
        block = [
            [gram[i * nvec : (i + 1) * nvec, j * nvec : (j + 1) * nvec] for j in range(2)] for i in range(4)
        ]
        cos_real = block[0][0] + block[1][1]
        cos_imag = block[0][1] - block[1][0]
        sin_real = block[2][0] + block[3][1]
        sin_imag = block[2][1] - block[3][0]
        half = 0.5 * scale
        turn_cos = half * turn_ref[moment, 0]
        turn_sin = half * turn_ref[moment, 1]
        back_real = cos_real - sin_imag
        back_imag = cos_imag + sin_real
        real = half * (cos_real + sin_imag) - (turn_cos * back_real - turn_sin * back_imag).T
        imag = half * (cos_imag - sin_real) + (turn_cos * back_imag + turn_sin * back_real).T
        return real, imag

    found = jnp.int32(0)
    for place in range(total):
        slice_index, moment, disp = parts_of(jnp.int32(place))
        out_ref[place] = item_ref[slice_index, moment, jnp.minimum(disp, NDISP - 2)]
        listed_ref[found] = place
        found = found + (disp == NDISP - 1).astype(jnp.int32)

    def finish(places):
        results = [bond(place, lhs_ref.at[index]) for index, place in enumerate(places)]
        for place, (real, imag) in zip(places, results):
            store_rounded(out_ref, (place,), real, imag)

    @pl.loop(0, lax.div(found, 2))
    def _(pair):
        finish([listed_ref[2 * pair], listed_ref[2 * pair + 1]])

    @pl.when(lax.rem(found, 2) == 1)
    def _():
        finish([listed_ref[found - 1]])


def layer_items(core, rows, item, own, ahead, phase, turn, scale):
    slices, _, _, nvec, width = own.shape
    devices, slots, _ = rows.shape
    total = slots * devices // 2
    whole = pl.BlockSpec(memory_space=pltpu.VMEM)
    return pl.pallas_call(
        functools.partial(layer_kernel, core, scale),
        in_specs=[pl.BlockSpec(memory_space=pltpu.SMEM)] + [whole] * 5,
        out_specs=whole,
        out_shape=jax.ShapeDtypeStruct((total, 2 * nvec + ROWS, nvec), jnp.bfloat16),
        scratch_shapes=[
            pltpu.VMEM((2, 4 * nvec, NCOL * width), jnp.bfloat16),
            pltpu.SMEM((total,), jnp.int32),
        ],
        compiler_params=pltpu.CompilerParams(vmem_limit_bytes=8 * MIB),
        cost_estimate=pl.CostEstimate(
            flops=total * 4 * nvec * nvec * NCOL * width,
            bytes_accessed=2 * own.size,
            transcendentals=0,
        ),
        name="layer_items",
    )(rows, item, own, ahead, phase, turn)


def add_kernel(places, *refs):
    for out_ref, entries in zip(refs[len(refs) - len(places) :], places):
        for index, entry in enumerate(entries):
            total = sum(refs[number][at].astype(jnp.float32) for number, at in entry)
            nvec = total.shape[1]
            if out_ref.dtype == jnp.float32:
                out_ref[index] = total
            else:
                left = total[2 * nvec :]
                store_rounded(out_ref, (index,), total[:nvec], total[nvec : 2 * nvec], left)


def added(groups):
    arrays = []

    def number(array):
        found = [place for place, other in enumerate(arrays) if other is array]
        if not found:
            arrays.append(array)
        return found[0] if found else len(arrays) - 1

    places = [[[(number(array), at) for array, at in entry] for entry in entries] for entries, _ in groups]
    tail = arrays[0].shape[1:]
    whole = pl.BlockSpec(memory_space=pltpu.VMEM)
    size = sum(len(entry) for entries in places for entry in entries) * math.prod(tail)
    return pl.pallas_call(
        functools.partial(add_kernel, places),
        in_specs=[whole] * len(arrays),
        out_specs=[whole] * len(groups),
        out_shape=[jax.ShapeDtypeStruct((len(entries),) + tail, dtype) for entries, dtype in groups],
        compiler_params=pltpu.CompilerParams(vmem_limit_bytes=8 * MIB),
        cost_estimate=pl.CostEstimate(flops=size, bytes_accessed=4 * size, transcendentals=0),
        name="added",
    )(*arrays)


class Chain:
    def __init__(self, entries, order):
        self.entries = entries
        self.order = order

    def chunks(self, step):
        far = [r for r in self.entries if r >> (self.order[step] - 1) & 1]
        if step + 1 == len(self.order):
            return [far]
        split = [[], []]
        for r in far:
            split[r >> (self.order[step + 1] - 1) & 1].append(r)
        return [split[1], split[0]]

    def send(self, step, far):
        bit = self.order[step]
        near = [r ^ (1 << (bit - 1)) for r in far]
        groups = [([self.entries[r] for r in far], jnp.bfloat16)]
        last = step + 1 == len(self.order)
        if step == 0 or last:
            kept = [self.entries[r] if step == 0 else self.entries[r][:2] for r in near]
            groups.append((kept, jnp.float32))
        outs = added(groups)
        arrived = exchanged(outs[0], 1 << bit)
        for at, r in enumerate(near):
            if step == 0:
                self.entries[r] = [(outs[1], at)]
            elif last:
                self.entries[r][:2] = [(outs[1], at)]
            self.entries[r].append((arrived, at))
        for r in far:
            del self.entries[r]


def mix_kernel(slot_ref, structure_ref, weight_ref, tau_in, out_ref, tau_ref, sems):
    count, spins, parts, nvec, width = out_ref.shape

    def copy(index, part):
        return pltpu.make_async_copy(
            tau_in.at[slot_ref[index], :, part], tau_ref.at[index, :, part], sems.at[index, part]
        )

    for index in range(count):
        for part in range(parts):
            copy(index, part).start()
    for index in range(count):
        base = structure_ref[index] * spins * spins
        weight = [[weight_ref[base + r * spins + s] for s in range(spins)] for r in range(spins)]
        for part in range(parts):
            copy(index, part).wait()
            for start in range(0, nvec, ROWS):
                rows = pl.ds(start, ROWS)
                tau = [tau_ref[index, s, part, rows, :].astype(jnp.float32) for s in range(spins)]
                for r in range(spins):
                    mixed = weight[r][0] * tau[0]
                    for s in range(1, spins):
                        mixed = mixed + weight[r][s] * tau[s]
                    out_ref[index, r, part, rows, :] = mixed.astype(jnp.bfloat16)


def mixed_perambulators(slots, structures, weights, perambulators):
    shape = (slots.shape[0],) + perambulators.shape[1:]
    scalar = pl.BlockSpec(memory_space=pltpu.SMEM)
    return pl.pallas_call(
        mix_kernel,
        in_specs=[scalar] * 3 + [pl.BlockSpec(memory_space=pltpu.HBM)],
        out_specs=pl.BlockSpec(memory_space=pltpu.VMEM),
        out_shape=jax.ShapeDtypeStruct(shape, jnp.bfloat16),
        scratch_shapes=[
            pltpu.VMEM(shape, jnp.bfloat16),
            pltpu.SemaphoreType.DMA(shape[::2][:2]),
        ],
        compiler_params=pltpu.CompilerParams(vmem_limit_bytes=8 * MIB),
        cost_estimate=pl.CostEstimate(
            flops=8 * math.prod(shape), bytes_accessed=4 * math.prod(shape), transcendentals=0
        ),
        name="mixed_perambulators",
    )(slots, structures, weights, in_hbm(perambulators))


def diagram_kernel(places, *refs):
    tau_ref, out_ref, block_ref, sems = refs[-4:]
    count, spins, _, nvec, width = tau_ref.shape

    def copy(index, r):
        return pltpu.make_async_copy(block_ref.at[index, r], out_ref.at[index, r], sems.at[index, r])

    for index, entry in enumerate(places):
        real, imag = restored(sum(refs[number][at].astype(jnp.float32) for number, at in entry))
        square = jnp.concatenate(
            [jnp.concatenate([real, -imag], 1), jnp.concatenate([imag, real], 1)], 0
        ).astype(jnp.bfloat16)
        for r in range(spins):
            tau = tau_ref[index, r].reshape(2 * nvec, width)
            block = jnp.dot(square, tau, preferred_element_type=jnp.float32)
            block_ref[index, r] = block.astype(jnp.bfloat16).reshape(2, nvec, width)
            copy(index, r).start()
    for index in range(count):
        for r in range(spins):
            copy(index, r).wait()


def diagrams(entries, tau):
    count, spins, _, nvec, width = tau.shape
    whole = pl.BlockSpec(memory_space=pltpu.VMEM)
    arrays = [array for entry in entries for array, _ in entry]
    places = []
    for entry in entries:
        start = sum(len(one) for one in places)
        places.append([(start + number, at) for number, (_, at) in enumerate(entry)])
    return pl.pallas_call(
        functools.partial(diagram_kernel, places),
        in_specs=[whole] * (len(arrays) + 1),
        out_specs=pl.BlockSpec(memory_space=pltpu.HBM),
        out_shape=jax.ShapeDtypeStruct(tau.shape, jnp.bfloat16),
        scratch_shapes=[
            pltpu.VMEM(tau.shape, jnp.bfloat16),
            pltpu.SemaphoreType.DMA((count, spins)),
        ],
        compiler_params=pltpu.CompilerParams(vmem_limit_bytes=8 * MIB),
        cost_estimate=pl.CostEstimate(
            flops=8 * nvec * nvec * width * spins * count, bytes_accessed=4 * tau.size, transcendentals=0
        ),
        name="diagrams",
    )(*arrays, tau)


def body(eigvecs, gauge_links, momenta, spin_mix, perambulators, contraction_list):
    slices, _, _, nvec, depth, plane = eigvecs.shape
    devices = lax.axis_size(SITES)
    position = lax.axis_index(SITES)
    bits = devices.bit_length() - 1
    total_z = depth * devices
    width = depth * plane
    scale = 1.0 / math.sqrt(NCOL * plane * total_z)
    place = position.reshape(1)
    rows, after, place = gathered(contraction_list, eigvecs, place)
    upper = shifted(after[:, :, :, :, :1, :], SITES, -1)
    vectors = eigvecs.reshape(slices, 2, NCOL, nvec, width)
    links = gauge_links.reshape(slices, 3, 2, NCOL, NCOL, 1, width)
    item, own, phase, turn = plane_items(place, momenta, vectors, links, total_z, plane, scale)
    chosen = contraction_list[:, 2] - position * perambulators.shape[0]
    tau = mixed_perambulators(chosen, contraction_list[:, 1], spin_mix.reshape(-1), perambulators)
    ahead = jnp.concatenate([eigvecs[:, :, :, :, 1:, :], upper], 4).reshape(vectors.shape)
    send = layer_items(1, rows, item, own, ahead, phase, turn, scale)
    keep = layer_items(0, rows, item, own, ahead, phase, turn, scale)
    slots = range(contraction_list.shape[0])
    other = exchanged(send, 1)
    sites = devices // 2
    chains = [
        Chain(
            {r: [(keep, slot * sites + r), (other, slot * sites + r)] for r in range(sites)},
            [2, 1, *range(3, bits)] if slot % 2 else [1, bits - 1, *range(2, bits - 1)],
        )
        for slot in slots
    ]
    for step in range(bits - 1):
        messages = [chain.chunks(step) for chain in chains]
        for part in range(len(messages[0])):
            for chain, far in zip(chains, messages):
                chain.send(step, far[part])
    return diagrams([chain.entries[0] for chain in chains], tau)


def solution(mesh):
    placed = (
        P("cfg", None, None, None, ("space", "diag"), None),
        P("cfg", None, None, None, None, ("space", "diag"), None),
        P(),
        P(),
        P(("cfg", "space", "diag"), None, None, None, None),
        P(("space", "diag"), None),
    )
    return jax.shard_map(
        body,
        mesh=mesh,
        in_specs=placed,
        out_specs=P(("cfg", "space", "diag"), None, None, None, None),
        check_vma=False,
    )
```

```python
import functools
import math

import jax
import jax.numpy as jnp
from jax import lax
from jax.experimental import pallas as pl
from jax.experimental.pallas import tpu as pltpu
from jax.sharding import PartitionSpec as P

NCOL = 3
NMOM = 4
NDISP = 4
LX = 16
LY = 16
LANES = 128
ROWS = 16
SITES = ("space", "diag")
MIB = 1024 * 1024
PLANE_LIMIT = 20 * MIB


def shifted(value, axis, by):
    size = lax.axis_size(axis)
    return lax.ppermute(value, axis, [(i, (i + by) % size) for i in range(size)])


def in_hbm(value):
    return pltpu.with_memory_space_constraint(value, pltpu.HBM)


def exchanged(value, mask):
    size = lax.axis_size(SITES)
    return lax.ppermute(value, SITES, [(i, i ^ mask) for i in range(size)])


def gathered(rows, early, late):
    bits = lax.axis_size(SITES).bit_length() - 1
    value = rows[None]
    for low in range(0, bits, 2):
        if low == 2:
            value, late = lax.optimization_barrier((value, late))
        arrived = [exchanged(value, step << low) for step in reversed(range(1, 1 << min(2, bits - low)))]
        if low == 0:
            arrived, early = lax.optimization_barrier((arrived, early))
        value = jnp.concatenate([value] + arrived[::-1])
    return value, early, late


def diagonal(value):
    size = value.shape[0]
    same = lax.broadcasted_iota(jnp.int32, value.shape, 0) == lax.broadcasted_iota(jnp.int32, value.shape, 1)
    return jnp.sum(jnp.where(same, value, 0.0), 0, keepdims=True).reshape(1, size)


def rounded(real, imag, left=None):
    planes = [value.astype(jnp.bfloat16) for value in (real, imag)]
    lost = [diagonal(value - plane.astype(jnp.float32)) for value, plane in zip((real, imag), planes)]
    tile = jnp.concatenate(lost + [jnp.zeros((ROWS - 2, real.shape[1]), jnp.float32)], 0)
    if left is not None:
        tile = tile + left
    return planes, tile.astype(jnp.bfloat16)


def store_rounded(ref, index, real, imag, left=None):
    nvec = real.shape[0]
    planes, tile = rounded(real, imag, left)
    ref[(*index, pl.ds(0, nvec))] = planes[0]
    ref[(*index, pl.ds(nvec, nvec))] = planes[1]
    ref[(*index, pl.ds(2 * nvec, ROWS))] = tile


def restored(total):
    nvec = total.shape[1]
    shape = (nvec, nvec)
    same = lax.broadcasted_iota(jnp.int32, shape, 0) == lax.broadcasted_iota(jnp.int32, shape, 1)
    return [
        total[part * nvec : (part + 1) * nvec] + jnp.where(same, total[2 * nvec + part : 2 * nvec + part + 1], 0.0)
        for part in range(2)
    ]


def color_product(matrix, real, imag, adjoint):
    rows = []
    for row in range(NCOL):
        real_part = imag_part = None
        for col in range(NCOL):
            if adjoint:
                mreal, mimag = matrix[0][col][row], matrix[1][col][row]
                one = mreal * real[col] + mimag * imag[col]
                two = mreal * imag[col] - mimag * real[col]
            else:
                mreal, mimag = matrix[0][row][col], matrix[1][row][col]
                one = mreal * real[col] - mimag * imag[col]
                two = mreal * imag[col] + mimag * real[col]
            real_part = one if real_part is None else real_part + one
            imag_part = two if imag_part is None else imag_part + two
        rows.append((real_part, imag_part))
    return rows


def color_loop(link, nvec, width, load, store, adjoint):
    height = math.gcd(nvec, 2 * ROWS)
    for lane in range(0, width, LANES):
        lanes = pl.ds(lane, LANES)
        matrix = [
            [[link(part, row, col, lanes) for col in range(NCOL)] for row in range(NCOL)] for part in range(2)
        ]
        for start in range(0, nvec, height):
            rows = pl.ds(start, height)
            real = [load(0, color, rows, lanes) for color in range(NCOL)]
            imag = [load(1, color, rows, lanes) for color in range(NCOL)]
            for color, (one, two) in enumerate(color_product(matrix, real, imag, adjoint)):
                store(0, color, rows, lanes, one)
                store(1, color, rows, lanes, two)


def fill_tables(position, total_z, plane, momenta_ref, phase_ref, turn_ref):
    width = phase_ref.shape[-1]
    flat = lax.broadcasted_iota(jnp.int32, (1, width), 1)
    xcoord = (flat % LX).astype(jnp.float32)
    ycoord = (flat % plane // LX).astype(jnp.float32)
    zcoord = (position * (width // plane) + flat // plane).astype(jnp.float32)
    for moment in range(NMOM):
        along_x = momenta_ref[moment, 0].astype(jnp.float32)
        along_y = momenta_ref[moment, 1].astype(jnp.float32)
        along_z = momenta_ref[moment, 2].astype(jnp.float32)
        angle = (
            2.0 * math.pi * (along_x * xcoord / LX + along_y * ycoord / LY + along_z * zcoord / total_z)
        )
        phase_ref[moment, 0] = jnp.cos(angle)
        phase_ref[moment, 1] = jnp.sin(angle)
        turn = jnp.full((1, turn_ref.shape[-1]), 2.0 * math.pi / total_z, jnp.float32) * along_z
        turn_ref[moment, 0] = jnp.cos(turn)
        turn_ref[moment, 1] = jnp.sin(turn)


def fill_moves(move_ref):
    width = move_ref.shape[-1]
    source = lax.broadcasted_iota(jnp.int32, (width, width), 0)
    site = lax.broadcasted_iota(jnp.int32, (width, width), 1)
    xcoord = site % LX
    ycoord = site // LX % LY
    for sign, by in enumerate((1, -1)):
        along_x = site - xcoord + (xcoord + LX + by) % LX
        along_y = site + ((ycoord + LY + by) % LY - ycoord) * LX
        move_ref[0, sign] = (source == along_x).astype(jnp.float32).astype(jnp.bfloat16)
        move_ref[1, sign] = (source == along_y).astype(jnp.float32).astype(jnp.bfloat16)


def plane_kernel(
    total_z, plane, scale,
    position_ref, momenta_in, vector_in, link_in,
    item_ref, own_ref, phase_ref, turn_ref,
    momenta_ref, vector_ref, link_ref,
    ahead_x_ref, ahead_y_ref, behind_x_ref, behind_y_ref, adjoint_x_ref, adjoint_y_ref,
    phased_ref, still_ref, moved_x_ref, moved_y_ref, move_ref, momenta_sem, sems,
):
    now = pl.program_id(0)
    slices, _, _, nvec, width = vector_ref.shape

    def copies(index):
        return (
            pltpu.make_async_copy(vector_in.at[index], vector_ref.at[index], sems.at[0, index]),
            pltpu.make_async_copy(link_in.at[index], link_ref.at[index], sems.at[1, index]),
        )

    @pl.when(now == 0)
    def _():
        moments = pltpu.make_async_copy(momenta_in, momenta_ref, momenta_sem)
        moments.start()
        for index in range(slices):
            for copy in copies(index):
                copy.start()
        fill_moves(move_ref)
        moments.wait()
        fill_tables(position_ref[0], total_z, plane, momenta_ref, phase_ref, turn_ref)

    for copy in copies(now):
        copy.wait()

    def linker(direction):
        return lambda part, row, col, lanes: link_ref[now, direction, part, row, col, :, lanes]

    def vector(part, color, rows, lanes):
        return vector_ref[now, part, color, rows, lanes].astype(jnp.float32)

    def gram(moved_ref, disp):
        product = lax.dot_general(
            phased_ref[...], moved_ref[...], (((1,), (1,)), ((), ())), preferred_element_type=jnp.float32
        )
        for moment in range(NMOM):
            start = 2 * moment * nvec
            upper = product[start : start + nvec]
            lower = product[start + nvec : start + 2 * nvec]
            factor = scale if disp == 0 else 0.5 * scale
            real = factor * (upper[:, :nvec] + lower[:, nvec:])
            imag = factor * (upper[:, nvec:] - lower[:, :nvec])
            store_rounded(item_ref, (0, moment, disp), real, imag)

    flat = vector_ref[now].reshape(2 * NCOL * nvec, width)
    for direction, ahead_ref in enumerate((ahead_x_ref, ahead_y_ref)):
        ahead_ref[...] = jnp.dot(
            flat, move_ref[direction, 0], preferred_element_type=jnp.float32
        ).reshape(ahead_ref.shape)

    for color in range(NCOL):
        span = pl.ds(color * width, width)
        for part in range(2):
            still_ref[pl.ds(part * nvec, nvec), span] = vector_ref[now, part, color]
        for start in range(0, nvec, ROWS):
            real = vector_ref[now, 0, color, pl.ds(start, ROWS), :].astype(jnp.float32)
            imag = vector_ref[now, 1, color, pl.ds(start, ROWS), :].astype(jnp.float32)
            for moment in range(NMOM):
                cosine = phase_ref[moment, 0]
                sine = phase_ref[moment, 1]
                first = 2 * moment * nvec + start
                phased_ref[pl.ds(first, ROWS), span] = (cosine * real - sine * imag).astype(jnp.bfloat16)
                phased_ref[pl.ds(first + nvec, ROWS), span] = (sine * real + cosine * imag).astype(jnp.bfloat16)
    gram(still_ref, 0)

    for direction, (adjoint_ref, behind_ref) in enumerate(
        ((adjoint_x_ref, behind_x_ref), (adjoint_y_ref, behind_y_ref))
    ):

        def adjoint(part, color, rows, lanes, value):
            adjoint_ref[part, color, rows, lanes] = value.astype(jnp.bfloat16)

        color_loop(linker(direction), nvec, width, vector, adjoint, True)
        behind_ref[...] = jnp.dot(
            adjoint_ref[...].reshape(2 * NCOL * nvec, width),
            move_ref[direction, 1],
            preferred_element_type=jnp.float32,
        ).reshape(behind_ref.shape)

    for direction, (ahead_ref, behind_ref, moved_ref) in enumerate(
        ((ahead_x_ref, behind_x_ref, moved_x_ref), (ahead_y_ref, behind_y_ref, moved_y_ref))
    ):

        def ahead(part, color, rows, lanes):
            return ahead_ref[part, color, rows, lanes]

        def forward(part, color, rows, lanes, value):
            moved_ref[
                pl.ds(part * nvec + rows.start, rows.size), pl.ds(color * width + lanes.start, lanes.size)
            ] = (value - behind_ref[part, color, rows, lanes]).astype(jnp.bfloat16)

        color_loop(linker(direction), nvec, width, ahead, forward, False)
        gram(moved_ref, direction + 1)

    def own(part, color, rows, lanes, value):
        own_ref[0, part, color, rows, lanes] = value

    color_loop(linker(2), nvec, width, vector, own, True)


def plane_items(position, momenta, vectors, links, total_z, plane, scale):
    slices, _, _, nvec, width = vectors.shape
    color_block = (2, NCOL, nvec, width)
    return pl.pallas_call(
        functools.partial(plane_kernel, total_z, plane, scale),
        grid=(slices,),
        in_specs=[pl.BlockSpec(memory_space=pltpu.SMEM)] + [pl.BlockSpec(memory_space=pltpu.HBM)] * 3,
        out_specs=[
            pl.BlockSpec((1, NMOM, NDISP - 1, 2 * nvec + ROWS, nvec), lambda t: (t, 0, 0, 0, 0)),
            pl.BlockSpec((1,) + color_block, lambda t: (t, 0, 0, 0, 0)),
            pl.BlockSpec((NMOM, 2, 1, width), lambda t: (0, 0, 0, 0)),
            pl.BlockSpec((NMOM, 2, 1, nvec), lambda t: (0, 0, 0, 0)),
        ],
        out_shape=[
            jax.ShapeDtypeStruct((slices, NMOM, NDISP - 1, 2 * nvec + ROWS, nvec), jnp.bfloat16),
            jax.ShapeDtypeStruct(vectors.shape, jnp.float32),
            jax.ShapeDtypeStruct((NMOM, 2, 1, width), jnp.float32),
            jax.ShapeDtypeStruct((NMOM, 2, 1, nvec), jnp.float32),
        ],
        scratch_shapes=[
            pltpu.SMEM(momenta.shape, jnp.int32),
            pltpu.VMEM(vectors.shape, jnp.bfloat16),
            pltpu.VMEM(links.shape, jnp.float32),
        ]
        + [pltpu.VMEM(color_block, jnp.float32)] * 4
        + [pltpu.VMEM(color_block, jnp.bfloat16)] * 2
        + [pltpu.VMEM((NMOM * 2 * nvec, NCOL * width), jnp.bfloat16)]
        + [pltpu.VMEM((2 * nvec, NCOL * width), jnp.bfloat16)] * 3
        + [
            pltpu.VMEM((2, 2, width, width), jnp.bfloat16),
            pltpu.SemaphoreType.DMA,
            pltpu.SemaphoreType.DMA((2, slices)),
        ],
        compiler_params=pltpu.CompilerParams(vmem_limit_bytes=PLANE_LIMIT),
        cost_estimate=pl.CostEstimate(
            flops=slices * 16 * NMOM * nvec * nvec * NCOL * width,
            bytes_accessed=6 * vectors.size + 4 * links.size,
            transcendentals=0,
        ),
        name="plane_items",
    )(position, in_hbm(momenta), in_hbm(vectors), in_hbm(links))


def layer_kernel(
    core, scale, rows_ref, item_ref, own_ref, ahead_ref, phase_ref, turn_ref, out_ref, lhs_ref, listed_ref
):
    nvec, width = own_ref.shape[3:]
    total = out_ref.shape[0]
    sites = rows_ref.shape[0] // 2

    def parts_of(place):
        item = rows_ref[2 * lax.rem(place, sites) + core, lax.div(place, sites), 0]
        rest = lax.rem(item, NMOM * NDISP)
        return lax.div(item, NMOM * NDISP), lax.div(rest, NDISP), lax.rem(rest, NDISP)

    def bond(place, lhs):
        slice_index, moment, _ = parts_of(place)
        cosine = phase_ref[moment, 0]
        sine = phase_ref[moment, 1]
        for color in range(NCOL):
            span = pl.ds(color * width, width)
            for part in range(2):
                value = own_ref[slice_index, part, color]
                lhs[pl.ds(part * nvec, nvec), span] = (cosine * value).astype(jnp.bfloat16)
                lhs[pl.ds((2 + part) * nvec, nvec), span] = (sine * value).astype(jnp.bfloat16)
        rhs = jnp.concatenate(
            [
                jnp.concatenate([ahead_ref[slice_index, part, color] for color in range(NCOL)], 1)
                for part in range(2)
            ],
            0,
        )
        gram = lax.dot_general(lhs[...], rhs, (((1,), (1,)), ((), ())), preferred_element_type=jnp.float32)
        block = [
            [gram[i * nvec : (i + 1) * nvec, j * nvec : (j + 1) * nvec] for j in range(2)] for i in range(4)
        ]
        cos_real = block[0][0] + block[1][1]
        cos_imag = block[0][1] - block[1][0]
        sin_real = block[2][0] + block[3][1]
        sin_imag = block[2][1] - block[3][0]
        half = 0.5 * scale
        turn_cos = half * turn_ref[moment, 0]
        turn_sin = half * turn_ref[moment, 1]
        back_real = cos_real - sin_imag
        back_imag = cos_imag + sin_real
        real = half * (cos_real + sin_imag) - (turn_cos * back_real - turn_sin * back_imag).T
        imag = half * (cos_imag - sin_real) + (turn_cos * back_imag + turn_sin * back_real).T
        return real, imag

    found = jnp.int32(0)
    for place in range(total):
        slice_index, moment, disp = parts_of(jnp.int32(place))
        out_ref[place] = item_ref[slice_index, moment, jnp.minimum(disp, NDISP - 2)]
        listed_ref[found] = place
        found = found + (disp == NDISP - 1).astype(jnp.int32)

    def finish(places):
        results = [bond(place, lhs_ref.at[index]) for index, place in enumerate(places)]
        for place, (real, imag) in zip(places, results):
            store_rounded(out_ref, (place,), real, imag)

    @pl.loop(0, lax.div(found, 2))
    def _(pair):
        finish([listed_ref[2 * pair], listed_ref[2 * pair + 1]])

    @pl.when(lax.rem(found, 2) == 1)
    def _():
        finish([listed_ref[found - 1]])


def layer_items(core, rows, item, own, ahead, phase, turn, scale):
    slices, _, _, nvec, width = own.shape
    devices, slots, _ = rows.shape
    total = slots * devices // 2
    whole = pl.BlockSpec(memory_space=pltpu.VMEM)
    return pl.pallas_call(
        functools.partial(layer_kernel, core, scale),
        in_specs=[pl.BlockSpec(memory_space=pltpu.SMEM)] + [whole] * 5,
        out_specs=whole,
        out_shape=jax.ShapeDtypeStruct((total, 2 * nvec + ROWS, nvec), jnp.bfloat16),
        scratch_shapes=[
            pltpu.VMEM((2, 4 * nvec, NCOL * width), jnp.bfloat16),
            pltpu.SMEM((total,), jnp.int32),
        ],
        compiler_params=pltpu.CompilerParams(vmem_limit_bytes=8 * MIB),
        cost_estimate=pl.CostEstimate(
            flops=total * 4 * nvec * nvec * NCOL * width,
            bytes_accessed=2 * own.size,
            transcendentals=0,
        ),
        name="layer_items",
    )(rows, item, own, ahead, phase, turn)


def add_kernel(places, *refs):
    for out_ref, entries in zip(refs[len(refs) - len(places) :], places):
        for index, entry in enumerate(entries):
            total = sum(refs[number][at].astype(jnp.float32) for number, at in entry)
            nvec = total.shape[1]
            if out_ref.dtype == jnp.float32:
                out_ref[index] = total
            else:
                left = total[2 * nvec :]
                store_rounded(out_ref, (index,), total[:nvec], total[nvec : 2 * nvec], left)


def added(groups):
    arrays = []

    def number(array):
        found = [place for place, other in enumerate(arrays) if other is array]
        if not found:
            arrays.append(array)
        return found[0] if found else len(arrays) - 1

    places = [[[(number(array), at) for array, at in entry] for entry in entries] for entries, _ in groups]
    tail = arrays[0].shape[1:]
    whole = pl.BlockSpec(memory_space=pltpu.VMEM)
    size = sum(len(entry) for entries in places for entry in entries) * math.prod(tail)
    return pl.pallas_call(
        functools.partial(add_kernel, places),
        in_specs=[whole] * len(arrays),
        out_specs=[whole] * len(groups),
        out_shape=[jax.ShapeDtypeStruct((len(entries),) + tail, dtype) for entries, dtype in groups],
        compiler_params=pltpu.CompilerParams(vmem_limit_bytes=8 * MIB),
        cost_estimate=pl.CostEstimate(flops=size, bytes_accessed=4 * size, transcendentals=0),
        name="added",
    )(*arrays)


class Chain:
    def __init__(self, entries, order):
        self.entries = entries
        self.order = order

    def chunks(self, step):
        far = [r for r in self.entries if r >> (self.order[step] - 1) & 1]
        if step + 1 == len(self.order):
            return [far]
        split = [[], []]
        for r in far:
            split[r >> (self.order[step + 1] - 1) & 1].append(r)
        return [split[1], split[0]]

    def send(self, step, far):
        bit = self.order[step]
        near = [r ^ (1 << (bit - 1)) for r in far]
        groups = [([self.entries[r] for r in far], jnp.bfloat16)]
        last = step + 1 == len(self.order)
        if step == 0 or last:
            kept = [self.entries[r] if step == 0 else self.entries[r][:2] for r in near]
            groups.append((kept, jnp.float32))
        outs = added(groups)
        arrived = exchanged(outs[0], 1 << bit)
        for at, r in enumerate(near):
            if step == 0:
                self.entries[r] = [(outs[1], at)]
            elif last:
                self.entries[r][:2] = [(outs[1], at)]
            self.entries[r].append((arrived, at))
        for r in far:
            del self.entries[r]


def mix_kernel(slot_ref, structure_ref, weight_ref, tau_in, out_ref, tau_ref, sems):
    count, spins, parts, nvec, width = out_ref.shape

    half = nvec // 2

    def copy(index, part, piece):
        rows = pl.ds(piece * half, half)
        return pltpu.make_async_copy(
            tau_in.at[slot_ref[index], :, part, rows],
            tau_ref.at[index, :, part, rows],
            sems.at[index, part, piece],
        )

    pieces = [(index, part, piece) for index in range(count) for part in range(parts) for piece in range(2)]
    for place in pieces:
        copy(*place).start()
    for index, part, piece in pieces:
        base = structure_ref[index] * spins * spins
        weight = [[weight_ref[base + r * spins + s] for s in range(spins)] for r in range(spins)]
        copy(index, part, piece).wait()
        for start in range(piece * half, (piece + 1) * half, ROWS):
            rows = pl.ds(start, ROWS)
            tau = [tau_ref[index, s, part, rows, :].astype(jnp.float32) for s in range(spins)]
            for r in range(spins):
                mixed = weight[r][0] * tau[0]
                for s in range(1, spins):
                    mixed = mixed + weight[r][s] * tau[s]
                out_ref[index, r, part, rows, :] = mixed.astype(jnp.bfloat16)


def mixed_perambulators(slots, structures, weights, perambulators):
    shape = (slots.shape[0],) + perambulators.shape[1:]
    scalar = pl.BlockSpec(memory_space=pltpu.SMEM)
    return pl.pallas_call(
        mix_kernel,
        in_specs=[scalar] * 3 + [pl.BlockSpec(memory_space=pltpu.HBM)],
        out_specs=pl.BlockSpec(memory_space=pltpu.VMEM),
        out_shape=jax.ShapeDtypeStruct(shape, jnp.bfloat16),
        scratch_shapes=[
            pltpu.VMEM(shape, jnp.bfloat16),
            pltpu.SemaphoreType.DMA(shape[::2][:2] + (2,)),
        ],
        compiler_params=pltpu.CompilerParams(vmem_limit_bytes=8 * MIB),
        cost_estimate=pl.CostEstimate(
            flops=8 * math.prod(shape), bytes_accessed=4 * math.prod(shape), transcendentals=0
        ),
        name="mixed_perambulators",
    )(slots, structures, weights, in_hbm(perambulators))


def diagram_kernel(places, *refs):
    tau_ref, out_ref, block_ref, sems = refs[-4:]
    count, spins, _, nvec, width = tau_ref.shape

    def copy(index, r):
        return pltpu.make_async_copy(block_ref.at[index, r], out_ref.at[index, r], sems.at[index, r])

    for index, entry in enumerate(places):
        real, imag = restored(sum(refs[number][at].astype(jnp.float32) for number, at in entry))
        square = jnp.concatenate(
            [jnp.concatenate([real, -imag], 1), jnp.concatenate([imag, real], 1)], 0
        ).astype(jnp.bfloat16)
        for r in range(spins):
            tau = tau_ref[index, r].reshape(2 * nvec, width)
            block = jnp.dot(square, tau, preferred_element_type=jnp.float32)
            block_ref[index, r] = block.astype(jnp.bfloat16).reshape(2, nvec, width)
            copy(index, r).start()
    for index in range(count):
        for r in range(spins):
            copy(index, r).wait()


def diagrams(entries, tau):
    count, spins, _, nvec, width = tau.shape
    whole = pl.BlockSpec(memory_space=pltpu.VMEM)
    arrays = [array for entry in entries for array, _ in entry]
    places = []
    for entry in entries:
        start = sum(len(one) for one in places)
        places.append([(start + number, at) for number, (_, at) in enumerate(entry)])
    return pl.pallas_call(
        functools.partial(diagram_kernel, places),
        in_specs=[whole] * (len(arrays) + 1),
        out_specs=pl.BlockSpec(memory_space=pltpu.HBM),
        out_shape=jax.ShapeDtypeStruct(tau.shape, jnp.bfloat16),
        scratch_shapes=[
            pltpu.VMEM(tau.shape, jnp.bfloat16),
            pltpu.SemaphoreType.DMA((count, spins)),
        ],
        compiler_params=pltpu.CompilerParams(vmem_limit_bytes=8 * MIB),
        cost_estimate=pl.CostEstimate(
            flops=8 * nvec * nvec * width * spins * count, bytes_accessed=4 * tau.size, transcendentals=0
        ),
        name="diagrams",
    )(*arrays, tau)


def body(eigvecs, gauge_links, momenta, spin_mix, perambulators, contraction_list):
    slices, _, _, nvec, depth, plane = eigvecs.shape
    devices = lax.axis_size(SITES)
    position = lax.axis_index(SITES)
    bits = devices.bit_length() - 1
    total_z = depth * devices
    width = depth * plane
    scale = 1.0 / math.sqrt(NCOL * plane * total_z)
    place = position.reshape(1)
    rows, after, place = gathered(contraction_list, eigvecs, place)
    upper = shifted(after[:, :, :, :, :1, :], SITES, -1)
    vectors = eigvecs.reshape(slices, 2, NCOL, nvec, width)
    links = gauge_links.reshape(slices, 3, 2, NCOL, NCOL, 1, width)
    item, own, phase, turn = plane_items(place, momenta, vectors, links, total_z, plane, scale)
    chosen = contraction_list[:, 2] - position * perambulators.shape[0]
    tau = mixed_perambulators(chosen, contraction_list[:, 1], spin_mix.reshape(-1), perambulators)
    ahead = jnp.concatenate([eigvecs[:, :, :, :, 1:, :], upper], 4).reshape(vectors.shape)
    send = layer_items(1, rows, item, own, ahead, phase, turn, scale)
    keep = layer_items(0, rows, item, own, ahead, phase, turn, scale)
    slots = range(contraction_list.shape[0])
    other = exchanged(send, 1)
    sites = devices // 2
    chains = [
        Chain(
            {r: [(keep, slot * sites + r), (other, slot * sites + r)] for r in range(sites)},
            [2, 1, *range(3, bits)] if slot % 2 else [1, bits - 1, *range(2, bits - 1)],
        )
        for slot in slots
    ]
    for step in range(bits - 1):
        messages = [chain.chunks(step) for chain in chains]
        for part in range(len(messages[0])):
            for chain, far in zip(chains, messages):
                chain.send(step, far[part])
    return diagrams([chain.entries[0] for chain in chains], tau)


def solution(mesh):
    placed = (
        P("cfg", None, None, None, ("space", "diag"), None),
        P("cfg", None, None, None, None, ("space", "diag"), None),
        P(),
        P(),
        P(("cfg", "space", "diag"), None, None, None, None),
        P(("space", "diag"), None),
    )
    return jax.shard_map(
        body,
        mesh=mesh,
        in_specs=placed,
        out_specs=P(("cfg", "space", "diag"), None, None, None, None),
        check_vma=False,
    )
```
